32 devices in a mesh: groups: 2 (over y), space: 4 (over z), member: 4 (over x, core).
Axes of the slice: x: 2, y: 2, z: 4, core: 2. Of those that a mesh axis runs over, the one named last changes fastest.
Arguments:
- latent: bfloat16 [8, 8192, 256], P('member', ('groups', 'space')), parts along dimension 1, may hold values from -6 to 6
- neighbours: int32 [4, 12288], P(None, ('groups', 'space')), parts along dimension 1, may hold values from 0 to 1535
- weights: float32 [4, 12288], P(None, ('groups', 'space')), parts along dimension 1, may hold values from 0.1 to 1
- targets: bfloat16 [12288, 128], P(('groups', 'space')), parts along dimension 0, may hold values from -6 to 6
- counts: int32 [8], P('groups'), parts along dimension 0, may hold values from 1 to 1536, 2048 in all
- w_one: bfloat16 [256, 256], replicated, may hold values from -0.375 to 0.375
- b_one: float32 [256], replicated, may hold values from -3 to 3
- w_two: bfloat16 [256, 256], replicated, may hold values from -0.375 to 0.375
- b_two: float32 [256], replicated, may hold values from -3 to 3
- w_three: bfloat16 [256, 128], replicated, may hold values from -0.375 to 0.375
Outputs:
- region_score: float32 [8], P('groups'), parts along dimension 0
- latent_grad: bfloat16 [8, 8192, 256], P('member', ('groups', 'space')), parts along dimension 1
- w_one_grad: float32 [512, 256], P('groups'), parts along dimension 0
- b_one_grad: float32 [512], P('groups'), parts along dimension 0
- w_two_grad: float32 [512, 256], P('groups'), parts along dimension 0
- b_two_grad: float32 [512], P('groups'), parts along dimension 0
- w_three_grad: float32 [512, 128], P('groups'), parts along dimension 0
The draws below stay inside these ranges and needn't reach their ends.
There are 2 independent parts, one for each index of `groups`. The reference program is written for one: setup_inputs(seed, part) draws one part's arguments, and reference() takes and returns one part's arrays. A program takes and returns all parts, laid end to end along the dimension named above; an argument that names none is the same for every part. Nothing has to cross between parts.
Inputs may be any that keep to these rules, and one draw needn't show every extreme that they name: The counts of one draw sum to 2048 and the largest equals 1536. `neighbours`: an entry below 256 names one of the last 256 nodes of the previous region, an entry of 1280 or more one of the first 256 nodes of the next region; the regions close into a loop.
All inputs are finite; a program needn't handle non-finite values.
Results may differ from the reference program's by a relative error of at most 0.018.
Values may be sent and summed in bfloat16 or wider, within the bound.
No kernel may reach another device: no remote copies, remote signals or barrier semaphores. Data moves between devices by JAX's collectives and lax.ppermute only.
A program may use at most 128 MiB of HBM per device.

```python
import math
import jax
import jax.numpy as jnp
import numpy as np
from jax import lax

F = 256
HID = 256
C = 128
K = 4
NODES_DEV = 1024
OBS_MEAN = 512
HALO = 256
OBS_CAP = 1536
M = 8
NODES = 4096
OBS_ALL = 6144
OBS_TOTAL = 2048
N_SPACE = 4


def with_ends(entries, rng, least, largest):
    spot = [jax.random.randint(jax.random.fold_in(rng, axis), (), 0, length) for axis, length in enumerate(entries.shape)]
    main_axis = entries.shape.index(max(entries.shape))
    beside = spot[:main_axis] + [(spot[main_axis] + 1) % entries.shape[main_axis]] + spot[main_axis + 1:]
    return entries.at[tuple(spot)].set(least).at[tuple(beside)].set(largest)


def level_of(key, dims, cuts, smallest, largest):
    def one(axis_at, shards_of):
        draws = jax.random.uniform(jax.random.fold_in(jax.random.fold_in(key, 6), axis_at), (shards_of,), jnp.float32, smallest / len(cuts), largest / len(cuts))
        return jnp.repeat(jnp.exp(draws), dims[axis_at] // shards_of).reshape((-1,) + (1,) * (len(dims) - axis_at - 1))

    factor_of = one(*cuts[0])
    for cut in cuts[1:]:
        factor_of = factor_of * one(*cut)
    return factor_of


def length_profile(number_of, total, most, skew):
    portions = [(1 << 20) // math.isqrt(standing ** skew) + 1 for standing in range(2, number_of + 1)]
    spare, given = total - most - (number_of - 1), [1] * (number_of - 1)
    while spare > 0:
        movable = [i for i in range(number_of - 1) if given[i] < most]
        whole, left = sum([portions[i] for i in movable]), spare
        for i in movable:
            more = min(most - given[i], max(1, left * portions[i] // whole), spare)
            given[i] = given[i] + more
            spare = spare - more
    return np.array([most] + given)


def ragged_sizes(key, amount, total, most, skew):
    if amount == 2:
        one = jax.random.randint(key, (), max(1, total - most), min(most, total - 1) + 1)
        return jnp.stack([one, total - one])
    lengths = jnp.asarray(length_profile(amount, total, most, skew), jnp.int32)
    twos = (amount - 1) // 2
    source_of, receiver = lengths[1:1 + 2 * twos:2], lengths[2:2 + 2 * twos:2]
    slack = jnp.minimum(source_of - 1, most - receiver)
    shifted = jax.random.randint(jax.random.fold_in(key, 1), (twos,), 0, 1 << 20) % (slack + 1)
    lengths = lengths.at[1:1 + 2 * twos:2].set(source_of - shifted).at[2:2 + 2 * twos:2].set(receiver + shifted)
    return lengths[jax.random.permutation(jax.random.fold_in(key, 2), amount)]


def centred(stream_key, dims, scale, limit, cuts=(), kind=jnp.bfloat16):
    gain = level_of(stream_key, dims, cuts, -0.22, 0.18) if cuts else 1.0
    values = jax.random.normal(stream_key, dims, jnp.float32) * scale * gain
    return jnp.minimum(jnp.maximum(values, -limit), limit).astype(kind)


def setup_inputs(seed: int = 0, part: int = 0) -> dict:
    key_of = jax.random.split(jax.random.key(seed), 11)
    own_keys = jax.random.split(jax.random.fold_in(key_of[10], part), 11)
    latent = centred(own_keys[0], (M, NODES, F), 1.0, 6.0, ((0, 4), (1, 4)))
    neighbours = with_ends(jax.random.randint(own_keys[1], (K, OBS_ALL), 0, NODES_DEV + 2 * HALO), jax.random.fold_in(own_keys[1], 1), 0, (NODES_DEV + 2 * HALO) - 1).astype(jnp.int32)
    weights = jnp.clip(0.1 + 0.9 * jax.random.uniform(own_keys[2], (K, OBS_ALL), jnp.float32) ** level_of(own_keys[2], (K, OBS_ALL), ((1, 4),), -0.2, 0.2), 0.1, 1.0)
    targets = centred(own_keys[3], (OBS_ALL, C), 1.0, 6.0, ((0, 4),))
    counts = ragged_sizes(own_keys[4], N_SPACE, OBS_TOTAL, OBS_CAP, 2).astype(jnp.int32)
    w_one = centred(key_of[5], (F, HID), F ** -0.5, 0.375)
    b_one = centred(key_of[6], (HID,), 0.5, 3.0, (), jnp.float32)
    w_two = centred(key_of[7], (HID, HID), HID ** -0.5, 0.375)
    b_two = centred(key_of[8], (HID,), 0.5, 3.0, (), jnp.float32)
    w_three = centred(key_of[9], (HID, C), HID ** -0.5, 0.375)
    return dict(latent=latent, neighbours=neighbours, weights=weights, targets=targets, counts=counts, w_one=w_one, b_one=b_one, w_two=w_two, b_two=b_two, w_three=w_three)


EPSILON = 1e-05

def dsilu(pre):
    sig = jax.nn.sigmoid(pre)
    return sig * (1.0 + pre * (1.0 - sig))

def left_dot(left, right):
    return lax.dot_general(left, right, (((0,), (0,)), ((), ())), preferred_element_type=jnp.float32)

def right_dot(left, right):
    return lax.dot_general(left, right, (((1,), (1,)), ((), ())), preferred_element_type=jnp.float32)

def decode_rows(inputs, w_one, b_one, w_two, b_two, w_three):
    pre_one = jnp.dot(inputs, w_one, preferred_element_type=jnp.float32) + b_one
    act_one = jax.nn.silu(pre_one).astype(jnp.bfloat16)
    pre_two = jnp.dot(act_one, w_two, preferred_element_type=jnp.float32) + b_two
    act_two = jax.nn.silu(pre_two).astype(jnp.bfloat16)
    decoded = jnp.dot(act_two, w_three, preferred_element_type=jnp.float32).astype(jnp.bfloat16)
    return ((pre_one, act_one, pre_two, act_two), decoded)

def decode_back(inputs, saved, d_decoded, w_one, w_two, w_three):
    pre_one, act_one, pre_two, act_two = saved
    g_three = left_dot(act_two, d_decoded)
    slope_two = right_dot(d_decoded, w_three) * dsilu(pre_two)
    d_two = slope_two.astype(jnp.bfloat16)
    g_btwo = lax.optimization_barrier(jnp.sum(slope_two, axis=0))
    g_two = left_dot(act_one, d_two)
    slope_one = right_dot(d_two, w_two) * dsilu(pre_one)
    d_one = slope_one.astype(jnp.bfloat16)
    g_bone = lax.optimization_barrier(jnp.sum(slope_one, axis=0))
    g_one = left_dot(inputs, d_one)
    d_inputs = right_dot(d_one, w_one).astype(jnp.bfloat16)
    return (d_inputs, (g_one, g_bone, g_two, g_btwo, g_three))

def ensemble_terms(own, everyone, target, offset):
    count = everyone.shape[0]
    all_values = everyone.astype(jnp.float32)
    target_values = target.astype(jnp.float32)

    def one_member(index):
        mine = lax.dynamic_index_in_dim(own, index, 0, keepdims=False).astype(jnp.float32)
        to_target = mine - target_values
        dist_target = jnp.sqrt(lax.optimization_barrier(jnp.sum(to_target * to_target, axis=-1)) + EPSILON)
        apart = mine[None] - all_values
        dist_pair = jnp.sqrt(lax.optimization_barrier(jnp.sum(apart * apart, axis=-1)) + EPSILON)
        other = (jnp.arange(count, dtype=jnp.int32) != offset + index).astype(jnp.float32)[:, None]
        score = dist_target - 0.5 / (count - 1) * lax.optimization_barrier(jnp.sum(other * dist_pair, axis=0))
        inverse = other / dist_pair
        grad = to_target / dist_target[:, None] - 1.0 / (count - 1) * lax.optimization_barrier(jnp.sum(apart * inverse[:, :, None], axis=0))
        return (score, grad)
    scores, grads = lax.map(one_member, jnp.arange(own.shape[0], dtype=jnp.int32))
    return (lax.optimization_barrier(jnp.sum(scores, axis=0)), grads)

def reference(latent, neighbours, weights, targets, counts, w_one, b_one, w_two, b_two, w_three):
    members, nodes, width = latent.shape
    regions = counts.shape[0]
    slots = OBS_CAP
    total = OBS_TOTAL
    ends = jnp.cumsum(counts).astype(jnp.int32)
    flat = jnp.arange(regions * slots, dtype=jnp.int32)
    home = flat // slots
    place = flat % slots
    live = place < counts[home]
    rank = (ends[home] - counts[home] + place).astype(jnp.int32)
    source = jnp.zeros((total,), jnp.int32).at[jnp.where(live, rank, total)].set(flat, mode='drop')
    row_region = source // slots
    local_index = neighbours[:, source]
    node = ((row_region[None, :] * NODES_DEV - HALO + local_index) % nodes).astype(jnp.int32)
    chosen = weights[:, source]
    mixed = jnp.zeros((members, total, width), jnp.float32)
    for k in range(K):
        mixed = mixed + chosen[k][None, :, None] * latent[:, node[k]].astype(jnp.float32)
    mixed = mixed.astype(jnp.bfloat16)
    inputs = mixed.reshape(members * total, width)
    saved, decoded = decode_rows(inputs, w_one, b_one, w_two, b_two, w_three)
    decoded = decoded.reshape(members, total, -1)
    score, grads = ensemble_terms(decoded, decoded, targets[source], jnp.int32(0))
    d_decoded = grads.astype(jnp.bfloat16).reshape(members * total, -1)
    d_inputs, sums = decode_back(inputs, saved, d_decoded, w_one, w_two, w_three)
    d_mixed = d_inputs.reshape(members, total, width).astype(jnp.float32)
    grad = jnp.zeros((members, nodes, width), jnp.float32)
    for k in range(K):
        grad = grad.at[:, node[k]].add(chosen[k][None, :, None] * d_mixed)
    tally = jnp.zeros((regions,), jnp.float32).at[row_region].add(score)
    region_score = tally / (OBS_MEAN * members)
    g_one, g_bone, g_two, g_btwo, g_three = sums
    return (region_score, grad.astype(jnp.bfloat16), g_one, g_bone, g_two, g_btwo, g_three)
```

```python
import jax
import jax.numpy as jnp
from jax import lax
from jax.experimental import pallas as pl
from jax.experimental.pallas import tpu as pltpu
from jax.sharding import PartitionSpec as P

K = 4
OBS_MEAN = 512
HALO = 256
EPSILON = 1e-05
BLOCK = 256
LANE = 128
CHUNK = 512
MIB = 1 << 20


def split(total, step):
    return [(start, min(step, total - start)) for start in range(0, total, step)]


def nt_dot(left, right):
    return lax.dot_general(
        left, right, (((1,), (1,)), ((), ())), preferred_element_type=jnp.float32
    )


def nn_dot(left, right):
    return jnp.dot(left, right, preferred_element_type=jnp.float32)


def kernel_call(body, out_shape, flops, moved, scratch=(), smem=0, operands=0):
    vmem = pl.BlockSpec(memory_space=pltpu.VMEM)
    specs = [pl.BlockSpec(memory_space=pltpu.SMEM)] * smem + [vmem] * (operands - smem)
    return pl.pallas_call(
        body,
        out_shape=out_shape,
        in_specs=specs,
        out_specs=jax.tree.map(lambda _: vmem, out_shape),
        scratch_shapes=list(scratch),
        compiler_params=pltpu.CompilerParams(vmem_limit_bytes=40 * MIB),
        cost_estimate=pl.CostEstimate(flops=flops, bytes_accessed=moved, transcendentals=0),
    )


def table_kernel(count_ref, nbr_ref, weight_ref, latent_ref, table_ref, part_ref):
    members, nodes, width = latent_ref.shape
    ext, slots = table_ref.shape
    live = lax.broadcasted_iota(jnp.int32, (1, slots), 1) < count_ref[0]
    nbr = [nbr_ref[k : k + 1, :] for k in range(K)]
    own = [jnp.where(live, weight_ref[k : k + 1, :], 0.0) for k in range(K)]
    joint = []
    for k in range(K):
        total = own[k]
        for j in range(K):
            if j != k:
                total = total + jnp.where(nbr[j] == nbr[k], own[j], 0.0)
        joint.append(total)
    groups = BLOCK // 16
    rows = (
        lax.broadcasted_iota(jnp.int32, (groups, 16, LANE), 0) * 16
        + lax.broadcasted_iota(jnp.int32, (groups, 16, LANE), 1)
    ).astype(jnp.float32).astype(jnp.bfloat16)
    for lo, size in split(slots, LANE):
        wide = [
            jnp.broadcast_to(joint[k][:, lo : lo + size], (16, size)).astype(jnp.bfloat16)
            for k in range(K)
        ]
        for b in range(ext // BLOCK):
            tile = jnp.zeros((groups, 16, size), jnp.bfloat16)
            for k in range(K):
                near = (nbr[k][:, lo : lo + size] - b * BLOCK).astype(jnp.float32)
                near = jnp.broadcast_to(near, (16, size)).astype(jnp.bfloat16)
                tile = jnp.where(rows[:, :, :size] == near[None], wide[k][None], tile)
            table_ref[b * BLOCK : (b + 1) * BLOCK, lo : lo + size] = tile.reshape(BLOCK, size)
    turned = jnp.concatenate([latent_ref[m].T for m in range(members)], axis=0)
    for lo, size in split(slots, CHUNK):
        part_ref[:, lo : lo + size] = nn_dot(
            turned, table_ref[HALO : HALO + nodes, lo : lo + size]
        )


def column(ref):
    height = ref.shape[1]
    return jnp.broadcast_to(ref[...], (LANE, height)).T


def forward_kernel(
    part_ref, table_ref, before_ref, after_ref, w_one_ref, b_one_ref, w_two_ref, b_two_ref, w_three_ref,
    mixed_ref, act_one_ref, slope_one_ref, act_two_ref, slope_two_ref, decoded_ref,
):
    members, _, width = before_ref.shape
    ext, slots = table_ref.shape
    ranks, _, _, share = decoded_ref.shape
    w_one, w_two, w_three = w_one_ref[...].T, w_two_ref[...].T, w_three_ref[...].T
    b_one, b_two = column(b_one_ref), column(b_two_ref)

    def layer(weight, bias, values, size):
        pre = nn_dot(weight, values) + jnp.concatenate([bias] * (size // LANE), axis=1)
        gate = 0.5 + 0.5 * jnp.tanh(0.5 * pre)
        act = pre * gate
        return act.astype(jnp.bfloat16), (gate + act * (1.0 - gate)).astype(jnp.bfloat16)

    for m in range(members):
        edges = jnp.concatenate([before_ref[m].T, after_ref[m].T], axis=1)
        for lo, size in split(slots, CHUNK):
            lanes = slice(lo, lo + size)
            rim = jnp.concatenate([table_ref[:HALO, lanes], table_ref[ext - HALO :, lanes]], axis=0)
            mixed = part_ref[m * width : (m + 1) * width, lanes] + nn_dot(edges, rim)
            mixed = mixed.astype(jnp.bfloat16)
            mixed_ref[m, :, lanes] = mixed
            act_one, slope_one = layer(w_one, b_one, mixed, size)
            act_one_ref[m, :, lanes] = act_one
            slope_one_ref[m, :, lanes] = slope_one
            act_two, slope_two = layer(w_two, b_two, act_one, size)
            act_two_ref[m, :, lanes] = act_two
            slope_two_ref[m, :, lanes] = slope_two
            decoded = nn_dot(w_three, act_two).astype(jnp.bfloat16)
            for q in range(ranks):
                first, last = max(lo, q * share), min(lo + size, (q + 1) * share)
                if first < last:
                    decoded_ref[q, m, :, first - q * share : last - q * share] = decoded[
                        :, first - lo : last - lo
                    ]


def score_kernel(where_ref, decoded_ref, target_ref, grad_ref, score_ref):
    ranks, members, channels, share = decoded_ref.shape
    count = ranks * members
    pairs = [(i, j) for i in range(count) for j in range(i + 1, count)]
    turned = target_ref[...].astype(jnp.float32).T
    total = jnp.zeros((1, LANE), jnp.float32)
    for lo, size in split(share, LANE):
        lanes = slice(lo, lo + size)

        def rows_of(c):
            values = [
                decoded_ref[i // members, i % members, c : c + 16, lanes].astype(jnp.float32)
                for i in range(count)
            ]
            return values, turned[c : c + 16, lanes]

        def fold(square):
            return square[:8] + square[8:]

        to_target = [jnp.zeros((8, size), jnp.float32)] * count
        apart = [jnp.zeros((8, size), jnp.float32)] * len(pairs)
        for c in range(0, channels, 16):
            values, goal = rows_of(c)
            for i in range(count):
                to_target[i] = to_target[i] + fold((values[i] - goal) ** 2)
            for p, (i, j) in enumerate(pairs):
                apart[p] = apart[p] + fold((values[i] - values[j]) ** 2)
        slot = where_ref[1] + lo + lax.broadcasted_iota(jnp.int32, (1, size), 1)
        live = (slot < where_ref[0]).astype(jnp.float32)
        score = jnp.zeros((1, size), jnp.float32)

        def inverse(square, scale):
            squared = jnp.sum(square, axis=0, keepdims=True) + EPSILON
            inv = lax.rsqrt(squared)
            return squared * inv * scale, jnp.broadcast_to(inv * (scale * live), (8, size))

        inv_target, inv_pair = [], []
        for square in to_target:
            dist, inv = inverse(square, 1.0)
            score = score + dist
            inv_target.append(inv)
        for square in apart:
            dist, inv = inverse(square, 1.0 / (count - 1))
            score = score - dist
            inv_pair.append(inv)
        score = score * live
        if size < LANE:
            score = jnp.concatenate([score, jnp.zeros((1, LANE - size), jnp.float32)], axis=1)
        total = total + score
        for c in range(0, channels, 16):
            values, goal = rows_of(c)
            halves = []
            for h in (0, 8):
                near = [v[h : h + 8] for v in values]
                grads = [(near[i] - goal[h : h + 8]) * inv_target[i] for i in range(count)]
                for p, (i, j) in enumerate(pairs):
                    term = (near[i] - near[j]) * inv_pair[p]
                    grads[i] = grads[i] - term
                    grads[j] = grads[j] + term
                halves.append(grads)
            for i in range(count):
                grad_ref[i // members, i % members, c : c + 16, lanes] = jnp.concatenate(
                    [halves[0][i], halves[1][i]], axis=0
                ).astype(jnp.bfloat16)
    score_ref[...] = total


def backward_kernel(
    region_ref, grad_ref, score_ref, mixed_ref, act_one_ref, slope_one_ref, act_two_ref, slope_two_ref,
    w_one_ref, w_two_ref, w_three_ref, sums_ref, d_mixed_ref, d_dec_ref, d_two_ref, d_one_ref,
):
    ranks, members, channels, share = grad_ref.shape
    _, width, slots = mixed_ref.shape
    hidden = act_one_ref.shape[1]
    for q in range(ranks):
        for m in range(members):
            d_dec_ref[m, :, q * share : (q + 1) * share] = grad_ref[q, m]
    w_one, w_two, w_three = w_one_ref[...], w_two_ref[...], w_three_ref[...]
    bias_one = jnp.zeros((hidden, LANE), jnp.float32)
    bias_two = jnp.zeros((hidden, LANE), jnp.float32)

    def lane_sum(values):
        return sum(values[:, lo : lo + LANE] for lo, _ in split(values.shape[1], LANE))

    for m in range(members):
        for lo, size in split(slots, CHUNK):
            lanes = slice(lo, lo + size)
            back = nn_dot(w_three, d_dec_ref[m, :, lanes]) * slope_two_ref[m, :, lanes].astype(jnp.float32)
            bias_two = bias_two + lane_sum(back)
            d_two = back.astype(jnp.bfloat16)
            d_two_ref[m, :, lanes] = d_two
            back = nn_dot(w_two, d_two) * slope_one_ref[m, :, lanes].astype(jnp.float32)
            bias_one = bias_one + lane_sum(back)
            d_one = back.astype(jnp.bfloat16)
            d_one_ref[m, :, lanes] = d_one
            d_mixed_ref[m * width : (m + 1) * width, lanes] = nn_dot(w_one, d_one).astype(jnp.bfloat16)

    def weight_sum(left_ref, right_ref):
        return sum(nt_dot(left_ref[m], right_ref[m]) for m in range(members))

    g_one = weight_sum(mixed_ref, d_one_ref)
    g_two = weight_sum(act_one_ref, d_two_ref)
    g_three = weight_sum(act_two_ref, d_dec_ref)
    kind = sums_ref.dtype
    sums_ref[:width] = g_one.astype(kind)
    sums_ref[width : width + hidden] = g_two.astype(kind)
    base, half = width + hidden, hidden // 2
    sums_ref[base : base + half, :channels] = g_three[:half].astype(kind)
    sums_ref[base : base + half, channels:] = g_three[half:].astype(kind)
    base = base + half
    rows_left = sums_ref.shape[0] - base
    region = lax.broadcasted_iota(jnp.int32, (1, hidden), 1) == region_ref[0]
    tally = jnp.where(region, jnp.sum(score_ref[...]), 0.0)
    high = tally.astype(jnp.bfloat16).astype(jnp.float32)
    extra = jnp.concatenate(
        [
            jnp.sum(bias_one.T, axis=0, keepdims=True),
            jnp.sum(bias_two.T, axis=0, keepdims=True),
            high,
            tally - high,
            jnp.zeros((12, hidden), jnp.float32),
        ],
        axis=0,
    )
    sums_ref[base : base + 16] = extra.astype(kind)
    if rows_left > 16:
        sums_ref[base + 16 :] = jnp.zeros((rows_left - 16, hidden), kind)


def rim_kernel(table_ref, d_mixed_ref, head_ref, tail_ref):
    members, _, width = head_ref.shape
    ext = table_ref.shape[0]
    for ref, start in ((head_ref, 0), (tail_ref, ext - HALO)):
        grads = nt_dot(table_ref[start : start + HALO, :], d_mixed_ref[...])
        for m in range(members):
            ref[m] = grads[:, m * width : (m + 1) * width].astype(jnp.bfloat16)


def own_kernel(table_ref, d_mixed_ref, own_ref):
    members, nodes, width = own_ref.shape
    for lo, size in split(nodes, BLOCK):
        grads = nt_dot(table_ref[HALO + lo : HALO + lo + size, :], d_mixed_ref[...])
        for m in range(members):
            own_ref[m, lo : lo + size] = grads[:, m * width : (m + 1) * width]


def shifted(shard, axis, by):
    length = lax.axis_size(axis)
    return lax.ppermute(shard, axis, [(i, (i + by) % length) for i in range(length)])


def per_device(latent, neighbours, weights, targets, counts, w_one, b_one, w_two, b_two, w_three):
    members, nodes, width = latent.shape
    slots, channels = targets.shape
    hidden = w_one.shape[1]
    ext = nodes + 2 * HALO
    region, regions = lax.axis_index("space"), lax.axis_size("space")
    rank, ranks = lax.axis_index("member"), lax.axis_size("member")
    share = slots // ranks
    bf16, f32 = jnp.bfloat16, jnp.float32
    shape = jax.ShapeDtypeStruct

    before = shifted(latent[:, nodes - HALO :], "space", 1)
    after = shifted(latent[:, :HALO], "space", -1)
    count = lax.dynamic_slice_in_dim(counts, region, 1)
    target = lax.dynamic_slice_in_dim(targets, rank * share, share)

    table, part = kernel_call(
        table_kernel,
        (shape((ext, slots), bf16), shape((members * width, slots), f32)),
        flops=2 * members * width * nodes * slots,
        moved=12 * MIB,
        smem=1,
        operands=4,
    )(count, neighbours, weights, latent)

    saved = shape((members, hidden, slots), bf16)
    mixed, act_one, slope_one, act_two, slope_two, decoded = kernel_call(
        forward_kernel,
        (shape((members, width, slots), bf16), saved, saved, saved, saved,
         shape((ranks, members, channels, share), bf16)),
        flops=2 * members * slots * (2 * HALO * width + width * hidden + hidden * hidden + hidden * channels),
        moved=16 * MIB,
        operands=9,
    )(part, table, before, after, w_one, b_one[None], w_two, b_two[None], w_three)

    everyone = lax.all_to_all(decoded, "member", 0, 0, tiled=True)
    place = jnp.concatenate([count, (rank * share)[None].astype(jnp.int32)])
    grads, score = kernel_call(
        score_kernel,
        (shape((ranks, members, channels, share), bf16), shape((1, LANE), f32)),
        flops=4 * MIB,
        moved=2 * MIB,
        smem=1,
        operands=3,
    )(place, everyone, target)
    d_decoded = lax.all_to_all(grads, "member", 0, 0, tiled=True)

    ways = regions * ranks
    used = width + hidden + hidden // 2 + 16
    rows = -(-used // (16 * ways)) * 16 * ways
    sums, d_mixed = kernel_call(
        backward_kernel,
        (shape((rows, hidden), bf16), shape((members * width, slots), bf16)),
        flops=4 * members * slots * (width * hidden + hidden * hidden + hidden * channels),
        moved=10 * MIB,
        scratch=(
            pltpu.VMEM((members, channels, slots), bf16),
            pltpu.VMEM((members, hidden, slots), bf16),
            pltpu.VMEM((members, hidden, slots), bf16),
        ),
        smem=1,
        operands=11,
    )(region[None].astype(jnp.int32), d_decoded, score, mixed, act_one, slope_one, act_two, slope_two,
      w_one, w_two, w_three)

    edge = shape((members, HALO, width), bf16)
    head, tail = kernel_call(
        rim_kernel, (edge, edge), flops=4 * members * HALO * width * slots, moved=3 * MIB, operands=2
    )(table, d_mixed)
    from_next = shifted(head, "space", -1)
    from_prev = shifted(tail, "space", 1)
    own = kernel_call(
        own_kernel,
        shape((members, nodes, width), f32),
        flops=2 * members * nodes * width * slots,
        moved=6 * MIB,
        operands=2,
    )(table, d_mixed)

    both = ("space", "member")
    pieces = lax.all_to_all(sums, both, 0, 0, tiled=True)
    piece = jnp.sum(pieces.reshape(ways, rows // ways, hidden).astype(f32), axis=0).astype(bf16)
    sums = lax.all_gather(piece, both, axis=0, tiled=True).astype(f32)

    latent_grad = jnp.concatenate(
        [own[:, :HALO] + from_prev.astype(f32), own[:, HALO : nodes - HALO],
         own[:, nodes - HALO :] + from_next.astype(f32)],
        axis=1,
    ).astype(bf16)
    g_one, g_two = sums[:width], sums[width : width + hidden]
    base, half = width + hidden, hidden // 2
    g_three = jnp.concatenate(
        [sums[base : base + half, :channels], sums[base : base + half, channels:]], axis=0
    )
    base = base + half
    tally = sums[base + 2, :regions] + sums[base + 3, :regions]
    region_score = tally / (OBS_MEAN * members * ranks)
    return (region_score, latent_grad, g_one, sums[base], g_two, sums[base + 1], g_three)


def solution(mesh):
    in_specs = (
        P("member", ("groups", "space"), None),
        P(None, ("groups", "space")),
        P(None, ("groups", "space")),
        P(("groups", "space"), None),
        P("groups"),
        P(),
        P(),
        P(),
        P(),
        P(),
    )
    out_specs = (
        P("groups"),
        P("member", ("groups", "space"), None),
        P("groups", None),
        P("groups"),
        P("groups", None),
        P("groups"),
        P("groups", None),
    )
    return jax.shard_map(
        per_device, mesh=mesh, in_specs=in_specs, out_specs=out_specs, check_vma=False
    )
```

```python
import jax
import jax.numpy as jnp
from jax import lax
from jax.experimental import pallas as pl
from jax.experimental.pallas import tpu as pltpu
from jax.sharding import PartitionSpec as P

K = 4
OBS_MEAN = 512
HALO = 256
EPSILON = 1e-05
BLOCK = 256
LANE = 128
CHUNK = 512
MIB = 1 << 20


def split(total, step):
    return [(start, min(step, total - start)) for start in range(0, total, step)]


def nt_dot(left, right):
    return lax.dot_general(
        left, right, (((1,), (1,)), ((), ())), preferred_element_type=jnp.float32
    )


def nn_dot(left, right):
    return jnp.dot(left, right, preferred_element_type=jnp.float32)


def kernel_call(body, out_shape, flops, moved, scratch=(), smem=0, operands=0):
    vmem = pl.BlockSpec(memory_space=pltpu.VMEM)
    specs = [pl.BlockSpec(memory_space=pltpu.SMEM)] * smem + [vmem] * (operands - smem)
    return pl.pallas_call(
        body,
        out_shape=out_shape,
        in_specs=specs,
        out_specs=jax.tree.map(lambda _: vmem, out_shape),
        scratch_shapes=list(scratch),
        compiler_params=pltpu.CompilerParams(vmem_limit_bytes=40 * MIB),
        cost_estimate=pl.CostEstimate(flops=flops, bytes_accessed=moved, transcendentals=0),
    )


def table_kernel(count_ref, nbr_ref, weight_ref, latent_ref, table_ref, *part_refs):
    members, nodes, width = latent_ref.shape
    ext, slots = table_ref.shape
    live = lax.broadcasted_iota(jnp.int32, (1, slots), 1) < count_ref[0]
    nbr = [nbr_ref[k : k + 1, :] for k in range(K)]
    own = [jnp.where(live, weight_ref[k : k + 1, :], 0.0) for k in range(K)]
    joint = []
    for k in range(K):
        total = own[k]
        for j in range(K):
            if j != k:
                total = total + jnp.where(nbr[j] == nbr[k], own[j], 0.0)
        joint.append(total)
    groups = BLOCK // 16
    rows = (
        lax.broadcasted_iota(jnp.int32, (groups, 16, LANE), 0) * 16
        + lax.broadcasted_iota(jnp.int32, (groups, 16, LANE), 1)
    ).astype(jnp.float32).astype(jnp.bfloat16)
    for lo, size in split(slots, LANE):
        wide = [
            jnp.broadcast_to(joint[k][:, lo : lo + size], (16, size)).astype(jnp.bfloat16)
            for k in range(K)
        ]
        for b in range(ext // BLOCK):
            tile = jnp.zeros((groups, 16, size), jnp.bfloat16)
            for k in range(K):
                near = (nbr[k][:, lo : lo + size] - b * BLOCK).astype(jnp.float32)
                near = jnp.broadcast_to(near, (16, size)).astype(jnp.bfloat16)
                tile = jnp.where(rows[:, :, :size] == near[None], wide[k][None], tile)
            table_ref[b * BLOCK : (b + 1) * BLOCK, lo : lo + size] = tile.reshape(BLOCK, size)
    turned = jnp.concatenate([latent_ref[m].T for m in range(members)], axis=0)
    for lo, size in split(slots, CHUNK):
        part = nn_dot(turned, table_ref[HALO : HALO + nodes, lo : lo + size])
        for m in range(members):
            part_refs[m][:, lo : lo + size] = part[m * width : (m + 1) * width]


def column(ref):
    height = ref.shape[1]
    return jnp.broadcast_to(ref[...], (LANE, height)).T


def forward_kernel(
    rank_ref, part_ref, table_ref, before_ref, after_ref, w_one_ref, b_one_ref, w_two_ref, b_two_ref, w_three_ref,
    mixed_ref, act_one_ref, slope_one_ref, act_two_ref, slope_two_ref, *decoded_refs,
):
    *decoded_refs, stage_ref = decoded_refs
    ext, slots = table_ref.shape
    ranks, _, share = stage_ref.shape
    w_one, w_two, w_three = w_one_ref[...].T, w_two_ref[...].T, w_three_ref[...].T
    b_one, b_two = column(b_one_ref), column(b_two_ref)

    def layer(weight, bias, values, size):
        pre = nn_dot(weight, values) + jnp.concatenate([bias] * (size // LANE), axis=1)
        gate = 0.5 + 0.5 * jnp.tanh(0.5 * pre)
        act = pre * gate
        return act.astype(jnp.bfloat16), (gate + act * (1.0 - gate)).astype(jnp.bfloat16)

    edges = jnp.concatenate([before_ref[...].T, after_ref[...].T], axis=1)
    for lo, size in split(slots, CHUNK):
        lanes = slice(lo, lo + size)
        rim = jnp.concatenate([table_ref[:HALO, lanes], table_ref[ext - HALO :, lanes]], axis=0)
        mixed = (part_ref[:, lanes] + nn_dot(edges, rim)).astype(jnp.bfloat16)
        mixed_ref[:, lanes] = mixed
        act_one, slope_one_ref[:, lanes] = layer(w_one, b_one, mixed, size)
        act_one_ref[:, lanes] = act_one
        act_two, slope_two_ref[:, lanes] = layer(w_two, b_two, act_one, size)
        act_two_ref[:, lanes] = act_two
        decoded = nn_dot(w_three, act_two).astype(jnp.bfloat16)
        for q in range(ranks):
            first, last = max(lo, q * share), min(lo + size, (q + 1) * share)
            if first < last:
                stage_ref[q ^ rank_ref[0], :, first - q * share : last - q * share] = decoded[
                    :, first - lo : last - lo
                ]
    for i in range(ranks):
        decoded_refs[i][...] = stage_ref[i]


def score_kernel(where_ref, target_ref, *refs):
    count = (len(refs) - 1) // 2
    decoded_refs, grad_refs, score_ref = refs[:count], refs[count : 2 * count], refs[2 * count]
    channels, share = decoded_refs[0].shape
    pairs = [(i, j) for i in range(count) for j in range(i + 1, count)]
    turned = target_ref[...].astype(jnp.float32).T
    total = jnp.zeros((1, LANE), jnp.float32)
    for lo, size in split(share, LANE):
        lanes = slice(lo, lo + size)

        def rows_of(c):
            values = [ref[c : c + 16, lanes].astype(jnp.float32) for ref in decoded_refs]
            return values, turned[c : c + 16, lanes]

        def fold(square):
            return square[:8] + square[8:]

        to_target = [jnp.zeros((8, size), jnp.float32)] * count
        apart = [jnp.zeros((8, size), jnp.float32)] * len(pairs)
        for c in range(0, channels, 16):
            values, goal = rows_of(c)
            for i in range(count):
                to_target[i] = to_target[i] + fold((values[i] - goal) ** 2)
            for p, (i, j) in enumerate(pairs):
                apart[p] = apart[p] + fold((values[i] - values[j]) ** 2)
        slot = where_ref[1] + lo + lax.broadcasted_iota(jnp.int32, (1, size), 1)
        live = (slot < where_ref[0]).astype(jnp.float32)
        score = jnp.zeros((1, size), jnp.float32)

        def inverse(square, scale):
            squared = jnp.sum(square, axis=0, keepdims=True) + EPSILON
            inv = lax.rsqrt(squared)
            return squared * inv * scale, jnp.broadcast_to(inv * (scale * live), (8, size))

        inv_target, inv_pair = [], []
        for square in to_target:
            dist, inv = inverse(square, 1.0)
            score = score + dist
            inv_target.append(inv)
        for square in apart:
            dist, inv = inverse(square, 1.0 / (count - 1))
            score = score - dist
            inv_pair.append(inv)
        score = score * live
        if size < LANE:
            score = jnp.concatenate([score, jnp.zeros((1, LANE - size), jnp.float32)], axis=1)
        total = total + score
        for c in range(0, channels, 16):
            values, goal = rows_of(c)
            halves = []
            for h in (0, 8):
                near = [v[h : h + 8] for v in values]
                grads = [(near[i] - goal[h : h + 8]) * inv_target[i] for i in range(count)]
                for p, (i, j) in enumerate(pairs):
                    term = (near[i] - near[j]) * inv_pair[p]
                    grads[i] = grads[i] - term
                    grads[j] = grads[j] + term
                halves.append(grads)
            for i in range(count):
                grad_refs[i][c : c + 16, lanes] = jnp.concatenate(
                    [halves[0][i], halves[1][i]], axis=0
                ).astype(jnp.bfloat16)
    score_ref[...] = total


def backward_kernel(rank_ref, table_ref, slope_one_ref, slope_two_ref, w_one_ref, w_two_ref, w_three_ref, *refs):
    *refs, stage_ref = refs
    ranks, channels, share = stage_ref.shape
    grad_refs = refs[:ranks]
    d_dec_ref, d_two_ref, d_one_ref, d_mixed_ref, bias_one_ref, bias_two_ref, head_ref, tail_ref = refs[ranks:]
    ext, slots = table_ref.shape
    hidden = slope_one_ref.shape[0]
    for i in range(ranks):
        stage_ref[rank_ref[0] ^ i] = grad_refs[i][...]
    for q in range(ranks):
        d_dec_ref[:, q * share : (q + 1) * share] = stage_ref[q]
    w_one, w_two, w_three = w_one_ref[...], w_two_ref[...], w_three_ref[...]
    bias_one = jnp.zeros((hidden, LANE), jnp.float32)
    bias_two = jnp.zeros((hidden, LANE), jnp.float32)

    def lane_sum(values):
        return sum(values[:, lo : lo + LANE] for lo, _ in split(values.shape[1], LANE))

    for lo, size in split(slots, CHUNK):
        lanes = slice(lo, lo + size)
        back = nn_dot(w_three, d_dec_ref[:, lanes]) * slope_two_ref[:, lanes].astype(jnp.float32)
        bias_two = bias_two + lane_sum(back)
        d_two = back.astype(jnp.bfloat16)
        d_two_ref[:, lanes] = d_two
        back = nn_dot(w_two, d_two) * slope_one_ref[:, lanes].astype(jnp.float32)
        bias_one = bias_one + lane_sum(back)
        d_one = back.astype(jnp.bfloat16)
        d_one_ref[:, lanes] = d_one
        d_mixed_ref[:, lanes] = nn_dot(w_one, d_one).astype(jnp.bfloat16)
    bias_one_ref[...] = bias_one
    bias_two_ref[...] = bias_two
    head_ref[...] = nt_dot(table_ref[:HALO, :], d_mixed_ref[...]).astype(jnp.bfloat16)
    tail_ref[...] = nt_dot(table_ref[ext - HALO :, :], d_mixed_ref[...]).astype(jnp.bfloat16)


def sums_kernel(members, place_ref, score_ref, *refs):
    *refs, keep_ref, send_ref, stage_ref = refs
    saved = [refs[8 * m : 8 * (m + 1)] for m in range(members)]
    width, _ = saved[0][0].shape
    hidden, _ = saved[0][1].shape
    channels, _ = saved[0][5].shape
    rows = stage_ref.shape[0] * stage_ref.shape[1]

    def weight_sum(left, right):
        return sum(nt_dot(member[left][...], member[right][...]) for member in saved)

    def lane_total(at):
        return jnp.sum(sum(member[at][...] for member in saved).T, axis=0, keepdims=True)

    g_three = weight_sum(2, 5)
    half = hidden // 2
    region = lax.broadcasted_iota(jnp.int32, (1, hidden), 1) == place_ref[0]
    tally = jnp.where(region, jnp.sum(score_ref[...]), 0.0)
    high = tally.astype(jnp.bfloat16).astype(jnp.float32)
    used = width + hidden + half + 4
    parts = [
        weight_sum(0, 3),
        weight_sum(1, 4),
        jnp.concatenate([g_three[:half], g_three[half:]], axis=1),
        lane_total(6),
        lane_total(7),
        high,
        tally - high,
        jnp.zeros((rows - used, hidden), jnp.float32),
    ]
    stage_ref[...] = jnp.concatenate(parts, axis=0).astype(stage_ref.dtype).reshape(stage_ref.shape)
    keep_ref[...] = stage_ref[place_ref[1]]
    send_ref[...] = stage_ref[1 - place_ref[1]]


def pair_sum_kernel(one_ref, other_ref, sum_ref):
    sum_ref[...] = (one_ref[...].astype(jnp.float32) + other_ref[...].astype(jnp.float32)).astype(sum_ref.dtype)


def piece_kernel(pieces_ref, out_ref):
    ways = pieces_ref.shape[0]
    total = pieces_ref[0].astype(jnp.float32)
    for i in range(1, ways):
        total = total + pieces_ref[i].astype(jnp.float32)
    total = total.astype(out_ref.dtype)
    for i in range(ways):
        out_ref[i] = total


def unpack_kernel(place_ref, mine_ref, other_ref, one_ref, b_one_ref, two_ref, b_two_ref, three_ref, tally_ref, stage_ref):
    stage_ref[place_ref[1]] = mine_ref[...]
    stage_ref[1 - place_ref[1]] = other_ref[...]
    sums = stage_ref[...].reshape(-1, mine_ref.shape[1]).astype(jnp.float32)
    width, hidden = one_ref.shape
    half, channels = hidden // 2, three_ref.shape[1]
    one_ref[...] = sums[:width]
    two_ref[...] = sums[width : width + hidden]
    base = width + hidden
    three_ref[:half] = sums[base : base + half, :channels]
    three_ref[half:] = sums[base : base + half, channels:]
    base = base + half
    last = sums[base : base + 8]
    b_one_ref[...] = last[0:1]
    b_two_ref[...] = last[1:2]
    tally_ref[...] = last[2:3] + last[3:4]


def own_kernel(table_ref, *refs):
    *d_mixed_refs, own_ref = refs
    members, nodes, _ = own_ref.shape
    for m in range(members):
        own_ref[m] = nt_dot(table_ref[HALO : HALO + nodes, :], d_mixed_refs[m][...])


def finish_kernel(own_ref, *refs):
    *refs, out_ref = refs
    members, nodes, _ = own_ref.shape
    for m in range(members):
        from_prev, from_next = refs[m][...], refs[members + m][...]
        out_ref[m, :HALO] = (own_ref[m, :HALO] + from_prev.astype(jnp.float32)).astype(jnp.bfloat16)
        out_ref[m, HALO : nodes - HALO] = own_ref[m, HALO : nodes - HALO].astype(jnp.bfloat16)
        out_ref[m, nodes - HALO :] = (own_ref[m, nodes - HALO :] + from_next.astype(jnp.float32)).astype(jnp.bfloat16)


MEMBER = ("pair", "core")


def shifted(shard, axis, by):
    length = lax.axis_size(axis)
    return lax.ppermute(shard, axis, [(i, (i + by) % length) for i in range(length)])


def swapped(block, by):
    return lax.ppermute(block, MEMBER, [(i, i ^ by) for i in range(lax.axis_size(MEMBER))])


def per_device(latent, neighbours, weights, targets, counts, w_one, b_one, w_two, b_two, w_three):
    members, nodes, width = latent.shape
    slots, channels = targets.shape
    hidden = w_one.shape[1]
    ext = nodes + 2 * HALO
    region, regions = lax.axis_index("space"), lax.axis_size("space")
    rank, ranks = lax.axis_index(MEMBER), lax.axis_size(MEMBER)
    core = lax.axis_index("core")
    share = slots // ranks
    bf16, f32 = jnp.bfloat16, jnp.float32
    shape = jax.ShapeDtypeStruct
    each = range(members)

    before, after = [], []
    for m in each:
        before.append(shifted(latent[m, nodes - HALO :], "space", 1))
        after.append(shifted(latent[m, :HALO], "space", -1))
    count = lax.dynamic_slice_in_dim(counts, region, 1)
    target = lax.dynamic_slice_in_dim(targets, rank * share, share)
    rank_at = rank[None].astype(jnp.int32)
    place = jnp.stack([region, core]).astype(jnp.int32)

    table, *part = kernel_call(
        table_kernel,
        (shape((ext, slots), bf16),) + (shape((width, slots), f32),) * members,
        flops=2 * members * width * nodes * slots,
        moved=12 * MIB,
        smem=1,
        operands=4,
    )(count, neighbours, weights, latent)

    saved_shape = shape((hidden, slots), bf16)
    block = shape((channels, share), bf16)
    saved, sent = [], []
    for m in each:
        out = kernel_call(
            forward_kernel,
            (shape((width, slots), bf16),) + (saved_shape,) * 4 + (block,) * ranks,
            flops=2 * slots * (2 * HALO * width + width * hidden + hidden * hidden + hidden * channels),
            moved=8 * MIB,
            scratch=(pltpu.VMEM((ranks, channels, share), bf16),),
            smem=1,
            operands=10,
        )(rank_at, part[m], table, before[m], after[m], w_one, b_one[None], w_two, b_two[None], w_three)
        saved.append(out[:5])
        sent.append([out[5]] + [swapped(out[5 + i], i) for i in range(1, ranks)])

    everyone = [sent[m][i] for m in each for i in range(ranks)]
    slots_at = jnp.concatenate([count, (rank * share)[None].astype(jnp.int32)])
    *grads, score = kernel_call(
        score_kernel,
        (block,) * len(everyone) + (shape((1, LANE), f32),),
        flops=4 * MIB,
        moved=2 * MIB,
        smem=1,
        operands=2 + len(everyone),
    )(slots_at, target, *everyone)

    edge = shape((HALO, width), bf16)
    bias = shape((hidden, LANE), f32)
    back, from_next, from_prev = [], [], []
    for m in each:
        own_grads = grads[m * ranks : (m + 1) * ranks]
        own_grads = [own_grads[0]] + [swapped(own_grads[i], i) for i in range(1, ranks)]
        *out, head, tail = kernel_call(
            backward_kernel,
            (shape((channels, slots), bf16), saved_shape, saved_shape, shape((width, slots), bf16), bias, bias, edge, edge),
            flops=2 * slots * (2 * HALO * width + width * hidden + hidden * hidden + hidden * channels),
            moved=6 * MIB,
            scratch=(pltpu.VMEM((ranks, channels, share), bf16),),
            smem=1,
            operands=7 + ranks,
        )(rank_at, table, saved[m][2], saved[m][4], w_one, w_two, w_three, *own_grads)
        back.append(out)
        from_next.append(shifted(head, "space", -1))
        from_prev.append(shifted(tail, "space", 1))

    ways = regions * ranks // 2
    rows = -(-(width + hidden + hidden // 2 + 4) // (32 * ways)) * 32 * ways
    half = shape((rows // 2, hidden), bf16)
    operands = []
    for m in each:
        d_dec, d_two, d_one, _, bias_one, bias_two = back[m]
        mixed, act_one, _, act_two, _ = saved[m]
        operands += [mixed, act_one, act_two, d_one, d_two, d_dec, bias_one, bias_two]
    keep, send = kernel_call(
        lambda *refs: sums_kernel(members, *refs),
        (half, half),
        flops=2 * members * slots * (width * hidden + hidden * hidden + hidden * channels),
        moved=10 * MIB,
        scratch=(pltpu.VMEM((2, rows // 2, hidden), bf16),),
        smem=1,
        operands=2 + len(operands),
    )(place, score, *operands)
    swap = [(0, 1), (1, 0)]
    other = lax.ppermute(send, "core", swap)
    own = kernel_call(
        own_kernel,
        shape((members, nodes, width), f32),
        flops=2 * members * nodes * width * slots,
        moved=6 * MIB,
        operands=1 + members,
    )(table, *[out[3] for out in back])
    total = kernel_call(pair_sum_kernel, half, flops=MIB, moved=MIB, operands=2)(keep, other)
    total, own = lax.optimization_barrier((total, own))
    both = ("space", "pair")
    pieces = lax.all_to_all(total, both, 0, 0, tiled=True).reshape(ways, rows // 2 // ways, hidden)
    spread = kernel_call(piece_kernel, shape(pieces.shape, bf16), flops=MIB, moved=MIB, operands=1)(pieces)
    mine = lax.all_to_all(spread.reshape(rows // 2, hidden), both, 0, 0, tiled=True)
    other = lax.ppermute(mine, "core", swap)
    row = shape((1, hidden), f32)
    g_one, g_bone, g_two, g_btwo, g_three, tally = kernel_call(
        unpack_kernel,
        (shape((width, hidden), f32), row, shape((hidden, hidden), f32), row, shape((hidden, channels), f32), row),
        flops=MIB,
        moved=2 * MIB,
        scratch=(pltpu.VMEM((2, rows // 2, hidden), bf16),),
        smem=1,
        operands=3,
    )(place, mine, other)

    latent_grad = kernel_call(
        finish_kernel,
        shape((members, nodes, width), bf16),
        flops=MIB,
        moved=3 * MIB,
        operands=1 + 2 * members,
    )(own, *from_prev, *from_next)
    region_score = tally[0, :regions] / (OBS_MEAN * members * ranks)
    return (region_score, latent_grad, g_one, g_bone[0], g_two, g_btwo[0], g_three)


def solution(mesh):
    groups, space, member = mesh.devices.shape
    inner = jax.sharding.Mesh(
        mesh.devices.reshape(groups, space, member // 2, 2), ("groups", "space") + MEMBER
    )
    in_specs = (
        P(MEMBER, ("groups", "space"), None),
        P(None, ("groups", "space")),
        P(None, ("groups", "space")),
        P(("groups", "space"), None),
        P("groups"),
        P(),
        P(),
        P(),
        P(),
        P(),
    )
    out_specs = (
        P("groups"),
        P(MEMBER, ("groups", "space"), None),
        P("groups", None),
        P("groups"),
        P("groups", None),
        P("groups"),
        P("groups", None),
    )
    return jax.shard_map(
        per_device, mesh=inner, in_specs=in_specs, out_specs=out_specs, check_vma=False
    )
```

```python
import jax
import jax.numpy as jnp
from jax import lax
from jax.experimental import pallas as pl
from jax.experimental.pallas import tpu as pltpu
from jax.sharding import PartitionSpec as P

K = 4
OBS_MEAN = 512
HALO = 256
EPSILON = 1e-05
BLOCK = 256
LANE = 128
CHUNK = 512
MIB = 1 << 20


def split(total, step):
    return [(start, min(step, total - start)) for start in range(0, total, step)]


def nt_dot(left, right):
    return lax.dot_general(
        left, right, (((1,), (1,)), ((), ())), preferred_element_type=jnp.float32
    )


def nn_dot(left, right):
    return jnp.dot(left, right, preferred_element_type=jnp.float32)


def kernel_call(body, out_shape, flops, moved, scratch=(), smem=0, hbm=0, operands=0):
    vmem = pl.BlockSpec(memory_space=pltpu.VMEM)
    specs = [pl.BlockSpec(memory_space=pltpu.SMEM)] * smem + [pl.BlockSpec(memory_space=pltpu.HBM)] * hbm
    return pl.pallas_call(
        body,
        out_shape=out_shape,
        in_specs=specs + [vmem] * (operands - len(specs)),
        out_specs=jax.tree.map(lambda _: vmem, out_shape),
        scratch_shapes=list(scratch),
        compiler_params=pltpu.CompilerParams(vmem_limit_bytes=40 * MIB),
        cost_estimate=pl.CostEstimate(flops=flops, bytes_accessed=moved, transcendentals=0),
    )


def table_kernel(region_ref, counts_ref, nbr_hbm, weight_hbm, latent_hbm, table_ref, *refs):
    *part_refs, nbr_ref, weight_ref, latent_ref, sems = refs
    members, nodes, width = latent_ref.shape
    ext, slots = table_ref.shape
    fetches = [
        pltpu.make_async_copy(source, to, sems.at[i])
        for i, (source, to) in enumerate(
            ((nbr_hbm, nbr_ref), (weight_hbm, weight_ref), (latent_hbm, latent_ref))
        )
    ]
    for fetch in fetches:
        fetch.start()
    fetches[0].wait()
    fetches[1].wait()
    live = lax.broadcasted_iota(jnp.int32, (1, slots), 1) < counts_ref[region_ref[0]]
    nbr = [nbr_ref[k : k + 1, :] for k in range(K)]
    own = [jnp.where(live, weight_ref[k : k + 1, :], 0.0) for k in range(K)]
    joint = []
    for k in range(K):
        total = own[k]
        for j in range(K):
            if j != k:
                total = total + jnp.where(nbr[j] == nbr[k], own[j], 0.0)
        joint.append(total)
    groups = BLOCK // 16
    rows = (
        lax.broadcasted_iota(jnp.int32, (groups, 16, LANE), 0) * 16
        + lax.broadcasted_iota(jnp.int32, (groups, 16, LANE), 1)
    ).astype(jnp.float32).astype(jnp.bfloat16)
    for lo, size in split(slots, LANE):
        wide = [
            jnp.broadcast_to(joint[k][:, lo : lo + size], (16, size)).astype(jnp.bfloat16)
            for k in range(K)
        ]
        for b in range(ext // BLOCK):
            tile = jnp.zeros((groups, 16, size), jnp.bfloat16)
            for k in range(K):
                near = (nbr[k][:, lo : lo + size] - b * BLOCK).astype(jnp.float32)
                near = jnp.broadcast_to(near, (16, size)).astype(jnp.bfloat16)
                tile = jnp.where(rows[:, :, :size] == near[None], wide[k][None], tile)
            table_ref[b * BLOCK : (b + 1) * BLOCK, lo : lo + size] = tile.reshape(BLOCK, size)
    fetches[2].wait()
    turned = jnp.concatenate([latent_ref[m].T for m in range(members)], axis=0)
    for lo, size in split(slots, CHUNK):
        part = nn_dot(turned, table_ref[HALO : HALO + nodes, lo : lo + size])
        for m in range(members):
            part_refs[m][:, lo : lo + size] = part[m * width : (m + 1) * width]


def column(ref):
    height = ref.shape[1]
    return jnp.broadcast_to(ref[...], (LANE, height)).T


def forward_kernel(
    rank_ref, part_ref, table_ref, before_ref, after_ref, w_one_ref, b_one_ref, w_two_ref, b_two_ref, w_three_ref,
    mixed_ref, act_one_ref, slope_one_ref, act_two_ref, slope_two_ref, *decoded_refs,
):
    *decoded_refs, stage_ref = decoded_refs
    ext, slots = table_ref.shape
    ranks, _, share = stage_ref.shape
    w_one, w_two, w_three = w_one_ref[...].T, w_two_ref[...].T, w_three_ref[...].T
    b_one, b_two = column(b_one_ref), column(b_two_ref)

    def layer(weight, bias, values, size):
        pre = nn_dot(weight, values) + jnp.concatenate([bias] * (size // LANE), axis=1)
        gate = 0.5 + 0.5 * jnp.tanh(0.5 * pre)
        act = pre * gate
        return act.astype(jnp.bfloat16), (gate + act * (1.0 - gate)).astype(jnp.bfloat16)

    edges = jnp.concatenate([before_ref[...].T, after_ref[...].T], axis=1)
    for lo, size in split(slots, CHUNK):
        lanes = slice(lo, lo + size)
        rim = jnp.concatenate([table_ref[:HALO, lanes], table_ref[ext - HALO :, lanes]], axis=0)
        mixed = (part_ref[:, lanes] + nn_dot(edges, rim)).astype(jnp.bfloat16)
        mixed_ref[:, lanes] = mixed
        act_one, slope_one_ref[:, lanes] = layer(w_one, b_one, mixed, size)
        act_one_ref[:, lanes] = act_one
        act_two, slope_two_ref[:, lanes] = layer(w_two, b_two, act_one, size)
        act_two_ref[:, lanes] = act_two
        decoded = nn_dot(w_three, act_two).astype(jnp.bfloat16)
        for q in range(ranks):
            first, last = max(lo, q * share), min(lo + size, (q + 1) * share)
            if first < last:
                stage_ref[q ^ rank_ref[0], :, first - q * share : last - q * share] = decoded[
                    :, first - lo : last - lo
                ]
    for i in range(ranks):
        decoded_refs[i][...] = stage_ref[i]


def score_kernel(region_ref, rank_ref, counts_ref, target_ref, *refs):
    count = (len(refs) - 1) // 2
    decoded_refs, grad_refs, score_ref = refs[:count], refs[count : 2 * count], refs[2 * count]
    channels, share = decoded_refs[0].shape
    pairs = [(i, j) for i in range(count) for j in range(i + 1, count)]
    turned = target_ref[...].astype(jnp.float32).T
    total = jnp.zeros((1, LANE), jnp.float32)
    for lo, size in split(share, LANE):
        lanes = slice(lo, lo + size)

        def rows_of(c):
            values = [ref[c : c + 16, lanes].astype(jnp.float32) for ref in decoded_refs]
            return values, turned[c : c + 16, lanes]

        def fold(square):
            return square[:8] + square[8:]

        to_target = [jnp.zeros((8, size), jnp.float32)] * count
        apart = [jnp.zeros((8, size), jnp.float32)] * len(pairs)
        for c in range(0, channels, 16):
            values, goal = rows_of(c)
            for i in range(count):
                to_target[i] = to_target[i] + fold((values[i] - goal) ** 2)
            for p, (i, j) in enumerate(pairs):
                apart[p] = apart[p] + fold((values[i] - values[j]) ** 2)
        slot = rank_ref[0] * share + lo + lax.broadcasted_iota(jnp.int32, (1, size), 1)
        live = (slot < counts_ref[region_ref[0]]).astype(jnp.float32)
        score = jnp.zeros((1, size), jnp.float32)

        def inverse(square, scale):
            squared = jnp.sum(square, axis=0, keepdims=True) + EPSILON
            inv = lax.rsqrt(squared)
            return squared * inv * scale, jnp.broadcast_to(inv * (scale * live), (8, size))

        inv_target, inv_pair = [], []
        for square in to_target:
            dist, inv = inverse(square, 1.0)
            score = score + dist
            inv_target.append(inv)
        for square in apart:
            dist, inv = inverse(square, 1.0 / (count - 1))
            score = score - dist
            inv_pair.append(inv)
        score = score * live
        if size < LANE:
            score = jnp.concatenate([score, jnp.zeros((1, LANE - size), jnp.float32)], axis=1)
        total = total + score
        for c in range(0, channels, 16):
            values, goal = rows_of(c)
            halves = []
            for h in (0, 8):
                near = [v[h : h + 8] for v in values]
                grads = [(near[i] - goal[h : h + 8]) * inv_target[i] for i in range(count)]
                for p, (i, j) in enumerate(pairs):
                    term = (near[i] - near[j]) * inv_pair[p]
                    grads[i] = grads[i] - term
                    grads[j] = grads[j] + term
                halves.append(grads)
            for i in range(count):
                grad_refs[i][c : c + 16, lanes] = jnp.concatenate(
                    [halves[0][i], halves[1][i]], axis=0
                ).astype(jnp.bfloat16)
    score_ref[...] = total


def backward(rank_ref, table_ref, slope_one_ref, slope_two_ref, w_one_ref, w_two_ref, w_three_ref, grad_refs, out_refs, stage_ref):
    d_dec_ref, d_two_ref, d_one_ref, d_mixed_ref, bias_one_ref, bias_two_ref, head_ref, tail_ref = out_refs
    ranks, channels, share = stage_ref.shape
    ext, slots = table_ref.shape
    hidden = slope_one_ref.shape[0]
    for i in range(ranks):
        stage_ref[rank_ref[0] ^ i] = grad_refs[i][...]
    for q in range(ranks):
        d_dec_ref[:, q * share : (q + 1) * share] = stage_ref[q]
    w_one, w_two, w_three = w_one_ref[...], w_two_ref[...], w_three_ref[...]
    bias_one = jnp.zeros((hidden, LANE), jnp.float32)
    bias_two = jnp.zeros((hidden, LANE), jnp.float32)

    def lane_sum(values):
        return sum(values[:, lo : lo + LANE] for lo, _ in split(values.shape[1], LANE))

    for lo, size in split(slots, CHUNK):
        lanes = slice(lo, lo + size)
        back = nn_dot(w_three, d_dec_ref[:, lanes]) * slope_two_ref[:, lanes].astype(jnp.float32)
        bias_two = bias_two + lane_sum(back)
        d_two = back.astype(jnp.bfloat16)
        d_two_ref[:, lanes] = d_two
        back = nn_dot(w_two, d_two) * slope_one_ref[:, lanes].astype(jnp.float32)
        bias_one = bias_one + lane_sum(back)
        d_one = back.astype(jnp.bfloat16)
        d_one_ref[:, lanes] = d_one
        d_mixed_ref[:, lanes] = nn_dot(w_one, d_one).astype(jnp.bfloat16)
    bias_one_ref[...] = bias_one
    bias_two_ref[...] = bias_two
    head_ref[...] = nt_dot(table_ref[:HALO, :], d_mixed_ref[...]).astype(jnp.bfloat16)
    tail_ref[...] = nt_dot(table_ref[ext - HALO :, :], d_mixed_ref[...]).astype(jnp.bfloat16)


def backward_kernel(ranks, *refs):
    backward(*refs[:7], refs[7 : 7 + ranks], refs[7 + ranks : -1], refs[-1])


def weights_kernel(mixed_ref, act_one_ref, act_two_ref, d_one_ref, d_two_ref, d_dec_ref, one_ref, two_ref, three_ref):
    one_ref[...] = nt_dot(mixed_ref[...], d_one_ref[...])
    two_ref[...] = nt_dot(act_one_ref[...], d_two_ref[...])
    three_ref[...] = nt_dot(act_two_ref[...], d_dec_ref[...])


def last_backward_kernel(ranks, earlier, region_ref, *refs):
    base, refs = refs[:7], refs[7:]
    grad_refs, refs = refs[:ranks], refs[ranks:]
    score_ref, mixed_ref, act_one_ref, act_two_ref = refs[:4]
    before, refs = refs[4 : 4 + 5 * earlier], refs[4 + 5 * earlier :]
    d_mixed_ref, head_ref, tail_ref = refs[:3]
    piece_refs = refs[3 : 3 + ranks]
    d_dec_ref, d_two_ref, d_one_ref, bias_one_ref, bias_two_ref, grad_stage_ref, stage_ref = refs[3 + ranks :]
    results = (d_dec_ref, d_two_ref, d_one_ref, d_mixed_ref, bias_one_ref, bias_two_ref, head_ref, tail_ref)
    backward(*base, grad_refs, results, grad_stage_ref)

    def with_earlier(at, value):
        return sum((before[5 * e + at][...] for e in range(earlier)), value)

    def bias_row(at, ref):
        return jnp.sum(with_earlier(at, ref[...]).T, axis=0, keepdims=True)

    hidden = act_one_ref.shape[0]
    half = hidden // 2
    g_one = with_earlier(0, nt_dot(mixed_ref[...], d_one_ref[...]))
    g_two = with_earlier(1, nt_dot(act_one_ref[...], d_two_ref[...]))
    g_three = with_earlier(2, nt_dot(act_two_ref[...], d_dec_ref[...]))
    region = lax.broadcasted_iota(jnp.int32, (1, hidden), 1) == region_ref[0]
    tally = jnp.where(region, jnp.sum(score_ref[...]), 0.0)
    high = tally.astype(jnp.bfloat16).astype(jnp.float32)
    parts = [
        g_one,
        g_two,
        jnp.concatenate([g_three[:half], g_three[half:]], axis=1),
        bias_row(3, bias_one_ref),
        bias_row(4, bias_two_ref),
        high,
        tally - high,
    ]
    used = sum(part.shape[0] for part in parts)
    parts.append(jnp.zeros((ranks * stage_ref.shape[1] - used, hidden), jnp.float32))
    stage_ref[...] = jnp.concatenate(parts, axis=0).astype(stage_ref.dtype).reshape(stage_ref.shape)
    for i in range(ranks):
        piece_refs[i][0] = stage_ref[base[0][0] ^ i]


def halve_kernel(count, *refs):
    for i in range(count):
        total = refs[i][...].astype(jnp.float32) + refs[count + i][...].astype(jnp.float32)
        refs[2 * count + i][...] = total.astype(refs[i].dtype)


def region_sum_kernel(region_ref, *refs):
    *refs, sum_ref, stage_ref = refs
    for i, ref in enumerate(refs):
        stage_ref[region_ref[0] ^ i] = ref[0]
    sum_ref[0] = sum(stage_ref[i].astype(jnp.float32) for i in range(len(refs))).astype(sum_ref.dtype)


def unpack_kernel(scale, rank_ref, *refs):
    *refs, stage_ref = refs
    ranks = stage_ref.shape[0]
    one_ref, b_one_ref, two_ref, b_two_ref, three_ref, tally_ref = refs[ranks:]
    for i in range(ranks):
        stage_ref[rank_ref[0] ^ i] = refs[i][0]
    width, hidden = one_ref.shape
    sums = stage_ref[...].reshape(-1, hidden).astype(jnp.float32)
    half, channels = hidden // 2, three_ref.shape[1]
    one_ref[...] = sums[:width]
    two_ref[...] = sums[width : width + hidden]
    base = width + hidden
    three_ref[:half] = sums[base : base + half, :channels]
    three_ref[half:] = sums[base : base + half, channels:]
    last = sums[base + half : base + half + 8]
    b_one_ref[...] = last[0:1]
    b_two_ref[...] = last[1:2]
    tally_ref[...] = (last[2:3] + last[3:4])[:, : tally_ref.shape[1]] * scale


def own_kernel(table_ref, *refs):
    *d_mixed_refs, own_ref = refs
    members, nodes, _ = own_ref.shape
    for m in range(members):
        own_ref[m] = nt_dot(table_ref[HALO : HALO + nodes, :], d_mixed_refs[m][...])


def finish_kernel(own_ref, *refs):
    *refs, out_ref = refs
    members, nodes, _ = own_ref.shape
    for m in range(members):
        from_prev, from_next = refs[m][...], refs[members + m][...]
        out_ref[m, :HALO] = (own_ref[m, :HALO] + from_prev.astype(jnp.float32)).astype(jnp.bfloat16)
        out_ref[m, HALO : nodes - HALO] = own_ref[m, HALO : nodes - HALO].astype(jnp.bfloat16)
        out_ref[m, nodes - HALO :] = (own_ref[m, nodes - HALO :] + from_next.astype(jnp.float32)).astype(jnp.bfloat16)


def shifted(shard, axis, by):
    length = lax.axis_size(axis)
    return lax.ppermute(shard, axis, [(i, (i + by) % length) for i in range(length)])


def swapped(block, axis, by):
    return lax.ppermute(block, axis, [(i, i ^ by) for i in range(lax.axis_size(axis))])


def per_device(latent, neighbours, weights, targets, counts, w_one, b_one, w_two, b_two, w_three):
    members, nodes, width = latent.shape
    slots, channels = targets.shape
    hidden = w_one.shape[1]
    ext = nodes + 2 * HALO
    region, regions = lax.axis_index("space"), lax.axis_size("space")
    rank, ranks = lax.axis_index("member"), lax.axis_size("member")
    share = slots // ranks
    bf16, f32 = jnp.bfloat16, jnp.float32
    shape = jax.ShapeDtypeStruct
    each = range(members)

    before, after = [], []
    for m in each:
        before.append(shifted(latent[m, nodes - HALO :], "space", 1))
        after.append(shifted(latent[m, :HALO], "space", -1))
    target = lax.dynamic_slice_in_dim(targets, rank * share, share)
    rank_at = rank[None].astype(jnp.int32)
    region_at = region[None].astype(jnp.int32)

    table, *part = kernel_call(
        table_kernel,
        (shape((ext, slots), bf16),) + (shape((width, slots), f32),) * members,
        flops=2 * members * width * nodes * slots,
        moved=12 * MIB,
        scratch=(
            pltpu.VMEM(neighbours.shape, jnp.int32),
            pltpu.VMEM(weights.shape, f32),
            pltpu.VMEM(latent.shape, bf16),
            pltpu.SemaphoreType.DMA((3,)),
        ),
        smem=2,
        hbm=3,
        operands=5,
    )(region_at, counts, neighbours, weights, latent)

    saved_shape = shape((hidden, slots), bf16)
    mixed_shape = shape((width, slots), bf16)
    block = shape((channels, share), bf16)
    dense = width * hidden + hidden * hidden + hidden * channels
    saved, sent = [], []
    for m in each:
        out = kernel_call(
            forward_kernel,
            (mixed_shape,) + (saved_shape,) * 4 + (block,) * ranks,
            flops=2 * slots * (2 * HALO * width + dense),
            moved=8 * MIB,
            scratch=(pltpu.VMEM((ranks, channels, share), bf16),),
            smem=1,
            operands=10,
        )(rank_at, part[m], table, before[m], after[m], w_one, b_one[None], w_two, b_two[None], w_three)
        saved.append(out[:5])
        sent.append([out[5]] + [swapped(out[5 + i], "member", i) for i in range(1, ranks)])

    everyone = [sent[m][i] for m in each for i in range(ranks)]
    *grads, score = kernel_call(
        score_kernel,
        (block,) * len(everyone) + (shape((1, LANE), f32),),
        flops=4 * MIB,
        moved=2 * MIB,
        smem=3,
        operands=4 + len(everyone),
    )(region_at, rank_at, counts, target, *everyone)

    edge = shape((HALO, width), bf16)
    bias = shape((hidden, LANE), f32)
    stage = pltpu.VMEM((ranks, channels, share), bf16)
    rows = -(-(width + hidden + hidden // 2 + 4) // (16 * ranks)) * 16
    piece = shape((1, rows, hidden), bf16)
    from_next, from_prev, d_mixed, carried = [], [], [], []
    for m in each:
        mixed, act_one, slope_one, act_two, slope_two = saved[m]
        given = grads[m * ranks : (m + 1) * ranks]
        given = [given[0]] + [swapped(given[i], "member", i) for i in range(1, ranks)]
        base = (rank_at, table, slope_one, slope_two, w_one, w_two, w_three, *given)
        if m < members - 1:
            d_dec, d_two, d_one, d_mix, bias_one, bias_two, head, tail = kernel_call(
                lambda *refs: backward_kernel(ranks, *refs),
                (shape((channels, slots), bf16), saved_shape, saved_shape, mixed_shape, bias, bias, edge, edge),
                flops=2 * slots * (2 * HALO * width + dense),
                moved=6 * MIB,
                scratch=(stage,),
                smem=1,
                operands=len(base),
            )(*base)
            carried += kernel_call(
                weights_kernel,
                (shape((width, hidden), f32), shape((hidden, hidden), f32), shape((hidden, channels), f32)),
                flops=2 * slots * dense,
                moved=4 * MIB,
                operands=6,
            )(mixed, act_one, act_two, d_one, d_two, d_dec)
            carried += [bias_one, bias_two]
        else:
            operands = (region_at, *base, score, mixed, act_one, act_two, *carried)
            d_mix, head, tail, *pieces = kernel_call(
                lambda *refs: last_backward_kernel(ranks, members - 1, *refs),
                (mixed_shape, edge, edge) + (piece,) * ranks,
                flops=2 * slots * (2 * HALO * width + 2 * dense),
                moved=10 * MIB,
                scratch=(
                    pltpu.VMEM((channels, slots), bf16),
                    pltpu.VMEM((hidden, slots), bf16),
                    pltpu.VMEM((hidden, slots), bf16),
                    pltpu.VMEM((hidden, LANE), f32),
                    pltpu.VMEM((hidden, LANE), f32),
                    stage,
                    pltpu.VMEM((ranks, rows, hidden), bf16),
                ),
                smem=2,
                operands=len(operands),
            )(*operands)
        d_mixed.append(d_mix)
        from_next.append(shifted(head, "space", -1))
        from_prev.append(shifted(tail, "space", 1))

    keep, send = pieces[::2], pieces[1::2]
    bit, other = 1, [swapped(block, "member", 1) for block in send]
    other, from_next[:-1], from_prev[:-1] = lax.optimization_barrier((other, from_next[:-1], from_prev[:-1]))
    while len(keep) > 1:
        both = kernel_call(
            lambda *refs: halve_kernel(len(keep), *refs), (piece,) * len(keep), flops=MIB, moved=MIB, operands=2 * len(keep)
        )(*keep, *other)
        keep, send = both[::2], both[1::2]
        bit = 2 * bit
        other = [swapped(block, "member", bit) for block in send]
    (quarter,) = kernel_call(
        lambda *refs: halve_kernel(1, *refs), (piece,), flops=MIB, moved=MIB, operands=2
    )(*keep, *other)
    quarters = [quarter] + [swapped(quarter, "space", i) for i in range(1, regions)]
    own = kernel_call(
        own_kernel,
        shape((members, nodes, width), f32),
        flops=2 * members * nodes * width * slots,
        moved=6 * MIB,
        operands=1 + members,
    )(table, *d_mixed)
    total = kernel_call(
        region_sum_kernel,
        piece,
        flops=MIB,
        moved=MIB,
        scratch=(pltpu.VMEM((regions, rows, hidden), bf16),),
        smem=1,
        operands=1 + regions,
    )(region_at, *quarters)
    latent_grad = kernel_call(
        finish_kernel,
        shape((members, nodes, width), bf16),
        flops=MIB,
        moved=3 * MIB,
        operands=1 + 2 * members,
    )(own, *from_prev, *from_next)
    total, latent_grad = lax.optimization_barrier((total, latent_grad))
    totals = {0: total}
    while bit:
        totals.update({i ^ bit: swapped(totals[i], "member", bit) for i in sorted(totals)})
        bit = bit // 2
    totals = [totals[i] for i in range(ranks)]
    row = shape((1, hidden), f32)
    g_one, g_bone, g_two, g_btwo, g_three, tally = kernel_call(
        lambda *refs: unpack_kernel(1.0 / (OBS_MEAN * members * ranks), *refs),
        (shape((width, hidden), f32), row, shape((hidden, hidden), f32), row, shape((hidden, channels), f32),
         shape((1, regions), f32)),
        flops=MIB,
        moved=2 * MIB,
        scratch=(pltpu.VMEM((ranks, rows, hidden), bf16),),
        smem=1,
        operands=1 + ranks,
    )(rank_at, *totals)
    return (tally[0], latent_grad, g_one, g_bone[0], g_two, g_btwo[0], g_three)


def solution(mesh):
    in_specs = (
        P("member", ("groups", "space"), None),
        P(None, ("groups", "space")),
        P(None, ("groups", "space")),
        P(("groups", "space"), None),
        P("groups"),
        P(),
        P(),
        P(),
        P(),
        P(),
    )
    out_specs = (
        P("groups"),
        P("member", ("groups", "space"), None),
        P("groups", None),
        P("groups"),
        P("groups", None),
        P("groups"),
        P("groups", None),
    )
    return jax.shard_map(
        per_device, mesh=mesh, in_specs=in_specs, out_specs=out_specs, check_vma=False
    )
```

```python
import jax
import jax.numpy as jnp
from jax import lax
from jax.experimental import pallas as pl
from jax.experimental.pallas import tpu as pltpu
from jax.sharding import PartitionSpec as P

K = 4
OBS_MEAN = 512
HALO = 256
EPSILON = 1e-05
BLOCK = 256
LANE = 128
CHUNK = 512
MIB = 1 << 20


def split(total, step):
    return [(start, min(step, total - start)) for start in range(0, total, step)]


def nt_dot(left, right):
    return lax.dot_general(
        left, right, (((1,), (1,)), ((), ())), preferred_element_type=jnp.float32
    )


def nn_dot(left, right):
    return jnp.dot(left, right, preferred_element_type=jnp.float32)


def kernel_call(body, out_shape, flops, moved, scratch=(), smem=0, operands=0):
    vmem = pl.BlockSpec(memory_space=pltpu.VMEM)
    specs = [pl.BlockSpec(memory_space=pltpu.SMEM)] * smem
    return pl.pallas_call(
        body,
        out_shape=out_shape,
        in_specs=specs + [vmem] * (operands - len(specs)),
        out_specs=jax.tree.map(lambda _: vmem, out_shape),
        scratch_shapes=list(scratch),
        compiler_params=pltpu.CompilerParams(vmem_limit_bytes=40 * MIB),
        cost_estimate=pl.CostEstimate(flops=flops, bytes_accessed=moved, transcendentals=0),
    )


def rims_kernel(latent_ref, *refs):
    members, nodes, _ = latent_ref.shape
    for m in range(members):
        refs[2 * m][...] = latent_ref[m, nodes - HALO :]
        refs[2 * m + 1][...] = latent_ref[m, :HALO]
    refs[-1][...] = latent_ref[...]


def table_kernel(region_ref, rank_ref, counts_ref, nbr_ref, weight_ref, latent_ref, table_ref, *part_refs):
    members, nodes, width = latent_ref.shape
    ext, slots = table_ref.shape
    live = lax.broadcasted_iota(jnp.int32, (1, slots), 1) < counts_ref[region_ref[0]]
    nbr = [nbr_ref[k : k + 1, :] for k in range(K)]
    own = [jnp.where(live, weight_ref[k : k + 1, :], 0.0) for k in range(K)]
    joint = []
    for k in range(K):
        total = own[k]
        for j in range(K):
            if j != k:
                total = total + jnp.where(nbr[j] == nbr[k], own[j], 0.0)
        joint.append(total)
    groups = BLOCK // 16
    rows = (
        lax.broadcasted_iota(jnp.int32, (groups, 16, LANE), 0) * 16
        + lax.broadcasted_iota(jnp.int32, (groups, 16, LANE), 1)
    ).astype(jnp.float32).astype(jnp.bfloat16)
    for lo, size in split(slots, LANE):
        wide = [
            jnp.broadcast_to(joint[k][:, lo : lo + size], (16, size)).astype(jnp.bfloat16)
            for k in range(K)
        ]
        for b in range(ext // BLOCK):
            tile = jnp.zeros((groups, 16, size), jnp.bfloat16)
            for k in range(K):
                near = (nbr[k][:, lo : lo + size] - b * BLOCK).astype(jnp.float32)
                near = jnp.broadcast_to(near, (16, size)).astype(jnp.bfloat16)
                tile = jnp.where(rows[:, :, :size] == near[None], wide[k][None], tile)
            table_ref[b * BLOCK : (b + 1) * BLOCK, lo : lo + size] = tile.reshape(BLOCK, size)
    turned = jnp.concatenate([latent_ref[m].T for m in range(members)], axis=0)
    for lo, size in split(slots, CHUNK):
        part = nn_dot(turned, table_ref[HALO : HALO + nodes, lo : lo + size])
        for m in range(members):
            part_refs[m][:, lo : lo + size] = part[m * width : (m + 1) * width]


def column(ref):
    height = ref.shape[1]
    return jnp.broadcast_to(ref[...], (LANE, height)).T


def forward_kernel(
    rank_ref, part_ref, table_ref, before_ref, after_ref, w_one_ref, b_one_ref, w_two_ref, b_two_ref, w_three_ref,
    mixed_ref, act_one_ref, slope_one_ref, act_two_ref, slope_two_ref, *decoded_refs,
):
    *decoded_refs, stage_ref = decoded_refs
    ext, slots = table_ref.shape
    ranks, _, share = stage_ref.shape
    w_one, w_two, w_three = w_one_ref[...].T * 0.5, w_two_ref[...].T * 0.5, w_three_ref[...].T
    b_one, b_two = column(b_one_ref) * 0.5, column(b_two_ref) * 0.5

    def layer(weight, bias, values, size):
        half = nn_dot(weight, values) + jnp.concatenate([bias] * (size // LANE), axis=1)
        gate = 1.0 + jnp.tanh(half)
        act = half * gate
        return act.astype(jnp.bfloat16), (gate + act * (2.0 - gate)).astype(jnp.bfloat16)

    edges = jnp.concatenate([before_ref[...].T, after_ref[...].T], axis=1)
    for lo, size in split(slots, CHUNK):
        lanes = slice(lo, lo + size)
        rim = jnp.concatenate([table_ref[:HALO, lanes], table_ref[ext - HALO :, lanes]], axis=0)
        mixed = (part_ref[:, lanes] + nn_dot(edges, rim)).astype(jnp.bfloat16)
        mixed_ref[:, lanes] = mixed
        act_one, slope_one_ref[:, lanes] = layer(w_one, b_one, mixed, size)
        act_one_ref[:, lanes] = act_one
        act_two, slope_two_ref[:, lanes] = layer(w_two, b_two, act_one, size)
        act_two_ref[:, lanes] = act_two
        decoded = nn_dot(w_three, act_two).astype(jnp.bfloat16)
        for q in range(ranks):
            first, last = max(lo, q * share), min(lo + size, (q + 1) * share)
            if first < last:
                stage_ref[q ^ rank_ref[0], :, first - q * share : last - q * share] = decoded[
                    :, first - lo : last - lo
                ]
    for i in range(ranks):
        decoded_refs[i][...] = stage_ref[i]


def score_kernel(region_ref, rank_ref, counts_ref, target_ref, *refs):
    count = (len(refs) - 1) // 2
    decoded_refs, grad_refs, score_ref = refs[:count], refs[count : 2 * count], refs[2 * count]
    channels, share = decoded_refs[0].shape
    pairs = [(i, j) for i in range(count) for j in range(i + 1, count)]
    first = pl.multiple_of(rank_ref[0] * share, 16)
    turned = target_ref[pl.ds(first, share), :].astype(jnp.float32).T
    total = jnp.zeros((1, LANE), jnp.float32)
    for lo, size in split(share, LANE):
        lanes = slice(lo, lo + size)

        def rows_of(c):
            values = [ref[c : c + 16, lanes].astype(jnp.float32) for ref in decoded_refs]
            return values, turned[c : c + 16, lanes]

        def fold(square):
            return square[:8] + square[8:]

        to_target = [jnp.zeros((8, size), jnp.float32)] * count
        apart = [jnp.zeros((8, size), jnp.float32)] * len(pairs)
        for c in range(0, channels, 16):
            values, goal = rows_of(c)
            for i in range(count):
                to_target[i] = to_target[i] + fold((values[i] - goal) ** 2)
            for p, (i, j) in enumerate(pairs):
                apart[p] = apart[p] + fold((values[i] - values[j]) ** 2)
        slot = first + lo + lax.broadcasted_iota(jnp.int32, (1, size), 1)
        live = (slot < counts_ref[region_ref[0]]).astype(jnp.float32)
        score = jnp.zeros((1, size), jnp.float32)

        def inverse(square, scale):
            squared = jnp.sum(square, axis=0, keepdims=True) + EPSILON
            inv = lax.rsqrt(squared)
            return squared * inv * scale, jnp.broadcast_to(inv * (scale * live), (8, size))

        inv_target, inv_pair = [], []
        for square in to_target:
            dist, inv = inverse(square, 1.0)
            score = score + dist
            inv_target.append(inv)
        for square in apart:
            dist, inv = inverse(square, 1.0 / (count - 1))
            score = score - dist
            inv_pair.append(inv)
        score = score * live
        if size < LANE:
            score = jnp.concatenate([score, jnp.zeros((1, LANE - size), jnp.float32)], axis=1)
        total = total + score
        for c in range(0, channels, 16):
            values, goal = rows_of(c)
            halves = []
            for h in (0, 8):
                near = [v[h : h + 8] for v in values]
                grads = [(near[i] - goal[h : h + 8]) * inv_target[i] for i in range(count)]
                for p, (i, j) in enumerate(pairs):
                    term = (near[i] - near[j]) * inv_pair[p]
                    grads[i] = grads[i] - term
                    grads[j] = grads[j] + term
                halves.append(grads)
            for i in range(count):
                grad_refs[i][c : c + 16, lanes] = jnp.concatenate(
                    [halves[0][i], halves[1][i]], axis=0
                ).astype(jnp.bfloat16)
    score_ref[...] = total


def backward(rank_ref, table_ref, slope_one_ref, slope_two_ref, w_one_ref, w_two_ref, w_three_ref, grad_refs, out_refs, stage_ref):
    d_dec_ref, d_two_ref, d_one_ref, d_mixed_ref, bias_one_ref, bias_two_ref, head_ref, tail_ref = out_refs
    ranks, channels, share = stage_ref.shape
    ext, slots = table_ref.shape
    hidden = slope_one_ref.shape[0]
    for i in range(ranks):
        stage_ref[rank_ref[0] ^ i] = grad_refs[i][...]
    for q in range(ranks):
        d_dec_ref[:, q * share : (q + 1) * share] = stage_ref[q]
    w_one, w_two, w_three = w_one_ref[...], w_two_ref[...] * 0.5, w_three_ref[...] * 0.5
    bias_one = jnp.zeros((hidden, LANE), jnp.float32)
    bias_two = jnp.zeros((hidden, LANE), jnp.float32)

    def lane_sum(values):
        return sum(values[:, lo : lo + LANE] for lo, _ in split(values.shape[1], LANE))

    for lo, size in split(slots, CHUNK):
        lanes = slice(lo, lo + size)
        back = nn_dot(w_three, d_dec_ref[:, lanes]) * slope_two_ref[:, lanes].astype(jnp.float32)
        bias_two = bias_two + lane_sum(back)
        d_two = back.astype(jnp.bfloat16)
        d_two_ref[:, lanes] = d_two
        back = nn_dot(w_two, d_two) * slope_one_ref[:, lanes].astype(jnp.float32)
        bias_one = bias_one + lane_sum(back)
        d_one = back.astype(jnp.bfloat16)
        d_one_ref[:, lanes] = d_one
        d_mixed_ref[:, lanes] = nn_dot(w_one, d_one).astype(jnp.bfloat16)
    bias_one_ref[...] = bias_one
    bias_two_ref[...] = bias_two
    head_ref[...] = nt_dot(table_ref[:HALO, :], d_mixed_ref[...]).astype(jnp.bfloat16)
    tail_ref[...] = nt_dot(table_ref[ext - HALO :, :], d_mixed_ref[...]).astype(jnp.bfloat16)


def backward_kernel(ranks, *refs):
    backward(*refs[:7], refs[7 : 7 + ranks], refs[7 + ranks : -1], refs[-1])


def weights_kernel(mixed_ref, act_one_ref, act_two_ref, d_one_ref, d_two_ref, d_dec_ref, one_ref, two_ref, three_ref):
    one_ref[...] = nt_dot(mixed_ref[...], d_one_ref[...])
    two_ref[...] = nt_dot(act_one_ref[...], d_two_ref[...])
    three_ref[...] = nt_dot(act_two_ref[...], d_dec_ref[...])


def last_backward_kernel(ranks, earlier, region_ref, *refs):
    base, refs = refs[:7], refs[7:]
    grad_refs, refs = refs[:ranks], refs[ranks:]
    score_ref, mixed_ref, act_one_ref, act_two_ref = refs[:4]
    before, refs = refs[4 : 4 + 5 * earlier], refs[4 + 5 * earlier :]
    d_mixed_ref, head_ref, tail_ref = refs[:3]
    piece_refs = refs[3 : 3 + ranks]
    d_dec_ref, d_two_ref, d_one_ref, bias_one_ref, bias_two_ref, grad_stage_ref, stage_ref = refs[3 + ranks :]
    results = (d_dec_ref, d_two_ref, d_one_ref, d_mixed_ref, bias_one_ref, bias_two_ref, head_ref, tail_ref)
    backward(*base, grad_refs, results, grad_stage_ref)

    def with_earlier(at, value):
        return sum((before[5 * e + at][...] for e in range(earlier)), value)

    def bias_row(at, ref):
        return jnp.sum(with_earlier(at, ref[...]).T, axis=0, keepdims=True)

    hidden = act_one_ref.shape[0]
    half = hidden // 2
    g_one = with_earlier(0, nt_dot(mixed_ref[...], d_one_ref[...]))
    g_two = with_earlier(1, nt_dot(act_one_ref[...], d_two_ref[...]))
    g_three = with_earlier(2, nt_dot(act_two_ref[...], d_dec_ref[...]))
    region = lax.broadcasted_iota(jnp.int32, (1, hidden), 1) == region_ref[0]
    tally = jnp.where(region, jnp.sum(score_ref[...]), 0.0)
    high = tally.astype(jnp.bfloat16).astype(jnp.float32)
    parts = [
        g_one,
        g_two,
        jnp.concatenate([g_three[:half], g_three[half:]], axis=1),
        bias_row(3, bias_one_ref),
        bias_row(4, bias_two_ref),
        high,
        tally - high,
    ]
    used = sum(part.shape[0] for part in parts)
    parts.append(jnp.zeros((ranks * stage_ref.shape[1] - used, hidden), jnp.float32))
    stage_ref[...] = jnp.concatenate(parts, axis=0).astype(stage_ref.dtype).reshape(stage_ref.shape)
    for i in range(ranks):
        piece_refs[i][0] = stage_ref[base[0][0] ^ i]


def halve_kernel(count, *refs):
    for i in range(count):
        total = refs[i][...].astype(jnp.float32) + refs[count + i][...].astype(jnp.float32)
        refs[2 * count + i][...] = total.astype(refs[i].dtype)


def region_sum_kernel(region_ref, *refs):
    *refs, sum_ref, stage_ref = refs
    for i, ref in enumerate(refs):
        stage_ref[region_ref[0] ^ i] = ref[0]
    sum_ref[0] = sum(stage_ref[i].astype(jnp.float32) for i in range(len(refs))).astype(sum_ref.dtype)


def unpack_kernel(scale, rank_ref, *refs):
    *refs, stage_ref = refs
    ranks = stage_ref.shape[0]
    one_ref, b_one_ref, two_ref, b_two_ref, three_ref, tally_ref = refs[ranks:]
    for i in range(ranks):
        stage_ref[rank_ref[0] ^ i] = refs[i][0]
    width, hidden = one_ref.shape
    sums = stage_ref[...].reshape(-1, hidden).astype(jnp.float32)
    half, channels = hidden // 2, three_ref.shape[1]
    one_ref[...] = sums[:width]
    two_ref[...] = sums[width : width + hidden]
    base = width + hidden
    three_ref[:half] = sums[base : base + half, :channels]
    three_ref[half:] = sums[base : base + half, channels:]
    last = sums[base + half : base + half + 8]
    b_one_ref[...] = last[0:1]
    b_two_ref[...] = last[1:2]
    tally_ref[...] = (last[2:3] + last[3:4])[:, : tally_ref.shape[1]] * scale


def own_kernel(table_ref, *refs):
    *d_mixed_refs, own_ref = refs
    members, nodes, _ = own_ref.shape
    for m in range(members):
        own_ref[m] = nt_dot(table_ref[HALO : HALO + nodes, :], d_mixed_refs[m][...])


def finish_kernel(own_ref, *refs):
    *refs, out_ref = refs
    members, nodes, _ = own_ref.shape
    for m in range(members):
        from_prev, from_next = refs[m][...], refs[members + m][...]
        out_ref[m, :HALO] = (own_ref[m, :HALO] + from_prev.astype(jnp.float32)).astype(jnp.bfloat16)
        out_ref[m, HALO : nodes - HALO] = own_ref[m, HALO : nodes - HALO].astype(jnp.bfloat16)
        out_ref[m, nodes - HALO :] = (own_ref[m, nodes - HALO :] + from_next.astype(jnp.float32)).astype(jnp.bfloat16)


def shifted(shard, axis, by):
    length = lax.axis_size(axis)
    return lax.ppermute(shard, axis, [(i, (i + by) % length) for i in range(length)])


def swapped(block, axis, by):
    return lax.ppermute(block, axis, [(i, i ^ by) for i in range(lax.axis_size(axis))])


def per_device(latent, neighbours, weights, targets, counts, w_one, b_one, w_two, b_two, w_three):
    members, nodes, width = latent.shape
    slots, channels = targets.shape
    hidden = w_one.shape[1]
    ext = nodes + 2 * HALO
    region, regions = lax.axis_index("space"), lax.axis_size("space")
    rank, ranks = lax.axis_index("member"), lax.axis_size("member")
    share = slots // ranks
    bf16, f32 = jnp.bfloat16, jnp.float32
    shape = jax.ShapeDtypeStruct
    each = range(members)

    edge = shape((HALO, width), bf16)
    *rims, latent = kernel_call(
        rims_kernel, (edge,) * (2 * members) + (shape(latent.shape, bf16),), flops=MIB, moved=3 * MIB, operands=1
    )(latent)
    before = [shifted(rims[2 * m], "space", 1) for m in each]
    after = [shifted(rims[2 * m + 1], "space", -1) for m in each]
    rank_at = rank[None].astype(jnp.int32)
    region_at = region[None].astype(jnp.int32)

    table, *part = kernel_call(
        table_kernel,
        (shape((ext, slots), bf16),) + (shape((width, slots), f32),) * members,
        flops=2 * members * width * nodes * slots,
        moved=12 * MIB,
        smem=3,
        operands=6,
    )(region_at, rank_at, counts, neighbours, weights, latent)

    saved_shape = shape((hidden, slots), bf16)
    mixed_shape = shape((width, slots), bf16)
    block = shape((channels, share), bf16)
    dense = width * hidden + hidden * hidden + hidden * channels
    saved, sent = [], []
    for m in each:
        out = kernel_call(
            forward_kernel,
            (mixed_shape,) + (saved_shape,) * 4 + (block,) * ranks,
            flops=2 * slots * (2 * HALO * width + dense),
            moved=8 * MIB,
            scratch=(pltpu.VMEM((ranks, channels, share), bf16),),
            smem=1,
            operands=10,
        )(rank_at, part[m], table, before[m], after[m], w_one, b_one[None], w_two, b_two[None], w_three)
        saved.append(out[:5])
        sent.append([out[5]] + [swapped(out[5 + i], "member", i) for i in range(1, ranks)])

    everyone = [sent[m][i] for m in each for i in range(ranks)]
    *grads, score = kernel_call(
        score_kernel,
        (block,) * len(everyone) + (shape((1, LANE), f32),),
        flops=4 * MIB,
        moved=2 * MIB,
        smem=3,
        operands=4 + len(everyone),
    )(region_at, rank_at, counts, targets, *everyone)

    bias = shape((hidden, LANE), f32)
    stage = pltpu.VMEM((ranks, channels, share), bf16)
    rows = -(-(width + hidden + hidden // 2 + 4) // (16 * ranks)) * 16
    piece = shape((1, rows, hidden), bf16)
    from_next, from_prev, d_mixed, carried = [], [], [], []
    for m in each:
        mixed, act_one, slope_one, act_two, slope_two = saved[m]
        given = grads[m * ranks : (m + 1) * ranks]
        given = [given[0]] + [swapped(given[i], "member", i) for i in range(1, ranks)]
        base = (rank_at, table, slope_one, slope_two, w_one, w_two, w_three, *given)
        if m < members - 1:
            d_dec, d_two, d_one, d_mix, bias_one, bias_two, head, tail = kernel_call(
                lambda *refs: backward_kernel(ranks, *refs),
                (shape((channels, slots), bf16), saved_shape, saved_shape, mixed_shape, bias, bias, edge, edge),
                flops=2 * slots * (2 * HALO * width + dense),
                moved=6 * MIB,
                scratch=(stage,),
                smem=1,
                operands=len(base),
            )(*base)
            carried += kernel_call(
                weights_kernel,
                (shape((width, hidden), f32), shape((hidden, hidden), f32), shape((hidden, channels), f32)),
                flops=2 * slots * dense,
                moved=4 * MIB,
                operands=6,
            )(mixed, act_one, act_two, d_one, d_two, d_dec)
            carried += [bias_one, bias_two]
        else:
            operands = (region_at, *base, score, mixed, act_one, act_two, *carried)
            d_mix, head, tail, *pieces = kernel_call(
                lambda *refs: last_backward_kernel(ranks, members - 1, *refs),
                (mixed_shape, edge, edge) + (piece,) * ranks,
                flops=2 * slots * (2 * HALO * width + 2 * dense),
                moved=10 * MIB,
                scratch=(
                    pltpu.VMEM((channels, slots), bf16),
                    pltpu.VMEM((hidden, slots), bf16),
                    pltpu.VMEM((hidden, slots), bf16),
                    pltpu.VMEM((hidden, LANE), f32),
                    pltpu.VMEM((hidden, LANE), f32),
                    stage,
                    pltpu.VMEM((ranks, rows, hidden), bf16),
                ),
                smem=2,
                operands=len(operands),
            )(*operands)
        d_mixed.append(d_mix)
        from_next.append(shifted(head, "space", -1))
        from_prev.append(shifted(tail, "space", 1))

    keep, send = pieces[::2], pieces[1::2]
    bit, other = 1, [swapped(block, "member", 1) for block in send]
    other, from_next[:-1], from_prev[:-1] = lax.optimization_barrier((other, from_next[:-1], from_prev[:-1]))
    while len(keep) > 1:
        both = kernel_call(
            lambda *refs: halve_kernel(len(keep), *refs), (piece,) * len(keep), flops=MIB, moved=MIB, operands=2 * len(keep)
        )(*keep, *other)
        keep, send = both[::2], both[1::2]
        bit = 2 * bit
        other = [swapped(block, "member", bit) for block in send]
    (quarter,) = kernel_call(
        lambda *refs: halve_kernel(1, *refs), (piece,), flops=MIB, moved=MIB, operands=2
    )(*keep, *other)
    quarters = [quarter] + [swapped(quarter, "space", i) for i in range(1, regions)]
    own = kernel_call(
        own_kernel,
        shape((members, nodes, width), f32),
        flops=2 * members * nodes * width * slots,
        moved=6 * MIB,
        operands=1 + members,
    )(table, *d_mixed)
    total = kernel_call(
        region_sum_kernel,
        piece,
        flops=MIB,
        moved=MIB,
        scratch=(pltpu.VMEM((regions, rows, hidden), bf16),),
        smem=1,
        operands=1 + regions,
    )(region_at, *quarters)
    latent_grad = kernel_call(
        finish_kernel,
        shape((members, nodes, width), bf16),
        flops=MIB,
        moved=3 * MIB,
        operands=1 + 2 * members,
    )(own, *from_prev, *from_next)
    total, latent_grad = lax.optimization_barrier((total, latent_grad))
    totals = {0: total}
    while bit:
        totals.update({i ^ bit: swapped(totals[i], "member", bit) for i in sorted(totals)})
        bit = bit // 2
    totals = [totals[i] for i in range(ranks)]
    row = shape((1, hidden), f32)
    g_one, g_bone, g_two, g_btwo, g_three, tally = kernel_call(
        lambda *refs: unpack_kernel(1.0 / (OBS_MEAN * members * ranks), *refs),
        (shape((width, hidden), f32), row, shape((hidden, hidden), f32), row, shape((hidden, channels), f32),
         shape((1, regions), f32)),
        flops=MIB,
        moved=2 * MIB,
        scratch=(pltpu.VMEM((ranks, rows, hidden), bf16),),
        smem=1,
        operands=1 + ranks,
    )(rank_at, *totals)
    return (tally[0], latent_grad, g_one, g_bone[0], g_two, g_btwo[0], g_three)


def solution(mesh):
    in_specs = (
        P("member", ("groups", "space"), None),
        P(None, ("groups", "space")),
        P(None, ("groups", "space")),
        P(("groups", "space"), None),
        P("groups"),
        P(),
        P(),
        P(),
        P(),
        P(),
    )
    out_specs = (
        P("groups"),
        P("member", ("groups", "space"), None),
        P("groups", None),
        P("groups"),
        P("groups", None),
        P("groups"),
        P("groups", None),
    )
    return jax.shard_map(
        per_device, mesh=mesh, in_specs=in_specs, out_specs=out_specs, check_vma=False
    )
```

```python
import jax
import jax.numpy as jnp
from jax import lax
from jax.experimental import pallas as pl
from jax.experimental.pallas import tpu as pltpu
from jax.sharding import PartitionSpec as P

K = 4
OBS_MEAN = 512
HALO = 256
EPSILON = 1e-05
BLOCK = 256
LANE = 128
CHUNK = 512
MIB = 1 << 20


def split(total, step):
    return [(start, min(step, total - start)) for start in range(0, total, step)]


def nt_dot(left, right):
    return lax.dot_general(
        left, right, (((1,), (1,)), ((), ())), preferred_element_type=jnp.float32
    )


def nn_dot(left, right):
    return jnp.dot(left, right, preferred_element_type=jnp.float32)


def kernel_call(body, out_shape, flops, moved, scratch=(), smem=0, operands=0):
    vmem = pl.BlockSpec(memory_space=pltpu.VMEM)
    specs = [pl.BlockSpec(memory_space=pltpu.SMEM)] * smem
    return pl.pallas_call(
        body,
        out_shape=out_shape,
        in_specs=specs + [vmem] * (operands - len(specs)),
        out_specs=jax.tree.map(lambda _: vmem, out_shape),
        scratch_shapes=list(scratch),
        compiler_params=pltpu.CompilerParams(vmem_limit_bytes=40 * MIB),
        cost_estimate=pl.CostEstimate(flops=flops, bytes_accessed=moved, transcendentals=0),
    )


def rims_kernel(latent_ref, *refs):
    members, nodes, _ = latent_ref.shape
    for m in range(members):
        refs[2 * m][...] = latent_ref[m, nodes - HALO :]
        refs[2 * m + 1][...] = latent_ref[m, :HALO]
    refs[-1][...] = latent_ref[...]


def table_kernel(region_ref, rank_ref, counts_ref, nbr_ref, weight_ref, latent_ref, table_ref, *part_refs):
    members, nodes, width = latent_ref.shape
    ext, slots = table_ref.shape
    live = lax.broadcasted_iota(jnp.int32, (1, slots), 1) < counts_ref[region_ref[0]]
    nbr = [nbr_ref[k : k + 1, :] for k in range(K)]
    own = [jnp.where(live, weight_ref[k : k + 1, :], 0.0) for k in range(K)]
    joint = []
    for k in range(K):
        total = own[k]
        for j in range(K):
            if j != k:
                total = total + jnp.where(nbr[j] == nbr[k], own[j], 0.0)
        joint.append(total)
    groups = BLOCK // 16
    rows = (
        lax.broadcasted_iota(jnp.int32, (groups, 16, LANE), 0) * 16
        + lax.broadcasted_iota(jnp.int32, (groups, 16, LANE), 1)
    ).astype(jnp.float32).astype(jnp.bfloat16)
    for lo, size in split(slots, LANE):
        wide = [
            jnp.broadcast_to(joint[k][:, lo : lo + size], (16, size)).astype(jnp.bfloat16)
            for k in range(K)
        ]
        for b in range(ext // BLOCK):
            tile = jnp.zeros((groups, 16, size), jnp.bfloat16)
            for k in range(K):
                near = (nbr[k][:, lo : lo + size] - b * BLOCK).astype(jnp.float32)
                near = jnp.broadcast_to(near, (16, size)).astype(jnp.bfloat16)
                tile = jnp.where(rows[:, :, :size] == near[None], wide[k][None], tile)
            table_ref[b * BLOCK : (b + 1) * BLOCK, lo : lo + size] = tile.reshape(BLOCK, size)
    turned = jnp.concatenate([latent_ref[m].T for m in range(members)], axis=0)
    for lo, size in split(slots, CHUNK):
        part = nn_dot(turned, table_ref[HALO : HALO + nodes, lo : lo + size])
        for m in range(members):
            part_refs[m][:, lo : lo + size] = part[m * width : (m + 1) * width]


def column(ref):
    height = ref.shape[1]
    return jnp.broadcast_to(ref[...], (LANE, height)).T


def forward_kernel(
    part_ref, table_ref, before_ref, after_ref, w_one_ref, b_one_ref, w_two_ref, b_two_ref, w_three_ref,
    mixed_ref, act_one_ref, slope_one_ref, act_two_ref, slope_two_ref, decoded_ref,
):
    ext, slots = table_ref.shape
    w_one, w_two, w_three = w_one_ref[...].T * 0.5, w_two_ref[...].T * 0.5, w_three_ref[...].T
    b_one, b_two = column(b_one_ref) * 0.5, column(b_two_ref) * 0.5

    def layer(weight, bias, values, size):
        half = nn_dot(weight, values) + jnp.concatenate([bias] * (size // LANE), axis=1)
        gate = 1.0 + jnp.tanh(half)
        act = half * gate
        return act.astype(jnp.bfloat16), (gate + act * (2.0 - gate)).astype(jnp.bfloat16)

    edges = jnp.concatenate([before_ref[...].T, after_ref[...].T], axis=1)
    for lo, size in split(slots, CHUNK):
        lanes = slice(lo, lo + size)
        rim = jnp.concatenate([table_ref[:HALO, lanes], table_ref[ext - HALO :, lanes]], axis=0)
        mixed = (part_ref[:, lanes] + nn_dot(edges, rim)).astype(jnp.bfloat16)
        mixed_ref[:, lanes] = mixed
        act_one, slope_one_ref[:, lanes] = layer(w_one, b_one, mixed, size)
        act_one_ref[:, lanes] = act_one
        act_two, slope_two_ref[:, lanes] = layer(w_two, b_two, act_one, size)
        act_two_ref[:, lanes] = act_two
        decoded_ref[:, lanes] = nn_dot(w_three, act_two).astype(jnp.bfloat16)


def score_kernel(mine, others, count, first, last, region_ref, counts_ref, *refs):
    own_refs, refs = refs[:mine], refs[mine:]
    other_refs, refs = refs[:others], refs[others:]
    if first:
        target_ref, refs = refs[0], refs[1:]
        old_refs, old_score = None, 0.0
    else:
        old_refs, old_score, refs = refs[:mine], refs[mine][...], refs[mine + 1 :]
    grad_refs, score_ref = refs[:mine], refs[mine]
    channels, slots = own_refs[0].shape
    inner = [(i, j) for i in range(mine) for j in range(i + 1, mine)] if first else []
    outer = [(i, mine + j) for i in range(mine) for j in range(others)]
    pairs = inner + outer
    shares = [1.0 / (count - 1)] * len(inner) + [0.5 / (count - 1)] * len(outer)
    live_count = counts_ref[region_ref[0]]

    def one_tile(at, total):
        start = pl.multiple_of(at * LANE, LANE)
        lanes = pl.ds(start, LANE)
        if first:
            turned = target_ref[lanes, :].astype(jnp.float32).T

        def rows_of(c):
            return [ref[c : c + 16, lanes].astype(jnp.float32) for ref in (*own_refs, *other_refs)]

        def fold(square):
            return square[:8] + square[8:]

        to_target = [jnp.zeros((8, LANE), jnp.float32)] * (mine if first else 0)
        apart = [jnp.zeros((8, LANE), jnp.float32)] * len(pairs)
        for c in range(0, channels, 16):
            values = rows_of(c)
            for i in range(len(to_target)):
                to_target[i] = to_target[i] + fold((values[i] - turned[c : c + 16]) ** 2)
            for p, (i, j) in enumerate(pairs):
                apart[p] = apart[p] + fold((values[i] - values[j]) ** 2)
        live = start + lax.broadcasted_iota(jnp.int32, (1, LANE), 1) < live_count
        score = jnp.zeros((1, LANE), jnp.float32)

        def inverse(square):
            squared = jnp.sum(square, axis=0, keepdims=True) + EPSILON
            inv = lax.rsqrt(squared)
            return squared * inv, inv

        inv_target, inv_pair = [], []
        for square in to_target:
            dist, inv = inverse(square)
            score = score + dist
            inv_target.append(jnp.broadcast_to(inv, (8, LANE)))
        for square, share in zip(apart, shares):
            dist, inv = inverse(square)
            score = score - dist * share
            inv_pair.append(jnp.broadcast_to(inv * (1.0 / (count - 1)), (8, LANE)))
        for c in range(0, channels, 16):
            values = rows_of(c)
            halves = []
            for h in (0, 8):
                near = [v[h : h + 8] for v in values]
                rows = slice(c + h, c + h + 8)
                if first:
                    grads = [(near[i] - turned[rows]) * inv_target[i] for i in range(mine)]
                else:
                    grads = [old_refs[i][rows, lanes] for i in range(mine)]
                for p, (i, j) in enumerate(pairs):
                    term = (near[i] - near[j]) * inv_pair[p]
                    grads[i] = grads[i] - term
                    if j < mine:
                        grads[j] = grads[j] + term
                halves.append(grads)
            for i in range(mine):
                grad = jnp.concatenate([halves[0][i], halves[1][i]], axis=0)
                if last:
                    grad = jnp.where(live, grad, 0.0)
                grad_refs[i][c : c + 16, lanes] = grad.astype(grad_refs[i].dtype)
        return total + jnp.where(live, score, 0.0)

    score_ref[...] = old_score + lax.fori_loop(0, slots // LANE, one_tile, jnp.zeros((1, LANE), jnp.float32))


def backward_kernel(members, ranks, region_ref, rank_ref, w_two_ref, w_three_ref, score_ref, *refs):
    saved = [refs[6 * m : 6 * (m + 1)] for m in range(members)]
    refs = refs[6 * members :]
    d_one_refs, refs = refs[:members], refs[members:]
    piece_refs, (d_two_ref, stage_ref) = refs[:ranks], refs[ranks:]
    w_two, w_three = w_two_ref[...] * 0.5, w_three_ref[...] * 0.5
    width, slots = saved[0][0].shape
    hidden = saved[0][1].shape[0]
    bias_one = jnp.zeros((hidden, LANE), jnp.float32)
    bias_two = jnp.zeros((hidden, LANE), jnp.float32)

    def lane_sum(values):
        return sum(values[:, lo : lo + LANE] for lo, _ in split(values.shape[1], LANE))

    g_one, g_two, g_three = 0.0, 0.0, 0.0
    for m in range(members):
        mixed_ref, act_one_ref, slope_one_ref, act_two_ref, slope_two_ref, d_dec_ref = saved[m]
        for lo, size in split(slots, CHUNK):
            lanes = slice(lo, lo + size)
            back = nn_dot(w_three, d_dec_ref[:, lanes]) * slope_two_ref[:, lanes].astype(jnp.float32)
            bias_two = bias_two + lane_sum(back)
            d_two = back.astype(jnp.bfloat16)
            d_two_ref[m, :, lanes] = d_two
            back = nn_dot(w_two, d_two) * slope_one_ref[:, lanes].astype(jnp.float32)
            bias_one = bias_one + lane_sum(back)
            d_one_refs[m][:, lanes] = back.astype(jnp.bfloat16)
        g_three = g_three + nt_dot(act_two_ref[...], d_dec_ref[...])
        g_two = g_two + nt_dot(act_one_ref[...], d_two_ref[m])
        g_one = g_one + nt_dot(mixed_ref[...], d_one_refs[m][...])
    half = hidden // 2
    region = lax.broadcasted_iota(jnp.int32, (1, hidden), 1) == region_ref[0]
    tally = jnp.where(region, jnp.sum(score_ref[...]), 0.0)
    high = tally.astype(jnp.bfloat16).astype(jnp.float32)
    parts = [
        g_one,
        g_two,
        jnp.concatenate([g_three[:half], g_three[half:]], axis=1),
        jnp.sum(bias_one.T, axis=0, keepdims=True),
        jnp.sum(bias_two.T, axis=0, keepdims=True),
        high,
        tally - high,
    ]
    used = sum(part.shape[0] for part in parts)
    parts.append(jnp.zeros((ranks * stage_ref.shape[1] - used, hidden), jnp.float32))
    stage_ref[...] = jnp.concatenate(parts, axis=0).astype(stage_ref.dtype).reshape(stage_ref.shape)
    for i in range(ranks):
        piece_refs[i][...] = stage_ref[rank_ref[0] ^ i]


def edges_kernel(members, table_ref, w_one_ref, *refs):
    d_one_refs, refs = refs[:members], refs[members:]
    d_mixed_refs, (head_ref, tail_ref) = refs[:members], refs[members:]
    ext = table_ref.shape[0]
    for m in range(members):
        d_mixed = nn_dot(w_one_ref[...], d_one_refs[m][...]).astype(jnp.bfloat16)
        d_mixed_refs[m][...] = d_mixed
        head_ref[m] = nt_dot(table_ref[:HALO, :], d_mixed).astype(jnp.bfloat16)
        tail_ref[m] = nt_dot(table_ref[ext - HALO :, :], d_mixed).astype(jnp.bfloat16)


def sum_kernel(count, *refs):
    for i in range(count):
        total = refs[i][...].astype(jnp.float32) + refs[count + i][...].astype(jnp.float32)
        refs[2 * count + i][...] = total.astype(refs[i].dtype)


def unpack_kernel(scale, rank_ref, *refs):
    *refs, stage_ref = refs
    ranks = stage_ref.shape[0]
    one_ref, b_one_ref, two_ref, b_two_ref, three_ref, tally_ref = refs[ranks:]
    for i in range(ranks):
        stage_ref[rank_ref[0] ^ i] = refs[i][...]
    width, hidden = one_ref.shape
    sums = stage_ref[...].reshape(-1, hidden).astype(jnp.float32)
    half, channels = hidden // 2, three_ref.shape[1]
    one_ref[...] = sums[:width]
    two_ref[...] = sums[width : width + hidden]
    base = width + hidden
    three_ref[:half] = sums[base : base + half, :channels]
    three_ref[half:] = sums[base : base + half, channels:]
    last = sums[base + half : base + half + 8]
    b_one_ref[...] = last[0:1]
    b_two_ref[...] = last[1:2]
    tally_ref[...] = (last[2:3] + last[3:4])[:, : tally_ref.shape[1]] * scale


def own_kernel(table_ref, *refs):
    *d_mixed_refs, own_ref = refs
    members, nodes, _ = own_ref.shape
    for m in range(members):
        own_ref[m] = nt_dot(table_ref[HALO : HALO + nodes, :], d_mixed_refs[m][...])


def finish_kernel(own_ref, from_prev_ref, from_next_ref, out_ref):
    nodes = own_ref.shape[1]
    from_prev, from_next = from_prev_ref[...].astype(jnp.float32), from_next_ref[...].astype(jnp.float32)
    out_ref[:, :HALO] = (own_ref[:, :HALO] + from_prev).astype(jnp.bfloat16)
    out_ref[:, HALO : nodes - HALO] = own_ref[:, HALO : nodes - HALO].astype(jnp.bfloat16)
    out_ref[:, nodes - HALO :] = (own_ref[:, nodes - HALO :] + from_next).astype(jnp.bfloat16)


def shifted(shard, axis, by):
    length = lax.axis_size(axis)
    return lax.ppermute(shard, axis, [(i, (i + by) % length) for i in range(length)])


def swapped(block, axis, by):
    return lax.ppermute(block, axis, [(i, i ^ by) for i in range(lax.axis_size(axis))])


def per_device(latent, neighbours, weights, targets, counts, w_one, b_one, w_two, b_two, w_three):
    members, nodes, width = latent.shape
    slots, channels = targets.shape
    hidden = w_one.shape[1]
    ext = nodes + 2 * HALO
    region, regions = lax.axis_index("space"), lax.axis_size("space")
    rank, ranks = lax.axis_index("member"), lax.axis_size("member")
    share = slots // ranks
    bf16, f32 = jnp.bfloat16, jnp.float32
    shape = jax.ShapeDtypeStruct
    each = range(members)

    edge = shape((HALO, width), bf16)
    *rims, latent = kernel_call(
        rims_kernel, (edge,) * (2 * members) + (shape(latent.shape, bf16),), flops=MIB, moved=3 * MIB, operands=1
    )(latent)
    before = [shifted(rims[2 * m], "space", 1) for m in each]
    after = [shifted(rims[2 * m + 1], "space", -1) for m in each]
    rank_at = rank[None].astype(jnp.int32)
    region_at = region[None].astype(jnp.int32)

    table, *part = kernel_call(
        table_kernel,
        (shape((ext, slots), bf16),) + (shape((width, slots), f32),) * members,
        flops=2 * members * width * nodes * slots,
        moved=12 * MIB,
        smem=3,
        operands=6,
    )(region_at, rank_at, counts, neighbours, weights, latent)

    saved_shape = shape((hidden, slots), bf16)
    mixed_shape = shape((width, slots), bf16)
    decoded_shape = shape((channels, slots), bf16)
    dense = width * hidden + hidden * hidden + hidden * channels
    saved, known = [], []
    for m in each:
        *kept, decoded = kernel_call(
            forward_kernel,
            (mixed_shape,) + (saved_shape,) * 4 + (decoded_shape,),
            flops=2 * slots * (2 * HALO * width + dense),
            moved=8 * MIB,
            operands=9,
        )(part[m], table, before[m], after[m], w_one, b_one[None], w_two, b_two[None], w_three)
        saved.append(kept)
        known.append({0: decoded})
        bit = 2
        while bit < ranks:
            known[m].update({i ^ bit: swapped(known[m][i], "member", bit) for i in sorted(known[m])})
            bit = 2 * bit
        known[m][1] = swapped(decoded, "member", 1)

    def scored(others, carried, first=False, last=False):
        operands = (region_at, counts, *[known[m][0] for m in each], *others, *carried)
        return kernel_call(
            lambda *refs: score_kernel(members, len(others), members * ranks, first, last, *refs),
            (shape((channels, slots), bf16 if last else f32),) * members + (shape((1, LANE), f32),),
            flops=4 * MIB,
            moved=2 * MIB,
            smem=2,
            operands=len(operands),
        )(*operands)

    near = [{i: block for i, block in known[m].items() if i > 1} for m in each]
    beside = [known[m][1] for m in each]
    near[:-1], beside = lax.optimization_barrier((near[:-1], beside))
    carried = scored(beside, [targets], first=True)
    near[-1], carried = lax.optimization_barrier((near[-1], carried))
    others = [block for blocks in near for block in blocks.values()]
    others += [swapped(block, "member", 1) for block in others]
    carried = scored(others, carried, last=True)
    *d_decoded, score = carried

    rows = -(-(width + hidden + hidden // 2 + 4) // (16 * ranks)) * 16
    piece = shape((rows, hidden), bf16)
    operands = [region_at, rank_at, w_two, w_three, score]
    for m in each:
        operands += [*saved[m], d_decoded[m]]
    out = kernel_call(
        lambda *refs: backward_kernel(members, ranks, *refs),
        (saved_shape,) * members + (piece,) * ranks,
        flops=4 * members * slots * dense,
        moved=10 * MIB,
        scratch=(pltpu.VMEM((members, hidden, slots), bf16), pltpu.VMEM((ranks, rows, hidden), bf16)),
        smem=2,
        operands=len(operands),
    )(*operands)
    d_one, pieces = out[:members], out[members:]

    def summed(ones, others):
        return kernel_call(
            lambda *refs: sum_kernel(len(ones), *refs), (piece,) * len(ones), flops=MIB, moved=MIB, operands=2 * len(ones)
        )(*ones, *others)

    both = shape((members, HALO, width), bf16)
    *d_mixed, head, tail = kernel_call(
        lambda *refs: edges_kernel(members, *refs),
        (mixed_shape,) * members + (both, both),
        flops=2 * members * slots * width * (hidden + 2 * HALO),
        moved=6 * MIB,
        operands=2 + members,
    )(table, w_one, *d_one)
    bit = 1
    while bit < ranks:
        received = [swapped(sent, "member", bit) for sent in pieces[1::2]]
        if bit == 1:
            received, head, tail = lax.optimization_barrier((received, head, tail))
        pieces = summed(pieces[::2], received)
        bit = 2 * bit
    from_next = shifted(head, "space", -1)
    from_prev = shifted(tail, "space", 1)
    own = kernel_call(
        own_kernel,
        shape((members, nodes, width), f32),
        flops=2 * members * nodes * width * slots,
        moved=6 * MIB,
        operands=1 + members,
    )(table, *d_mixed)
    (total,) = pieces
    step = 1
    while step < regions:
        (total,) = summed([total], [swapped(total, "space", step)])
        step = 2 * step
    latent_grad = kernel_call(
        finish_kernel,
        shape((members, nodes, width), bf16),
        flops=MIB,
        moved=3 * MIB,
        operands=3,
    )(own, from_prev, from_next)
    total, latent_grad = lax.optimization_barrier((total, latent_grad))
    totals = {0: total}
    while bit > 1:
        bit = bit // 2
        totals.update({i ^ bit: swapped(totals[i], "member", bit) for i in sorted(totals)})
    totals = [totals[i] for i in range(ranks)]
    row = shape((1, hidden), f32)
    g_one, g_bone, g_two, g_btwo, g_three, tally = kernel_call(
        lambda *refs: unpack_kernel(1.0 / (OBS_MEAN * members * ranks), *refs),
        (shape((width, hidden), f32), row, shape((hidden, hidden), f32), row, shape((hidden, channels), f32),
         shape((1, regions), f32)),
        flops=MIB,
        moved=2 * MIB,
        scratch=(pltpu.VMEM((ranks, rows, hidden), bf16),),
        smem=1,
        operands=1 + ranks,
    )(rank_at, *totals)
    return (tally[0], latent_grad, g_one, g_bone[0], g_two, g_btwo[0], g_three)


def solution(mesh):
    in_specs = (
        P("member", ("groups", "space"), None),
        P(None, ("groups", "space")),
        P(None, ("groups", "space")),
        P(("groups", "space"), None),
        P("groups"),
        P(),
        P(),
        P(),
        P(),
        P(),
    )
    out_specs = (
        P("groups"),
        P("member", ("groups", "space"), None),
        P("groups", None),
        P("groups"),
        P("groups", None),
        P("groups"),
        P("groups", None),
    )
    return jax.shard_map(
        per_device, mesh=mesh, in_specs=in_specs, out_specs=out_specs, check_vma=False
    )
```

```python
import jax
import jax.numpy as jnp
from jax import lax
from jax.experimental import pallas as pl
from jax.experimental.pallas import tpu as pltpu
from jax.sharding import PartitionSpec as P

K = 4
OBS_MEAN = 512
HALO = 256
EPSILON = 1e-05
BLOCK = 256
LANE = 128
CHUNK = 512
MIB = 1 << 20


def split(total, step):
    return [(start, min(step, total - start)) for start in range(0, total, step)]


def nt_dot(left, right):
    return lax.dot_general(
        left, right, (((1,), (1,)), ((), ())), preferred_element_type=jnp.float32
    )


def nn_dot(left, right):
    return jnp.dot(left, right, preferred_element_type=jnp.float32)


def kernel_call(body, out_shape, flops, moved, scratch=(), smem=0, operands=0):
    vmem = pl.BlockSpec(memory_space=pltpu.VMEM)
    specs = [pl.BlockSpec(memory_space=pltpu.SMEM)] * smem
    return pl.pallas_call(
        body,
        out_shape=out_shape,
        in_specs=specs + [vmem] * (operands - len(specs)),
        out_specs=jax.tree.map(lambda _: vmem, out_shape),
        scratch_shapes=list(scratch),
        compiler_params=pltpu.CompilerParams(vmem_limit_bytes=40 * MIB),
        cost_estimate=pl.CostEstimate(flops=flops, bytes_accessed=moved, transcendentals=0),
    )


def rims_kernel(latent_ref, *refs):
    members, nodes, _ = latent_ref.shape
    for m in range(members):
        refs[2 * m][...] = latent_ref[m, nodes - HALO :]
        refs[2 * m + 1][...] = latent_ref[m, :HALO]
    refs[-1][...] = latent_ref[...]


def table_kernel(region_ref, rank_ref, counts_ref, nbr_ref, weight_ref, latent_ref, table_ref, part_ref):
    nodes = latent_ref.shape[1]
    ext, slots = table_ref.shape
    live = lax.broadcasted_iota(jnp.int32, (1, slots), 1) < counts_ref[region_ref[0]]
    nbr = [nbr_ref[k : k + 1, :] for k in range(K)]
    own = [jnp.where(live, weight_ref[k : k + 1, :], 0.0) for k in range(K)]
    joint = []
    for k in range(K):
        total = own[k]
        for j in range(K):
            if j != k:
                total = total + jnp.where(nbr[j] == nbr[k], own[j], 0.0)
        joint.append(total)
    groups = BLOCK // 16
    rows = (
        lax.broadcasted_iota(jnp.int32, (groups, 16, LANE), 0) * 16
        + lax.broadcasted_iota(jnp.int32, (groups, 16, LANE), 1)
    ).astype(jnp.float32).astype(jnp.bfloat16)
    for lo, size in split(slots, LANE):
        wide = [
            jnp.broadcast_to(joint[k][:, lo : lo + size], (16, size)).astype(jnp.bfloat16)
            for k in range(K)
        ]
        for b in range(ext // BLOCK):
            tile = jnp.zeros((groups, 16, size), jnp.bfloat16)
            for k in range(K):
                near = (nbr[k][:, lo : lo + size] - b * BLOCK).astype(jnp.float32)
                near = jnp.broadcast_to(near, (16, size)).astype(jnp.bfloat16)
                tile = jnp.where(rows[:, :, :size] == near[None], wide[k][None], tile)
            table_ref[b * BLOCK : (b + 1) * BLOCK, lo : lo + size] = tile.reshape(BLOCK, size)
    turned = latent_ref[0].T
    for lo, size in split(slots, CHUNK):
        part_ref[:, lo : lo + size] = nn_dot(turned, table_ref[HALO : HALO + nodes, lo : lo + size])


def column(ref):
    height = ref.shape[1]
    return jnp.broadcast_to(ref[...], (LANE, height)).T


def forward_kernel(
    member, own_ref, table_ref, before_ref, after_ref, w_one_ref, b_one_ref, w_two_ref, b_two_ref, w_three_ref,
    mixed_ref, act_one_ref, slope_one_ref, act_two_ref, slope_two_ref, decoded_ref,
):
    ext, slots = table_ref.shape
    w_one, w_two, w_three = w_one_ref[...].T * 0.5, w_two_ref[...].T * 0.5, w_three_ref[...].T
    b_one, b_two = column(b_one_ref) * 0.5, column(b_two_ref) * 0.5

    def layer(weight, bias, values, size):
        half = nn_dot(weight, values) + jnp.concatenate([bias] * (size // LANE), axis=1)
        gate = 1.0 + jnp.tanh(half)
        act = half * gate
        return act.astype(jnp.bfloat16), (gate + act * (2.0 - gate)).astype(jnp.bfloat16)

    if member:
        nodes = jnp.concatenate([before_ref[...].T, own_ref[member].T, after_ref[...].T], axis=1)
    else:
        nodes = jnp.concatenate([before_ref[...].T, after_ref[...].T], axis=1)
    for lo, size in split(slots, CHUNK):
        lanes = slice(lo, lo + size)
        if member:
            mixed = nn_dot(nodes, table_ref[:, lanes])
        else:
            rims = jnp.concatenate([table_ref[:HALO, lanes], table_ref[ext - HALO :, lanes]], axis=0)
            mixed = own_ref[:, lanes] + nn_dot(nodes, rims)
        mixed = mixed.astype(jnp.bfloat16)
        mixed_ref[:, lanes] = mixed
        act_one, slope_one_ref[:, lanes] = layer(w_one, b_one, mixed, size)
        act_one_ref[:, lanes] = act_one
        act_two, slope_two_ref[:, lanes] = layer(w_two, b_two, act_one, size)
        act_two_ref[:, lanes] = act_two
        decoded_ref[:, lanes] = nn_dot(w_three, act_two).astype(jnp.bfloat16)


def score_kernel(mine, others, count, first, last, region_ref, counts_ref, *refs):
    own_refs, refs = refs[:mine], refs[mine:]
    other_refs, refs = refs[:others], refs[others:]
    if first:
        target_ref, refs = refs[0], refs[1:]
        old_refs, old_score = None, 0.0
    else:
        old_refs, old_score, refs = refs[:mine], refs[mine][...], refs[mine + 1 :]
    grad_refs, score_ref = refs[:mine], refs[mine]
    channels, slots = own_refs[0].shape
    inner = [(i, j) for i in range(mine) for j in range(i + 1, mine)] if first else []
    outer = [(i, mine + j) for i in range(mine) for j in range(others)]
    pairs = inner + outer
    shares = [1.0 / (count - 1)] * len(inner) + [0.5 / (count - 1)] * len(outer)
    live_count = counts_ref[region_ref[0]]

    def one_tile(at, total):
        start = pl.multiple_of(at * LANE, LANE)
        lanes = pl.ds(start, LANE)
        if first:
            turned = target_ref[lanes, :].astype(jnp.float32).T

        def rows_of(c):
            return [ref[c : c + 16, lanes].astype(jnp.float32) for ref in (*own_refs, *other_refs)]

        def fold(square):
            return square[:8] + square[8:]

        to_target = [jnp.zeros((8, LANE), jnp.float32)] * (mine if first else 0)
        apart = [jnp.zeros((8, LANE), jnp.float32)] * len(pairs)
        for c in range(0, channels, 16):
            values = rows_of(c)
            for i in range(len(to_target)):
                to_target[i] = to_target[i] + fold((values[i] - turned[c : c + 16]) ** 2)
            for p, (i, j) in enumerate(pairs):
                apart[p] = apart[p] + fold((values[i] - values[j]) ** 2)
        live = start + lax.broadcasted_iota(jnp.int32, (1, LANE), 1) < live_count
        score = jnp.zeros((1, LANE), jnp.float32)

        def inverse(square):
            squared = jnp.sum(square, axis=0, keepdims=True) + EPSILON
            inv = lax.rsqrt(squared)
            return squared * inv, inv

        inv_target, inv_pair = [], []
        for square in to_target:
            dist, inv = inverse(square)
            score = score + dist
            inv_target.append(jnp.broadcast_to(inv, (8, LANE)))
        for square, share in zip(apart, shares):
            dist, inv = inverse(square)
            score = score - dist * share
            inv_pair.append(jnp.broadcast_to(inv * (1.0 / (count - 1)), (8, LANE)))
        for c in range(0, channels, 16):
            values = rows_of(c)
            halves = []
            for h in (0, 8):
                near = [v[h : h + 8] for v in values]
                rows = slice(c + h, c + h + 8)
                if first:
                    grads = [(near[i] - turned[rows]) * inv_target[i] for i in range(mine)]
                else:
                    grads = [old_refs[i][rows, lanes] for i in range(mine)]
                for p, (i, j) in enumerate(pairs):
                    term = (near[i] - near[j]) * inv_pair[p]
                    grads[i] = grads[i] - term
                    if j < mine:
                        grads[j] = grads[j] + term
                halves.append(grads)
            for i in range(mine):
                grad = jnp.concatenate([halves[0][i], halves[1][i]], axis=0)
                if last:
                    grad = jnp.where(live, grad, 0.0)
                grad_refs[i][c : c + 16, lanes] = grad.astype(grad_refs[i].dtype)
        return total + jnp.where(live, score, 0.0)

    score_ref[...] = old_score + lax.fori_loop(0, slots // LANE, one_tile, jnp.zeros((1, LANE), jnp.float32))


def backward_kernel(members, ranks, region_ref, rank_ref, w_two_ref, w_three_ref, score_ref, *refs):
    saved = [refs[6 * m : 6 * (m + 1)] for m in range(members)]
    refs = refs[6 * members :]
    d_one_refs, refs = refs[:members], refs[members:]
    piece_refs, (d_two_ref, stage_ref) = refs[:ranks], refs[ranks:]
    w_two, w_three = w_two_ref[...] * 0.5, w_three_ref[...] * 0.5
    width, slots = saved[0][0].shape
    hidden = saved[0][1].shape[0]
    bias_one = jnp.zeros((hidden, LANE), jnp.float32)
    bias_two = jnp.zeros((hidden, LANE), jnp.float32)

    def lane_sum(values):
        return sum(values[:, lo : lo + LANE] for lo, _ in split(values.shape[1], LANE))

    g_one, g_two, g_three = 0.0, 0.0, 0.0
    for m in range(members):
        mixed_ref, act_one_ref, slope_one_ref, act_two_ref, slope_two_ref, d_dec_ref = saved[m]
        for lo, size in split(slots, CHUNK):
            lanes = slice(lo, lo + size)
            back = nn_dot(w_three, d_dec_ref[:, lanes]) * slope_two_ref[:, lanes].astype(jnp.float32)
            bias_two = bias_two + lane_sum(back)
            d_two = back.astype(jnp.bfloat16)
            d_two_ref[m, :, lanes] = d_two
            back = nn_dot(w_two, d_two) * slope_one_ref[:, lanes].astype(jnp.float32)
            bias_one = bias_one + lane_sum(back)
            d_one_refs[m][:, lanes] = back.astype(jnp.bfloat16)
        g_three = g_three + nt_dot(act_two_ref[...], d_dec_ref[...])
        g_two = g_two + nt_dot(act_one_ref[...], d_two_ref[m])
        g_one = g_one + nt_dot(mixed_ref[...], d_one_refs[m][...])
    half = hidden // 2
    region = lax.broadcasted_iota(jnp.int32, (1, hidden), 1) == region_ref[0]
    tally = jnp.where(region, jnp.sum(score_ref[...]), 0.0)
    high = tally.astype(jnp.bfloat16).astype(jnp.float32)
    parts = [
        g_one,
        g_two,
        jnp.concatenate([g_three[:half], g_three[half:]], axis=1),
        jnp.sum(bias_one.T, axis=0, keepdims=True),
        jnp.sum(bias_two.T, axis=0, keepdims=True),
        high,
        tally - high,
    ]
    used = sum(part.shape[0] for part in parts)
    parts.append(jnp.zeros((ranks * stage_ref.shape[1] - used, hidden), jnp.float32))
    stage_ref[...] = jnp.concatenate(parts, axis=0).astype(stage_ref.dtype).reshape(stage_ref.shape)
    for i in range(ranks):
        piece_refs[i][...] = stage_ref[rank_ref[0] ^ i]


def edges_kernel(members, table_ref, w_one_ref, *refs):
    d_one_refs, refs = refs[:members], refs[members:]
    d_mixed_refs, (head_ref, tail_ref) = refs[:members], refs[members:]
    ext = table_ref.shape[0]
    for m in range(members):
        d_mixed = nn_dot(w_one_ref[...], d_one_refs[m][...]).astype(jnp.bfloat16)
        d_mixed_refs[m][...] = d_mixed
        head_ref[m] = nt_dot(table_ref[:HALO, :], d_mixed).astype(jnp.bfloat16)
        tail_ref[m] = nt_dot(table_ref[ext - HALO :, :], d_mixed).astype(jnp.bfloat16)


def sum_kernel(count, *refs):
    for i in range(count):
        total = refs[i][...].astype(jnp.float32) + refs[count + i][...].astype(jnp.float32)
        refs[2 * count + i][...] = total.astype(refs[i].dtype)


def unpack_kernel(scale, rank_ref, *refs):
    *refs, stage_ref = refs
    ranks = stage_ref.shape[0]
    one_ref, b_one_ref, two_ref, b_two_ref, three_ref, tally_ref = refs[ranks:]
    for i in range(ranks):
        stage_ref[rank_ref[0] ^ i] = refs[i][...]
    width, hidden = one_ref.shape
    sums = stage_ref[...].reshape(-1, hidden).astype(jnp.float32)
    half, channels = hidden // 2, three_ref.shape[1]
    one_ref[...] = sums[:width]
    two_ref[...] = sums[width : width + hidden]
    base = width + hidden
    three_ref[:half] = sums[base : base + half, :channels]
    three_ref[half:] = sums[base : base + half, channels:]
    last = sums[base + half : base + half + 8]
    b_one_ref[...] = last[0:1]
    b_two_ref[...] = last[1:2]
    tally_ref[...] = (last[2:3] + last[3:4])[:, : tally_ref.shape[1]] * scale


def own_kernel(table_ref, *refs):
    *d_mixed_refs, own_ref = refs
    members, nodes, _ = own_ref.shape
    for m in range(members):
        own_ref[m] = nt_dot(table_ref[HALO : HALO + nodes, :], d_mixed_refs[m][...])


def finish_kernel(own_ref, from_prev_ref, from_next_ref, out_ref):
    nodes = own_ref.shape[1]
    from_prev, from_next = from_prev_ref[...].astype(jnp.float32), from_next_ref[...].astype(jnp.float32)
    out_ref[:, :HALO] = (own_ref[:, :HALO] + from_prev).astype(jnp.bfloat16)
    out_ref[:, HALO : nodes - HALO] = own_ref[:, HALO : nodes - HALO].astype(jnp.bfloat16)
    out_ref[:, nodes - HALO :] = (own_ref[:, nodes - HALO :] + from_next).astype(jnp.bfloat16)


def shifted(shard, axis, by):
    length = lax.axis_size(axis)
    return lax.ppermute(shard, axis, [(i, (i + by) % length) for i in range(length)])


def swapped(block, axis, by):
    return lax.ppermute(block, axis, [(i, i ^ by) for i in range(lax.axis_size(axis))])


def per_device(latent, neighbours, weights, targets, counts, w_one, b_one, w_two, b_two, w_three):
    members, nodes, width = latent.shape
    slots, channels = targets.shape
    hidden = w_one.shape[1]
    ext = nodes + 2 * HALO
    region, regions = lax.axis_index("space"), lax.axis_size("space")
    rank, ranks = lax.axis_index("member"), lax.axis_size("member")
    share = slots // ranks
    bf16, f32 = jnp.bfloat16, jnp.float32
    shape = jax.ShapeDtypeStruct
    each = range(members)

    edge = shape((HALO, width), bf16)
    *rims, latent = kernel_call(
        rims_kernel, (edge,) * (2 * members) + (shape(latent.shape, bf16),), flops=MIB, moved=3 * MIB, operands=1
    )(latent)
    before = [shifted(rims[2 * m], "space", 1) for m in each]
    after = [shifted(rims[2 * m + 1], "space", -1) for m in each]
    rank_at = rank[None].astype(jnp.int32)
    region_at = region[None].astype(jnp.int32)

    table, part = kernel_call(
        table_kernel,
        (shape((ext, slots), bf16), shape((width, slots), f32)),
        flops=2 * width * nodes * slots,
        moved=12 * MIB,
        smem=3,
        operands=6,
    )(region_at, rank_at, counts, neighbours, weights, latent)

    saved_shape = shape((hidden, slots), bf16)
    mixed_shape = shape((width, slots), bf16)
    decoded_shape = shape((channels, slots), bf16)
    dense = width * hidden + hidden * hidden + hidden * channels
    saved, known = [], []
    for m in each:
        *kept, decoded = kernel_call(
            lambda *refs: forward_kernel(m, *refs),
            (mixed_shape,) + (saved_shape,) * 4 + (decoded_shape,),
            flops=2 * slots * ((ext if m else 2 * HALO) * width + dense),
            moved=8 * MIB,
            operands=9,
        )(latent if m else part, table, before[m], after[m], w_one, b_one[None], w_two, b_two[None], w_three)
        saved.append(kept)
        known.append({0: decoded})
        bit = 2
        while bit < ranks:
            known[m].update({i ^ bit: swapped(known[m][i], "member", bit) for i in sorted(known[m])})
            bit = 2 * bit
        known[m][1] = swapped(decoded, "member", 1)

    def scored(others, carried, first=False, last=False):
        operands = (region_at, counts, *[known[m][0] for m in each], *others, *carried)
        return kernel_call(
            lambda *refs: score_kernel(members, len(others), members * ranks, first, last, *refs),
            (shape((channels, slots), bf16 if last else f32),) * members + (shape((1, LANE), f32),),
            flops=4 * MIB,
            moved=2 * MIB,
            smem=2,
            operands=len(operands),
        )(*operands)

    near = [{i: block for i, block in known[m].items() if i > 1} for m in each]
    early = [known[m][1] for m in each] + [block for blocks in near[:-1] for block in blocks.values()]
    carried = scored(early, [targets], first=True)
    near[-1], carried = lax.optimization_barrier((near[-1], carried))
    others = [*near[-1].values()]
    others += [swapped(block, "member", 1) for blocks in near for block in blocks.values()]
    carried = scored(others, carried, last=True)
    *d_decoded, score = carried

    rows = -(-(width + hidden + hidden // 2 + 4) // (16 * ranks)) * 16
    piece = shape((rows, hidden), bf16)
    operands = [region_at, rank_at, w_two, w_three, score]
    for m in each:
        operands += [*saved[m], d_decoded[m]]
    out = kernel_call(
        lambda *refs: backward_kernel(members, ranks, *refs),
        (saved_shape,) * members + (piece,) * ranks,
        flops=4 * members * slots * dense,
        moved=10 * MIB,
        scratch=(pltpu.VMEM((members, hidden, slots), bf16), pltpu.VMEM((ranks, rows, hidden), bf16)),
        smem=2,
        operands=len(operands),
    )(*operands)
    d_one, pieces = out[:members], out[members:]

    def summed(ones, others):
        return kernel_call(
            lambda *refs: sum_kernel(len(ones), *refs), (piece,) * len(ones), flops=MIB, moved=MIB, operands=2 * len(ones)
        )(*ones, *others)

    both = shape((members, HALO, width), bf16)
    *d_mixed, head, tail = kernel_call(
        lambda *refs: edges_kernel(members, *refs),
        (mixed_shape,) * members + (both, both),
        flops=2 * members * slots * width * (hidden + 2 * HALO),
        moved=6 * MIB,
        operands=2 + members,
    )(table, w_one, *d_one)
    bit = 1
    while bit < ranks:
        received = [swapped(sent, "member", bit) for sent in pieces[1::2]]
        if bit == 1:
            received, head, tail = lax.optimization_barrier((received, head, tail))
        pieces = summed(pieces[::2], received)
        bit = 2 * bit
    own = kernel_call(
        own_kernel,
        shape((members, nodes, width), f32),
        flops=2 * members * nodes * width * slots,
        moved=6 * MIB,
        operands=1 + members,
    )(table, *d_mixed)
    (total,) = pieces
    step = 1
    while step < regions:
        (total,) = summed([total], [swapped(total, "space", step)])
        step = 2 * step
        if step == regions // 2:
            total, head, tail = lax.optimization_barrier((total, head, tail))
            from_next = shifted(head, "space", -1)
            from_prev = shifted(tail, "space", 1)
    latent_grad = kernel_call(
        finish_kernel,
        shape((members, nodes, width), bf16),
        flops=MIB,
        moved=3 * MIB,
        operands=3,
    )(own, from_prev, from_next)
    totals = {0: total}
    while bit > 1:
        bit = bit // 2
        totals.update({i ^ bit: swapped(totals[i], "member", bit) for i in sorted(totals)})
    totals = [totals[i] for i in range(ranks)]
    totals, latent_grad = lax.optimization_barrier((totals, latent_grad))
    row = shape((1, hidden), f32)
    g_one, g_bone, g_two, g_btwo, g_three, tally = kernel_call(
        lambda *refs: unpack_kernel(1.0 / (OBS_MEAN * members * ranks), *refs),
        (shape((width, hidden), f32), row, shape((hidden, hidden), f32), row, shape((hidden, channels), f32),
         shape((1, regions), f32)),
        flops=MIB,
        moved=2 * MIB,
        scratch=(pltpu.VMEM((ranks, rows, hidden), bf16),),
        smem=1,
        operands=1 + ranks,
    )(rank_at, *totals)
    return (tally[0], latent_grad, g_one, g_bone[0], g_two, g_btwo[0], g_three)


def solution(mesh):
    in_specs = (
        P("member", ("groups", "space"), None),
        P(None, ("groups", "space")),
        P(None, ("groups", "space")),
        P(("groups", "space"), None),
        P("groups"),
        P(),
        P(),
        P(),
        P(),
        P(),
    )
    out_specs = (
        P("groups"),
        P("member", ("groups", "space"), None),
        P("groups", None),
        P("groups"),
        P("groups", None),
        P("groups"),
        P("groups", None),
    )
    return jax.shard_map(
        per_device, mesh=mesh, in_specs=in_specs, out_specs=out_specs, check_vma=False
    )
```

```python
import jax
import jax.numpy as jnp
from jax import lax
from jax.experimental import pallas as pl
from jax.experimental.pallas import tpu as pltpu
from jax.sharding import PartitionSpec as P

K = 4
OBS_MEAN = 512
HALO = 256
EPSILON = 1e-05
BLOCK = 256
LANE = 128
CHUNK = 512
MIB = 1 << 20


def split(total, step):
    return [(start, min(step, total - start)) for start in range(0, total, step)]


def nt_dot(left, right):
    return lax.dot_general(
        left, right, (((1,), (1,)), ((), ())), preferred_element_type=jnp.float32
    )


def nn_dot(left, right):
    return jnp.dot(left, right, preferred_element_type=jnp.float32)


def kernel_call(body, out_shape, flops, moved, scratch=(), smem=0, operands=0):
    vmem = pl.BlockSpec(memory_space=pltpu.VMEM)
    specs = [pl.BlockSpec(memory_space=pltpu.SMEM)] * smem
    return pl.pallas_call(
        body,
        out_shape=out_shape,
        in_specs=specs + [vmem] * (operands - len(specs)),
        out_specs=jax.tree.map(lambda _: vmem, out_shape),
        scratch_shapes=list(scratch),
        compiler_params=pltpu.CompilerParams(vmem_limit_bytes=40 * MIB),
        cost_estimate=pl.CostEstimate(flops=flops, bytes_accessed=moved, transcendentals=0),
    )


def rims_kernel(latent_ref, *refs):
    members, nodes, _ = latent_ref.shape
    for m in range(members):
        refs[2 * m][...] = latent_ref[m, nodes - HALO :]
        refs[2 * m + 1][...] = latent_ref[m, :HALO]
    refs[-1][...] = latent_ref[...]


def table_kernel(region_ref, rank_ref, counts_ref, nbr_ref, weight_ref, latent_ref, table_ref, part_ref):
    nodes = latent_ref.shape[1]
    ext, slots = table_ref.shape
    live = lax.broadcasted_iota(jnp.int32, (1, slots), 1) < counts_ref[region_ref[0]]
    nbr = [nbr_ref[k : k + 1, :] for k in range(K)]
    own = [jnp.where(live, weight_ref[k : k + 1, :], 0.0) for k in range(K)]
    joint = []
    for k in range(K):
        total = own[k]
        for j in range(K):
            if j != k:
                total = total + jnp.where(nbr[j] == nbr[k], own[j], 0.0)
        joint.append(total)
    groups = BLOCK // 16
    rows = (
        lax.broadcasted_iota(jnp.int32, (groups, 16, LANE), 0) * 16
        + lax.broadcasted_iota(jnp.int32, (groups, 16, LANE), 1)
    ).astype(jnp.float32).astype(jnp.bfloat16)
    for lo, size in split(slots, LANE):
        wide = [
            jnp.broadcast_to(joint[k][:, lo : lo + size], (16, size)).astype(jnp.bfloat16)
            for k in range(K)
        ]
        for b in range(ext // BLOCK):
            tile = jnp.zeros((groups, 16, size), jnp.bfloat16)
            for k in range(K):
                near = (nbr[k][:, lo : lo + size] - b * BLOCK).astype(jnp.float32)
                near = jnp.broadcast_to(near, (16, size)).astype(jnp.bfloat16)
                tile = jnp.where(rows[:, :, :size] == near[None], wide[k][None], tile)
            table_ref[b * BLOCK : (b + 1) * BLOCK, lo : lo + size] = tile.reshape(BLOCK, size)
    turned = latent_ref[0].T
    for lo, size in split(slots, CHUNK):
        part_ref[:, lo : lo + size] = nn_dot(turned, table_ref[HALO : HALO + nodes, lo : lo + size])


def column(ref):
    height = ref.shape[1]
    return jnp.broadcast_to(ref[...], (LANE, height)).T


def forward_kernel(
    member, own_ref, table_ref, before_ref, after_ref, w_one_ref, b_one_ref, w_two_ref, b_two_ref, w_three_ref,
    mixed_ref, act_one_ref, slope_one_ref, act_two_ref, slope_two_ref, decoded_ref,
):
    ext, slots = table_ref.shape
    w_one, w_two, w_three = w_one_ref[...].T * 0.5, w_two_ref[...].T * 0.5, w_three_ref[...].T
    b_one, b_two = column(b_one_ref) * 0.5, column(b_two_ref) * 0.5

    def layer(weight, bias, values, size):
        half = nn_dot(weight, values) + jnp.concatenate([bias] * (size // LANE), axis=1)
        gate = 1.0 + jnp.tanh(half)
        act = half * gate
        return act.astype(jnp.bfloat16), (gate + act * (2.0 - gate)).astype(jnp.bfloat16)

    if member:
        nodes = jnp.concatenate([before_ref[...].T, own_ref[member].T, after_ref[...].T], axis=1)
    else:
        nodes = jnp.concatenate([before_ref[...].T, after_ref[...].T], axis=1)
    for lo, size in split(slots, CHUNK):
        lanes = slice(lo, lo + size)
        if member:
            mixed = nn_dot(nodes, table_ref[:, lanes])
        else:
            rims = jnp.concatenate([table_ref[:HALO, lanes], table_ref[ext - HALO :, lanes]], axis=0)
            mixed = own_ref[:, lanes] + nn_dot(nodes, rims)
        mixed = mixed.astype(jnp.bfloat16)
        mixed_ref[:, lanes] = mixed
        act_one, slope_one_ref[:, lanes] = layer(w_one, b_one, mixed, size)
        act_one_ref[:, lanes] = act_one
        act_two, slope_two_ref[:, lanes] = layer(w_two, b_two, act_one, size)
        act_two_ref[:, lanes] = act_two
        decoded_ref[:, lanes] = nn_dot(w_three, act_two).astype(jnp.bfloat16)


def score_kernel(mine, others, count, first, last, region_ref, counts_ref, *refs):
    own_refs, refs = refs[:mine], refs[mine:]
    other_refs, refs = refs[:others], refs[others:]
    if first:
        target_ref, refs = refs[0], refs[1:]
        old_refs, old_score = None, 0.0
    else:
        old_refs, old_score, refs = refs[:mine], refs[mine][...], refs[mine + 1 :]
    grad_refs, score_ref = refs[:mine], refs[mine]
    channels, slots = own_refs[0].shape
    inner = [(i, j) for i in range(mine) for j in range(i + 1, mine)] if first else []
    outer = [(i, mine + j) for i in range(mine) for j in range(others)]
    pairs = inner + outer
    shares = [1.0 / (count - 1)] * len(inner) + [0.5 / (count - 1)] * len(outer)
    live_count = counts_ref[region_ref[0]]

    def one_tile(at, total):
        start = pl.multiple_of(at * LANE, LANE)
        lanes = pl.ds(start, LANE)
        if first:
            turned = target_ref[lanes, :].astype(jnp.float32).T

        def rows_of(c):
            return [ref[c : c + 16, lanes].astype(jnp.float32) for ref in (*own_refs, *other_refs)]

        def fold(square):
            return square[:8] + square[8:]

        to_target = [jnp.zeros((8, LANE), jnp.float32)] * (mine if first else 0)
        apart = [jnp.zeros((8, LANE), jnp.float32)] * len(pairs)
        for c in range(0, channels, 16):
            values = rows_of(c)
            for i in range(len(to_target)):
                to_target[i] = to_target[i] + fold((values[i] - turned[c : c + 16]) ** 2)
            for p, (i, j) in enumerate(pairs):
                apart[p] = apart[p] + fold((values[i] - values[j]) ** 2)
        live = start + lax.broadcasted_iota(jnp.int32, (1, LANE), 1) < live_count
        score = jnp.zeros((1, LANE), jnp.float32)

        def inverse(square):
            squared = jnp.sum(square, axis=0, keepdims=True) + EPSILON
            inv = lax.rsqrt(squared)
            return squared * inv, inv

        inv_target, inv_pair = [], []
        for square in to_target:
            dist, inv = inverse(square)
            score = score + dist
            inv_target.append(jnp.broadcast_to(inv, (8, LANE)))
        for square, share in zip(apart, shares):
            dist, inv = inverse(square)
            score = score - dist * share
            inv_pair.append(jnp.broadcast_to(inv * (1.0 / (count - 1)), (8, LANE)))
        for c in range(0, channels, 16):
            values = rows_of(c)
            halves = []
            for h in (0, 8):
                near = [v[h : h + 8] for v in values]
                rows = slice(c + h, c + h + 8)
                if first:
                    grads = [(near[i] - turned[rows]) * inv_target[i] for i in range(mine)]
                else:
                    grads = [old_refs[i][rows, lanes] for i in range(mine)]
                for p, (i, j) in enumerate(pairs):
                    term = (near[i] - near[j]) * inv_pair[p]
                    grads[i] = grads[i] - term
                    if j < mine:
                        grads[j] = grads[j] + term
                halves.append(grads)
            for i in range(mine):
                grad = jnp.concatenate([halves[0][i], halves[1][i]], axis=0)
                if last:
                    grad = jnp.where(live, grad, 0.0)
                grad_refs[i][c : c + 16, lanes] = grad.astype(grad_refs[i].dtype)
        return total + jnp.where(live, score, 0.0)

    score_ref[...] = old_score + lax.fori_loop(0, slots // LANE, one_tile, jnp.zeros((1, LANE), jnp.float32))


def backward_kernel(members, ranks, region_ref, rank_ref, w_two_ref, w_three_ref, score_ref, *refs):
    saved = [refs[6 * m : 6 * (m + 1)] for m in range(members)]
    refs = refs[6 * members :]
    d_one_refs, refs = refs[:members], refs[members:]
    piece_refs, (d_two_ref, stage_ref) = refs[:ranks], refs[ranks:]
    w_two, w_three = w_two_ref[...] * 0.5, w_three_ref[...] * 0.5
    width, slots = saved[0][0].shape
    hidden = saved[0][1].shape[0]
    bias_one = jnp.zeros((hidden, LANE), jnp.float32)
    bias_two = jnp.zeros((hidden, LANE), jnp.float32)

    def lane_sum(values):
        return sum(values[:, lo : lo + LANE] for lo, _ in split(values.shape[1], LANE))

    g_one, g_two, g_three = 0.0, 0.0, 0.0
    for m in range(members):
        mixed_ref, act_one_ref, slope_one_ref, act_two_ref, slope_two_ref, d_dec_ref = saved[m]
        for lo, size in split(slots, CHUNK):
            lanes = slice(lo, lo + size)
            back = nn_dot(w_three, d_dec_ref[:, lanes]) * slope_two_ref[:, lanes].astype(jnp.float32)
            bias_two = bias_two + lane_sum(back)
            d_two = back.astype(jnp.bfloat16)
            d_two_ref[m, :, lanes] = d_two
            back = nn_dot(w_two, d_two) * slope_one_ref[:, lanes].astype(jnp.float32)
            bias_one = bias_one + lane_sum(back)
            d_one_refs[m][:, lanes] = back.astype(jnp.bfloat16)
        g_three = g_three + nt_dot(act_two_ref[...], d_dec_ref[...])
        g_two = g_two + nt_dot(act_one_ref[...], d_two_ref[m])
        g_one = g_one + nt_dot(mixed_ref[...], d_one_refs[m][...])
    half = hidden // 2
    region = lax.broadcasted_iota(jnp.int32, (1, hidden), 1) == region_ref[0]
    tally = jnp.where(region, jnp.sum(score_ref[...]), 0.0)
    high = tally.astype(jnp.bfloat16).astype(jnp.float32)
    parts = [
        g_one,
        g_two,
        jnp.concatenate([g_three[:half], g_three[half:]], axis=1),
        jnp.sum(bias_one.T, axis=0, keepdims=True),
        jnp.sum(bias_two.T, axis=0, keepdims=True),
        high,
        tally - high,
    ]
    used = sum(part.shape[0] for part in parts)
    parts.append(jnp.zeros((ranks * stage_ref.shape[1] - used, hidden), jnp.float32))
    stage_ref[...] = jnp.concatenate(parts, axis=0).astype(stage_ref.dtype).reshape(stage_ref.shape)
    for i in range(ranks):
        piece_refs[i][...] = stage_ref[rank_ref[0] ^ i]


def edges_kernel(members, table_ref, w_one_ref, *refs):
    d_one_refs, refs = refs[:members], refs[members:]
    ext = table_ref.shape[0]
    for m in range(members):
        d_mixed_ref, head_ref, tail_ref = refs[3 * m : 3 * (m + 1)]
        d_mixed = nn_dot(w_one_ref[...], d_one_refs[m][...]).astype(jnp.bfloat16)
        d_mixed_ref[...] = d_mixed
        head_ref[...] = nt_dot(table_ref[:HALO, :], d_mixed).astype(jnp.bfloat16)
        tail_ref[...] = nt_dot(table_ref[ext - HALO :, :], d_mixed).astype(jnp.bfloat16)


def sum_kernel(count, *refs):
    for i in range(count):
        total = refs[i][...].astype(jnp.float32) + refs[count + i][...].astype(jnp.float32)
        refs[2 * count + i][...] = total.astype(refs[i].dtype)


def unpack_kernel(scale, rank_ref, *refs):
    *refs, stage_ref = refs
    ranks = stage_ref.shape[0]
    one_ref, b_one_ref, two_ref, b_two_ref, three_ref, tally_ref = refs[ranks:]
    for i in range(ranks):
        stage_ref[rank_ref[0] ^ i] = refs[i][...]
    width, hidden = one_ref.shape
    sums = stage_ref[...].reshape(-1, hidden).astype(jnp.float32)
    half, channels = hidden // 2, three_ref.shape[1]
    one_ref[...] = sums[:width]
    two_ref[...] = sums[width : width + hidden]
    base = width + hidden
    three_ref[:half] = sums[base : base + half, :channels]
    three_ref[half:] = sums[base : base + half, channels:]
    last = sums[base + half : base + half + 8]
    b_one_ref[...] = last[0:1]
    b_two_ref[...] = last[1:2]
    tally_ref[...] = (last[2:3] + last[3:4])[:, : tally_ref.shape[1]] * scale


def own_kernel(table_ref, *refs):
    *d_mixed_refs, own_ref = refs
    members, nodes, _ = own_ref.shape
    for m in range(members):
        own_ref[m] = nt_dot(table_ref[HALO : HALO + nodes, :], d_mixed_refs[m][...])


def finish_kernel(own_ref, *refs):
    *refs, out_ref = refs
    members, nodes, _ = own_ref.shape
    for m in range(members):
        from_next, from_prev = refs[2 * m][...].astype(jnp.float32), refs[2 * m + 1][...].astype(jnp.float32)
        out_ref[m, :HALO] = (own_ref[m, :HALO] + from_prev).astype(jnp.bfloat16)
        out_ref[m, HALO : nodes - HALO] = own_ref[m, HALO : nodes - HALO].astype(jnp.bfloat16)
        out_ref[m, nodes - HALO :] = (own_ref[m, nodes - HALO :] + from_next).astype(jnp.bfloat16)


def shifted(shard, axis, by):
    length = lax.axis_size(axis)
    return lax.ppermute(shard, axis, [(i, (i + by) % length) for i in range(length)])


def swapped(block, axis, by):
    return lax.ppermute(block, axis, [(i, i ^ by) for i in range(lax.axis_size(axis))])


def per_device(latent, neighbours, weights, targets, counts, w_one, b_one, w_two, b_two, w_three):
    members, nodes, width = latent.shape
    slots, channels = targets.shape
    hidden = w_one.shape[1]
    ext = nodes + 2 * HALO
    region, regions = lax.axis_index("space"), lax.axis_size("space")
    rank, ranks = lax.axis_index("member"), lax.axis_size("member")
    share = slots // ranks
    bf16, f32 = jnp.bfloat16, jnp.float32
    shape = jax.ShapeDtypeStruct
    each = range(members)

    edge = shape((HALO, width), bf16)
    *rims, latent = kernel_call(
        rims_kernel, (edge,) * (2 * members) + (shape(latent.shape, bf16),), flops=MIB, moved=3 * MIB, operands=1
    )(latent)
    before = [shifted(rims[2 * m], "space", 1) for m in each]
    after = [shifted(rims[2 * m + 1], "space", -1) for m in each]
    rank_at = rank[None].astype(jnp.int32)
    region_at = region[None].astype(jnp.int32)

    table, part = kernel_call(
        table_kernel,
        (shape((ext, slots), bf16), shape((width, slots), f32)),
        flops=2 * width * nodes * slots,
        moved=12 * MIB,
        smem=3,
        operands=6,
    )(region_at, rank_at, counts, neighbours, weights, latent)

    saved_shape = shape((hidden, slots), bf16)
    mixed_shape = shape((width, slots), bf16)
    decoded_shape = shape((channels, slots), bf16)
    dense = width * hidden + hidden * hidden + hidden * channels
    saved, known = [], []
    for m in each:
        *kept, decoded = kernel_call(
            lambda *refs: forward_kernel(m, *refs),
            (mixed_shape,) + (saved_shape,) * 4 + (decoded_shape,),
            flops=2 * slots * ((ext if m else 2 * HALO) * width + dense),
            moved=8 * MIB,
            operands=9,
        )(latent if m else part, table, before[m], after[m], w_one, b_one[None], w_two, b_two[None], w_three)
        saved.append(kept)
        known.append({0: decoded})
        bit = 2
        while bit < ranks:
            known[m].update({i ^ bit: swapped(known[m][i], "member", bit) for i in sorted(known[m])})
            bit = 2 * bit
        known[m][1] = swapped(decoded, "member", 1)

    def scored(others, carried, first=False, last=False):
        operands = (region_at, counts, *[known[m][0] for m in each], *others, *carried)
        return kernel_call(
            lambda *refs: score_kernel(members, len(others), members * ranks, first, last, *refs),
            (shape((channels, slots), bf16 if last else f32),) * members + (shape((1, LANE), f32),),
            flops=4 * MIB,
            moved=2 * MIB,
            smem=2,
            operands=len(operands),
        )(*operands)

    near = [{i: block for i, block in known[m].items() if i > 1} for m in each]
    early = [known[m][1] for m in each] + [block for blocks in near[:-1] for block in blocks.values()]
    carried = scored(early, [targets], first=True)
    near[-1], carried = lax.optimization_barrier((near[-1], carried))
    others = [*near[-1].values()]
    others += [swapped(block, "member", 1) for blocks in near for block in blocks.values()]
    carried = scored(others, carried, last=True)
    *d_decoded, score = carried

    rows = -(-(width + hidden + hidden // 2 + 4) // (16 * ranks)) * 16
    piece = shape((rows, hidden), bf16)
    operands = [region_at, rank_at, w_two, w_three, score]
    for m in each:
        operands += [*saved[m], d_decoded[m]]
    out = kernel_call(
        lambda *refs: backward_kernel(members, ranks, *refs),
        (saved_shape,) * members + (piece,) * ranks,
        flops=4 * members * slots * dense,
        moved=10 * MIB,
        scratch=(pltpu.VMEM((members, hidden, slots), bf16), pltpu.VMEM((ranks, rows, hidden), bf16)),
        smem=2,
        operands=len(operands),
    )(*operands)
    d_one, pieces = out[:members], out[members:]

    def summed(ones, others):
        return kernel_call(
            lambda *refs: sum_kernel(len(ones), *refs), (piece,) * len(ones), flops=MIB, moved=MIB, operands=2 * len(ones)
        )(*ones, *others)

    out = kernel_call(
        lambda *refs: edges_kernel(members, *refs),
        (mixed_shape, edge, edge) * members,
        flops=2 * members * slots * width * (hidden + 2 * HALO),
        moved=6 * MIB,
        operands=2 + members,
    )(table, w_one, *d_one)
    d_mixed, heads, tails = out[::3], out[1::3], out[2::3]

    def returned(m):
        return [shifted(heads[m], "space", -1), shifted(tails[m], "space", 1)]

    bit = 1
    while bit < ranks:
        received = [swapped(sent, "member", bit) for sent in pieces[1::2]]
        if bit == 1:
            received, heads, tails = lax.optimization_barrier((received, heads, tails))
        pieces = summed(pieces[::2], received)
        bit = 2 * bit
    own = kernel_call(
        own_kernel,
        shape((members, nodes, width), f32),
        flops=2 * members * nodes * width * slots,
        moved=6 * MIB,
        operands=1 + members,
    )(table, *d_mixed)
    edges = [block for m in each[:-1] for block in returned(m)]
    (total,) = pieces
    step = 1
    while step < regions:
        (total,) = summed([total], [swapped(total, "space", step)])
        step = 2 * step
        if step == regions // 2:
            total, edges, own, heads, tails = lax.optimization_barrier((total, edges, own, heads, tails))
            edges = [*edges, *returned(members - 1)]
    latent_grad = kernel_call(
        finish_kernel,
        shape((members, nodes, width), bf16),
        flops=MIB,
        moved=3 * MIB,
        operands=1 + 2 * members,
    )(own, *edges)
    totals = {0: total}
    while bit > 1:
        bit = bit // 2
        if bit == 1:
            totals[ranks // 2], latent_grad = lax.optimization_barrier((totals[ranks // 2], latent_grad))
        totals.update({i ^ bit: swapped(totals[i], "member", bit) for i in sorted(totals)})
    totals = [totals[i] for i in range(ranks)]
    row = shape((1, hidden), f32)
    g_one, g_bone, g_two, g_btwo, g_three, tally = kernel_call(
        lambda *refs: unpack_kernel(1.0 / (OBS_MEAN * members * ranks), *refs),
        (shape((width, hidden), f32), row, shape((hidden, hidden), f32), row, shape((hidden, channels), f32),
         shape((1, regions), f32)),
        flops=MIB,
        moved=2 * MIB,
        scratch=(pltpu.VMEM((ranks, rows, hidden), bf16),),
        smem=1,
        operands=1 + ranks,
    )(rank_at, *totals)
    return (tally[0], latent_grad, g_one, g_bone[0], g_two, g_btwo[0], g_three)


def solution(mesh):
    in_specs = (
        P("member", ("groups", "space"), None),
        P(None, ("groups", "space")),
        P(None, ("groups", "space")),
        P(("groups", "space"), None),
        P("groups"),
        P(),
        P(),
        P(),
        P(),
        P(),
    )
    out_specs = (
        P("groups"),
        P("member", ("groups", "space"), None),
        P("groups", None),
        P("groups"),
        P("groups", None),
        P("groups"),
        P("groups", None),
    )
    return jax.shard_map(
        per_device, mesh=mesh, in_specs=in_specs, out_specs=out_specs, check_vma=False
    )
```

```python
import jax
import jax.numpy as jnp
from jax import lax
from jax.experimental import pallas as pl
from jax.experimental.pallas import tpu as pltpu
from jax.sharding import PartitionSpec as P

K = 4
OBS_MEAN = 512
HALO = 256
EPSILON = 1e-05
BLOCK = 256
LANE = 128
CHUNK = 512
MIB = 1 << 20


def split(total, step):
    return [(start, min(step, total - start)) for start in range(0, total, step)]


def nt_dot(left, right):
    return lax.dot_general(
        left, right, (((1,), (1,)), ((), ())), preferred_element_type=jnp.float32
    )


def nn_dot(left, right):
    return jnp.dot(left, right, preferred_element_type=jnp.float32)


def kernel_call(body, out_shape, flops, moved, scratch=(), smem=0, operands=0):
    vmem = pl.BlockSpec(memory_space=pltpu.VMEM)
    specs = [pl.BlockSpec(memory_space=pltpu.SMEM)] * smem
    return pl.pallas_call(
        body,
        out_shape=out_shape,
        in_specs=specs + [vmem] * (operands - len(specs)),
        out_specs=jax.tree.map(lambda _: vmem, out_shape),
        scratch_shapes=list(scratch),
        compiler_params=pltpu.CompilerParams(vmem_limit_bytes=24 * MIB),
        cost_estimate=pl.CostEstimate(flops=flops, bytes_accessed=moved, transcendentals=0),
    )


def rims_kernel(latent_ref, *refs):
    members, nodes, _ = latent_ref.shape
    for m in range(members):
        refs[2 * m][...] = latent_ref[m, nodes - HALO :]
        refs[2 * m + 1][...] = latent_ref[m, :HALO]
    refs[-1][...] = latent_ref[...]


def table_kernel(region_ref, rank_ref, counts_ref, nbr_ref, weight_ref, latent_ref, table_ref, part_ref):
    nodes = latent_ref.shape[1]
    ext, slots = table_ref.shape
    live = lax.broadcasted_iota(jnp.int32, (1, slots), 1) < counts_ref[region_ref[0]]
    nbr = [nbr_ref[k : k + 1, :] for k in range(K)]
    own = [jnp.where(live, weight_ref[k : k + 1, :], 0.0) for k in range(K)]
    joint = []
    for k in range(K):
        total = own[k]
        for j in range(K):
            if j != k:
                total = total + jnp.where(nbr[j] == nbr[k], own[j], 0.0)
        joint.append(total)
    groups = BLOCK // 16
    rows = (
        lax.broadcasted_iota(jnp.int32, (groups, 16, LANE), 0) * 16
        + lax.broadcasted_iota(jnp.int32, (groups, 16, LANE), 1)
    ).astype(jnp.float32).astype(jnp.bfloat16)
    turned = latent_ref[0].T
    for start, length in split(slots, CHUNK):
        for lo, size in split(length, LANE):
            lanes = slice(start + lo, start + lo + size)
            wide = [jnp.broadcast_to(joint[k][:, lanes], (16, size)).astype(jnp.bfloat16) for k in range(K)]
            for b in range(ext // BLOCK):
                tile = jnp.zeros((groups, 16, size), jnp.bfloat16)
                for k in range(K):
                    near = (nbr[k][:, lanes] - b * BLOCK).astype(jnp.float32)
                    near = jnp.broadcast_to(near, (16, size)).astype(jnp.bfloat16)
                    tile = jnp.where(rows[:, :, :size] == near[None], wide[k][None], tile)
                table_ref[b * BLOCK : (b + 1) * BLOCK, lanes] = tile.reshape(BLOCK, size)
        lanes = slice(start, start + length)
        part_ref[:, lanes] = nn_dot(turned, table_ref[HALO : HALO + nodes, lanes])


def column(ref):
    height = ref.shape[1]
    return jnp.broadcast_to(ref[...], (LANE, height)).T


def forward_kernel(
    member, own_ref, table_ref, before_ref, after_ref, w_one_ref, b_one_ref, w_two_ref, b_two_ref, w_three_ref,
    mixed_ref, act_one_ref, slope_one_ref, act_two_ref, slope_two_ref, decoded_ref,
):
    ext, slots = table_ref.shape
    w_one, w_two, w_three = w_one_ref[...].T * 0.5, w_two_ref[...].T * 0.5, w_three_ref[...].T
    b_one, b_two = column(b_one_ref) * 0.5, column(b_two_ref) * 0.5

    def layer(weight, bias, values, size):
        half = nn_dot(weight, values) + jnp.concatenate([bias] * (size // LANE), axis=1)
        gate = 1.0 + jnp.tanh(half)
        act = half * gate
        return act.astype(jnp.bfloat16), (gate + act * (2.0 - gate)).astype(jnp.bfloat16)

    if member:
        nodes = jnp.concatenate([before_ref[...].T, own_ref[member].T, after_ref[...].T], axis=1)
    else:
        nodes = jnp.concatenate([before_ref[...].T, after_ref[...].T], axis=1)
    for lo, size in split(slots, CHUNK):
        lanes = slice(lo, lo + size)
        if member:
            mixed = nn_dot(nodes, table_ref[:, lanes])
        else:
            rims = jnp.concatenate([table_ref[:HALO, lanes], table_ref[ext - HALO :, lanes]], axis=0)
            mixed = own_ref[:, lanes] + nn_dot(nodes, rims)
        mixed = mixed.astype(jnp.bfloat16)
        mixed_ref[:, lanes] = mixed
        act_one, slope_one_ref[:, lanes] = layer(w_one, b_one, mixed, size)
        act_one_ref[:, lanes] = act_one
        act_two, slope_two_ref[:, lanes] = layer(w_two, b_two, act_one, size)
        act_two_ref[:, lanes] = act_two
        decoded_ref[:, lanes] = nn_dot(w_three, act_two).astype(jnp.bfloat16)


def score_kernel(mine, others, count, first, last, region_ref, counts_ref, *refs):
    own_refs, refs = refs[:mine], refs[mine:]
    other_refs, refs = refs[:others], refs[others:]
    if first:
        target_ref, refs = refs[0], refs[1:]
        old_refs, old_score = None, 0.0
    else:
        old_refs, old_score, refs = refs[:mine], refs[mine][...], refs[mine + 1 :]
    grad_refs, score_ref = refs[:mine], refs[mine]
    channels, slots = own_refs[0].shape
    inner = [(i, j) for i in range(mine) for j in range(i + 1, mine)] if first else []
    outer = [(i, mine + j) for i in range(mine) for j in range(others)]
    pairs = inner + outer
    shares = [1.0 / (count - 1)] * len(inner) + [0.5 / (count - 1)] * len(outer)
    live_count = counts_ref[region_ref[0]]

    def one_tile(at, total):
        start = pl.multiple_of(at * LANE, LANE)
        lanes = pl.ds(start, LANE)
        if first:
            turned = target_ref[lanes, :].astype(jnp.float32).T

        def rows_of(c):
            return [ref[c : c + 16, lanes].astype(jnp.float32) for ref in (*own_refs, *other_refs)]

        def fold(square):
            return square[:8] + square[8:]

        to_target = [jnp.zeros((8, LANE), jnp.float32)] * (mine if first else 0)
        apart = [jnp.zeros((8, LANE), jnp.float32)] * len(pairs)
        for c in range(0, channels, 16):
            values = rows_of(c)
            for i in range(len(to_target)):
                to_target[i] = to_target[i] + fold((values[i] - turned[c : c + 16]) ** 2)
            for p, (i, j) in enumerate(pairs):
                apart[p] = apart[p] + fold((values[i] - values[j]) ** 2)
        live = start + lax.broadcasted_iota(jnp.int32, (1, LANE), 1) < live_count
        score = jnp.zeros((1, LANE), jnp.float32)

        def inverse(square):
            squared = jnp.sum(square, axis=0, keepdims=True) + EPSILON
            inv = lax.rsqrt(squared)
            return squared * inv, inv

        inv_target, inv_pair = [], []
        for square in to_target:
            dist, inv = inverse(square)
            score = score + dist
            inv_target.append(jnp.broadcast_to(inv, (8, LANE)))
        for square, share in zip(apart, shares):
            dist, inv = inverse(square)
            score = score - dist * share
            inv_pair.append(jnp.broadcast_to(inv * (1.0 / (count - 1)), (8, LANE)))
        for c in range(0, channels, 16):
            values = rows_of(c)
            halves = []
            for h in (0, 8):
                near = [v[h : h + 8] for v in values]
                rows = slice(c + h, c + h + 8)
                if first:
                    grads = [(near[i] - turned[rows]) * inv_target[i] for i in range(mine)]
                else:
                    grads = [old_refs[i][rows, lanes] for i in range(mine)]
                for p, (i, j) in enumerate(pairs):
                    term = (near[i] - near[j]) * inv_pair[p]
                    grads[i] = grads[i] - term
                    if j < mine:
                        grads[j] = grads[j] + term
                halves.append(grads)
            for i in range(mine):
                grad = jnp.concatenate([halves[0][i], halves[1][i]], axis=0)
                if last:
                    grad = jnp.where(live, grad, 0.0)
                grad_refs[i][c : c + 16, lanes] = grad.astype(grad_refs[i].dtype)
        return total + jnp.where(live, score, 0.0)

    score_ref[...] = old_score + lax.fori_loop(0, slots // LANE, one_tile, jnp.zeros((1, LANE), jnp.float32))


def rims_back(table_ref, w_one, d_one, refs):
    d_mixed_ref, head_ref, tail_ref = refs
    ext = table_ref.shape[0]
    d_mixed = nn_dot(w_one, d_one).astype(jnp.bfloat16)
    d_mixed_ref[...] = d_mixed
    head_ref[...] = nt_dot(table_ref[:HALO, :], d_mixed).astype(jnp.bfloat16)
    tail_ref[...] = nt_dot(table_ref[ext - HALO :, :], d_mixed).astype(jnp.bfloat16)


def backward_kernel(members, table_ref, w_one_ref, w_two_ref, w_three_ref, *refs):
    saved = [refs[3 * m : 3 * (m + 1)] for m in range(members)]
    refs = refs[3 * members :]
    d_one_refs, d_two_refs, refs = refs[:members], refs[members : 2 * members], refs[2 * members :]
    bias_one_ref, bias_two_ref, *rim_refs = refs
    w_one, w_two, w_three = w_one_ref[...], w_two_ref[...] * 0.5, w_three_ref[...] * 0.5
    hidden, slots = saved[0][0].shape
    bias_one = jnp.zeros((hidden, LANE), jnp.float32)
    bias_two = jnp.zeros((hidden, LANE), jnp.float32)

    def lane_sum(values):
        return sum(values[:, lo : lo + LANE] for lo, _ in split(values.shape[1], LANE))

    for m in range(members):
        slope_one_ref, slope_two_ref, d_dec_ref = saved[m]
        for lo, size in split(slots, CHUNK):
            lanes = slice(lo, lo + size)
            back = nn_dot(w_three, d_dec_ref[:, lanes]) * slope_two_ref[:, lanes].astype(jnp.float32)
            bias_two = bias_two + lane_sum(back)
            d_two = back.astype(jnp.bfloat16)
            d_two_refs[m][:, lanes] = d_two
            back = nn_dot(w_two, d_two) * slope_one_ref[:, lanes].astype(jnp.float32)
            bias_one = bias_one + lane_sum(back)
            d_one_refs[m][:, lanes] = back.astype(jnp.bfloat16)
        if m < members - 1:
            rims_back(table_ref, w_one, d_one_refs[m][...], rim_refs[3 * m : 3 * (m + 1)])
    bias_one_ref[...] = bias_one
    bias_two_ref[...] = bias_two


def sums_kernel(members, ranks, region_ref, rank_ref, table_ref, w_one_ref, score_ref, bias_one_ref, bias_two_ref, *refs):
    saved = [refs[6 * m : 6 * (m + 1)] for m in range(members)]
    refs = refs[6 * members :]
    rim_refs, piece_refs, stage_ref = refs[:3], refs[3 : 3 + ranks], refs[3 + ranks]
    hidden = bias_one_ref.shape[0]
    half = hidden // 2
    g_one, g_two, g_three = 0.0, 0.0, 0.0
    for mixed_ref, act_one_ref, act_two_ref, d_one_ref, d_two_ref, d_dec_ref in saved:
        g_one = g_one + nt_dot(mixed_ref[...], d_one_ref[...])
        g_two = g_two + nt_dot(act_one_ref[...], d_two_ref[...])
        g_three = g_three + nt_dot(act_two_ref[...], d_dec_ref[...])
    region = lax.broadcasted_iota(jnp.int32, (1, hidden), 1) == region_ref[0]
    tally = jnp.where(region, jnp.sum(score_ref[...]), 0.0)
    high = tally.astype(jnp.bfloat16).astype(jnp.float32)
    parts = [
        g_one,
        g_two,
        jnp.concatenate([g_three[:half], g_three[half:]], axis=1),
        jnp.sum(bias_one_ref[...].T, axis=0, keepdims=True),
        jnp.sum(bias_two_ref[...].T, axis=0, keepdims=True),
        high,
        tally - high,
    ]
    used = sum(part.shape[0] for part in parts)
    parts.append(jnp.zeros((ranks * stage_ref.shape[1] - used, hidden), jnp.float32))
    stage_ref[...] = jnp.concatenate(parts, axis=0).astype(stage_ref.dtype).reshape(stage_ref.shape)
    for i in range(ranks):
        piece_refs[i][...] = stage_ref[rank_ref[0] ^ i]
    rims_back(table_ref, w_one_ref[...], saved[-1][3][...], rim_refs)


def sum_kernel(*refs):
    *refs, sum_ref = refs
    sum_ref[...] = sum(ref[...].astype(jnp.float32) for ref in refs).astype(sum_ref.dtype)


def unpack_kernel(scale, rank_ref, *refs):
    *refs, stage_ref = refs
    ranks = stage_ref.shape[0]
    one_ref, b_one_ref, two_ref, b_two_ref, three_ref, tally_ref = refs[ranks:]
    for i in range(ranks):
        stage_ref[rank_ref[0] ^ i] = refs[i][...]
    width, hidden = one_ref.shape
    sums = stage_ref[...].reshape(-1, hidden).astype(jnp.float32)
    half, channels = hidden // 2, three_ref.shape[1]
    one_ref[...] = sums[:width]
    two_ref[...] = sums[width : width + hidden]
    base = width + hidden
    three_ref[:half] = sums[base : base + half, :channels]
    three_ref[half:] = sums[base : base + half, channels:]
    last = sums[base + half : base + half + 8]
    b_one_ref[...] = last[0:1]
    b_two_ref[...] = last[1:2]
    tally_ref[...] = (last[2:3] + last[3:4])[:, : tally_ref.shape[1]] * scale


def own_kernel(table_ref, *refs):
    *d_mixed_refs, own_ref = refs
    members, nodes, _ = own_ref.shape
    for m in range(members):
        own_ref[m] = nt_dot(table_ref[HALO : HALO + nodes, :], d_mixed_refs[m][...])


def finish_kernel(own_ref, *refs):
    *refs, out_ref = refs
    members, nodes, _ = own_ref.shape
    for m in range(members):
        from_next, from_prev = refs[2 * m][...].astype(jnp.float32), refs[2 * m + 1][...].astype(jnp.float32)
        out_ref[m, :HALO] = (own_ref[m, :HALO] + from_prev).astype(jnp.bfloat16)
        out_ref[m, HALO : nodes - HALO] = own_ref[m, HALO : nodes - HALO].astype(jnp.bfloat16)
        out_ref[m, nodes - HALO :] = (own_ref[m, nodes - HALO :] + from_next).astype(jnp.bfloat16)


def shifted(shard, axis, by):
    length = lax.axis_size(axis)
    return lax.ppermute(shard, axis, [(i, (i + by) % length) for i in range(length)])


def swapped(block, axis, by):
    return lax.ppermute(block, axis, [(i, i ^ by) for i in range(lax.axis_size(axis))])


def per_device(latent, neighbours, weights, targets, counts, w_one, b_one, w_two, b_two, w_three):
    members, nodes, width = latent.shape
    slots, channels = targets.shape
    hidden = w_one.shape[1]
    ext = nodes + 2 * HALO
    region, regions = lax.axis_index("space"), lax.axis_size("space")
    rank, ranks = lax.axis_index("member"), lax.axis_size("member")
    share = slots // ranks
    bf16, f32 = jnp.bfloat16, jnp.float32
    shape = jax.ShapeDtypeStruct
    each = range(members)

    edge = shape((HALO, width), bf16)
    *rims, latent = kernel_call(
        rims_kernel, (edge,) * (2 * members) + (shape(latent.shape, bf16),), flops=4 << 30, moved=3 * MIB, operands=1
    )(latent)
    before = [shifted(rims[2 * m], "space", 1) for m in each]
    after = [shifted(rims[2 * m + 1], "space", -1) for m in each]
    rank_at = rank[None].astype(jnp.int32)
    region_at = region[None].astype(jnp.int32)

    table, part = kernel_call(
        table_kernel,
        (shape((ext, slots), bf16), shape((width, slots), f32)),
        flops=2 * width * nodes * slots,
        moved=12 * MIB,
        smem=3,
        operands=6,
    )(region_at, rank_at, counts, neighbours, weights, latent)

    saved_shape = shape((hidden, slots), bf16)
    mixed_shape = shape((width, slots), bf16)
    decoded_shape = shape((channels, slots), bf16)
    dense = width * hidden + hidden * hidden + hidden * channels
    saved, known = [], []
    for m in each:
        *kept, decoded = kernel_call(
            lambda *refs: forward_kernel(m, *refs),
            (mixed_shape,) + (saved_shape,) * 4 + (decoded_shape,),
            flops=2 * slots * ((ext if m else 2 * HALO) * width + dense),
            moved=8 * MIB,
            operands=9,
        )(latent if m else part, table, before[m], after[m], w_one, b_one[None], w_two, b_two[None], w_three)
        saved.append(kept)
        known.append({0: decoded})
        bit = 2
        while bit < ranks:
            known[m].update({i ^ bit: swapped(known[m][i], "member", bit) for i in sorted(known[m])})
            bit = 2 * bit
        known[m][1] = swapped(decoded, "member", 1)

    def scored(others, carried, first=False, last=False):
        operands = (region_at, counts, *[known[m][0] for m in each], *others, *carried)
        return kernel_call(
            lambda *refs: score_kernel(members, len(others), members * ranks, first, last, *refs),
            (shape((channels, slots), bf16 if last else f32),) * members + (shape((1, LANE), f32),),
            flops=4 * MIB,
            moved=2 * MIB,
            smem=2,
            operands=len(operands),
        )(*operands)

    near = [{i: block for i, block in known[m].items() if i > 1} for m in each]
    early = [known[m][1] for m in each] + [block for blocks in near[:-1] for block in blocks.values()]
    carried = scored(early, [targets], first=True)
    near[-1], carried = lax.optimization_barrier((near[-1], carried))
    others = [*near[-1].values()]
    others += [swapped(block, "member", 1) for blocks in near for block in blocks.values()]
    carried = scored(others, carried, last=True)
    *d_decoded, score = carried

    rows = -(-(width + hidden + hidden // 2 + 4) // (16 * ranks)) * 16
    piece = shape((rows, hidden), bf16)
    bias = shape((hidden, LANE), f32)
    one_rims = (mixed_shape, edge, edge)
    operands = [table, w_one, w_two, w_three]
    for m in each:
        operands += [saved[m][2], saved[m][4], d_decoded[m]]
    out = kernel_call(
        lambda *refs: backward_kernel(members, *refs),
        (saved_shape,) * (2 * members) + (bias, bias) + one_rims * (members - 1),
        flops=2 * members * slots * dense,
        moved=10 * MIB,
        operands=len(operands),
    )(*operands)
    d_one, d_two, (bias_one, bias_two), rims = (
        out[:members], out[members : 2 * members], out[2 * members : 2 * members + 2], out[2 * members + 2 :]
    )

    def returned(head, tail):
        return [shifted(head, "space", -1), shifted(tail, "space", 1)]

    edges = [block for m in each[:-1] for block in returned(*rims[3 * m + 1 : 3 * m + 3])]
    operands = [region_at, rank_at, table, w_one, score, bias_one, bias_two]
    for m in each:
        mixed, act_one, _, act_two, _ = saved[m]
        operands += [mixed, act_one, act_two, d_one[m], d_two[m], d_decoded[m]]
    d_mixed, head, tail, *pieces = kernel_call(
        lambda *refs: sums_kernel(members, ranks, *refs),
        one_rims + (piece,) * ranks,
        flops=2 * members * slots * dense,
        moved=10 * MIB,
        scratch=(pltpu.VMEM((ranks, rows, hidden), bf16),),
        smem=2,
        operands=len(operands),
    )(*operands)
    d_mixed = [*rims[::3], d_mixed]

    def summed(*blocks):
        return kernel_call(sum_kernel, piece, flops=MIB, moved=MIB, operands=len(blocks))(*blocks)

    pieces = [pieces[0]] + [swapped(pieces[i], "member", i) for i in range(1, ranks)]
    pieces, edges = lax.optimization_barrier((pieces, edges))
    total = summed(*pieces)
    edges = [*edges, *returned(head, tail)]
    own = kernel_call(
        own_kernel,
        shape((members, nodes, width), f32),
        flops=2 * members * nodes * width * slots,
        moved=6 * MIB,
        operands=1 + members,
    )(table, *d_mixed)
    step = 1
    while step < regions:
        total = summed(total, swapped(total, "space", step))
        step = 2 * step
        if step == regions // 2:
            total, own = lax.optimization_barrier((total, own))
    totals = {0: total}
    bit = 2
    while bit < ranks:
        totals.update({i ^ bit: swapped(totals[i], "member", bit) for i in sorted(totals)})
        bit = 2 * bit
    beside = swapped(total, "member", 1)
    beside, edges = lax.optimization_barrier((beside, edges))
    latent_grad = kernel_call(
        finish_kernel,
        shape((members, nodes, width), bf16),
        flops=MIB,
        moved=3 * MIB,
        operands=1 + 2 * members,
    )(own, *edges)
    across = {i: block for i, block in totals.items() if i}
    across, latent_grad = lax.optimization_barrier((across, latent_grad))
    totals.update({i ^ 1: swapped(block, "member", 1) for i, block in across.items()})
    totals.update(across)
    totals[1] = beside
    totals = [totals[i] for i in range(ranks)]
    row = shape((1, hidden), f32)
    g_one, g_bone, g_two, g_btwo, g_three, tally = kernel_call(
        lambda *refs: unpack_kernel(1.0 / (OBS_MEAN * members * ranks), *refs),
        (shape((width, hidden), f32), row, shape((hidden, hidden), f32), row, shape((hidden, channels), f32),
         shape((1, regions), f32)),
        flops=MIB,
        moved=2 * MIB,
        scratch=(pltpu.VMEM((ranks, rows, hidden), bf16),),
        smem=1,
        operands=1 + ranks,
    )(rank_at, *totals)
    return (tally[0], latent_grad, g_one, g_bone[0], g_two, g_btwo[0], g_three)


def solution(mesh):
    in_specs = (
        P("member", ("groups", "space"), None),
        P(None, ("groups", "space")),
        P(None, ("groups", "space")),
        P(("groups", "space"), None),
        P("groups"),
        P(),
        P(),
        P(),
        P(),
        P(),
    )
    out_specs = (
        P("groups"),
        P("member", ("groups", "space"), None),
        P("groups", None),
        P("groups"),
        P("groups", None),
        P("groups"),
        P("groups", None),
    )
    return jax.shard_map(
        per_device, mesh=mesh, in_specs=in_specs, out_specs=out_specs, check_vma=False
    )
```

```python
import jax
import jax.numpy as jnp
from jax import lax
from jax.experimental import pallas as pl
from jax.experimental.pallas import tpu as pltpu
from jax.sharding import PartitionSpec as P

K = 4
OBS_MEAN = 512
HALO = 256
EPSILON = 1e-05
BLOCK = 256
LANE = 128
CHUNK = 512
MIB = 1 << 20


def split(total, step):
    return [(start, min(step, total - start)) for start in range(0, total, step)]


def nt_dot(left, right):
    return lax.dot_general(
        left, right, (((1,), (1,)), ((), ())), preferred_element_type=jnp.float32
    )


def nn_dot(left, right):
    return jnp.dot(left, right, preferred_element_type=jnp.float32)


def kernel_call(body, out_shape, flops, moved, scratch=(), smem=0, operands=0):
    vmem = pl.BlockSpec(memory_space=pltpu.VMEM)
    specs = [pl.BlockSpec(memory_space=pltpu.SMEM)] * smem
    return pl.pallas_call(
        body,
        out_shape=out_shape,
        in_specs=specs + [vmem] * (operands - len(specs)),
        out_specs=jax.tree.map(lambda _: vmem, out_shape),
        scratch_shapes=list(scratch),
        compiler_params=pltpu.CompilerParams(vmem_limit_bytes=24 * MIB),
        cost_estimate=pl.CostEstimate(flops=flops, bytes_accessed=moved, transcendentals=0),
    )


def rims_kernel(latent_ref, *refs):
    members, nodes, _ = latent_ref.shape
    for m in range(members):
        refs[2 * m][...] = latent_ref[m, nodes - HALO :]
        refs[2 * m + 1][...] = latent_ref[m, :HALO]
    refs[-1][...] = latent_ref[...]


def table_kernel(region_ref, rank_ref, counts_ref, nbr_ref, weight_ref, latent_ref, table_ref, part_ref):
    nodes = latent_ref.shape[1]
    ext, slots = table_ref.shape
    live = lax.broadcasted_iota(jnp.int32, (1, slots), 1) < counts_ref[region_ref[0]]
    nbr = [nbr_ref[k : k + 1, :] for k in range(K)]
    own = [jnp.where(live, weight_ref[k : k + 1, :], 0.0) for k in range(K)]
    joint = []
    for k in range(K):
        total = own[k]
        for j in range(K):
            if j != k:
                total = total + jnp.where(nbr[j] == nbr[k], own[j], 0.0)
        joint.append(total)
    groups = BLOCK // 16
    rows = (
        lax.broadcasted_iota(jnp.int32, (groups, 16, LANE), 0) * 16
        + lax.broadcasted_iota(jnp.int32, (groups, 16, LANE), 1)
    ).astype(jnp.float32).astype(jnp.bfloat16)
    turned = latent_ref[0].T
    for start, length in split(slots, CHUNK):
        for lo, size in split(length, LANE):
            lanes = slice(start + lo, start + lo + size)
            wide = [jnp.broadcast_to(joint[k][:, lanes], (16, size)).astype(jnp.bfloat16) for k in range(K)]
            for b in range(ext // BLOCK):
                tile = jnp.zeros((groups, 16, size), jnp.bfloat16)
                for k in range(K):
                    near = (nbr[k][:, lanes] - b * BLOCK).astype(jnp.float32)
                    near = jnp.broadcast_to(near, (16, size)).astype(jnp.bfloat16)
                    tile = jnp.where(rows[:, :, :size] == near[None], wide[k][None], tile)
                table_ref[b * BLOCK : (b + 1) * BLOCK, lanes] = tile.reshape(BLOCK, size)
        lanes = slice(start, start + length)
        part_ref[:, lanes] = nn_dot(turned, table_ref[HALO : HALO + nodes, lanes])


def column(ref):
    height = ref.shape[1]
    return jnp.broadcast_to(ref[...], (LANE, height)).T


def forward_kernel(
    member, own_ref, table_ref, before_ref, after_ref, w_one_ref, b_one_ref, w_two_ref, b_two_ref, w_three_ref,
    mixed_ref, act_one_ref, slope_one_ref, act_two_ref, slope_two_ref, decoded_ref,
):
    ext, slots = table_ref.shape
    w_one, w_two, w_three = w_one_ref[...].T * 0.5, w_two_ref[...].T * 0.5, w_three_ref[...].T
    b_one, b_two = column(b_one_ref) * 0.5, column(b_two_ref) * 0.5

    def layer(weight, bias, values, size):
        half = nn_dot(weight, values) + jnp.concatenate([bias] * (size // LANE), axis=1)
        gate = 1.0 + jnp.tanh(half)
        act = half * gate
        return act.astype(jnp.bfloat16), (gate + act * (2.0 - gate)).astype(jnp.bfloat16)

    if member:
        nodes = jnp.concatenate([before_ref[...].T, own_ref[member].T, after_ref[...].T], axis=1)
    else:
        nodes = jnp.concatenate([before_ref[...].T, after_ref[...].T], axis=1)
    for lo, size in split(slots, CHUNK):
        lanes = slice(lo, lo + size)
        if member:
            mixed = nn_dot(nodes, table_ref[:, lanes])
        else:
            rims = jnp.concatenate([table_ref[:HALO, lanes], table_ref[ext - HALO :, lanes]], axis=0)
            mixed = own_ref[:, lanes] + nn_dot(nodes, rims)
        mixed = mixed.astype(jnp.bfloat16)
        mixed_ref[:, lanes] = mixed
        act_one, slope_one_ref[:, lanes] = layer(w_one, b_one, mixed, size)
        act_one_ref[:, lanes] = act_one
        act_two, slope_two_ref[:, lanes] = layer(w_two, b_two, act_one, size)
        act_two_ref[:, lanes] = act_two
        decoded_ref[:, lanes] = nn_dot(w_three, act_two).astype(jnp.bfloat16)


def score_kernel(mine, others, count, first, last, region_ref, counts_ref, *refs):
    own_refs, refs = refs[:mine], refs[mine:]
    other_refs, refs = refs[:others], refs[others:]
    if first:
        target_ref, refs = refs[0], refs[1:]
        old_refs, old_score = None, 0.0
    else:
        old_refs, old_score, refs = refs[:mine], refs[mine][...], refs[mine + 1 :]
    grad_refs, score_ref = refs[:mine], refs[mine]
    channels, slots = own_refs[0].shape
    inner = [(i, j) for i in range(mine) for j in range(i + 1, mine)] if first else []
    outer = [(i, mine + j) for i in range(mine) for j in range(others)]
    pairs = inner + outer
    shares = [1.0 / (count - 1)] * len(inner) + [0.5 / (count - 1)] * len(outer)
    live_count = counts_ref[region_ref[0]]

    def one_tile(at, total):
        start = pl.multiple_of(at * LANE, LANE)
        lanes = pl.ds(start, LANE)
        if first:
            turned = target_ref[lanes, :].astype(jnp.float32).T

        def rows_of(c):
            return [ref[c : c + 16, lanes].astype(jnp.float32) for ref in (*own_refs, *other_refs)]

        def fold(square):
            return square[:8] + square[8:]

        to_target = [jnp.zeros((8, LANE), jnp.float32)] * (mine if first else 0)
        apart = [jnp.zeros((8, LANE), jnp.float32)] * len(pairs)
        for c in range(0, channels, 16):
            values = rows_of(c)
            for i in range(len(to_target)):
                to_target[i] = to_target[i] + fold((values[i] - turned[c : c + 16]) ** 2)
            for p, (i, j) in enumerate(pairs):
                apart[p] = apart[p] + fold((values[i] - values[j]) ** 2)
        live = start + lax.broadcasted_iota(jnp.int32, (1, LANE), 1) < live_count
        score = jnp.zeros((1, LANE), jnp.float32)

        def inverse(square):
            squared = jnp.sum(square, axis=0, keepdims=True) + EPSILON
            inv = lax.rsqrt(squared)
            return squared * inv, inv

        inv_target, inv_pair = [], []
        for square in to_target:
            dist, inv = inverse(square)
            score = score + dist
            inv_target.append(jnp.broadcast_to(inv, (8, LANE)))
        for square, share in zip(apart, shares):
            dist, inv = inverse(square)
            score = score - dist * share
            inv_pair.append(jnp.broadcast_to(inv * (1.0 / (count - 1)), (8, LANE)))
        for c in range(0, channels, 16):
            values = rows_of(c)
            halves = []
            for h in (0, 8):
                near = [v[h : h + 8] for v in values]
                rows = slice(c + h, c + h + 8)
                if first:
                    grads = [(near[i] - turned[rows]) * inv_target[i] for i in range(mine)]
                else:
                    grads = [old_refs[i][rows, lanes] for i in range(mine)]
                for p, (i, j) in enumerate(pairs):
                    term = (near[i] - near[j]) * inv_pair[p]
                    grads[i] = grads[i] - term
                    if j < mine:
                        grads[j] = grads[j] + term
                halves.append(grads)
            for i in range(mine):
                grad = jnp.concatenate([halves[0][i], halves[1][i]], axis=0)
                if last:
                    grad = jnp.where(live, grad, 0.0)
                grad_refs[i][c : c + 16, lanes] = grad.astype(grad_refs[i].dtype)
        return total + jnp.where(live, score, 0.0)

    score_ref[...] = old_score + lax.fori_loop(0, slots // LANE, one_tile, jnp.zeros((1, LANE), jnp.float32))


def backward_kernel(members, table_ref, w_one_ref, w_two_ref, w_three_ref, *refs):
    saved = [refs[3 * m : 3 * (m + 1)] for m in range(members)]
    refs = refs[3 * members :]
    d_one_refs, d_two_refs, d_mixed_refs = (refs[i * members : (i + 1) * members] for i in range(3))
    bias_one_ref, bias_two_ref, head_ref, tail_ref = refs[3 * members :]
    w_one, w_two, w_three = w_one_ref[...], w_two_ref[...] * 0.5, w_three_ref[...] * 0.5
    hidden, slots = saved[0][0].shape
    ext = table_ref.shape[0]
    bias_one = jnp.zeros((hidden, LANE), jnp.float32)
    bias_two = jnp.zeros((hidden, LANE), jnp.float32)

    def lane_sum(values):
        return sum(values[:, lo : lo + LANE] for lo, _ in split(values.shape[1], LANE))

    for m in range(members):
        slope_one_ref, slope_two_ref, d_dec_ref = saved[m]
        for lo, size in split(slots, CHUNK):
            lanes = slice(lo, lo + size)
            back = nn_dot(w_three, d_dec_ref[:, lanes]) * slope_two_ref[:, lanes].astype(jnp.float32)
            bias_two = bias_two + lane_sum(back)
            d_two = back.astype(jnp.bfloat16)
            d_two_refs[m][:, lanes] = d_two
            back = nn_dot(w_two, d_two) * slope_one_ref[:, lanes].astype(jnp.float32)
            bias_one = bias_one + lane_sum(back)
            d_one = back.astype(jnp.bfloat16)
            d_one_refs[m][:, lanes] = d_one
            d_mixed_refs[m][:, lanes] = nn_dot(w_one, d_one).astype(jnp.bfloat16)
        head_ref[m] = nt_dot(table_ref[:HALO, :], d_mixed_refs[m][...]).astype(jnp.bfloat16)
        tail_ref[m] = nt_dot(table_ref[ext - HALO :, :], d_mixed_refs[m][...]).astype(jnp.bfloat16)
    bias_one_ref[...] = bias_one
    bias_two_ref[...] = bias_two


def sums_kernel(members, ranks, region_ref, rank_ref, score_ref, bias_one_ref, bias_two_ref, *refs):
    saved = [refs[6 * m : 6 * (m + 1)] for m in range(members)]
    *piece_refs, stage_ref = refs[6 * members :]
    hidden = bias_one_ref.shape[0]
    half = hidden // 2
    g_one, g_two, g_three = 0.0, 0.0, 0.0
    for mixed_ref, act_one_ref, act_two_ref, d_one_ref, d_two_ref, d_dec_ref in saved:
        g_one = g_one + nt_dot(mixed_ref[...], d_one_ref[...])
        g_two = g_two + nt_dot(act_one_ref[...], d_two_ref[...])
        g_three = g_three + nt_dot(act_two_ref[...], d_dec_ref[...])
    region = lax.broadcasted_iota(jnp.int32, (1, hidden), 1) == region_ref[0]
    tally = jnp.where(region, jnp.sum(score_ref[...]), 0.0)
    high = tally.astype(jnp.bfloat16).astype(jnp.float32)
    parts = [
        g_one,
        g_two,
        jnp.concatenate([g_three[:half], g_three[half:]], axis=1),
        jnp.sum(bias_one_ref[...].T, axis=0, keepdims=True),
        jnp.sum(bias_two_ref[...].T, axis=0, keepdims=True),
        high,
        tally - high,
    ]
    used = sum(part.shape[0] for part in parts)
    parts.append(jnp.zeros((ranks * stage_ref.shape[1] - used, hidden), jnp.float32))
    stage_ref[...] = jnp.concatenate(parts, axis=0).astype(stage_ref.dtype).reshape(stage_ref.shape)
    for i in range(ranks):
        piece_refs[i][...] = stage_ref[rank_ref[0] ^ i]


def sum_kernel(*refs):
    count = len(refs) // 3
    for i in range(count):
        total = refs[i][...].astype(jnp.float32) + refs[count + i][...].astype(jnp.float32)
        refs[2 * count + i][...] = total.astype(refs[i].dtype)


def unpack_kernel(scale, rank_ref, *refs):
    *refs, stage_ref = refs
    ranks = stage_ref.shape[0]
    one_ref, b_one_ref, two_ref, b_two_ref, three_ref, tally_ref = refs[ranks:]
    for i in range(ranks):
        stage_ref[rank_ref[0] ^ i] = refs[i][...]
    width, hidden = one_ref.shape
    sums = stage_ref[...].reshape(-1, hidden).astype(jnp.float32)
    half, channels = hidden // 2, three_ref.shape[1]
    one_ref[...] = sums[:width]
    two_ref[...] = sums[width : width + hidden]
    base = width + hidden
    three_ref[:half] = sums[base : base + half, :channels]
    three_ref[half:] = sums[base : base + half, channels:]
    last = sums[base + half : base + half + 8]
    b_one_ref[...] = last[0:1]
    b_two_ref[...] = last[1:2]
    tally_ref[...] = (last[2:3] + last[3:4])[:, : tally_ref.shape[1]] * scale


def own_kernel(table_ref, *refs):
    *d_mixed_refs, own_ref = refs
    members, nodes, _ = own_ref.shape
    for m in range(members):
        own_ref[m] = nt_dot(table_ref[HALO : HALO + nodes, :], d_mixed_refs[m][...])


def finish_kernel(own_ref, from_next_ref, from_prev_ref, out_ref):
    nodes = own_ref.shape[1]
    from_next, from_prev = from_next_ref[...].astype(jnp.float32), from_prev_ref[...].astype(jnp.float32)
    out_ref[:, :HALO] = (own_ref[:, :HALO] + from_prev).astype(jnp.bfloat16)
    out_ref[:, HALO : nodes - HALO] = own_ref[:, HALO : nodes - HALO].astype(jnp.bfloat16)
    out_ref[:, nodes - HALO :] = (own_ref[:, nodes - HALO :] + from_next).astype(jnp.bfloat16)


def shifted(shard, axis, by):
    length = lax.axis_size(axis)
    return lax.ppermute(shard, axis, [(i, (i + by) % length) for i in range(length)])


def swapped(block, axis, by):
    return lax.ppermute(block, axis, [(i, i ^ by) for i in range(lax.axis_size(axis))])


def per_device(latent, neighbours, weights, targets, counts, w_one, b_one, w_two, b_two, w_three):
    members, nodes, width = latent.shape
    slots, channels = targets.shape
    hidden = w_one.shape[1]
    ext = nodes + 2 * HALO
    region, regions = lax.axis_index("space"), lax.axis_size("space")
    rank, ranks = lax.axis_index("member"), lax.axis_size("member")
    share = slots // ranks
    bf16, f32 = jnp.bfloat16, jnp.float32
    shape = jax.ShapeDtypeStruct
    each = range(members)

    edge = shape((HALO, width), bf16)
    *rims, latent = kernel_call(
        rims_kernel, (edge,) * (2 * members) + (shape(latent.shape, bf16),), flops=4 << 30, moved=3 * MIB, operands=1
    )(latent)
    before = [shifted(rims[2 * m], "space", 1) for m in each]
    after = [shifted(rims[2 * m + 1], "space", -1) for m in each]
    rank_at = rank[None].astype(jnp.int32)
    region_at = region[None].astype(jnp.int32)

    table, part = kernel_call(
        table_kernel,
        (shape((ext, slots), bf16), shape((width, slots), f32)),
        flops=2 * width * nodes * slots,
        moved=12 * MIB,
        smem=3,
        operands=6,
    )(region_at, rank_at, counts, neighbours, weights, latent)

    saved_shape = shape((hidden, slots), bf16)
    mixed_shape = shape((width, slots), bf16)
    decoded_shape = shape((channels, slots), bf16)
    dense = width * hidden + hidden * hidden + hidden * channels
    saved, known = [], []
    for m in each:
        *kept, decoded = kernel_call(
            lambda *refs: forward_kernel(m, *refs),
            (mixed_shape,) + (saved_shape,) * 4 + (decoded_shape,),
            flops=2 * slots * ((ext if m else 2 * HALO) * width + dense),
            moved=8 * MIB,
            operands=9,
        )(latent if m else part, table, before[m], after[m], w_one, b_one[None], w_two, b_two[None], w_three)
        saved.append(kept)
        known.append({0: decoded})
        bit = 2
        while bit < ranks:
            known[m].update({i ^ bit: swapped(known[m][i], "member", bit) for i in sorted(known[m])})
            bit = 2 * bit
        known[m][1] = swapped(decoded, "member", 1)

    def scored(others, carried, first=False, last=False):
        operands = (region_at, counts, *[known[m][0] for m in each], *others, *carried)
        return kernel_call(
            lambda *refs: score_kernel(members, len(others), members * ranks, first, last, *refs),
            (shape((channels, slots), bf16 if last else f32),) * members + (shape((1, LANE), f32),),
            flops=4 * MIB,
            moved=2 * MIB,
            smem=2,
            operands=len(operands),
        )(*operands)

    near = [{i: block for i, block in known[m].items() if i > 1} for m in each]
    early = [known[m][1] for m in each] + [block for blocks in near[:-1] for block in blocks.values()]
    carried = scored(early, [targets], first=True)
    near[-1], carried = lax.optimization_barrier((near[-1], carried))
    others = [*near[-1].values()]
    others += [swapped(block, "member", 1) for blocks in near for block in blocks.values()]
    carried = scored(others, carried, last=True)
    *d_decoded, score = carried

    rows = -(-(width + hidden + hidden // 2 + 4) // (16 * ranks)) * 16
    piece = shape((rows, hidden), bf16)
    bias = shape((hidden, LANE), f32)
    rims = shape((members, HALO, width), bf16)
    operands = [table, w_one, w_two, w_three]
    for m in each:
        operands += [saved[m][2], saved[m][4], d_decoded[m]]
    out = kernel_call(
        lambda *refs: backward_kernel(members, *refs),
        (saved_shape,) * (2 * members) + (mixed_shape,) * members + (bias, bias, rims, rims),
        flops=2 * members * slots * (dense + 2 * HALO * width),
        moved=10 * MIB,
        operands=len(operands),
    )(*operands)
    d_one, d_two, d_mixed = (out[i * members : (i + 1) * members] for i in range(3))
    bias_one, bias_two, head, tail = out[3 * members :]
    from_next = shifted(head, "space", -1)
    operands = [region_at, rank_at, score, bias_one, bias_two]
    for m in each:
        mixed, act_one, _, act_two, _ = saved[m]
        operands += [mixed, act_one, act_two, d_one[m], d_two[m], d_decoded[m]]
    pieces = kernel_call(
        lambda *refs: sums_kernel(members, ranks, *refs),
        (piece,) * ranks,
        flops=2 * members * slots * dense,
        moved=10 * MIB,
        scratch=(pltpu.VMEM((ranks, rows, hidden), bf16),),
        smem=2,
        operands=len(operands),
    )(*operands)

    def summed(ones, others):
        return kernel_call(
            sum_kernel, (piece,) * len(ones), flops=MIB, moved=MIB, operands=2 * len(ones)
        )(*ones, *others)

    bit = 1
    while bit < ranks:
        received = [swapped(sent, "member", bit) for sent in pieces[1::2]]
        if bit == ranks // 2:
            received, from_next = lax.optimization_barrier((received, from_next))
        pieces = summed(pieces[::2], received)
        bit = 2 * bit
    (total,) = pieces
    from_prev = shifted(tail, "space", 1)
    own = kernel_call(
        own_kernel,
        shape((members, nodes, width), f32),
        flops=2 * members * nodes * width * slots,
        moved=6 * MIB,
        operands=1 + members,
    )(table, *d_mixed)
    step = 1
    while step < regions:
        (total,) = summed([total], [swapped(total, "space", step)])
        step = 2 * step
        if step == regions // 2:
            total, own = lax.optimization_barrier((total, own))
    totals = {0: total}
    bit = 2
    while bit < ranks:
        totals.update({i ^ bit: swapped(totals[i], "member", bit) for i in sorted(totals)})
        bit = 2 * bit
    beside = swapped(total, "member", 1)
    beside, from_prev = lax.optimization_barrier((beside, from_prev))
    latent_grad = kernel_call(
        finish_kernel,
        shape((members, nodes, width), bf16),
        flops=MIB,
        moved=3 * MIB,
        operands=3,
    )(own, from_next, from_prev)
    across = {i: block for i, block in totals.items() if i}
    across, latent_grad = lax.optimization_barrier((across, latent_grad))
    totals.update({i ^ 1: swapped(block, "member", 1) for i, block in across.items()})
    totals.update(across)
    totals[1] = beside
    totals = [totals[i] for i in range(ranks)]
    row = shape((1, hidden), f32)
    g_one, g_bone, g_two, g_btwo, g_three, tally = kernel_call(
        lambda *refs: unpack_kernel(1.0 / (OBS_MEAN * members * ranks), *refs),
        (shape((width, hidden), f32), row, shape((hidden, hidden), f32), row, shape((hidden, channels), f32),
         shape((1, regions), f32)),
        flops=MIB,
        moved=2 * MIB,
        scratch=(pltpu.VMEM((ranks, rows, hidden), bf16),),
        smem=1,
        operands=1 + ranks,
    )(rank_at, *totals)
    return (tally[0], latent_grad, g_one, g_bone[0], g_two, g_btwo[0], g_three)


def solution(mesh):
    in_specs = (
        P("member", ("groups", "space"), None),
        P(None, ("groups", "space")),
        P(None, ("groups", "space")),
        P(("groups", "space"), None),
        P("groups"),
        P(),
        P(),
        P(),
        P(),
        P(),
    )
    out_specs = (
        P("groups"),
        P("member", ("groups", "space"), None),
        P("groups", None),
        P("groups"),
        P("groups", None),
        P("groups"),
        P("groups", None),
    )
    return jax.shard_map(
        per_device, mesh=mesh, in_specs=in_specs, out_specs=out_specs, check_vma=False
    )
```

```python
import jax
import jax.numpy as jnp
from jax import lax
from jax.experimental import pallas as pl
from jax.experimental.pallas import tpu as pltpu
from jax.sharding import PartitionSpec as P

K = 4
OBS_MEAN = 512
HALO = 256
EPSILON = 1e-05
BLOCK = 256
LANE = 128
CHUNK = 512
MIB = 1 << 20


def split(total, step):
    return [(start, min(step, total - start)) for start in range(0, total, step)]


def nt_dot(left, right):
    return lax.dot_general(
        left, right, (((1,), (1,)), ((), ())), preferred_element_type=jnp.float32
    )


def nn_dot(left, right):
    return jnp.dot(left, right, preferred_element_type=jnp.float32)


def kernel_call(body, out_shape, flops, moved, scratch=(), smem=0, operands=0):
    vmem = pl.BlockSpec(memory_space=pltpu.VMEM)
    specs = [pl.BlockSpec(memory_space=pltpu.SMEM)] * smem
    return pl.pallas_call(
        body,
        out_shape=out_shape,
        in_specs=specs + [vmem] * (operands - len(specs)),
        out_specs=jax.tree.map(lambda _: vmem, out_shape),
        scratch_shapes=list(scratch),
        compiler_params=pltpu.CompilerParams(vmem_limit_bytes=24 * MIB),
        cost_estimate=pl.CostEstimate(flops=flops, bytes_accessed=moved, transcendentals=0),
    )


def cut_rims(latent_ref, member, last_ref, first_ref):
    nodes = latent_ref.shape[1]
    last_ref[...] = latent_ref[member, nodes - HALO :]
    first_ref[...] = latent_ref[member, :HALO]


def rims_kernel(latent_ref, last_ref, first_ref, copy_ref):
    cut_rims(latent_ref, 0, last_ref, first_ref)
    copy_ref[...] = latent_ref[...]


def table_kernel(region_ref, rank_ref, counts_ref, nbr_ref, weight_ref, latent_ref, table_ref, part_ref, *rim_refs):
    members, nodes, _ = latent_ref.shape
    for m in range(1, members):
        cut_rims(latent_ref, m, *rim_refs[2 * m - 2 : 2 * m])
    ext, slots = table_ref.shape
    live = lax.broadcasted_iota(jnp.int32, (1, slots), 1) < counts_ref[region_ref[0]]
    nbr = [nbr_ref[k : k + 1, :] for k in range(K)]
    own = [jnp.where(live, weight_ref[k : k + 1, :], 0.0) for k in range(K)]
    joint = []
    for k in range(K):
        total = own[k]
        for j in range(K):
            if j != k:
                total = total + jnp.where(nbr[j] == nbr[k], own[j], 0.0)
        joint.append(total)
    groups = BLOCK // 16
    rows = (
        lax.broadcasted_iota(jnp.int32, (groups, 16, LANE), 0) * 16
        + lax.broadcasted_iota(jnp.int32, (groups, 16, LANE), 1)
    ).astype(jnp.float32).astype(jnp.bfloat16)
    turned = latent_ref[0].T
    for start, length in split(slots, CHUNK):
        for lo, size in split(length, LANE):
            lanes = slice(start + lo, start + lo + size)
            wide = [jnp.broadcast_to(joint[k][:, lanes], (16, size)).astype(jnp.bfloat16) for k in range(K)]
            for b in range(ext // BLOCK):
                tile = jnp.zeros((groups, 16, size), jnp.bfloat16)
                for k in range(K):
                    near = (nbr[k][:, lanes] - b * BLOCK).astype(jnp.float32)
                    near = jnp.broadcast_to(near, (16, size)).astype(jnp.bfloat16)
                    tile = jnp.where(rows[:, :, :size] == near[None], wide[k][None], tile)
                table_ref[b * BLOCK : (b + 1) * BLOCK, lanes] = tile.reshape(BLOCK, size)
        lanes = slice(start, start + length)
        part_ref[:, lanes] = nn_dot(turned, table_ref[HALO : HALO + nodes, lanes])


def column(ref):
    height = ref.shape[1]
    return jnp.broadcast_to(ref[...], (LANE, height)).T


def forward_kernel(
    member, own_ref, table_ref, before_ref, after_ref, w_one_ref, b_one_ref, w_two_ref, b_two_ref, w_three_ref,
    mixed_ref, act_one_ref, slope_one_ref, act_two_ref, slope_two_ref, decoded_ref,
):
    ext, slots = table_ref.shape
    w_one, w_two, w_three = w_one_ref[...].T * 0.5, w_two_ref[...].T * 0.5, w_three_ref[...].T
    b_one, b_two = column(b_one_ref) * 0.5, column(b_two_ref) * 0.5

    def layer(weight, bias, values, size):
        half = nn_dot(weight, values) + jnp.concatenate([bias] * (size // LANE), axis=1)
        gate = 1.0 + jnp.tanh(half)
        act = half * gate
        return act.astype(jnp.bfloat16), (gate + act * (2.0 - gate)).astype(jnp.bfloat16)

    if member:
        nodes = jnp.concatenate([before_ref[...].T, own_ref[member].T, after_ref[...].T], axis=1)
    else:
        nodes = jnp.concatenate([before_ref[...].T, after_ref[...].T], axis=1)
    for lo, size in split(slots, CHUNK):
        lanes = slice(lo, lo + size)
        if member:
            mixed = nn_dot(nodes, table_ref[:, lanes])
        else:
            rims = jnp.concatenate([table_ref[:HALO, lanes], table_ref[ext - HALO :, lanes]], axis=0)
            mixed = own_ref[:, lanes] + nn_dot(nodes, rims)
        mixed = mixed.astype(jnp.bfloat16)
        mixed_ref[:, lanes] = mixed
        act_one, slope_one_ref[:, lanes] = layer(w_one, b_one, mixed, size)
        act_one_ref[:, lanes] = act_one
        act_two, slope_two_ref[:, lanes] = layer(w_two, b_two, act_one, size)
        act_two_ref[:, lanes] = act_two
        decoded_ref[:, lanes] = nn_dot(w_three, act_two).astype(jnp.bfloat16)


def score_kernel(mine, others, count, first, last, region_ref, counts_ref, *refs):
    own_refs, refs = refs[:mine], refs[mine:]
    other_refs, refs = refs[:others], refs[others:]
    if first:
        target_ref, refs = refs[0], refs[1:]
        old_refs, old_score = None, 0.0
    else:
        old_refs, old_score, refs = refs[:mine], refs[mine][...], refs[mine + 1 :]
    grad_refs, score_ref = refs[:mine], refs[mine]
    channels, slots = own_refs[0].shape
    inner = [(i, j) for i in range(mine) for j in range(i + 1, mine)] if first else []
    outer = [(i, mine + j) for i in range(mine) for j in range(others)]
    pairs = inner + outer
    shares = [1.0 / (count - 1)] * len(inner) + [0.5 / (count - 1)] * len(outer)
    live_count = counts_ref[region_ref[0]]

    def one_tile(at, total):
        start = pl.multiple_of(at * LANE, LANE)
        lanes = pl.ds(start, LANE)
        if first:
            turned = target_ref[lanes, :].astype(jnp.float32).T

        def rows_of(c):
            return [ref[c : c + 16, lanes].astype(jnp.float32) for ref in (*own_refs, *other_refs)]

        def fold(square):
            return square[:8] + square[8:]

        to_target = [jnp.zeros((8, LANE), jnp.float32)] * (mine if first else 0)
        apart = [jnp.zeros((8, LANE), jnp.float32)] * len(pairs)
        for c in range(0, channels, 16):
            values = rows_of(c)
            for i in range(len(to_target)):
                to_target[i] = to_target[i] + fold((values[i] - turned[c : c + 16]) ** 2)
            for p, (i, j) in enumerate(pairs):
                apart[p] = apart[p] + fold((values[i] - values[j]) ** 2)
        live = start + lax.broadcasted_iota(jnp.int32, (1, LANE), 1) < live_count
        score = jnp.zeros((1, LANE), jnp.float32)

        def inverse(square):
            squared = jnp.sum(square, axis=0, keepdims=True) + EPSILON
            inv = lax.rsqrt(squared)
            return squared * inv, inv

        inv_target, inv_pair = [], []
        for square in to_target:
            dist, inv = inverse(square)
            score = score + dist
            inv_target.append(jnp.broadcast_to(inv, (8, LANE)))
        for square, share in zip(apart, shares):
            dist, inv = inverse(square)
            score = score - dist * share
            inv_pair.append(jnp.broadcast_to(inv * (1.0 / (count - 1)), (8, LANE)))
        for c in range(0, channels, 16):
            values = rows_of(c)
            halves = []
            for h in (0, 8):
                near = [v[h : h + 8] for v in values]
                rows = slice(c + h, c + h + 8)
                if first:
                    grads = [(near[i] - turned[rows]) * inv_target[i] for i in range(mine)]
                else:
                    grads = [old_refs[i][rows, lanes] for i in range(mine)]
                for p, (i, j) in enumerate(pairs):
                    term = (near[i] - near[j]) * inv_pair[p]
                    grads[i] = grads[i] - term
                    if j < mine:
                        grads[j] = grads[j] + term
                halves.append(grads)
            for i in range(mine):
                grad = jnp.concatenate([halves[0][i], halves[1][i]], axis=0)
                if last:
                    grad = jnp.where(live, grad, 0.0)
                grad_refs[i][c : c + 16, lanes] = grad.astype(grad_refs[i].dtype)
        return total + jnp.where(live, score, 0.0)

    score_ref[...] = old_score + lax.fori_loop(0, slots // LANE, one_tile, jnp.zeros((1, LANE), jnp.float32))


def backward_kernel(members, ranks, region_ref, rank_ref, w_two_ref, w_three_ref, score_ref, *refs):
    saved = [refs[6 * m : 6 * (m + 1)] for m in range(members)]
    refs = refs[6 * members :]
    d_one_refs, piece_refs, (d_two_ref, stage_ref) = refs[:members], refs[members:-2], refs[-2:]
    w_two, w_three = w_two_ref[...] * 0.5, w_three_ref[...] * 0.5
    hidden, slots = saved[0][1].shape
    bias_one = jnp.zeros((hidden, LANE), jnp.float32)
    bias_two = jnp.zeros((hidden, LANE), jnp.float32)
    g_one, g_two, g_three = 0.0, 0.0, 0.0

    def lane_sum(values):
        return sum(values[:, lo : lo + LANE] for lo, _ in split(values.shape[1], LANE))

    for m in range(members):
        mixed_ref, act_one_ref, slope_one_ref, act_two_ref, slope_two_ref, d_dec_ref = saved[m]
        for lo, size in split(slots, CHUNK):
            lanes = slice(lo, lo + size)
            back = nn_dot(w_three, d_dec_ref[:, lanes]) * slope_two_ref[:, lanes].astype(jnp.float32)
            bias_two = bias_two + lane_sum(back)
            d_two = back.astype(jnp.bfloat16)
            d_two_ref[m, :, lanes] = d_two
            back = nn_dot(w_two, d_two) * slope_one_ref[:, lanes].astype(jnp.float32)
            bias_one = bias_one + lane_sum(back)
            d_one_refs[m][:, lanes] = back.astype(jnp.bfloat16)
        g_three = g_three + nt_dot(act_two_ref[...], d_dec_ref[...])
        g_two = g_two + nt_dot(act_one_ref[...], d_two_ref[m])
        g_one = g_one + nt_dot(mixed_ref[...], d_one_refs[m][...])
    half = hidden // 2
    region = lax.broadcasted_iota(jnp.int32, (1, hidden), 1) == region_ref[0]
    tally = jnp.where(region, jnp.sum(score_ref[...]), 0.0)
    high = tally.astype(jnp.bfloat16).astype(jnp.float32)
    parts = [
        g_one,
        g_two,
        jnp.concatenate([g_three[:half], g_three[half:]], axis=1),
        jnp.sum(bias_one.T, axis=0, keepdims=True),
        jnp.sum(bias_two.T, axis=0, keepdims=True),
        high,
        tally - high,
    ]
    used = sum(part.shape[0] for part in parts)
    parts.append(jnp.zeros((ranks * stage_ref.shape[1] - used, hidden), jnp.float32))
    stage_ref[...] = jnp.concatenate(parts, axis=0).astype(stage_ref.dtype).reshape(stage_ref.shape)
    for i in range(ranks):
        piece_refs[i][...] = stage_ref[rank_ref[0] ^ i]


def edges_kernel(members, table_ref, w_one_ref, *refs):
    d_one_refs, refs = refs[:members], refs[members:]
    ext = table_ref.shape[0]
    rows = jnp.concatenate([table_ref[:HALO, :], table_ref[ext - HALO :, :]], axis=0)
    for m in range(members):
        d_mixed_ref, head_ref, tail_ref = refs[3 * m : 3 * (m + 1)]
        d_mixed = nn_dot(w_one_ref[...], d_one_refs[m][...]).astype(jnp.bfloat16)
        d_mixed_ref[...] = d_mixed
        grads = nt_dot(rows, d_mixed).astype(jnp.bfloat16)
        head_ref[...] = grads[:HALO]
        tail_ref[...] = grads[HALO:]


def sum_kernel(count, *refs):
    for i in range(count):
        total = refs[i][...].astype(jnp.float32) + refs[count + i][...].astype(jnp.float32)
        refs[2 * count + i][...] = total.astype(refs[i].dtype)


def unpack_kernel(scale, rank_ref, *refs):
    *refs, stage_ref = refs
    ranks = stage_ref.shape[0]
    one_ref, b_one_ref, two_ref, b_two_ref, three_ref, tally_ref = refs[ranks:]
    for i in range(ranks):
        stage_ref[rank_ref[0] ^ i] = refs[i][...]
    width, hidden = one_ref.shape
    sums = stage_ref[...].reshape(-1, hidden).astype(jnp.float32)
    half, channels = hidden // 2, three_ref.shape[1]
    one_ref[...] = sums[:width]
    two_ref[...] = sums[width : width + hidden]
    base = width + hidden
    three_ref[:half] = sums[base : base + half, :channels]
    three_ref[half:] = sums[base : base + half, channels:]
    last = sums[base + half : base + half + 8]
    b_one_ref[...] = last[0:1]
    b_two_ref[...] = last[1:2]
    tally_ref[...] = (last[2:3] + last[3:4])[:, : tally_ref.shape[1]] * scale


def own_kernel(table_ref, *refs):
    *d_mixed_refs, own_ref = refs
    members, nodes, _ = own_ref.shape
    for m in range(members):
        own_ref[m] = nt_dot(table_ref[HALO : HALO + nodes, :], d_mixed_refs[m][...])


def finish_kernel(own_ref, *refs):
    *refs, out_ref = refs
    members, nodes, _ = own_ref.shape
    for m in range(members):
        from_next, from_prev = refs[2 * m][...].astype(jnp.float32), refs[2 * m + 1][...].astype(jnp.float32)
        out_ref[m, :HALO] = (own_ref[m, :HALO] + from_prev).astype(jnp.bfloat16)
        out_ref[m, HALO : nodes - HALO] = own_ref[m, HALO : nodes - HALO].astype(jnp.bfloat16)
        out_ref[m, nodes - HALO :] = (own_ref[m, nodes - HALO :] + from_next).astype(jnp.bfloat16)


def shifted(shard, axis, by):
    length = lax.axis_size(axis)
    return lax.ppermute(shard, axis, [(i, (i + by) % length) for i in range(length)])


def swapped(block, axis, by):
    return lax.ppermute(block, axis, [(i, i ^ by) for i in range(lax.axis_size(axis))])


def per_device(latent, neighbours, weights, targets, counts, w_one, b_one, w_two, b_two, w_three):
    members, nodes, width = latent.shape
    slots, channels = targets.shape
    hidden = w_one.shape[1]
    ext = nodes + 2 * HALO
    region, regions = lax.axis_index("space"), lax.axis_size("space")
    rank, ranks = lax.axis_index("member"), lax.axis_size("member")
    share = slots // ranks
    bf16, f32 = jnp.bfloat16, jnp.float32
    shape = jax.ShapeDtypeStruct
    each = range(members)

    edge = shape((HALO, width), bf16)
    last, first, latent = kernel_call(
        rims_kernel, (edge, edge, shape(latent.shape, bf16)), flops=4 << 30, moved=3 * MIB, operands=1
    )(latent)
    before, after = [shifted(last, "space", 1)], [shifted(first, "space", -1)]
    rank_at = rank[None].astype(jnp.int32)
    region_at = region[None].astype(jnp.int32)

    table, part, *rims = kernel_call(
        table_kernel,
        (shape((ext, slots), bf16), shape((width, slots), f32)) + (edge,) * (2 * members - 2),
        flops=2 * width * nodes * slots,
        moved=12 * MIB,
        smem=3,
        operands=6,
    )(region_at, rank_at, counts, neighbours, weights, latent)
    before += [shifted(block, "space", 1) for block in rims[::2]]
    after += [shifted(block, "space", -1) for block in rims[1::2]]

    saved_shape = shape((hidden, slots), bf16)
    mixed_shape = shape((width, slots), bf16)
    decoded_shape = shape((channels, slots), bf16)
    dense = width * hidden + hidden * hidden + hidden * channels
    saved, decoded, beside, across = [], [], [], []
    for m in each:
        *kept, block = kernel_call(
            lambda *refs: forward_kernel(m, *refs),
            (mixed_shape,) + (saved_shape,) * 4 + (decoded_shape,),
            flops=2 * slots * ((ext if m else 2 * HALO) * width + dense),
            moved=8 * MIB,
            operands=9,
        )(latent if m else part, table, before[m], after[m], w_one, b_one[None], w_two, b_two[None], w_three)
        saved.append(kept)
        decoded.append(block)
        blocks, bit = {0: block}, 2
        while bit < ranks:
            blocks.update({i ^ bit: swapped(blocks[i], "member", bit) for i in sorted(blocks)})
            bit = 2 * bit
        across.append([blocks[i] for i in sorted(blocks) if i])
        beside.append(swapped(block, "member", 1))

    def scored(others, carried, first=False, last=False):
        operands = (region_at, counts, *decoded, *others, *carried)
        return kernel_call(
            lambda *refs: score_kernel(members, len(others), members * ranks, first, last, *refs),
            (shape((channels, slots), bf16 if last else f32),) * members + (shape((1, LANE), f32),),
            flops=4 * MIB,
            moved=2 * MIB,
            smem=2,
            operands=len(operands),
        )(*operands)

    carried = scored(beside + [block for blocks in across[:-1] for block in blocks], [targets], first=True)
    across[-1], carried = lax.optimization_barrier((across[-1], carried))
    others = [*across[-1]] + [swapped(block, "member", 1) for blocks in across for block in blocks]
    *grads, score = scored(others, carried, last=True)

    rows = -(-(width + hidden + hidden // 2 + 4) // (16 * ranks)) * 16
    piece = shape((rows, hidden), bf16)
    operands = [region_at, rank_at, w_two, w_three, score]
    for m in each:
        operands += [*saved[m], grads[m]]
    out = kernel_call(
        lambda *refs: backward_kernel(members, ranks, *refs),
        (saved_shape,) * members + (piece,) * ranks,
        flops=4 * members * slots * dense,
        moved=10 * MIB,
        scratch=(pltpu.VMEM((members, hidden, slots), bf16), pltpu.VMEM((ranks, rows, hidden), bf16)),
        smem=2,
        operands=len(operands),
    )(*operands)
    d_one, pieces = out[:members], out[members:]

    def summed(ones, others):
        return kernel_call(
            lambda *refs: sum_kernel(len(ones), *refs), (piece,) * len(ones), flops=MIB, moved=MIB, operands=2 * len(ones)
        )(*ones, *others)

    out = kernel_call(
        lambda *refs: edges_kernel(members, *refs),
        (mixed_shape, edge, edge) * members,
        flops=2 * members * slots * width * (hidden + 2 * HALO),
        moved=6 * MIB,
        operands=2 + members,
    )(table, w_one, *d_one)
    d_mixed, heads, tails = out[::3], out[1::3], out[2::3]

    def returned(m):
        return [shifted(heads[m], "space", -1), shifted(tails[m], "space", 1)]

    bit = 1
    while bit < ranks:
        received = [swapped(sent, "member", bit) for sent in pieces[1::2]]
        if bit == 1:
            received, heads, tails = lax.optimization_barrier((received, heads, tails))
        pieces = summed(pieces[::2], received)
        bit = 2 * bit
    own = kernel_call(
        own_kernel,
        shape((members, nodes, width), f32),
        flops=2 * members * nodes * width * slots,
        moved=6 * MIB,
        operands=1 + members,
    )(table, *d_mixed)
    edges = [block for m in each[:-1] for block in returned(m)]
    (total,) = pieces
    step = 1
    while step < regions:
        (total,) = summed([total], [swapped(total, "space", step)])
        step = 2 * step
        if step == regions // 2:
            total, edges, own, heads, tails = lax.optimization_barrier((total, edges, own, heads, tails))
            edges = [*edges, *returned(members - 1)]
    totals = {0: total}
    bit = 2
    while bit < ranks:
        totals.update({i ^ bit: swapped(totals[i], "member", bit) for i in sorted(totals)})
        bit = 2 * bit
    totals[1] = swapped(total, "member", 1)
    totals[1], edges = lax.optimization_barrier((totals[1], edges))
    latent_grad = kernel_call(
        finish_kernel,
        shape((members, nodes, width), bf16),
        flops=MIB,
        moved=3 * MIB,
        operands=1 + 2 * members,
    )(own, *edges)
    far = {i: block for i, block in totals.items() if i > 1}
    far, latent_grad = lax.optimization_barrier((far, latent_grad))
    totals.update(far)
    totals.update({i ^ 1: swapped(block, "member", 1) for i, block in far.items()})
    totals = [totals[i] for i in range(ranks)]
    row = shape((1, hidden), f32)
    g_one, g_bone, g_two, g_btwo, g_three, tally = kernel_call(
        lambda *refs: unpack_kernel(1.0 / (OBS_MEAN * members * ranks), *refs),
        (shape((width, hidden), f32), row, shape((hidden, hidden), f32), row, shape((hidden, channels), f32),
         shape((1, regions), f32)),
        flops=MIB,
        moved=2 * MIB,
        scratch=(pltpu.VMEM((ranks, rows, hidden), bf16),),
        smem=1,
        operands=1 + ranks,
    )(rank_at, *totals)
    return (tally[0], latent_grad, g_one, g_bone[0], g_two, g_btwo[0], g_three)


def solution(mesh):
    in_specs = (
        P("member", ("groups", "space"), None),
        P(None, ("groups", "space")),
        P(None, ("groups", "space")),
        P(("groups", "space"), None),
        P("groups"),
        P(),
        P(),
        P(),
        P(),
        P(),
    )
    out_specs = (
        P("groups"),
        P("member", ("groups", "space"), None),
        P("groups", None),
        P("groups"),
        P("groups", None),
        P("groups"),
        P("groups", None),
    )
    return jax.shard_map(
        per_device, mesh=mesh, in_specs=in_specs, out_specs=out_specs, check_vma=False
    )
```

```python
import jax
import jax.numpy as jnp
from jax import lax
from jax.experimental import pallas as pl
from jax.experimental.pallas import tpu as pltpu
from jax.sharding import PartitionSpec as P

K = 4
OBS_MEAN = 512
HALO = 256
EPSILON = 1e-05
BLOCK = 256
LANE = 128
CHUNK = 512
MIB = 1 << 20


def split(total, step):
    return [(start, min(step, total - start)) for start in range(0, total, step)]


def nt_dot(left, right):
    return lax.dot_general(
        left, right, (((1,), (1,)), ((), ())), preferred_element_type=jnp.float32
    )


def nn_dot(left, right):
    return jnp.dot(left, right, preferred_element_type=jnp.float32)


def kernel_call(body, out_shape, flops, moved, scratch=(), smem=0, operands=0):
    vmem = pl.BlockSpec(memory_space=pltpu.VMEM)
    specs = [pl.BlockSpec(memory_space=pltpu.SMEM)] * smem
    return pl.pallas_call(
        body,
        out_shape=out_shape,
        in_specs=specs + [vmem] * (operands - len(specs)),
        out_specs=jax.tree.map(lambda _: vmem, out_shape),
        scratch_shapes=list(scratch),
        compiler_params=pltpu.CompilerParams(vmem_limit_bytes=24 * MIB),
        cost_estimate=pl.CostEstimate(flops=flops, bytes_accessed=moved, transcendentals=0),
    )


def cut_rims(latent_ref, member, last_ref, first_ref):
    nodes = latent_ref.shape[1]
    last_ref[...] = latent_ref[member, nodes - HALO :]
    first_ref[...] = latent_ref[member, :HALO]


def rims_kernel(latent_ref, last_ref, first_ref, copy_ref):
    cut_rims(latent_ref, 0, last_ref, first_ref)
    copy_ref[...] = latent_ref[...]


def table_kernel(region_ref, rank_ref, counts_ref, nbr_ref, weight_ref, latent_ref, table_ref, part_ref, *rim_refs):
    members, nodes, _ = latent_ref.shape
    for m in range(1, members):
        cut_rims(latent_ref, m, *rim_refs[2 * m - 2 : 2 * m])
    ext, slots = table_ref.shape
    live = lax.broadcasted_iota(jnp.int32, (1, slots), 1) < counts_ref[region_ref[0]]
    nbr = [nbr_ref[k : k + 1, :] for k in range(K)]
    own = [jnp.where(live, weight_ref[k : k + 1, :], 0.0) for k in range(K)]
    joint = []
    for k in range(K):
        total = own[k]
        for j in range(K):
            if j != k:
                total = total + jnp.where(nbr[j] == nbr[k], own[j], 0.0)
        joint.append(total)
    groups = BLOCK // 16
    rows = (
        lax.broadcasted_iota(jnp.int32, (groups, 16, LANE), 0) * 16
        + lax.broadcasted_iota(jnp.int32, (groups, 16, LANE), 1)
    ).astype(jnp.float32).astype(jnp.bfloat16)
    turned = latent_ref[0].T
    for start, length in split(slots, CHUNK):
        for lo, size in split(length, LANE):
            lanes = slice(start + lo, start + lo + size)
            wide = [jnp.broadcast_to(joint[k][:, lanes], (16, size)).astype(jnp.bfloat16) for k in range(K)]
            for b in range(ext // BLOCK):
                tile = jnp.zeros((groups, 16, size), jnp.bfloat16)
                for k in range(K):
                    near = (nbr[k][:, lanes] - b * BLOCK).astype(jnp.float32)
                    near = jnp.broadcast_to(near, (16, size)).astype(jnp.bfloat16)
                    tile = jnp.where(rows[:, :, :size] == near[None], wide[k][None], tile)
                table_ref[b * BLOCK : (b + 1) * BLOCK, lanes] = tile.reshape(BLOCK, size)
        lanes = slice(start, start + length)
        part_ref[:, lanes] = nn_dot(turned, table_ref[HALO : HALO + nodes, lanes])


def column(ref):
    height = ref.shape[1]
    return jnp.broadcast_to(ref[...], (LANE, height)).T


def forward_kernel(
    member, own_ref, table_ref, before_ref, after_ref, w_one_ref, b_one_ref, w_two_ref, b_two_ref, w_three_ref,
    mixed_ref, act_one_ref, slope_one_ref, act_two_ref, slope_two_ref, decoded_ref,
):
    ext, slots = table_ref.shape
    w_one, w_two, w_three = w_one_ref[...].T * 0.5, w_two_ref[...].T * 0.5, w_three_ref[...].T
    b_one, b_two = column(b_one_ref) * 0.5, column(b_two_ref) * 0.5

    def layer(weight, bias, values, size):
        half = nn_dot(weight, values) + jnp.concatenate([bias] * (size // LANE), axis=1)
        gate = 1.0 + jnp.tanh(half)
        act = half * gate
        return act.astype(jnp.bfloat16), (gate + act * (2.0 - gate)).astype(jnp.bfloat16)

    if member:
        nodes = jnp.concatenate([before_ref[...].T, own_ref[member].T, after_ref[...].T], axis=1)
    else:
        nodes = jnp.concatenate([before_ref[...].T, after_ref[...].T], axis=1)
    for lo, size in split(slots, CHUNK):
        lanes = slice(lo, lo + size)
        if member:
            mixed = nn_dot(nodes, table_ref[:, lanes])
        else:
            rims = jnp.concatenate([table_ref[:HALO, lanes], table_ref[ext - HALO :, lanes]], axis=0)
            mixed = own_ref[:, lanes] + nn_dot(nodes, rims)
        mixed = mixed.astype(jnp.bfloat16)
        mixed_ref[:, lanes] = mixed
        act_one, slope_one_ref[:, lanes] = layer(w_one, b_one, mixed, size)
        act_one_ref[:, lanes] = act_one
        act_two, slope_two_ref[:, lanes] = layer(w_two, b_two, act_one, size)
        act_two_ref[:, lanes] = act_two
        decoded_ref[:, lanes] = nn_dot(w_three, act_two).astype(jnp.bfloat16)


def score_kernel(mine, others, count, first, last, region_ref, counts_ref, *refs):
    own_refs, refs = refs[:mine], refs[mine:]
    other_refs, refs = refs[:others], refs[others:]
    if first:
        target_ref, refs = refs[0], refs[1:]
        old_refs, old_score = None, 0.0
    else:
        old_refs, old_score, refs = refs[:mine], refs[mine][...], refs[mine + 1 :]
    grad_refs, score_ref = refs[:mine], refs[mine]
    channels, slots = own_refs[0].shape
    inner = [(i, j) for i in range(mine) for j in range(i + 1, mine)] if first else []
    outer = [(i, mine + j) for i in range(mine) for j in range(others)]
    pairs = inner + outer
    shares = [1.0 / (count - 1)] * len(inner) + [0.5 / (count - 1)] * len(outer)
    live_count = counts_ref[region_ref[0]]

    def one_tile(at, total):
        start = pl.multiple_of(at * LANE, LANE)
        lanes = pl.ds(start, LANE)
        if first:
            turned = target_ref[lanes, :].astype(jnp.float32).T

        def rows_of(c):
            return [ref[c : c + 16, lanes].astype(jnp.float32) for ref in (*own_refs, *other_refs)]

        def fold(square):
            return square[:8] + square[8:]

        to_target = [jnp.zeros((8, LANE), jnp.float32)] * (mine if first else 0)
        apart = [jnp.zeros((8, LANE), jnp.float32)] * len(pairs)
        for c in range(0, channels, 16):
            values = rows_of(c)
            for i in range(len(to_target)):
                to_target[i] = to_target[i] + fold((values[i] - turned[c : c + 16]) ** 2)
            for p, (i, j) in enumerate(pairs):
                apart[p] = apart[p] + fold((values[i] - values[j]) ** 2)
        live = start + lax.broadcasted_iota(jnp.int32, (1, LANE), 1) < live_count
        score = jnp.zeros((1, LANE), jnp.float32)

        def inverse(square):
            squared = jnp.sum(square, axis=0, keepdims=True) + EPSILON
            inv = lax.rsqrt(squared)
            return squared * inv, inv

        inv_target, inv_pair = [], []
        for square in to_target:
            dist, inv = inverse(square)
            score = score + dist
            inv_target.append(jnp.broadcast_to(inv, (8, LANE)))
        for square, share in zip(apart, shares):
            dist, inv = inverse(square)
            score = score - dist * share
            inv_pair.append(jnp.broadcast_to(inv * (1.0 / (count - 1)), (8, LANE)))
        for c in range(0, channels, 16):
            values = rows_of(c)
            halves = []
            for h in (0, 8):
                near = [v[h : h + 8] for v in values]
                rows = slice(c + h, c + h + 8)
                if first:
                    grads = [(near[i] - turned[rows]) * inv_target[i] for i in range(mine)]
                else:
                    grads = [old_refs[i][rows, lanes] for i in range(mine)]
                for p, (i, j) in enumerate(pairs):
                    term = (near[i] - near[j]) * inv_pair[p]
                    grads[i] = grads[i] - term
                    if j < mine:
                        grads[j] = grads[j] + term
                halves.append(grads)
            for i in range(mine):
                grad = jnp.concatenate([halves[0][i], halves[1][i]], axis=0)
                if last:
                    grad = jnp.where(live, grad, 0.0)
                grad_refs[i][c : c + 16, lanes] = grad.astype(grad_refs[i].dtype)
        return total + jnp.where(live, score, 0.0)

    score_ref[...] = old_score + lax.fori_loop(0, slots // LANE, one_tile, jnp.zeros((1, LANE), jnp.float32))


def backward_kernel(members, ranks, region_ref, rank_ref, w_two_ref, w_three_ref, score_ref, *refs):
    saved = [refs[6 * m : 6 * (m + 1)] for m in range(members)]
    refs = refs[6 * members :]
    d_one_refs, piece_refs, (d_two_ref, stage_ref) = refs[:members], refs[members:-2], refs[-2:]
    w_two, w_three = w_two_ref[...] * 0.5, w_three_ref[...] * 0.5
    hidden, slots = saved[0][1].shape
    bias_one = jnp.zeros((hidden, LANE), jnp.float32)
    bias_two = jnp.zeros((hidden, LANE), jnp.float32)
    g_one, g_two, g_three = 0.0, 0.0, 0.0

    def lane_sum(values):
        return sum(values[:, lo : lo + LANE] for lo, _ in split(values.shape[1], LANE))

    for m in range(members):
        mixed_ref, act_one_ref, slope_one_ref, act_two_ref, slope_two_ref, d_dec_ref = saved[m]
        for lo, size in split(slots, CHUNK):
            lanes = slice(lo, lo + size)
            back = nn_dot(w_three, d_dec_ref[:, lanes]) * slope_two_ref[:, lanes].astype(jnp.float32)
            bias_two = bias_two + lane_sum(back)
            d_two = back.astype(jnp.bfloat16)
            d_two_ref[m, :, lanes] = d_two
            back = nn_dot(w_two, d_two) * slope_one_ref[:, lanes].astype(jnp.float32)
            bias_one = bias_one + lane_sum(back)
            d_one_refs[m][:, lanes] = back.astype(jnp.bfloat16)
        g_three = g_three + nt_dot(act_two_ref[...], d_dec_ref[...])
        g_two = g_two + nt_dot(act_one_ref[...], d_two_ref[m])
        g_one = g_one + nt_dot(mixed_ref[...], d_one_refs[m][...])
    half = hidden // 2
    region = lax.broadcasted_iota(jnp.int32, (1, hidden), 1) == region_ref[0]
    tally = jnp.where(region, jnp.sum(score_ref[...]), 0.0)
    high = tally.astype(jnp.bfloat16).astype(jnp.float32)
    parts = [
        g_one,
        g_two,
        jnp.concatenate([g_three[:half], g_three[half:]], axis=1),
        jnp.sum(bias_one.T, axis=0, keepdims=True),
        jnp.sum(bias_two.T, axis=0, keepdims=True),
        high,
        tally - high,
    ]
    used = sum(part.shape[0] for part in parts)
    parts.append(jnp.zeros((ranks * stage_ref.shape[1] - used, hidden), jnp.float32))
    stage_ref[...] = jnp.concatenate(parts, axis=0).astype(stage_ref.dtype).reshape(stage_ref.shape)
    for i in range(ranks):
        piece_refs[i][...] = stage_ref[rank_ref[0] ^ i]


def edges_kernel(members, table_ref, w_one_ref, *refs):
    d_one_refs, d_mixed_refs, (head_ref, tail_ref) = refs[:members], refs[members : 2 * members], refs[2 * members :]
    ext = table_ref.shape[0]
    rows = jnp.concatenate([table_ref[:HALO, :], table_ref[ext - HALO :, :]], axis=0)
    for m in range(members):
        d_mixed = nn_dot(w_one_ref[...], d_one_refs[m][...]).astype(jnp.bfloat16)
        d_mixed_refs[m][...] = d_mixed
        grads = nt_dot(rows, d_mixed).astype(jnp.bfloat16)
        head_ref[m] = grads[:HALO]
        tail_ref[m] = grads[HALO:]


def sum_kernel(count, *refs):
    for i in range(count):
        total = refs[i][...].astype(jnp.float32) + refs[count + i][...].astype(jnp.float32)
        refs[2 * count + i][...] = total.astype(refs[i].dtype)


def unpack_kernel(scale, rank_ref, *refs):
    *refs, stage_ref = refs
    ranks = stage_ref.shape[0]
    one_ref, b_one_ref, two_ref, b_two_ref, three_ref, tally_ref = refs[ranks:]
    for i in range(ranks):
        stage_ref[rank_ref[0] ^ i] = refs[i][...]
    width, hidden = one_ref.shape
    sums = stage_ref[...].reshape(-1, hidden).astype(jnp.float32)
    half, channels = hidden // 2, three_ref.shape[1]
    one_ref[...] = sums[:width]
    two_ref[...] = sums[width : width + hidden]
    base = width + hidden
    three_ref[:half] = sums[base : base + half, :channels]
    three_ref[half:] = sums[base : base + half, channels:]
    last = sums[base + half : base + half + 8]
    b_one_ref[...] = last[0:1]
    b_two_ref[...] = last[1:2]
    tally_ref[...] = (last[2:3] + last[3:4])[:, : tally_ref.shape[1]] * scale


def own_kernel(table_ref, *refs):
    *d_mixed_refs, own_ref = refs
    members, nodes, _ = own_ref.shape
    for m in range(members):
        own_ref[m] = nt_dot(table_ref[HALO : HALO + nodes, :], d_mixed_refs[m][...])


def finish_kernel(own_ref, from_next_ref, from_prev_ref, out_ref):
    nodes = own_ref.shape[1]
    from_next, from_prev = from_next_ref[...].astype(jnp.float32), from_prev_ref[...].astype(jnp.float32)
    out_ref[:, :HALO] = (own_ref[:, :HALO] + from_prev).astype(jnp.bfloat16)
    out_ref[:, HALO : nodes - HALO] = own_ref[:, HALO : nodes - HALO].astype(jnp.bfloat16)
    out_ref[:, nodes - HALO :] = (own_ref[:, nodes - HALO :] + from_next).astype(jnp.bfloat16)


def shifted(shard, axis, by):
    length = lax.axis_size(axis)
    return lax.ppermute(shard, axis, [(i, (i + by) % length) for i in range(length)])


def swapped(block, axis, by):
    return lax.ppermute(block, axis, [(i, i ^ by) for i in range(lax.axis_size(axis))])


def per_device(latent, neighbours, weights, targets, counts, w_one, b_one, w_two, b_two, w_three):
    members, nodes, width = latent.shape
    slots, channels = targets.shape
    hidden = w_one.shape[1]
    ext = nodes + 2 * HALO
    region, regions = lax.axis_index("space"), lax.axis_size("space")
    rank, ranks = lax.axis_index("member"), lax.axis_size("member")
    share = slots // ranks
    bf16, f32 = jnp.bfloat16, jnp.float32
    shape = jax.ShapeDtypeStruct
    each = range(members)

    edge = shape((HALO, width), bf16)
    last, first, latent = kernel_call(
        rims_kernel, (edge, edge, shape(latent.shape, bf16)), flops=4 << 30, moved=3 * MIB, operands=1
    )(latent)
    before, after = [shifted(last, "space", 1)], [shifted(first, "space", -1)]
    rank_at = rank[None].astype(jnp.int32)
    region_at = region[None].astype(jnp.int32)

    table, part, *rims = kernel_call(
        table_kernel,
        (shape((ext, slots), bf16), shape((width, slots), f32)) + (edge,) * (2 * members - 2),
        flops=2 * width * nodes * slots,
        moved=12 * MIB,
        smem=3,
        operands=6,
    )(region_at, rank_at, counts, neighbours, weights, latent)
    before += [shifted(block, "space", 1) for block in rims[::2]]
    after += [shifted(block, "space", -1) for block in rims[1::2]]

    saved_shape = shape((hidden, slots), bf16)
    mixed_shape = shape((width, slots), bf16)
    decoded_shape = shape((channels, slots), bf16)
    dense = width * hidden + hidden * hidden + hidden * channels
    saved, decoded, beside, across = [], [], [], []
    for m in each:
        *kept, block = kernel_call(
            lambda *refs: forward_kernel(m, *refs),
            (mixed_shape,) + (saved_shape,) * 4 + (decoded_shape,),
            flops=2 * slots * ((ext if m else 2 * HALO) * width + dense),
            moved=8 * MIB,
            operands=9,
        )(latent if m else part, table, before[m], after[m], w_one, b_one[None], w_two, b_two[None], w_three)
        saved.append(kept)
        decoded.append(block)
        blocks, bit = {0: block}, 2
        while bit < ranks:
            blocks.update({i ^ bit: swapped(blocks[i], "member", bit) for i in sorted(blocks)})
            bit = 2 * bit
        across.append([blocks[i] for i in sorted(blocks) if i])
        beside.append(swapped(block, "member", 1))

    def scored(others, carried, first=False, last=False):
        operands = (region_at, counts, *decoded, *others, *carried)
        return kernel_call(
            lambda *refs: score_kernel(members, len(others), members * ranks, first, last, *refs),
            (shape((channels, slots), bf16 if last else f32),) * members + (shape((1, LANE), f32),),
            flops=4 * MIB,
            moved=2 * MIB,
            smem=2,
            operands=len(operands),
        )(*operands)

    carried = scored(beside + [block for blocks in across[:-1] for block in blocks], [targets], first=True)
    across[-1], carried = lax.optimization_barrier((across[-1], carried))
    others = [*across[-1]] + [swapped(block, "member", 1) for blocks in across for block in blocks]
    *grads, score = scored(others, carried, last=True)

    rows = -(-(width + hidden + hidden // 2 + 4) // (16 * ranks)) * 16
    piece = shape((rows, hidden), bf16)
    operands = [region_at, rank_at, w_two, w_three, score]
    for m in each:
        operands += [*saved[m], grads[m]]
    out = kernel_call(
        lambda *refs: backward_kernel(members, ranks, *refs),
        (saved_shape,) * members + (piece,) * ranks,
        flops=4 * members * slots * dense,
        moved=10 * MIB,
        scratch=(pltpu.VMEM((members, hidden, slots), bf16), pltpu.VMEM((ranks, rows, hidden), bf16)),
        smem=2,
        operands=len(operands),
    )(*operands)
    d_one, pieces = out[:members], out[members:]

    def summed(ones, others):
        return kernel_call(
            lambda *refs: sum_kernel(len(ones), *refs), (piece,) * len(ones), flops=MIB, moved=MIB, operands=2 * len(ones)
        )(*ones, *others)

    rims = shape((members, HALO, width), bf16)
    *d_mixed, head, tail = kernel_call(
        lambda *refs: edges_kernel(members, *refs),
        (mixed_shape,) * members + (rims, rims),
        flops=2 * members * slots * width * (hidden + 2 * HALO),
        moved=6 * MIB,
        operands=2 + members,
    )(table, w_one, *d_one)

    bit = 1
    while bit < ranks:
        received = [swapped(sent, "member", bit) for sent in pieces[1::2]]
        if bit == 1:
            received, head, tail = lax.optimization_barrier((received, head, tail))
        pieces = summed(pieces[::2], received)
        bit = 2 * bit
    own = kernel_call(
        own_kernel,
        shape((members, nodes, width), f32),
        flops=2 * members * nodes * width * slots,
        moved=6 * MIB,
        operands=1 + members,
    )(table, *d_mixed)
    from_next = shifted(head, "space", -1)
    (total,) = pieces
    step = 1
    while step < regions:
        (total,) = summed([total], [swapped(total, "space", step)])
        step = 2 * step
        if step == regions // 2:
            total, from_next, own, tail = lax.optimization_barrier((total, from_next, own, tail))
            from_prev = shifted(tail, "space", 1)
    totals = {0: total}
    bit = 2
    while bit < ranks:
        totals.update({i ^ bit: swapped(totals[i], "member", bit) for i in sorted(totals)})
        bit = 2 * bit
    totals.update({i ^ 1: swapped(block, "member", 1) for i, block in totals.items()})
    latent_grad = kernel_call(
        finish_kernel,
        shape((members, nodes, width), bf16),
        flops=MIB,
        moved=3 * MIB,
        operands=3,
    )(own, from_next, from_prev)
    totals = [totals[i] for i in range(ranks)]
    totals, latent_grad = lax.optimization_barrier((totals, latent_grad))
    row = shape((1, hidden), f32)
    g_one, g_bone, g_two, g_btwo, g_three, tally = kernel_call(
        lambda *refs: unpack_kernel(1.0 / (OBS_MEAN * members * ranks), *refs),
        (shape((width, hidden), f32), row, shape((hidden, hidden), f32), row, shape((hidden, channels), f32),
         shape((1, regions), f32)),
        flops=MIB,
        moved=2 * MIB,
        scratch=(pltpu.VMEM((ranks, rows, hidden), bf16),),
        smem=1,
        operands=1 + ranks,
    )(rank_at, *totals)
    return (tally[0], latent_grad, g_one, g_bone[0], g_two, g_btwo[0], g_three)


def solution(mesh):
    in_specs = (
        P("member", ("groups", "space"), None),
        P(None, ("groups", "space")),
        P(None, ("groups", "space")),
        P(("groups", "space"), None),
        P("groups"),
        P(),
        P(),
        P(),
        P(),
        P(),
    )
    out_specs = (
        P("groups"),
        P("member", ("groups", "space"), None),
        P("groups", None),
        P("groups"),
        P("groups", None),
        P("groups"),
        P("groups", None),
    )
    return jax.shard_map(
        per_device, mesh=mesh, in_specs=in_specs, out_specs=out_specs, check_vma=False
    )
```

```python
import jax
import jax.numpy as jnp
from jax import lax
from jax.experimental import pallas as pl
from jax.experimental.pallas import tpu as pltpu
from jax.sharding import PartitionSpec as P

K = 4
OBS_MEAN = 512
HALO = 256
EPSILON = 1e-05
BLOCK = 256
LANE = 128
CHUNK = 512
MIB = 1 << 20


def split(total, step):
    return [(start, min(step, total - start)) for start in range(0, total, step)]


def nt_dot(left, right):
    return lax.dot_general(
        left, right, (((1,), (1,)), ((), ())), preferred_element_type=jnp.float32
    )


def nn_dot(left, right):
    return jnp.dot(left, right, preferred_element_type=jnp.float32)


def kernel_call(body, out_shape, flops, moved, scratch=(), smem=0, operands=0):
    vmem = pl.BlockSpec(memory_space=pltpu.VMEM)
    specs = [pl.BlockSpec(memory_space=pltpu.SMEM)] * smem
    return pl.pallas_call(
        body,
        out_shape=out_shape,
        in_specs=specs + [vmem] * (operands - len(specs)),
        out_specs=jax.tree.map(lambda _: vmem, out_shape),
        scratch_shapes=list(scratch),
        compiler_params=pltpu.CompilerParams(vmem_limit_bytes=24 * MIB),
        cost_estimate=pl.CostEstimate(flops=flops, bytes_accessed=moved, transcendentals=0),
    )


def cut_rims(latent_ref, member, last_ref, first_ref):
    nodes = latent_ref.shape[1]
    last_ref[...] = latent_ref[member, nodes - HALO :]
    first_ref[...] = latent_ref[member, :HALO]


def rims_kernel(latent_ref, last_ref, first_ref, copy_ref):
    cut_rims(latent_ref, 0, last_ref, first_ref)
    copy_ref[...] = latent_ref[...]


def table_kernel(region_ref, rank_ref, counts_ref, nbr_ref, weight_ref, latent_ref, table_ref, part_ref, *rim_refs):
    members, nodes, _ = latent_ref.shape
    for m in range(1, members):
        cut_rims(latent_ref, m, *rim_refs[2 * m - 2 : 2 * m])
    ext, slots = table_ref.shape
    live = lax.broadcasted_iota(jnp.int32, (1, slots), 1) < counts_ref[region_ref[0]]
    nbr = [nbr_ref[k : k + 1, :] for k in range(K)]
    own = [jnp.where(live, weight_ref[k : k + 1, :], 0.0) for k in range(K)]
    joint = []
    for k in range(K):
        total = own[k]
        for j in range(K):
            if j != k:
                total = total + jnp.where(nbr[j] == nbr[k], own[j], 0.0)
        joint.append(total)
    groups = BLOCK // 16
    rows = (
        lax.broadcasted_iota(jnp.int32, (groups, 16, LANE), 0) * 16
        + lax.broadcasted_iota(jnp.int32, (groups, 16, LANE), 1)
    ).astype(jnp.float32).astype(jnp.bfloat16)
    turned = latent_ref[0].T
    for start, length in split(slots, CHUNK):
        for lo, size in split(length, LANE):
            lanes = slice(start + lo, start + lo + size)
            wide = [jnp.broadcast_to(joint[k][:, lanes], (16, size)).astype(jnp.bfloat16) for k in range(K)]
            for b in range(ext // BLOCK):
                tile = jnp.zeros((groups, 16, size), jnp.bfloat16)
                for k in range(K):
                    near = (nbr[k][:, lanes] - b * BLOCK).astype(jnp.float32)
                    near = jnp.broadcast_to(near, (16, size)).astype(jnp.bfloat16)
                    tile = jnp.where(rows[:, :, :size] == near[None], wide[k][None], tile)
                table_ref[b * BLOCK : (b + 1) * BLOCK, lanes] = tile.reshape(BLOCK, size)
        lanes = slice(start, start + length)
        part_ref[:, lanes] = nn_dot(turned, table_ref[HALO : HALO + nodes, lanes])


def column(ref):
    height = ref.shape[1]
    return jnp.broadcast_to(ref[...], (LANE, height)).T


def forward_kernel(
    member, own_ref, table_ref, before_ref, after_ref, w_one_ref, b_one_ref, w_two_ref, b_two_ref, w_three_ref,
    mixed_ref, act_one_ref, slope_one_ref, act_two_ref, slope_two_ref, decoded_ref,
):
    ext, slots = table_ref.shape
    w_one, w_two, w_three = w_one_ref[...].T * 0.5, w_two_ref[...].T * 0.5, w_three_ref[...].T
    b_one, b_two = column(b_one_ref) * 0.5, column(b_two_ref) * 0.5

    def layer(weight, bias, values, size):
        half = nn_dot(weight, values) + jnp.concatenate([bias] * (size // LANE), axis=1)
        gate = 1.0 + jnp.tanh(half)
        act = half * gate
        return act.astype(jnp.bfloat16), (gate + act * (2.0 - gate)).astype(jnp.bfloat16)

    if member:
        nodes = jnp.concatenate([before_ref[...].T, own_ref[member].T, after_ref[...].T], axis=1)
    else:
        nodes = jnp.concatenate([before_ref[...].T, after_ref[...].T], axis=1)
    for lo, size in split(slots, CHUNK):
        lanes = slice(lo, lo + size)
        if member:
            mixed = nn_dot(nodes, table_ref[:, lanes])
        else:
            rims = jnp.concatenate([table_ref[:HALO, lanes], table_ref[ext - HALO :, lanes]], axis=0)
            mixed = own_ref[:, lanes] + nn_dot(nodes, rims)
        mixed = mixed.astype(jnp.bfloat16)
        mixed_ref[:, lanes] = mixed
        act_one, slope_one_ref[:, lanes] = layer(w_one, b_one, mixed, size)
        act_one_ref[:, lanes] = act_one
        act_two, slope_two_ref[:, lanes] = layer(w_two, b_two, act_one, size)
        act_two_ref[:, lanes] = act_two
        decoded_ref[:, lanes] = nn_dot(w_three, act_two).astype(jnp.bfloat16)


def score_kernel(mine, others, count, first, last, region_ref, counts_ref, *refs):
    own_refs, refs = refs[:mine], refs[mine:]
    other_refs, refs = refs[:others], refs[others:]
    if first:
        target_ref, refs = refs[0], refs[1:]
        old_refs, old_score = None, 0.0
    else:
        old_refs, old_score, refs = refs[:mine], refs[mine][...], refs[mine + 1 :]
    grad_refs, score_ref = refs[:mine], refs[mine]
    channels, slots = own_refs[0].shape
    inner = [(i, j) for i in range(mine) for j in range(i + 1, mine)] if first else []
    outer = [(i, mine + j) for i in range(mine) for j in range(others)]
    pairs = inner + outer
    shares = [1.0 / (count - 1)] * len(inner) + [0.5 / (count - 1)] * len(outer)
    live_count = counts_ref[region_ref[0]]

    def one_tile(at, total):
        start = pl.multiple_of(at * LANE, LANE)
        lanes = pl.ds(start, LANE)
        if first:
            turned = target_ref[lanes, :].astype(jnp.float32).T

        def rows_of(c):
            return [ref[c : c + 16, lanes].astype(jnp.float32) for ref in (*own_refs, *other_refs)]

        def fold(square):
            return square[:8] + square[8:]

        to_target = [jnp.zeros((8, LANE), jnp.float32)] * (mine if first else 0)
        apart = [jnp.zeros((8, LANE), jnp.float32)] * len(pairs)
        for c in range(0, channels, 16):
            values = rows_of(c)
            for i in range(len(to_target)):
                to_target[i] = to_target[i] + fold((values[i] - turned[c : c + 16]) ** 2)
            for p, (i, j) in enumerate(pairs):
                apart[p] = apart[p] + fold((values[i] - values[j]) ** 2)
        live = start + lax.broadcasted_iota(jnp.int32, (1, LANE), 1) < live_count
        score = jnp.zeros((1, LANE), jnp.float32)

        def inverse(square):
            squared = jnp.sum(square, axis=0, keepdims=True) + EPSILON
            inv = lax.rsqrt(squared)
            return squared * inv, inv

        inv_target, inv_pair = [], []
        for square in to_target:
            dist, inv = inverse(square)
            score = score + dist
            inv_target.append(jnp.broadcast_to(inv, (8, LANE)))
        for square, share in zip(apart, shares):
            dist, inv = inverse(square)
            score = score - dist * share
            inv_pair.append(jnp.broadcast_to(inv * (1.0 / (count - 1)), (8, LANE)))
        for c in range(0, channels, 16):
            values = rows_of(c)
            halves = []
            for h in (0, 8):
                near = [v[h : h + 8] for v in values]
                rows = slice(c + h, c + h + 8)
                if first:
                    grads = [(near[i] - turned[rows]) * inv_target[i] for i in range(mine)]
                else:
                    grads = [old_refs[i][rows, lanes] for i in range(mine)]
                for p, (i, j) in enumerate(pairs):
                    term = (near[i] - near[j]) * inv_pair[p]
                    grads[i] = grads[i] - term
                    if j < mine:
                        grads[j] = grads[j] + term
                halves.append(grads)
            for i in range(mine):
                grad = jnp.concatenate([halves[0][i], halves[1][i]], axis=0)
                if last:
                    grad = jnp.where(live, grad, 0.0)
                grad_refs[i][c : c + 16, lanes] = grad.astype(grad_refs[i].dtype)
        return total + jnp.where(live, score, 0.0)

    score_ref[...] = old_score + lax.fori_loop(0, slots // LANE, one_tile, jnp.zeros((1, LANE), jnp.float32))


def backward_kernel(members, ranks, region_ref, rank_ref, w_two_ref, w_three_ref, score_ref, *refs):
    saved = [refs[6 * m : 6 * (m + 1)] for m in range(members)]
    refs = refs[6 * members :]
    d_one_refs, piece_refs, (d_two_ref, stage_ref) = refs[:members], refs[members:-2], refs[-2:]
    w_two, w_three = w_two_ref[...] * 0.5, w_three_ref[...] * 0.5
    hidden, slots = saved[0][1].shape
    bias_one = jnp.zeros((hidden, LANE), jnp.float32)
    bias_two = jnp.zeros((hidden, LANE), jnp.float32)
    g_one, g_two, g_three = 0.0, 0.0, 0.0

    def lane_sum(values):
        return sum(values[:, lo : lo + LANE] for lo, _ in split(values.shape[1], LANE))

    for m in range(members):
        mixed_ref, act_one_ref, slope_one_ref, act_two_ref, slope_two_ref, d_dec_ref = saved[m]
        for lo, size in split(slots, CHUNK):
            lanes = slice(lo, lo + size)
            back = nn_dot(w_three, d_dec_ref[:, lanes]) * slope_two_ref[:, lanes].astype(jnp.float32)
            bias_two = bias_two + lane_sum(back)
            d_two = back.astype(jnp.bfloat16)
            d_two_ref[m, :, lanes] = d_two
            back = nn_dot(w_two, d_two) * slope_one_ref[:, lanes].astype(jnp.float32)
            bias_one = bias_one + lane_sum(back)
            d_one_refs[m][:, lanes] = back.astype(jnp.bfloat16)
        g_three = g_three + nt_dot(act_two_ref[...], d_dec_ref[...])
        g_two = g_two + nt_dot(act_one_ref[...], d_two_ref[m])
        g_one = g_one + nt_dot(mixed_ref[...], d_one_refs[m][...])
    half = hidden // 2
    region = lax.broadcasted_iota(jnp.int32, (1, hidden), 1) == region_ref[0]
    tally = jnp.where(region, jnp.sum(score_ref[...]), 0.0)
    high = tally.astype(jnp.bfloat16).astype(jnp.float32)
    parts = [
        g_one,
        g_two,
        jnp.concatenate([g_three[:half], g_three[half:]], axis=1),
        jnp.sum(bias_one.T, axis=0, keepdims=True),
        jnp.sum(bias_two.T, axis=0, keepdims=True),
        high,
        tally - high,
    ]
    used = sum(part.shape[0] for part in parts)
    parts.append(jnp.zeros((ranks * stage_ref.shape[1] - used, hidden), jnp.float32))
    stage_ref[...] = jnp.concatenate(parts, axis=0).astype(stage_ref.dtype).reshape(stage_ref.shape)
    for i in range(ranks):
        piece_refs[i][...] = stage_ref[rank_ref[0] ^ i]


def edges_kernel(members, table_ref, w_one_ref, *refs):
    d_one_refs, d_mixed_refs, (head_ref, *tail_refs) = refs[:members], refs[members : 2 * members], refs[2 * members :]
    ext = table_ref.shape[0]
    rows = jnp.concatenate([table_ref[:HALO, :], table_ref[ext - HALO :, :]], axis=0)
    for m in range(members):
        d_mixed = nn_dot(w_one_ref[...], d_one_refs[m][...]).astype(jnp.bfloat16)
        d_mixed_refs[m][...] = d_mixed
        grads = nt_dot(rows, d_mixed).astype(jnp.bfloat16)
        head_ref[m] = grads[:HALO]
        tail_refs[m][...] = grads[HALO:]


def sum_kernel(count, *refs):
    for i in range(count):
        total = refs[i][...].astype(jnp.float32) + refs[count + i][...].astype(jnp.float32)
        refs[2 * count + i][...] = total.astype(refs[i].dtype)


def unpack_kernel(scale, rank_ref, *refs):
    *refs, stage_ref = refs
    ranks = stage_ref.shape[0]
    one_ref, b_one_ref, two_ref, b_two_ref, three_ref, tally_ref = refs[ranks:]
    for i in range(ranks):
        stage_ref[rank_ref[0] ^ i] = refs[i][...]
    width, hidden = one_ref.shape
    sums = stage_ref[...].reshape(-1, hidden).astype(jnp.float32)
    half, channels = hidden // 2, three_ref.shape[1]
    one_ref[...] = sums[:width]
    two_ref[...] = sums[width : width + hidden]
    base = width + hidden
    three_ref[:half] = sums[base : base + half, :channels]
    three_ref[half:] = sums[base : base + half, channels:]
    last = sums[base + half : base + half + 8]
    b_one_ref[...] = last[0:1]
    b_two_ref[...] = last[1:2]
    tally_ref[...] = (last[2:3] + last[3:4])[:, : tally_ref.shape[1]] * scale


def own_kernel(table_ref, *refs):
    *d_mixed_refs, own_ref = refs
    members, nodes, _ = own_ref.shape
    for m in range(members):
        own_ref[m] = nt_dot(table_ref[HALO : HALO + nodes, :], d_mixed_refs[m][...])


def finish_kernel(own_ref, from_next_ref, *refs):
    *from_prev_refs, out_ref = refs
    members, nodes, _ = own_ref.shape
    for m in range(members):
        from_next, from_prev = from_next_ref[m].astype(jnp.float32), from_prev_refs[m][...].astype(jnp.float32)
        out_ref[m, :HALO] = (own_ref[m, :HALO] + from_prev).astype(jnp.bfloat16)
        out_ref[m, HALO : nodes - HALO] = own_ref[m, HALO : nodes - HALO].astype(jnp.bfloat16)
        out_ref[m, nodes - HALO :] = (own_ref[m, nodes - HALO :] + from_next).astype(jnp.bfloat16)


def shifted(shard, axis, by):
    length = lax.axis_size(axis)
    return lax.ppermute(shard, axis, [(i, (i + by) % length) for i in range(length)])


def swapped(block, axis, by):
    return lax.ppermute(block, axis, [(i, i ^ by) for i in range(lax.axis_size(axis))])


def per_device(latent, neighbours, weights, targets, counts, w_one, b_one, w_two, b_two, w_three):
    members, nodes, width = latent.shape
    slots, channels = targets.shape
    hidden = w_one.shape[1]
    ext = nodes + 2 * HALO
    region, regions = lax.axis_index("space"), lax.axis_size("space")
    rank, ranks = lax.axis_index("member"), lax.axis_size("member")
    share = slots // ranks
    bf16, f32 = jnp.bfloat16, jnp.float32
    shape = jax.ShapeDtypeStruct
    each = range(members)

    edge = shape((HALO, width), bf16)
    last, first, latent = kernel_call(
        rims_kernel, (edge, edge, shape(latent.shape, bf16)), flops=4 << 30, moved=3 * MIB, operands=1
    )(latent)
    before, after = [shifted(last, "space", 1)], [shifted(first, "space", -1)]
    rank_at = rank[None].astype(jnp.int32)
    region_at = region[None].astype(jnp.int32)

    table, part, *rims = kernel_call(
        table_kernel,
        (shape((ext, slots), bf16), shape((width, slots), f32)) + (edge,) * (2 * members - 2),
        flops=2 * width * nodes * slots,
        moved=12 * MIB,
        smem=3,
        operands=6,
    )(region_at, rank_at, counts, neighbours, weights, latent)
    before += [shifted(block, "space", 1) for block in rims[::2]]
    after += [shifted(block, "space", -1) for block in rims[1::2]]

    saved_shape = shape((hidden, slots), bf16)
    mixed_shape = shape((width, slots), bf16)
    decoded_shape = shape((channels, slots), bf16)
    dense = width * hidden + hidden * hidden + hidden * channels
    saved, decoded, beside, across = [], [], [], []
    for m in each:
        *kept, block = kernel_call(
            lambda *refs: forward_kernel(m, *refs),
            (mixed_shape,) + (saved_shape,) * 4 + (decoded_shape,),
            flops=2 * slots * ((ext if m else 2 * HALO) * width + dense),
            moved=8 * MIB,
            operands=9,
        )(latent if m else part, table, before[m], after[m], w_one, b_one[None], w_two, b_two[None], w_three)
        saved.append(kept)
        decoded.append(block)
        blocks, bit = {0: block}, 2
        while bit < ranks:
            blocks.update({i ^ bit: swapped(blocks[i], "member", bit) for i in sorted(blocks)})
            bit = 2 * bit
        across.append([blocks[i] for i in sorted(blocks) if i])
        beside.append(swapped(block, "member", 1))

    def scored(others, carried, first=False, last=False):
        operands = (region_at, counts, *decoded, *others, *carried)
        return kernel_call(
            lambda *refs: score_kernel(members, len(others), members * ranks, first, last, *refs),
            (shape((channels, slots), bf16 if last else f32),) * members + (shape((1, LANE), f32),),
            flops=4 * MIB,
            moved=2 * MIB,
            smem=2,
            operands=len(operands),
        )(*operands)

    carried = scored(beside + [block for blocks in across[:-1] for block in blocks], [targets], first=True)
    across[-1], carried = lax.optimization_barrier((across[-1], carried))
    others = [*across[-1]] + [swapped(block, "member", 1) for blocks in across for block in blocks]
    *grads, score = scored(others, carried, last=True)

    rows = -(-(width + hidden + hidden // 2 + 4) // (16 * ranks)) * 16
    piece = shape((rows, hidden), bf16)
    operands = [region_at, rank_at, w_two, w_three, score]
    for m in each:
        operands += [*saved[m], grads[m]]
    out = kernel_call(
        lambda *refs: backward_kernel(members, ranks, *refs),
        (saved_shape,) * members + (piece,) * ranks,
        flops=4 * members * slots * dense,
        moved=10 * MIB,
        scratch=(pltpu.VMEM((members, hidden, slots), bf16), pltpu.VMEM((ranks, rows, hidden), bf16)),
        smem=2,
        operands=len(operands),
    )(*operands)
    d_one, pieces = out[:members], out[members:]

    def summed(ones, others):
        return kernel_call(
            lambda *refs: sum_kernel(len(ones), *refs), (piece,) * len(ones), flops=MIB, moved=MIB, operands=2 * len(ones)
        )(*ones, *others)

    rims = shape((members, HALO, width), bf16)
    out = kernel_call(
        lambda *refs: edges_kernel(members, *refs),
        (mixed_shape,) * members + (rims,) + (edge,) * members,
        flops=2 * members * slots * width * (hidden + 2 * HALO),
        moved=6 * MIB,
        operands=2 + members,
    )(table, w_one, *d_one)
    d_mixed, head, tails = out[:members], out[members], out[members + 1 :]

    bit = 1
    while bit < ranks:
        received = [swapped(sent, "member", bit) for sent in pieces[1::2]]
        if bit == 1:
            received, head, tails = lax.optimization_barrier((received, head, tails))
        pieces = summed(pieces[::2], received)
        bit = 2 * bit
    own = kernel_call(
        own_kernel,
        shape((members, nodes, width), f32),
        flops=2 * members * nodes * width * slots,
        moved=6 * MIB,
        operands=1 + members,
    )(table, *d_mixed)
    from_next = shifted(head, "space", -1)
    from_prev = [shifted(tail, "space", 1) for tail in tails[:-1]]
    (total,) = pieces
    step = 1
    while step < regions:
        if 2 * step == regions:
            total, from_next, from_prev, own = lax.optimization_barrier((total, from_next, from_prev, own))
        (total,) = summed([total], [swapped(total, "space", step)])
        step = 2 * step
    total, last_tail = lax.optimization_barrier((total, tails[-1]))
    from_prev = [*from_prev, shifted(last_tail, "space", 1)]
    totals = {0: total}
    bit = 2
    while bit < ranks:
        totals.update({i ^ bit: swapped(totals[i], "member", bit) for i in sorted(totals)})
        bit = 2 * bit
    totals.update({i ^ 1: swapped(block, "member", 1) for i, block in totals.items()})
    latent_grad = kernel_call(
        finish_kernel,
        shape((members, nodes, width), bf16),
        flops=MIB,
        moved=3 * MIB,
        operands=2 + members,
    )(own, from_next, *from_prev)
    totals = [totals[i] for i in range(ranks)]
    totals, latent_grad = lax.optimization_barrier((totals, latent_grad))
    row = shape((1, hidden), f32)
    g_one, g_bone, g_two, g_btwo, g_three, tally = kernel_call(
        lambda *refs: unpack_kernel(1.0 / (OBS_MEAN * members * ranks), *refs),
        (shape((width, hidden), f32), row, shape((hidden, hidden), f32), row, shape((hidden, channels), f32),
         shape((1, regions), f32)),
        flops=MIB,
        moved=2 * MIB,
        scratch=(pltpu.VMEM((ranks, rows, hidden), bf16),),
        smem=1,
        operands=1 + ranks,
    )(rank_at, *totals)
    return (tally[0], latent_grad, g_one, g_bone[0], g_two, g_btwo[0], g_three)


def solution(mesh):
    in_specs = (
        P("member", ("groups", "space"), None),
        P(None, ("groups", "space")),
        P(None, ("groups", "space")),
        P(("groups", "space"), None),
        P("groups"),
        P(),
        P(),
        P(),
        P(),
        P(),
    )
    out_specs = (
        P("groups"),
        P("member", ("groups", "space"), None),
        P("groups", None),
        P("groups"),
        P("groups", None),
        P("groups"),
        P("groups", None),
    )
    return jax.shard_map(
        per_device, mesh=mesh, in_specs=in_specs, out_specs=out_specs, check_vma=False
    )
```

```python
import jax
import jax.numpy as jnp
from jax import lax
from jax.experimental import pallas as pl
from jax.experimental.pallas import tpu as pltpu
from jax.sharding import PartitionSpec as P

K = 4
OBS_MEAN = 512
HALO = 256
EPSILON = 1e-05
BLOCK = 256
LANE = 128
CHUNK = 512
MIB = 1 << 20


def split(total, step):
    return [(start, min(step, total - start)) for start in range(0, total, step)]


def nt_dot(left, right):
    return lax.dot_general(
        left, right, (((1,), (1,)), ((), ())), preferred_element_type=jnp.float32
    )


def nn_dot(left, right):
    return jnp.dot(left, right, preferred_element_type=jnp.float32)


def kernel_call(body, out_shape, flops, moved, scratch=(), smem=0, operands=0):
    vmem = pl.BlockSpec(memory_space=pltpu.VMEM)
    specs = [pl.BlockSpec(memory_space=pltpu.SMEM)] * smem
    return pl.pallas_call(
        body,
        out_shape=out_shape,
        in_specs=specs + [vmem] * (operands - len(specs)),
        out_specs=jax.tree.map(lambda _: vmem, out_shape),
        scratch_shapes=list(scratch),
        compiler_params=pltpu.CompilerParams(vmem_limit_bytes=24 * MIB),
        cost_estimate=pl.CostEstimate(flops=flops, bytes_accessed=moved, transcendentals=0),
    )


def rim_starts(region_ref, length):
    odd = lax.rem(region_ref[0], 2)
    far = length - HALO
    return [pl.ds(pl.multiple_of(start, HALO), HALO) for start in ((1 - odd) * far, odd * far)]


def cut_rims(region_ref, latent_ref, member, *rim_refs):
    for ref, rows in zip(rim_refs, rim_starts(region_ref, latent_ref.shape[1])):
        ref[...] = latent_ref[member, rows]


def rims_kernel(region_ref, latent_ref, one_ref, other_ref, copy_ref):
    cut_rims(region_ref, latent_ref, 0, one_ref, other_ref)
    copy_ref[...] = latent_ref[...]


def table_kernel(region_ref, rank_ref, counts_ref, nbr_ref, weight_ref, latent_ref, table_ref, part_ref, *rim_refs):
    members, nodes, _ = latent_ref.shape
    for m in range(1, members):
        cut_rims(region_ref, latent_ref, m, *rim_refs[2 * m - 2 : 2 * m])
    ext, slots = table_ref.shape
    live = lax.broadcasted_iota(jnp.int32, (1, slots), 1) < counts_ref[region_ref[0]]
    nbr = [nbr_ref[k : k + 1, :] for k in range(K)]
    own = [jnp.where(live, weight_ref[k : k + 1, :], 0.0) for k in range(K)]
    joint = []
    for k in range(K):
        total = own[k]
        for j in range(K):
            if j != k:
                total = total + jnp.where(nbr[j] == nbr[k], own[j], 0.0)
        joint.append(total)
    groups = BLOCK // 16
    rows = (
        lax.broadcasted_iota(jnp.int32, (groups, 16, LANE), 0) * 16
        + lax.broadcasted_iota(jnp.int32, (groups, 16, LANE), 1)
    ).astype(jnp.float32).astype(jnp.bfloat16)
    turned = latent_ref[0].T
    for start, length in split(slots, CHUNK):
        for lo, size in split(length, LANE):
            lanes = slice(start + lo, start + lo + size)
            wide = [jnp.broadcast_to(joint[k][:, lanes], (16, size)).astype(jnp.bfloat16) for k in range(K)]
            for b in range(ext // BLOCK):
                tile = jnp.zeros((groups, 16, size), jnp.bfloat16)
                for k in range(K):
                    near = (nbr[k][:, lanes] - b * BLOCK).astype(jnp.float32)
                    near = jnp.broadcast_to(near, (16, size)).astype(jnp.bfloat16)
                    tile = jnp.where(rows[:, :, :size] == near[None], wide[k][None], tile)
                table_ref[b * BLOCK : (b + 1) * BLOCK, lanes] = tile.reshape(BLOCK, size)
        lanes = slice(start, start + length)
        part_ref[:, lanes] = nn_dot(turned, table_ref[HALO : HALO + nodes, lanes])


def column(ref):
    height = ref.shape[1]
    return jnp.broadcast_to(ref[...], (LANE, height)).T


def forward_kernel(
    member, region_ref, own_ref, table_ref, one_ref, other_ref, w_one_ref, b_one_ref, w_two_ref, b_two_ref, w_three_ref,
    mixed_ref, act_one_ref, slope_one_ref, act_two_ref, slope_two_ref, decoded_ref,
):
    ext, slots = table_ref.shape
    w_one, w_two, w_three = w_one_ref[...].T * 0.5, w_two_ref[...].T * 0.5, w_three_ref[...].T
    b_one, b_two = column(b_one_ref) * 0.5, column(b_two_ref) * 0.5

    def layer(weight, bias, values, size):
        half = nn_dot(weight, values) + jnp.concatenate([bias] * (size // LANE), axis=1)
        gate = 1.0 + jnp.tanh(half)
        act = half * gate
        return act.astype(jnp.bfloat16), (gate + act * (2.0 - gate)).astype(jnp.bfloat16)

    edges = jnp.concatenate([one_ref[...].T, other_ref[...].T], axis=1)
    own = own_ref[member].T if member else None
    for lo, size in split(slots, CHUNK):
        lanes = slice(lo, lo + size)
        rims = jnp.concatenate([table_ref[rows, lanes] for rows in rim_starts(region_ref, ext)], axis=0)
        share = nn_dot(own, table_ref[HALO : ext - HALO, lanes]) if member else own_ref[:, lanes]
        mixed = share + nn_dot(edges, rims)
        mixed = mixed.astype(jnp.bfloat16)
        mixed_ref[:, lanes] = mixed
        act_one, slope_one_ref[:, lanes] = layer(w_one, b_one, mixed, size)
        act_one_ref[:, lanes] = act_one
        act_two, slope_two_ref[:, lanes] = layer(w_two, b_two, act_one, size)
        act_two_ref[:, lanes] = act_two
        decoded_ref[:, lanes] = nn_dot(w_three, act_two).astype(jnp.bfloat16)


def score_kernel(mine, others, count, first, last, region_ref, counts_ref, *refs):
    own_refs, refs = refs[:mine], refs[mine:]
    other_refs, refs = refs[:others], refs[others:]
    if first:
        target_ref, refs = refs[0], refs[1:]
        old_refs, old_score = None, 0.0
    else:
        old_refs, old_score, refs = refs[:mine], refs[mine][...], refs[mine + 1 :]
    grad_refs, score_ref = refs[:mine], refs[mine]
    channels, slots = own_refs[0].shape
    inner = [(i, j) for i in range(mine) for j in range(i + 1, mine)] if first else []
    outer = [(i, mine + j) for i in range(mine) for j in range(others)]
    pairs = inner + outer
    shares = [1.0 / (count - 1)] * len(inner) + [0.5 / (count - 1)] * len(outer)
    live_count = counts_ref[region_ref[0]]

    def one_tile(at, total):
        start = pl.multiple_of(at * LANE, LANE)
        lanes = pl.ds(start, LANE)
        if first:
            turned = target_ref[lanes, :].astype(jnp.float32).T

        def rows_of(c):
            return [ref[c : c + 16, lanes].astype(jnp.float32) for ref in (*own_refs, *other_refs)]

        def fold(square):
            return square[:8] + square[8:]

        to_target = [jnp.zeros((8, LANE), jnp.float32)] * (mine if first else 0)
        apart = [jnp.zeros((8, LANE), jnp.float32)] * len(pairs)
        for c in range(0, channels, 16):
            values = rows_of(c)
            for i in range(len(to_target)):
                to_target[i] = to_target[i] + fold((values[i] - turned[c : c + 16]) ** 2)
            for p, (i, j) in enumerate(pairs):
                apart[p] = apart[p] + fold((values[i] - values[j]) ** 2)
        live = start + lax.broadcasted_iota(jnp.int32, (1, LANE), 1) < live_count
        score = jnp.zeros((1, LANE), jnp.float32)

        def inverse(square):
            squared = jnp.sum(square, axis=0, keepdims=True) + EPSILON
            inv = lax.rsqrt(squared)
            return squared * inv, inv

        inv_target, inv_pair = [], []
        for square in to_target:
            dist, inv = inverse(square)
            score = score + dist
            inv_target.append(jnp.broadcast_to(inv, (8, LANE)))
        for square, share in zip(apart, shares):
            dist, inv = inverse(square)
            score = score - dist * share
            inv_pair.append(jnp.broadcast_to(inv * (1.0 / (count - 1)), (8, LANE)))
        for c in range(0, channels, 16):
            values = rows_of(c)
            halves = []
            for h in (0, 8):
                near = [v[h : h + 8] for v in values]
                rows = slice(c + h, c + h + 8)
                if first:
                    grads = [(near[i] - turned[rows]) * inv_target[i] for i in range(mine)]
                else:
                    grads = [old_refs[i][rows, lanes] for i in range(mine)]
                for p, (i, j) in enumerate(pairs):
                    term = (near[i] - near[j]) * inv_pair[p]
                    grads[i] = grads[i] - term
                    if j < mine:
                        grads[j] = grads[j] + term
                halves.append(grads)
            for i in range(mine):
                grad = jnp.concatenate([halves[0][i], halves[1][i]], axis=0)
                if last:
                    grad = jnp.where(live, grad, 0.0)
                grad_refs[i][c : c + 16, lanes] = grad.astype(grad_refs[i].dtype)
        return total + jnp.where(live, score, 0.0)

    score_ref[...] = old_score + lax.fori_loop(0, slots // LANE, one_tile, jnp.zeros((1, LANE), jnp.float32))


def backward_kernel(members, ranks, region_ref, rank_ref, w_two_ref, w_three_ref, score_ref, *refs):
    saved = [refs[6 * m : 6 * (m + 1)] for m in range(members)]
    refs = refs[6 * members :]
    d_one_refs, piece_refs, (d_two_ref, stage_ref) = refs[:members], refs[members:-2], refs[-2:]
    w_two, w_three = w_two_ref[...] * 0.5, w_three_ref[...] * 0.5
    hidden, slots = saved[0][1].shape
    bias_one = jnp.zeros((hidden, LANE), jnp.float32)
    bias_two = jnp.zeros((hidden, LANE), jnp.float32)
    g_one, g_two, g_three = 0.0, 0.0, 0.0

    def lane_sum(values):
        return sum(values[:, lo : lo + LANE] for lo, _ in split(values.shape[1], LANE))

    for m in range(members):
        mixed_ref, act_one_ref, slope_one_ref, act_two_ref, slope_two_ref, d_dec_ref = saved[m]
        for lo, size in split(slots, CHUNK):
            lanes = slice(lo, lo + size)
            back = nn_dot(w_three, d_dec_ref[:, lanes]) * slope_two_ref[:, lanes].astype(jnp.float32)
            bias_two = bias_two + lane_sum(back)
            d_two = back.astype(jnp.bfloat16)
            d_two_ref[m, :, lanes] = d_two
            back = nn_dot(w_two, d_two) * slope_one_ref[:, lanes].astype(jnp.float32)
            bias_one = bias_one + lane_sum(back)
            d_one_refs[m][:, lanes] = back.astype(jnp.bfloat16)
        g_three = g_three + nt_dot(act_two_ref[...], d_dec_ref[...])
        g_two = g_two + nt_dot(act_one_ref[...], d_two_ref[m])
        g_one = g_one + nt_dot(mixed_ref[...], d_one_refs[m][...])
    half = hidden // 2
    region = lax.broadcasted_iota(jnp.int32, (1, hidden), 1) == region_ref[0]
    tally = jnp.where(region, jnp.sum(score_ref[...]), 0.0)
    high = tally.astype(jnp.bfloat16).astype(jnp.float32)
    parts = [
        g_one,
        g_two,
        jnp.concatenate([g_three[:half], g_three[half:]], axis=1),
        jnp.sum(bias_one.T, axis=0, keepdims=True),
        jnp.sum(bias_two.T, axis=0, keepdims=True),
        high,
        tally - high,
    ]
    used = sum(part.shape[0] for part in parts)
    parts.append(jnp.zeros((ranks * stage_ref.shape[1] - used, hidden), jnp.float32))
    stage_ref[...] = jnp.concatenate(parts, axis=0).astype(stage_ref.dtype).reshape(stage_ref.shape)
    for i in range(ranks):
        piece_refs[i][...] = stage_ref[rank_ref[0] ^ i]


def edges_kernel(members, region_ref, table_ref, w_one_ref, *refs):
    d_one_refs, refs = refs[:members], refs[members:]
    ext = table_ref.shape[0]
    rows = jnp.concatenate([table_ref[rows, :] for rows in rim_starts(region_ref, ext)], axis=0)
    for m in range(members):
        d_mixed_ref, one_ref, other_ref = refs[3 * m : 3 * (m + 1)]
        d_mixed = nn_dot(w_one_ref[...], d_one_refs[m][...]).astype(jnp.bfloat16)
        d_mixed_ref[...] = d_mixed
        grads = nt_dot(rows, d_mixed).astype(jnp.bfloat16)
        one_ref[...] = grads[:HALO]
        other_ref[...] = grads[HALO:]


def sum_kernel(count, *refs):
    for i in range(count):
        total = refs[i][...].astype(jnp.float32) + refs[count + i][...].astype(jnp.float32)
        refs[2 * count + i][...] = total.astype(refs[i].dtype)


def unpack_kernel(scale, rank_ref, *refs):
    *refs, stage_ref = refs
    ranks = stage_ref.shape[0]
    one_ref, b_one_ref, two_ref, b_two_ref, three_ref, tally_ref = refs[ranks:]
    for i in range(ranks):
        stage_ref[rank_ref[0] ^ i] = refs[i][...]
    width, hidden = one_ref.shape
    sums = stage_ref[...].reshape(-1, hidden).astype(jnp.float32)
    half, channels = hidden // 2, three_ref.shape[1]
    one_ref[...] = sums[:width]
    two_ref[...] = sums[width : width + hidden]
    base = width + hidden
    three_ref[:half] = sums[base : base + half, :channels]
    three_ref[half:] = sums[base : base + half, channels:]
    last = sums[base + half : base + half + 8]
    b_one_ref[...] = last[0:1]
    b_two_ref[...] = last[1:2]
    tally_ref[...] = (last[2:3] + last[3:4])[:, : tally_ref.shape[1]] * scale


def own_kernel(table_ref, *refs):
    *d_mixed_refs, own_ref = refs
    members, nodes, _ = own_ref.shape
    for m in range(members):
        own_ref[m] = nt_dot(table_ref[HALO : HALO + nodes, :], d_mixed_refs[m][...])


def finish_kernel(region_ref, own_ref, *refs):
    *refs, out_ref = refs
    members, nodes, _ = own_ref.shape
    out_ref[:, HALO : nodes - HALO] = own_ref[:, HALO : nodes - HALO].astype(jnp.bfloat16)
    for m in range(members):
        for ref, rows in zip(refs[2 * m : 2 * (m + 1)], rim_starts(region_ref, nodes)):
            out_ref[m, rows] = (own_ref[m, rows] + ref[...].astype(jnp.float32)).astype(jnp.bfloat16)


def exchanged(blocks):
    size = lax.axis_size("space")
    one = [(i, i ^ 1) for i in range(size)]
    other = [(i, (i + 1) % size if i % 2 else (i - 1) % size) for i in range(size)]
    return [lax.ppermute(block, "space", pairs) for block, pairs in zip(blocks, (one, other))]


def swapped(block, axis, by):
    return lax.ppermute(block, axis, [(i, i ^ by) for i in range(lax.axis_size(axis))])


def per_device(latent, neighbours, weights, targets, counts, w_one, b_one, w_two, b_two, w_three):
    members, nodes, width = latent.shape
    slots, channels = targets.shape
    hidden = w_one.shape[1]
    ext = nodes + 2 * HALO
    region, regions = lax.axis_index("space"), lax.axis_size("space")
    rank, ranks = lax.axis_index("member"), lax.axis_size("member")
    share = slots // ranks
    bf16, f32 = jnp.bfloat16, jnp.float32
    shape = jax.ShapeDtypeStruct
    each = range(members)

    edge = shape((HALO, width), bf16)
    region_at = region[None].astype(jnp.int32)
    *rims, latent = kernel_call(
        rims_kernel, (edge, edge, shape(latent.shape, bf16)), flops=4 << 30, moved=3 * MIB, smem=1, operands=2
    )(region_at, latent)
    halo = [exchanged(rims)]
    rank_at = rank[None].astype(jnp.int32)

    table, part, *rims = kernel_call(
        table_kernel,
        (shape((ext, slots), bf16), shape((width, slots), f32)) + (edge,) * (2 * members - 2),
        flops=2 * width * nodes * slots,
        moved=12 * MIB,
        smem=3,
        operands=6,
    )(region_at, rank_at, counts, neighbours, weights, latent)
    halo += [exchanged(rims[2 * m : 2 * m + 2]) for m in range(members - 1)]

    saved_shape = shape((hidden, slots), bf16)
    mixed_shape = shape((width, slots), bf16)
    decoded_shape = shape((channels, slots), bf16)
    dense = width * hidden + hidden * hidden + hidden * channels
    saved, decoded, beside, across = [], [], [], []
    for m in each:
        *kept, block = kernel_call(
            lambda *refs: forward_kernel(m, *refs),
            (mixed_shape,) + (saved_shape,) * 4 + (decoded_shape,),
            flops=2 * slots * ((ext if m else 2 * HALO) * width + dense),
            moved=8 * MIB,
            smem=1,
            operands=10,
        )(region_at, latent if m else part, table, *halo[m], w_one, b_one[None], w_two, b_two[None], w_three)
        saved.append(kept)
        decoded.append(block)
        blocks, bit = {0: block}, 2
        while bit < ranks:
            blocks.update({i ^ bit: swapped(blocks[i], "member", bit) for i in sorted(blocks)})
            bit = 2 * bit
        across.append([blocks[i] for i in sorted(blocks) if i])
        beside.append(swapped(block, "member", 1))

    def scored(others, carried, first=False, last=False):
        operands = (region_at, counts, *decoded, *others, *carried)
        return kernel_call(
            lambda *refs: score_kernel(members, len(others), members * ranks, first, last, *refs),
            (shape((channels, slots), bf16 if last else f32),) * members + (shape((1, LANE), f32),),
            flops=4 * MIB,
            moved=2 * MIB,
            smem=2,
            operands=len(operands),
        )(*operands)

    carried = scored(beside + [block for blocks in across[:-1] for block in blocks], [targets], first=True)
    across[-1], carried = lax.optimization_barrier((across[-1], carried))
    others = [*across[-1]] + [swapped(block, "member", 1) for blocks in across for block in blocks]
    *grads, score = scored(others, carried, last=True)

    rows = -(-(width + hidden + hidden // 2 + 4) // (16 * ranks)) * 16
    piece = shape((rows, hidden), bf16)
    operands = [region_at, rank_at, w_two, w_three, score]
    for m in each:
        operands += [*saved[m], grads[m]]
    out = kernel_call(
        lambda *refs: backward_kernel(members, ranks, *refs),
        (saved_shape,) * members + (piece,) * ranks,
        flops=4 * members * slots * dense,
        moved=10 * MIB,
        scratch=(pltpu.VMEM((members, hidden, slots), bf16), pltpu.VMEM((ranks, rows, hidden), bf16)),
        smem=2,
        operands=len(operands),
    )(*operands)
    d_one, pieces = out[:members], out[members:]

    def summed(ones, others):
        return kernel_call(
            lambda *refs: sum_kernel(len(ones), *refs), (piece,) * len(ones), flops=MIB, moved=MIB, operands=2 * len(ones)
        )(*ones, *others)

    out = kernel_call(
        lambda *refs: edges_kernel(members, *refs),
        (mixed_shape, edge, edge) * members,
        flops=2 * members * slots * width * (hidden + 2 * HALO),
        moved=6 * MIB,
        smem=1,
        operands=3 + members,
    )(region_at, table, w_one, *d_one)
    d_mixed, rims = out[::3], [out[3 * m + 1 : 3 * m + 3] for m in each]

    bit = 1
    while bit < ranks:
        received = [swapped(sent, "member", bit) for sent in pieces[1::2]]
        if bit == 1:
            received, rims = lax.optimization_barrier((received, rims))
        pieces = summed(pieces[::2], received)
        bit = 2 * bit
    own = kernel_call(
        own_kernel,
        shape((members, nodes, width), f32),
        flops=2 * members * nodes * width * slots,
        moved=6 * MIB,
        operands=1 + members,
    )(table, *d_mixed)
    edges = [block for m in each[:-1] for block in exchanged(rims[m])]
    (total,) = pieces
    step = 1
    while step < regions:
        (total,) = summed([total], [swapped(total, "space", step)])
        step = 2 * step
        if step == regions // 2:
            total, edges, own, rims = lax.optimization_barrier((total, edges, own, rims))
            edges = [*edges, *exchanged(rims[-1])]
    totals = {0: total}
    bit = 2
    while bit < ranks:
        totals.update({i ^ bit: swapped(totals[i], "member", bit) for i in sorted(totals)})
        bit = 2 * bit
    far = {i: block for i, block in totals.items() if i}
    far, edges = lax.optimization_barrier((far, edges))
    totals.update(far)
    totals.update({i ^ 1: swapped(block, "member", 1) for i, block in totals.items()})
    latent_grad = kernel_call(
        finish_kernel,
        shape((members, nodes, width), bf16),
        flops=MIB,
        moved=3 * MIB,
        smem=1,
        operands=2 + 2 * members,
    )(region_at, own, *edges)
    totals = [totals[i] for i in range(ranks)]
    totals, latent_grad = lax.optimization_barrier((totals, latent_grad))
    row = shape((1, hidden), f32)
    g_one, g_bone, g_two, g_btwo, g_three, tally = kernel_call(
        lambda *refs: unpack_kernel(1.0 / (OBS_MEAN * members * ranks), *refs),
        (shape((width, hidden), f32), row, shape((hidden, hidden), f32), row, shape((hidden, channels), f32),
         shape((1, regions), f32)),
        flops=MIB,
        moved=2 * MIB,
        scratch=(pltpu.VMEM((ranks, rows, hidden), bf16),),
        smem=1,
        operands=1 + ranks,
    )(rank_at, *totals)
    return (tally[0], latent_grad, g_one, g_bone[0], g_two, g_btwo[0], g_three)


def solution(mesh):
    in_specs = (
        P("member", ("groups", "space"), None),
        P(None, ("groups", "space")),
        P(None, ("groups", "space")),
        P(("groups", "space"), None),
        P("groups"),
        P(),
        P(),
        P(),
        P(),
        P(),
    )
    out_specs = (
        P("groups"),
        P("member", ("groups", "space"), None),
        P("groups", None),
        P("groups"),
        P("groups", None),
        P("groups"),
        P("groups", None),
    )
    return jax.shard_map(
        per_device, mesh=mesh, in_specs=in_specs, out_specs=out_specs, check_vma=False
    )
```

```python
import jax
import jax.numpy as jnp
from jax import lax
from jax.experimental import pallas as pl
from jax.experimental.pallas import tpu as pltpu
from jax.sharding import PartitionSpec as P

K = 4
OBS_MEAN = 512
HALO = 256
EPSILON = 1e-05
BLOCK = 256
LANE = 128
CHUNK = 512
MIB = 1 << 20


def split(total, step):
    return [(start, min(step, total - start)) for start in range(0, total, step)]


def nt_dot(left, right):
    return lax.dot_general(
        left, right, (((1,), (1,)), ((), ())), preferred_element_type=jnp.float32
    )


def nn_dot(left, right):
    return jnp.dot(left, right, preferred_element_type=jnp.float32)


def kernel_call(body, out_shape, flops, moved, scratch=(), smem=0, operands=0):
    vmem = pl.BlockSpec(memory_space=pltpu.VMEM)
    specs = [pl.BlockSpec(memory_space=pltpu.SMEM)] * smem
    return pl.pallas_call(
        body,
        out_shape=out_shape,
        in_specs=specs + [vmem] * (operands - len(specs)),
        out_specs=jax.tree.map(lambda _: vmem, out_shape),
        scratch_shapes=list(scratch),
        compiler_params=pltpu.CompilerParams(vmem_limit_bytes=24 * MIB),
        cost_estimate=pl.CostEstimate(flops=flops, bytes_accessed=moved, transcendentals=0),
    )


def rim_starts(region_ref, length):
    odd = lax.rem(region_ref[0], 2)
    far = length - HALO
    return [pl.ds(pl.multiple_of(start, HALO), HALO) for start in ((1 - odd) * far, odd * far)]


def cut_rims(region_ref, latent_ref, member, *rim_refs):
    for ref, rows in zip(rim_refs, rim_starts(region_ref, latent_ref.shape[1])):
        ref[...] = latent_ref[member, rows]


def rims_kernel(region_ref, latent_ref, one_ref, other_ref, copy_ref):
    cut_rims(region_ref, latent_ref, 0, one_ref, other_ref)
    copy_ref[...] = latent_ref[...]


def table_kernel(region_ref, rank_ref, counts_ref, nbr_ref, weight_ref, latent_ref, table_ref, part_ref, *rim_refs):
    members, nodes, _ = latent_ref.shape
    for m in range(1, members):
        cut_rims(region_ref, latent_ref, m, *rim_refs[2 * m - 2 : 2 * m])
    ext, slots = table_ref.shape
    live = lax.broadcasted_iota(jnp.int32, (1, slots), 1) < counts_ref[region_ref[0]]
    nbr = [nbr_ref[k : k + 1, :] for k in range(K)]
    own = [jnp.where(live, weight_ref[k : k + 1, :], 0.0) for k in range(K)]
    joint = []
    for k in range(K):
        total = own[k]
        for j in range(K):
            if j != k:
                total = total + jnp.where(nbr[j] == nbr[k], own[j], 0.0)
        joint.append(total)
    groups = BLOCK // 16
    rows = (
        lax.broadcasted_iota(jnp.int32, (groups, 16, LANE), 0) * 16
        + lax.broadcasted_iota(jnp.int32, (groups, 16, LANE), 1)
    ).astype(jnp.float32).astype(jnp.bfloat16)
    turned = latent_ref[0].T
    for start, length in split(slots, CHUNK):
        for lo, size in split(length, LANE):
            lanes = slice(start + lo, start + lo + size)
            wide = [jnp.broadcast_to(joint[k][:, lanes], (16, size)).astype(jnp.bfloat16) for k in range(K)]
            for b in range(ext // BLOCK):
                tile = jnp.zeros((groups, 16, size), jnp.bfloat16)
                for k in range(K):
                    near = (nbr[k][:, lanes] - b * BLOCK).astype(jnp.float32)
                    near = jnp.broadcast_to(near, (16, size)).astype(jnp.bfloat16)
                    tile = jnp.where(rows[:, :, :size] == near[None], wide[k][None], tile)
                table_ref[b * BLOCK : (b + 1) * BLOCK, lanes] = tile.reshape(BLOCK, size)
        lanes = slice(start, start + length)
        part_ref[:, lanes] = nn_dot(turned, table_ref[HALO : HALO + nodes, lanes])


def column(ref):
    height = ref.shape[1]
    return jnp.broadcast_to(ref[...], (LANE, height)).T


def forward_kernel(
    member, region_ref, own_ref, table_ref, one_ref, other_ref, w_one_ref, b_one_ref, w_two_ref, b_two_ref, w_three_ref,
    mixed_ref, act_one_ref, slope_one_ref, act_two_ref, slope_two_ref, decoded_ref,
):
    ext, slots = table_ref.shape
    w_one, w_two, w_three = w_one_ref[...].T * 0.5, w_two_ref[...].T * 0.5, w_three_ref[...].T
    b_one, b_two = column(b_one_ref) * 0.5, column(b_two_ref) * 0.5

    def layer(weight, bias, values, size):
        half = nn_dot(weight, values) + jnp.concatenate([bias] * (size // LANE), axis=1)
        gate = 1.0 + jnp.tanh(half)
        act = half * gate
        return act.astype(jnp.bfloat16), (gate + act * (2.0 - gate)).astype(jnp.bfloat16)

    edges = jnp.concatenate([one_ref[...].T, other_ref[...].T], axis=1)
    own = own_ref[member].T if member else None
    for lo, size in split(slots, CHUNK):
        lanes = slice(lo, lo + size)
        rims = jnp.concatenate([table_ref[rows, lanes] for rows in rim_starts(region_ref, ext)], axis=0)
        share = nn_dot(own, table_ref[HALO : ext - HALO, lanes]) if member else own_ref[:, lanes]
        mixed = share + nn_dot(edges, rims)
        mixed = mixed.astype(jnp.bfloat16)
        mixed_ref[:, lanes] = mixed
        act_one, slope_one_ref[:, lanes] = layer(w_one, b_one, mixed, size)
        act_one_ref[:, lanes] = act_one
        act_two, slope_two_ref[:, lanes] = layer(w_two, b_two, act_one, size)
        act_two_ref[:, lanes] = act_two
        decoded_ref[:, lanes] = nn_dot(w_three, act_two).astype(jnp.bfloat16)


def score_kernel(mine, others, count, first, last, region_ref, counts_ref, *refs):
    own_refs, refs = refs[:mine], refs[mine:]
    other_refs, refs = refs[:others], refs[others:]
    if first:
        target_ref, refs = refs[0], refs[1:]
        old_refs, old_score = None, 0.0
    else:
        old_refs, old_score, refs = refs[:mine], refs[mine][...], refs[mine + 1 :]
    grad_refs, score_ref = refs[:mine], refs[mine]
    channels, slots = own_refs[0].shape
    inner = [(i, j) for i in range(mine) for j in range(i + 1, mine)] if first else []
    outer = [(i, mine + j) for i in range(mine) for j in range(others)]
    pairs = inner + outer
    shares = [1.0 / (count - 1)] * len(inner) + [0.5 / (count - 1)] * len(outer)
    live_count = counts_ref[region_ref[0]]

    def one_tile(at, total):
        start = pl.multiple_of(at * LANE, LANE)
        lanes = pl.ds(start, LANE)
        if first:
            turned = target_ref[lanes, :].astype(jnp.float32).T

        def rows_of(c):
            return [ref[c : c + 16, lanes].astype(jnp.float32) for ref in (*own_refs, *other_refs)]

        def fold(square):
            return square[:8] + square[8:]

        to_target = [jnp.zeros((8, LANE), jnp.float32)] * (mine if first else 0)
        apart = [jnp.zeros((8, LANE), jnp.float32)] * len(pairs)
        for c in range(0, channels, 16):
            values = rows_of(c)
            for i in range(len(to_target)):
                to_target[i] = to_target[i] + fold((values[i] - turned[c : c + 16]) ** 2)
            for p, (i, j) in enumerate(pairs):
                apart[p] = apart[p] + fold((values[i] - values[j]) ** 2)
        live = start + lax.broadcasted_iota(jnp.int32, (1, LANE), 1) < live_count
        score = jnp.zeros((1, LANE), jnp.float32)

        def inverse(square):
            squared = jnp.sum(square, axis=0, keepdims=True) + EPSILON
            inv = lax.rsqrt(squared)
            return squared * inv, inv

        inv_target, inv_pair = [], []
        for square in to_target:
            dist, inv = inverse(square)
            score = score + dist
            inv_target.append(jnp.broadcast_to(inv, (8, LANE)))
        for square, share in zip(apart, shares):
            dist, inv = inverse(square)
            score = score - dist * share
            inv_pair.append(jnp.broadcast_to(inv * (1.0 / (count - 1)), (8, LANE)))
        for c in range(0, channels, 16):
            values = rows_of(c)
            halves = []
            for h in (0, 8):
                near = [v[h : h + 8] for v in values]
                rows = slice(c + h, c + h + 8)
                if first:
                    grads = [(near[i] - turned[rows]) * inv_target[i] for i in range(mine)]
                else:
                    grads = [old_refs[i][rows, lanes] for i in range(mine)]
                for p, (i, j) in enumerate(pairs):
                    term = (near[i] - near[j]) * inv_pair[p]
                    grads[i] = grads[i] - term
                    if j < mine:
                        grads[j] = grads[j] + term
                halves.append(grads)
            for i in range(mine):
                grad = jnp.concatenate([halves[0][i], halves[1][i]], axis=0)
                if last:
                    grad = jnp.where(live, grad, 0.0)
                grad_refs[i][c : c + 16, lanes] = grad.astype(grad_refs[i].dtype)
        return total + jnp.where(live, score, 0.0)

    score_ref[...] = old_score + lax.fori_loop(0, slots // LANE, one_tile, jnp.zeros((1, LANE), jnp.float32))


def backward_kernel(members, ranks, region_ref, rank_ref, w_two_ref, w_three_ref, score_ref, *refs):
    saved = [refs[6 * m : 6 * (m + 1)] for m in range(members)]
    refs = refs[6 * members :]
    d_one_refs, piece_refs, (d_two_ref, stage_ref) = refs[:members], refs[members:-2], refs[-2:]
    w_two, w_three = w_two_ref[...] * 0.5, w_three_ref[...] * 0.5
    hidden, slots = saved[0][1].shape
    bias_one = jnp.zeros((hidden, LANE), jnp.float32)
    bias_two = jnp.zeros((hidden, LANE), jnp.float32)
    g_one, g_two, g_three = 0.0, 0.0, 0.0

    def lane_sum(values):
        return sum(values[:, lo : lo + LANE] for lo, _ in split(values.shape[1], LANE))

    for m in range(members):
        mixed_ref, act_one_ref, slope_one_ref, act_two_ref, slope_two_ref, d_dec_ref = saved[m]
        for lo, size in split(slots, CHUNK):
            lanes = slice(lo, lo + size)
            back = nn_dot(w_three, d_dec_ref[:, lanes]) * slope_two_ref[:, lanes].astype(jnp.float32)
            bias_two = bias_two + lane_sum(back)
            d_two = back.astype(jnp.bfloat16)
            d_two_ref[m, :, lanes] = d_two
            back = nn_dot(w_two, d_two) * slope_one_ref[:, lanes].astype(jnp.float32)
            bias_one = bias_one + lane_sum(back)
            d_one_refs[m][:, lanes] = back.astype(jnp.bfloat16)
        g_three = g_three + nt_dot(act_two_ref[...], d_dec_ref[...])
        g_two = g_two + nt_dot(act_one_ref[...], d_two_ref[m])
        g_one = g_one + nt_dot(mixed_ref[...], d_one_refs[m][...])
    half = hidden // 2
    region = lax.broadcasted_iota(jnp.int32, (1, hidden), 1) == region_ref[0]
    tally = jnp.where(region, jnp.sum(score_ref[...]), 0.0)
    high = tally.astype(jnp.bfloat16).astype(jnp.float32)
    parts = [
        g_one,
        g_two,
        jnp.concatenate([g_three[:half], g_three[half:]], axis=1),
        jnp.sum(bias_one.T, axis=0, keepdims=True),
        jnp.sum(bias_two.T, axis=0, keepdims=True),
        high,
        tally - high,
    ]
    used = sum(part.shape[0] for part in parts)
    parts.append(jnp.zeros((ranks * stage_ref.shape[1] - used, hidden), jnp.float32))
    stage_ref[...] = jnp.concatenate(parts, axis=0).astype(stage_ref.dtype).reshape(stage_ref.shape)
    for i in range(ranks):
        piece_refs[i][...] = stage_ref[rank_ref[0] ^ i]


def edges_kernel(members, region_ref, table_ref, w_one_ref, *refs):
    d_one_refs, d_mixed_refs, (one_ref, other_ref) = refs[:members], refs[members : 2 * members], refs[2 * members :]
    ext = table_ref.shape[0]
    rows = jnp.concatenate([table_ref[rows, :] for rows in rim_starts(region_ref, ext)], axis=0)
    for m in range(members):
        d_mixed = nn_dot(w_one_ref[...], d_one_refs[m][...]).astype(jnp.bfloat16)
        d_mixed_refs[m][...] = d_mixed
        grads = nt_dot(rows, d_mixed).astype(jnp.bfloat16)
        one_ref[m] = grads[:HALO]
        other_ref[m] = grads[HALO:]


def sum_kernel(count, *refs):
    for i in range(count):
        total = refs[i][...].astype(jnp.float32) + refs[count + i][...].astype(jnp.float32)
        refs[2 * count + i][...] = total.astype(refs[i].dtype)


def unpack_kernel(scale, rank_ref, *refs):
    *refs, stage_ref = refs
    ranks = stage_ref.shape[0]
    one_ref, b_one_ref, two_ref, b_two_ref, three_ref, tally_ref = refs[ranks:]
    for i in range(ranks):
        stage_ref[rank_ref[0] ^ i] = refs[i][...]
    width, hidden = one_ref.shape
    sums = stage_ref[...].reshape(-1, hidden).astype(jnp.float32)
    half, channels = hidden // 2, three_ref.shape[1]
    one_ref[...] = sums[:width]
    two_ref[...] = sums[width : width + hidden]
    base = width + hidden
    three_ref[:half] = sums[base : base + half, :channels]
    three_ref[half:] = sums[base : base + half, channels:]
    last = sums[base + half : base + half + 8]
    b_one_ref[...] = last[0:1]
    b_two_ref[...] = last[1:2]
    tally_ref[...] = (last[2:3] + last[3:4])[:, : tally_ref.shape[1]] * scale


def own_kernel(table_ref, *refs):
    *d_mixed_refs, own_ref = refs
    members, nodes, _ = own_ref.shape
    for m in range(members):
        own_ref[m] = nt_dot(table_ref[HALO : HALO + nodes, :], d_mixed_refs[m][...])


def finish_kernel(region_ref, own_ref, one_ref, other_ref, out_ref):
    nodes = own_ref.shape[1]
    out_ref[:, HALO : nodes - HALO] = own_ref[:, HALO : nodes - HALO].astype(jnp.bfloat16)
    for ref, rows in zip((one_ref, other_ref), rim_starts(region_ref, nodes)):
        out_ref[:, rows] = (own_ref[:, rows] + ref[...].astype(jnp.float32)).astype(jnp.bfloat16)


def exchanged(block, second):
    size = lax.axis_size("space")
    pairs = [(i, (i + 1) % size if i % 2 else (i - 1) % size) if second else (i, i ^ 1) for i in range(size)]
    return lax.ppermute(block, "space", pairs)


def swapped(block, axis, by):
    return lax.ppermute(block, axis, [(i, i ^ by) for i in range(lax.axis_size(axis))])


def per_device(latent, neighbours, weights, targets, counts, w_one, b_one, w_two, b_two, w_three):
    members, nodes, width = latent.shape
    slots, channels = targets.shape
    hidden = w_one.shape[1]
    ext = nodes + 2 * HALO
    region, regions = lax.axis_index("space"), lax.axis_size("space")
    rank, ranks = lax.axis_index("member"), lax.axis_size("member")
    share = slots // ranks
    bf16, f32 = jnp.bfloat16, jnp.float32
    shape = jax.ShapeDtypeStruct
    each = range(members)

    edge = shape((HALO, width), bf16)
    region_at = region[None].astype(jnp.int32)
    *rims, latent = kernel_call(
        rims_kernel, (edge, edge, shape(latent.shape, bf16)), flops=4 << 30, moved=3 * MIB, smem=1, operands=2
    )(region_at, latent)
    halo = [[exchanged(rims[0], False), exchanged(rims[1], True)]]
    rank_at = rank[None].astype(jnp.int32)

    table, part, *rims = kernel_call(
        table_kernel,
        (shape((ext, slots), bf16), shape((width, slots), f32)) + (edge,) * (2 * members - 2),
        flops=2 * width * nodes * slots,
        moved=12 * MIB,
        smem=3,
        operands=6,
    )(region_at, rank_at, counts, neighbours, weights, latent)
    halo += [[exchanged(rims[2 * m], False), exchanged(rims[2 * m + 1], True)] for m in range(members - 1)]

    saved_shape = shape((hidden, slots), bf16)
    mixed_shape = shape((width, slots), bf16)
    decoded_shape = shape((channels, slots), bf16)
    dense = width * hidden + hidden * hidden + hidden * channels
    saved, decoded, beside, across = [], [], [], []
    for m in each:
        *kept, block = kernel_call(
            lambda *refs: forward_kernel(m, *refs),
            (mixed_shape,) + (saved_shape,) * 4 + (decoded_shape,),
            flops=2 * slots * ((ext if m else 2 * HALO) * width + dense),
            moved=8 * MIB,
            smem=1,
            operands=10,
        )(region_at, latent if m else part, table, *halo[m], w_one, b_one[None], w_two, b_two[None], w_three)
        saved.append(kept)
        decoded.append(block)
        blocks, bit = {0: block}, 2
        while bit < ranks:
            blocks.update({i ^ bit: swapped(blocks[i], "member", bit) for i in sorted(blocks)})
            bit = 2 * bit
        across.append([blocks[i] for i in sorted(blocks) if i])
        beside.append(swapped(block, "member", 1))

    def scored(others, carried, first=False, last=False):
        operands = (region_at, counts, *decoded, *others, *carried)
        return kernel_call(
            lambda *refs: score_kernel(members, len(others), members * ranks, first, last, *refs),
            (shape((channels, slots), bf16 if last else f32),) * members + (shape((1, LANE), f32),),
            flops=4 * MIB,
            moved=2 * MIB,
            smem=2,
            operands=len(operands),
        )(*operands)

    carried = scored(beside + [block for blocks in across[:-1] for block in blocks], [targets], first=True)
    across[-1], carried = lax.optimization_barrier((across[-1], carried))
    others = [*across[-1]] + [swapped(block, "member", 1) for blocks in across for block in blocks]
    *grads, score = scored(others, carried, last=True)

    rows = -(-(width + hidden + hidden // 2 + 4) // (16 * ranks)) * 16
    piece = shape((rows, hidden), bf16)
    operands = [region_at, rank_at, w_two, w_three, score]
    for m in each:
        operands += [*saved[m], grads[m]]
    out = kernel_call(
        lambda *refs: backward_kernel(members, ranks, *refs),
        (saved_shape,) * members + (piece,) * ranks,
        flops=4 * members * slots * dense,
        moved=10 * MIB,
        scratch=(pltpu.VMEM((members, hidden, slots), bf16), pltpu.VMEM((ranks, rows, hidden), bf16)),
        smem=2,
        operands=len(operands),
    )(*operands)
    d_one, pieces = out[:members], out[members:]

    def summed(ones, others):
        return kernel_call(
            lambda *refs: sum_kernel(len(ones), *refs), (piece,) * len(ones), flops=MIB, moved=MIB, operands=2 * len(ones)
        )(*ones, *others)

    out = kernel_call(
        lambda *refs: edges_kernel(members, *refs),
        (mixed_shape,) * members + (shape((members, HALO, width), bf16),) * 2,
        flops=2 * members * slots * width * (hidden + 2 * HALO),
        moved=6 * MIB,
        smem=1,
        operands=3 + members,
    )(region_at, table, w_one, *d_one)
    d_mixed, rims = out[:members], out[members:]

    bit = 1
    while bit < ranks:
        received = [swapped(sent, "member", bit) for sent in pieces[1::2]]
        if bit == 1:
            received, rims = lax.optimization_barrier((received, rims))
        pieces = summed(pieces[::2], received)
        bit = 2 * bit
    own = kernel_call(
        own_kernel,
        shape((members, nodes, width), f32),
        flops=2 * members * nodes * width * slots,
        moved=6 * MIB,
        operands=1 + members,
    )(table, *d_mixed)
    other = exchanged(rims[1], True)
    (total,) = pieces
    step = 1
    while step < regions:
        (total,) = summed([total], [swapped(total, "space", step)])
        step = 2 * step
        if 2 * step == regions:
            total, other, own, rims = lax.optimization_barrier((total, other, own, rims))
            one = exchanged(rims[0], False)
    totals = {0: total}
    bit = 2
    while bit < ranks:
        totals.update({i ^ bit: swapped(totals[i], "member", bit) for i in sorted(totals)})
        bit = 2 * bit
    totals.update({i ^ 1: swapped(block, "member", 1) for i, block in totals.items()})
    latent_grad = kernel_call(
        finish_kernel,
        shape((members, nodes, width), bf16),
        flops=MIB,
        moved=3 * MIB,
        smem=1,
        operands=4,
    )(region_at, own, one, other)
    totals = [totals[i] for i in range(ranks)]
    totals, latent_grad = lax.optimization_barrier((totals, latent_grad))
    row = shape((1, hidden), f32)
    g_one, g_bone, g_two, g_btwo, g_three, tally = kernel_call(
        lambda *refs: unpack_kernel(1.0 / (OBS_MEAN * members * ranks), *refs),
        (shape((width, hidden), f32), row, shape((hidden, hidden), f32), row, shape((hidden, channels), f32),
         shape((1, regions), f32)),
        flops=MIB,
        moved=2 * MIB,
        scratch=(pltpu.VMEM((ranks, rows, hidden), bf16),),
        smem=1,
        operands=1 + ranks,
    )(rank_at, *totals)
    return (tally[0], latent_grad, g_one, g_bone[0], g_two, g_btwo[0], g_three)


def solution(mesh):
    in_specs = (
        P("member", ("groups", "space"), None),
        P(None, ("groups", "space")),
        P(None, ("groups", "space")),
        P(("groups", "space"), None),
        P("groups"),
        P(),
        P(),
        P(),
        P(),
        P(),
    )
    out_specs = (
        P("groups"),
        P("member", ("groups", "space"), None),
        P("groups", None),
        P("groups"),
        P("groups", None),
        P("groups"),
        P("groups", None),
    )
    return jax.shard_map(
        per_device, mesh=mesh, in_specs=in_specs, out_specs=out_specs, check_vma=False
    )
```

```python
import jax
import jax.numpy as jnp
from jax import lax
from jax.experimental import pallas as pl
from jax.experimental.pallas import tpu as pltpu
from jax.sharding import PartitionSpec as P

K = 4
OBS_MEAN = 512
HALO = 256
EPSILON = 1e-05
BLOCK = 256
LANE = 128
CHUNK = 512
MIB = 1 << 20


def split(total, step):
    return [(start, min(step, total - start)) for start in range(0, total, step)]


def nt_dot(left, right):
    return lax.dot_general(
        left, right, (((1,), (1,)), ((), ())), preferred_element_type=jnp.float32
    )


def nn_dot(left, right):
    return jnp.dot(left, right, preferred_element_type=jnp.float32)


def kernel_call(body, out_shape, flops, moved, scratch=(), smem=0, operands=0):
    vmem = pl.BlockSpec(memory_space=pltpu.VMEM)
    specs = [pl.BlockSpec(memory_space=pltpu.SMEM)] * smem
    return pl.pallas_call(
        body,
        out_shape=out_shape,
        in_specs=specs + [vmem] * (operands - len(specs)),
        out_specs=jax.tree.map(lambda _: vmem, out_shape),
        scratch_shapes=list(scratch),
        compiler_params=pltpu.CompilerParams(vmem_limit_bytes=24 * MIB),
        cost_estimate=pl.CostEstimate(flops=flops, bytes_accessed=moved, transcendentals=0),
    )


def rim_starts(region_ref, length):
    odd = lax.rem(region_ref[0], 2)
    far = length - HALO
    return [pl.ds(pl.multiple_of(start, HALO), HALO) for start in ((1 - odd) * far, odd * far)]


def cut_rims(region_ref, latent_ref, member, *rim_refs):
    for ref, rows in zip(rim_refs, rim_starts(region_ref, latent_ref.shape[1])):
        ref[...] = latent_ref[member, rows]


def rims_kernel(region_ref, latent_ref, one_ref, other_ref, copy_ref):
    cut_rims(region_ref, latent_ref, 0, one_ref, other_ref)
    copy_ref[...] = latent_ref[...]


def table_kernel(region_ref, rank_ref, counts_ref, nbr_ref, weight_ref, latent_ref, table_ref, part_ref, *rim_refs):
    members, nodes, _ = latent_ref.shape
    for m in range(1, members):
        cut_rims(region_ref, latent_ref, m, *rim_refs[2 * m - 2 : 2 * m])
    ext, slots = table_ref.shape
    live = lax.broadcasted_iota(jnp.int32, (1, slots), 1) < counts_ref[region_ref[0]]
    nbr = [nbr_ref[k : k + 1, :] for k in range(K)]
    own = [jnp.where(live, weight_ref[k : k + 1, :], 0.0) for k in range(K)]
    joint = []
    for k in range(K):
        total = own[k]
        for j in range(K):
            if j != k:
                total = total + jnp.where(nbr[j] == nbr[k], own[j], 0.0)
        joint.append(total)
    groups = BLOCK // 16
    rows = (
        lax.broadcasted_iota(jnp.int32, (groups, 16, LANE), 0) * 16
        + lax.broadcasted_iota(jnp.int32, (groups, 16, LANE), 1)
    ).astype(jnp.float32).astype(jnp.bfloat16)
    turned = latent_ref[0].T
    for start, length in split(slots, CHUNK):
        for lo, size in split(length, LANE):
            lanes = slice(start + lo, start + lo + size)
            wide = [jnp.broadcast_to(joint[k][:, lanes], (16, size)).astype(jnp.bfloat16) for k in range(K)]
            for b in range(ext // BLOCK):
                tile = jnp.zeros((groups, 16, size), jnp.bfloat16)
                for k in range(K):
                    near = (nbr[k][:, lanes] - b * BLOCK).astype(jnp.float32)
                    near = jnp.broadcast_to(near, (16, size)).astype(jnp.bfloat16)
                    tile = jnp.where(rows[:, :, :size] == near[None], wide[k][None], tile)
                table_ref[b * BLOCK : (b + 1) * BLOCK, lanes] = tile.reshape(BLOCK, size)
        lanes = slice(start, start + length)
        part_ref[:, lanes] = nn_dot(turned, table_ref[HALO : HALO + nodes, lanes])


def column(ref):
    height = ref.shape[1]
    return jnp.broadcast_to(ref[...], (LANE, height)).T


def forward_kernel(
    member, region_ref, own_ref, table_ref, one_ref, other_ref, w_one_ref, b_one_ref, w_two_ref, b_two_ref, w_three_ref,
    mixed_ref, act_one_ref, slope_one_ref, act_two_ref, slope_two_ref, decoded_ref,
):
    ext, slots = table_ref.shape
    w_one, w_two, w_three = w_one_ref[...].T * 0.5, w_two_ref[...].T * 0.5, w_three_ref[...].T
    b_one, b_two = column(b_one_ref) * 0.5, column(b_two_ref) * 0.5

    def layer(weight, bias, values, size):
        half = nn_dot(weight, values) + jnp.concatenate([bias] * (size // LANE), axis=1)
        gate = 1.0 + jnp.tanh(half)
        act = half * gate
        return act.astype(jnp.bfloat16), (gate + act * (2.0 - gate)).astype(jnp.bfloat16)

    edges = jnp.concatenate([one_ref[...].T, other_ref[...].T], axis=1)
    own = own_ref[member].T if member else None
    for lo, size in split(slots, CHUNK):
        lanes = slice(lo, lo + size)
        rims = jnp.concatenate([table_ref[rows, lanes] for rows in rim_starts(region_ref, ext)], axis=0)
        share = nn_dot(own, table_ref[HALO : ext - HALO, lanes]) if member else own_ref[:, lanes]
        mixed = share + nn_dot(edges, rims)
        mixed = mixed.astype(jnp.bfloat16)
        mixed_ref[:, lanes] = mixed
        act_one, slope_one_ref[:, lanes] = layer(w_one, b_one, mixed, size)
        act_one_ref[:, lanes] = act_one
        act_two, slope_two_ref[:, lanes] = layer(w_two, b_two, act_one, size)
        act_two_ref[:, lanes] = act_two
        decoded_ref[:, lanes] = nn_dot(w_three, act_two).astype(jnp.bfloat16)


def score_kernel(mine, others, count, first, last, region_ref, counts_ref, *refs):
    own_refs, refs = refs[:mine], refs[mine:]
    other_refs, refs = refs[:others], refs[others:]
    if first:
        target_ref, refs = refs[0], refs[1:]
        old_refs, old_score = None, 0.0
    else:
        old_refs, old_score, refs = refs[:mine], refs[mine][...], refs[mine + 1 :]
    grad_refs, score_ref = refs[:mine], refs[mine]
    channels, slots = own_refs[0].shape
    inner = [(i, j) for i in range(mine) for j in range(i + 1, mine)] if first else []
    outer = [(i, mine + j) for i in range(mine) for j in range(others)]
    pairs = inner + outer
    shares = [1.0 / (count - 1)] * len(inner) + [0.5 / (count - 1)] * len(outer)
    live_count = counts_ref[region_ref[0]]

    def one_tile(at, total):
        start = pl.multiple_of(at * LANE, LANE)
        lanes = pl.ds(start, LANE)
        if first:
            turned = target_ref[lanes, :].astype(jnp.float32).T

        def rows_of(c):
            return [ref[c : c + 16, lanes].astype(jnp.float32) for ref in (*own_refs, *other_refs)]

        def fold(square):
            return square[:8] + square[8:]

        to_target = [jnp.zeros((8, LANE), jnp.float32)] * (mine if first else 0)
        apart = [jnp.zeros((8, LANE), jnp.float32)] * len(pairs)
        for c in range(0, channels, 16):
            values = rows_of(c)
            for i in range(len(to_target)):
                to_target[i] = to_target[i] + fold((values[i] - turned[c : c + 16]) ** 2)
            for p, (i, j) in enumerate(pairs):
                apart[p] = apart[p] + fold((values[i] - values[j]) ** 2)
        live = start + lax.broadcasted_iota(jnp.int32, (1, LANE), 1) < live_count
        score = jnp.zeros((1, LANE), jnp.float32)

        def inverse(square):
            squared = jnp.sum(square, axis=0, keepdims=True) + EPSILON
            inv = lax.rsqrt(squared)
            return squared * inv, inv

        inv_target, inv_pair = [], []
        for square in to_target:
            dist, inv = inverse(square)
            score = score + dist
            inv_target.append(jnp.broadcast_to(inv, (8, LANE)))
        for square, share in zip(apart, shares):
            dist, inv = inverse(square)
            score = score - dist * share
            inv_pair.append(jnp.broadcast_to(inv * (1.0 / (count - 1)), (8, LANE)))
        for c in range(0, channels, 16):
            values = rows_of(c)
            halves = []
            for h in (0, 8):
                near = [v[h : h + 8] for v in values]
                rows = slice(c + h, c + h + 8)
                if first:
                    grads = [(near[i] - turned[rows]) * inv_target[i] for i in range(mine)]
                else:
                    grads = [old_refs[i][rows, lanes] for i in range(mine)]
                for p, (i, j) in enumerate(pairs):
                    term = (near[i] - near[j]) * inv_pair[p]
                    grads[i] = grads[i] - term
                    if j < mine:
                        grads[j] = grads[j] + term
                halves.append(grads)
            for i in range(mine):
                grad = jnp.concatenate([halves[0][i], halves[1][i]], axis=0)
                if last:
                    grad = jnp.where(live, grad, 0.0)
                grad_refs[i][c : c + 16, lanes] = grad.astype(grad_refs[i].dtype)
        return total + jnp.where(live, score, 0.0)

    score_ref[...] = old_score + lax.fori_loop(0, slots // LANE, one_tile, jnp.zeros((1, LANE), jnp.float32))


def backward_kernel(members, ranks, region_ref, rank_ref, w_two_ref, w_three_ref, score_ref, *refs):
    saved = [refs[6 * m : 6 * (m + 1)] for m in range(members)]
    refs = refs[6 * members :]
    d_one_refs, piece_refs, (d_two_ref, stage_ref) = refs[:members], refs[members:-2], refs[-2:]
    w_two, w_three = w_two_ref[...] * 0.5, w_three_ref[...] * 0.5
    hidden, slots = saved[0][1].shape
    bias_one = jnp.zeros((hidden, LANE), jnp.float32)
    bias_two = jnp.zeros((hidden, LANE), jnp.float32)
    g_one, g_two, g_three = 0.0, 0.0, 0.0

    def lane_sum(values):
        return sum(values[:, lo : lo + LANE] for lo, _ in split(values.shape[1], LANE))

    for m in range(members):
        mixed_ref, act_one_ref, slope_one_ref, act_two_ref, slope_two_ref, d_dec_ref = saved[m]
        for lo, size in split(slots, CHUNK):
            lanes = slice(lo, lo + size)
            back = nn_dot(w_three, d_dec_ref[:, lanes]) * slope_two_ref[:, lanes].astype(jnp.float32)
            bias_two = bias_two + lane_sum(back)
            d_two = back.astype(jnp.bfloat16)
            d_two_ref[m, :, lanes] = d_two
            back = nn_dot(w_two, d_two) * slope_one_ref[:, lanes].astype(jnp.float32)
            bias_one = bias_one + lane_sum(back)
            d_one_refs[m][:, lanes] = back.astype(jnp.bfloat16)
        g_three = g_three + nt_dot(act_two_ref[...], d_dec_ref[...])
        g_two = g_two + nt_dot(act_one_ref[...], d_two_ref[m])
        g_one = g_one + nt_dot(mixed_ref[...], d_one_refs[m][...])
    half = hidden // 2
    region = lax.broadcasted_iota(jnp.int32, (1, hidden), 1) == region_ref[0]
    tally = jnp.where(region, jnp.sum(score_ref[...]), 0.0)
    high = tally.astype(jnp.bfloat16).astype(jnp.float32)
    parts = [
        g_one,
        g_two,
        jnp.concatenate([g_three[:half], g_three[half:]], axis=1),
        jnp.sum(bias_one.T, axis=0, keepdims=True),
        jnp.sum(bias_two.T, axis=0, keepdims=True),
        high,
        tally - high,
    ]
    used = sum(part.shape[0] for part in parts)
    parts.append(jnp.zeros((ranks * stage_ref.shape[1] - used, hidden), jnp.float32))
    stage_ref[...] = jnp.concatenate(parts, axis=0).astype(stage_ref.dtype).reshape(stage_ref.shape)
    for i in range(ranks):
        piece_refs[i][...] = stage_ref[rank_ref[0] ^ i]


def edges_kernel(members, region_ref, table_ref, w_one_ref, *refs):
    d_one_refs, d_mixed_refs, (one_ref, other_ref) = refs[:members], refs[members : 2 * members], refs[2 * members :]
    ext = table_ref.shape[0]
    rows = jnp.concatenate([table_ref[rows, :] for rows in rim_starts(region_ref, ext)], axis=0)
    for m in range(members):
        d_mixed = nn_dot(w_one_ref[...], d_one_refs[m][...]).astype(jnp.bfloat16)
        d_mixed_refs[m][...] = d_mixed
        grads = nt_dot(rows, d_mixed).astype(jnp.bfloat16)
        one_ref[m] = grads[:HALO]
        other_ref[m] = grads[HALO:]


def sum_kernel(count, *refs):
    for i in range(count):
        total = refs[i][...].astype(jnp.float32) + refs[count + i][...].astype(jnp.float32)
        refs[2 * count + i][...] = total.astype(refs[i].dtype)


def unpack_kernel(scale, rank_ref, *refs):
    *refs, stage_ref = refs
    ranks = stage_ref.shape[0]
    one_ref, b_one_ref, two_ref, b_two_ref, three_ref, tally_ref = refs[ranks:]
    for i in range(ranks):
        stage_ref[rank_ref[0] ^ i] = refs[i][...]
    width, hidden = one_ref.shape
    sums = stage_ref[...].reshape(-1, hidden).astype(jnp.float32)
    half, channels = hidden // 2, three_ref.shape[1]
    one_ref[...] = sums[:width]
    two_ref[...] = sums[width : width + hidden]
    base = width + hidden
    three_ref[:half] = sums[base : base + half, :channels]
    three_ref[half:] = sums[base : base + half, channels:]
    last = sums[base + half : base + half + 8]
    b_one_ref[...] = last[0:1]
    b_two_ref[...] = last[1:2]
    tally_ref[...] = (last[2:3] + last[3:4])[:, : tally_ref.shape[1]] * scale


def own_kernel(table_ref, *refs):
    *d_mixed_refs, own_ref = refs
    members, nodes, _ = own_ref.shape
    for m in range(members):
        own_ref[m] = nt_dot(table_ref[HALO : HALO + nodes, :], d_mixed_refs[m][...])


def finish_kernel(region_ref, own_ref, one_ref, other_ref, out_ref):
    nodes = own_ref.shape[1]
    out_ref[:, HALO : nodes - HALO] = own_ref[:, HALO : nodes - HALO].astype(jnp.bfloat16)
    for ref, rows in zip((one_ref, other_ref), rim_starts(region_ref, nodes)):
        out_ref[:, rows] = (own_ref[:, rows] + ref[...].astype(jnp.float32)).astype(jnp.bfloat16)


def exchanged(block, second):
    size = lax.axis_size("space")
    pairs = [(i, (i + 1) % size if i % 2 else (i - 1) % size) if second else (i, i ^ 1) for i in range(size)]
    return lax.ppermute(block, "space", pairs)


def swapped(block, axis, by):
    return lax.ppermute(block, axis, [(i, i ^ by) for i in range(lax.axis_size(axis))])


def per_device(latent, neighbours, weights, targets, counts, w_one, b_one, w_two, b_two, w_three):
    members, nodes, width = latent.shape
    slots, channels = targets.shape
    hidden = w_one.shape[1]
    ext = nodes + 2 * HALO
    region, regions = lax.axis_index("space"), lax.axis_size("space")
    rank, ranks = lax.axis_index("member"), lax.axis_size("member")
    share = slots // ranks
    bf16, f32 = jnp.bfloat16, jnp.float32
    shape = jax.ShapeDtypeStruct
    each = range(members)

    edge = shape((HALO, width), bf16)
    region_at = region[None].astype(jnp.int32)
    *rims, latent = kernel_call(
        rims_kernel, (edge, edge, shape(latent.shape, bf16)), flops=4 << 30, moved=3 * MIB, smem=1, operands=2
    )(region_at, latent)
    halo = [[exchanged(rims[0], False), exchanged(rims[1], True)]]
    rank_at = rank[None].astype(jnp.int32)

    table, part, *rims = kernel_call(
        table_kernel,
        (shape((ext, slots), bf16), shape((width, slots), f32)) + (edge,) * (2 * members - 2),
        flops=2 * width * nodes * slots,
        moved=12 * MIB,
        smem=3,
        operands=6,
    )(region_at, rank_at, counts, neighbours, weights, latent)
    halo += [[exchanged(rims[2 * m], False), exchanged(rims[2 * m + 1], True)] for m in range(members - 1)]

    saved_shape = shape((hidden, slots), bf16)
    mixed_shape = shape((width, slots), bf16)
    decoded_shape = shape((channels, slots), bf16)
    dense = width * hidden + hidden * hidden + hidden * channels
    saved, decoded, beside, across = [], [], [], []
    for m in each:
        *kept, block = kernel_call(
            lambda *refs: forward_kernel(m, *refs),
            (mixed_shape,) + (saved_shape,) * 4 + (decoded_shape,),
            flops=2 * slots * ((ext if m else 2 * HALO) * width + dense),
            moved=8 * MIB,
            smem=1,
            operands=10,
        )(region_at, latent if m else part, table, *halo[m], w_one, b_one[None], w_two, b_two[None], w_three)
        saved.append(kept)
        decoded.append(block)
        blocks, bit = {0: block}, 2
        while bit < ranks:
            blocks.update({i ^ bit: swapped(blocks[i], "member", bit) for i in sorted(blocks)})
            bit = 2 * bit
        across.append([blocks[i] for i in sorted(blocks) if i])
        beside.append(swapped(block, "member", 1))

    def scored(others, carried, first=False, last=False):
        operands = (region_at, counts, *decoded, *others, *carried)
        return kernel_call(
            lambda *refs: score_kernel(members, len(others), members * ranks, first, last, *refs),
            (shape((channels, slots), bf16 if last else f32),) * members + (shape((1, LANE), f32),),
            flops=4 * MIB,
            moved=2 * MIB,
            smem=2,
            operands=len(operands),
        )(*operands)

    carried = scored(beside + [block for blocks in across[:-1] for block in blocks], [targets], first=True)
    across[-1], carried = lax.optimization_barrier((across[-1], carried))
    others = [*across[-1]] + [swapped(block, "member", 1) for blocks in across for block in blocks]
    *grads, score = scored(others, carried, last=True)

    rows = -(-(width + hidden + hidden // 2 + 4) // (16 * ranks)) * 16
    piece = shape((rows, hidden), bf16)
    operands = [region_at, rank_at, w_two, w_three, score]
    for m in each:
        operands += [*saved[m], grads[m]]
    out = kernel_call(
        lambda *refs: backward_kernel(members, ranks, *refs),
        (saved_shape,) * members + (piece,) * ranks,
        flops=4 * members * slots * dense,
        moved=10 * MIB,
        scratch=(pltpu.VMEM((members, hidden, slots), bf16), pltpu.VMEM((ranks, rows, hidden), bf16)),
        smem=2,
        operands=len(operands),
    )(*operands)
    d_one, pieces = out[:members], out[members:]

    def summed(ones, others):
        return kernel_call(
            lambda *refs: sum_kernel(len(ones), *refs), (piece,) * len(ones), flops=MIB, moved=MIB, operands=2 * len(ones)
        )(*ones, *others)

    out = kernel_call(
        lambda *refs: edges_kernel(members, *refs),
        (mixed_shape,) * members + (shape((members, HALO, width), bf16),) * 2,
        flops=2 * members * slots * width * (hidden + 2 * HALO),
        moved=6 * MIB,
        smem=1,
        operands=3 + members,
    )(region_at, table, w_one, *d_one)
    d_mixed, rims = out[:members], out[members:]

    bit = 1
    while bit < ranks:
        received = [swapped(sent, "member", bit) for sent in pieces[1::2]]
        if bit == 1:
            received, rims = lax.optimization_barrier((received, rims))
        pieces = summed(pieces[::2], received)
        bit = 2 * bit
    own = kernel_call(
        own_kernel,
        shape((members, nodes, width), f32),
        flops=2 * members * nodes * width * slots,
        moved=6 * MIB,
        operands=1 + members,
    )(table, *d_mixed)
    other = exchanged(rims[1], True)
    (total,) = pieces
    step = 1
    while step < regions:
        received = swapped(total, "space", step)
        step = 2 * step
        if step == regions:
            received, other = lax.optimization_barrier((received, other))
        (total,) = summed([total], [received])
        if 2 * step == regions:
            total, own, rims = lax.optimization_barrier((total, own, rims))
            one = exchanged(rims[0], False)
    totals = {0: total}
    bit = 2
    while bit < ranks:
        totals.update({i ^ bit: swapped(totals[i], "member", bit) for i in sorted(totals)})
        bit = 2 * bit
    totals.update({i ^ 1: swapped(block, "member", 1) for i, block in totals.items()})
    latent_grad = kernel_call(
        finish_kernel,
        shape((members, nodes, width), bf16),
        flops=MIB,
        moved=3 * MIB,
        smem=1,
        operands=4,
    )(region_at, own, one, other)
    totals = [totals[i] for i in range(ranks)]
    totals, latent_grad = lax.optimization_barrier((totals, latent_grad))
    row = shape((1, hidden), f32)
    g_one, g_bone, g_two, g_btwo, g_three, tally = kernel_call(
        lambda *refs: unpack_kernel(1.0 / (OBS_MEAN * members * ranks), *refs),
        (shape((width, hidden), f32), row, shape((hidden, hidden), f32), row, shape((hidden, channels), f32),
         shape((1, regions), f32)),
        flops=MIB,
        moved=2 * MIB,
        scratch=(pltpu.VMEM((ranks, rows, hidden), bf16),),
        smem=1,
        operands=1 + ranks,
    )(rank_at, *totals)
    return (tally[0], latent_grad, g_one, g_bone[0], g_two, g_btwo[0], g_three)


def solution(mesh):
    in_specs = (
        P("member", ("groups", "space"), None),
        P(None, ("groups", "space")),
        P(None, ("groups", "space")),
        P(("groups", "space"), None),
        P("groups"),
        P(),
        P(),
        P(),
        P(),
        P(),
    )
    out_specs = (
        P("groups"),
        P("member", ("groups", "space"), None),
        P("groups", None),
        P("groups"),
        P("groups", None),
        P("groups"),
        P("groups", None),
    )
    return jax.shard_map(
        per_device, mesh=mesh, in_specs=in_specs, out_specs=out_specs, check_vma=False
    )
```

```python
import jax
import jax.numpy as jnp
from jax import lax
from jax.experimental import pallas as pl
from jax.experimental.pallas import tpu as pltpu
from jax.sharding import PartitionSpec as P

K = 4
OBS_MEAN = 512
HALO = 256
EPSILON = 1e-05
BLOCK = 256
LANE = 128
CHUNK = 256
MIB = 1 << 20


def split(total, step):
    return [(start, min(step, total - start)) for start in range(0, total, step)]


def nt_dot(left, right):
    return lax.dot_general(
        left, right, (((1,), (1,)), ((), ())), preferred_element_type=jnp.float32
    )


def nn_dot(left, right):
    return jnp.dot(left, right, preferred_element_type=jnp.float32)


def kernel_call(body, out_shape, flops, moved, scratch=(), smem=0, operands=0):
    vmem = pl.BlockSpec(memory_space=pltpu.VMEM)
    specs = [pl.BlockSpec(memory_space=pltpu.SMEM)] * smem
    return pl.pallas_call(
        body,
        out_shape=out_shape,
        in_specs=specs + [vmem] * (operands - len(specs)),
        out_specs=jax.tree.map(lambda _: vmem, out_shape),
        scratch_shapes=list(scratch),
        compiler_params=pltpu.CompilerParams(vmem_limit_bytes=24 * MIB),
        cost_estimate=pl.CostEstimate(flops=flops, bytes_accessed=moved, transcendentals=0),
    )


def rim_starts(region_ref, length):
    odd = lax.rem(region_ref[0], 2)
    far = length - HALO
    return [pl.ds(pl.multiple_of(start, HALO), HALO) for start in ((1 - odd) * far, odd * far)]


def cut_rims(region_ref, latent_ref, member, *rim_refs):
    for ref, rows in zip(rim_refs, rim_starts(region_ref, latent_ref.shape[1])):
        ref[...] = latent_ref[member, rows]


def rims_kernel(region_ref, latent_ref, one_ref, other_ref, copy_ref):
    cut_rims(region_ref, latent_ref, 0, one_ref, other_ref)
    copy_ref[...] = latent_ref[...]


def table_kernel(region_ref, rank_ref, counts_ref, nbr_ref, weight_ref, latent_ref, table_ref, part_ref, *rim_refs):
    members, nodes, _ = latent_ref.shape
    for m in range(1, members):
        cut_rims(region_ref, latent_ref, m, *rim_refs[2 * m - 2 : 2 * m])
    ext, slots = table_ref.shape
    live = lax.broadcasted_iota(jnp.int32, (1, slots), 1) < counts_ref[region_ref[0]]
    nbr = [nbr_ref[k : k + 1, :] for k in range(K)]
    own = [jnp.where(live, weight_ref[k : k + 1, :], 0.0) for k in range(K)]
    joint = []
    for k in range(K):
        total = own[k]
        for j in range(K):
            if j != k:
                total = total + jnp.where(nbr[j] == nbr[k], own[j], 0.0)
        joint.append(total)
    groups = BLOCK // 16
    rows = (
        lax.broadcasted_iota(jnp.int32, (groups, 16, LANE), 0) * 16
        + lax.broadcasted_iota(jnp.int32, (groups, 16, LANE), 1)
    ).astype(jnp.float32).astype(jnp.bfloat16)
    turned = latent_ref[0].T
    for start, length in split(slots, CHUNK):
        for lo, size in split(length, LANE):
            lanes = slice(start + lo, start + lo + size)
            wide = [jnp.broadcast_to(joint[k][:, lanes], (16, size)).astype(jnp.bfloat16) for k in range(K)]
            for b in range(ext // BLOCK):
                tile = jnp.zeros((groups, 16, size), jnp.bfloat16)
                for k in range(K):
                    near = (nbr[k][:, lanes] - b * BLOCK).astype(jnp.float32)
                    near = jnp.broadcast_to(near, (16, size)).astype(jnp.bfloat16)
                    tile = jnp.where(rows[:, :, :size] == near[None], wide[k][None], tile)
                table_ref[b * BLOCK : (b + 1) * BLOCK, lanes] = tile.reshape(BLOCK, size)
        lanes = slice(start, start + length)
        part_ref[:, lanes] = nn_dot(turned, table_ref[HALO : HALO + nodes, lanes])


def column(ref):
    height = ref.shape[1]
    return jnp.broadcast_to(ref[...], (LANE, height)).T


def forward_kernel(
    member, region_ref, own_ref, table_ref, one_ref, other_ref, w_one_ref, b_one_ref, w_two_ref, b_two_ref, w_three_ref,
    mixed_ref, act_one_ref, slope_one_ref, act_two_ref, slope_two_ref, decoded_ref,
):
    ext, slots = table_ref.shape
    w_one, w_two, w_three = w_one_ref[...].T * 0.5, w_two_ref[...].T * 0.5, w_three_ref[...].T
    b_one, b_two = column(b_one_ref) * 0.5, column(b_two_ref) * 0.5

    def layer(weight, bias, values, size):
        half = nn_dot(weight, values) + jnp.concatenate([bias] * (size // LANE), axis=1)
        gate = 1.0 + jnp.tanh(half)
        act = half * gate
        return act.astype(jnp.bfloat16), (gate + act * (2.0 - gate)).astype(jnp.bfloat16)

    edges = jnp.concatenate([one_ref[...].T, other_ref[...].T], axis=1)
    own = own_ref[member].T if member else None
    for lo, size in split(slots, CHUNK):
        lanes = slice(lo, lo + size)
        rims = jnp.concatenate([table_ref[rows, lanes] for rows in rim_starts(region_ref, ext)], axis=0)
        share = nn_dot(own, table_ref[HALO : ext - HALO, lanes]) if member else own_ref[:, lanes]
        mixed = share + nn_dot(edges, rims)
        mixed = mixed.astype(jnp.bfloat16)
        mixed_ref[:, lanes] = mixed
        act_one, slope_one_ref[:, lanes] = layer(w_one, b_one, mixed, size)
        act_one_ref[:, lanes] = act_one
        act_two, slope_two_ref[:, lanes] = layer(w_two, b_two, act_one, size)
        act_two_ref[:, lanes] = act_two
        decoded_ref[:, lanes] = nn_dot(w_three, act_two).astype(jnp.bfloat16)


def score_kernel(mine, others, count, first, last, region_ref, counts_ref, *refs):
    own_refs, refs = refs[:mine], refs[mine:]
    other_refs, refs = refs[:others], refs[others:]
    if first:
        target_ref, refs = refs[0], refs[1:]
        old_refs, old_score = None, 0.0
    else:
        old_refs, old_score, refs = refs[:mine], refs[mine][...], refs[mine + 1 :]
    grad_refs, score_ref = refs[:mine], refs[mine]
    channels, slots = own_refs[0].shape
    inner = [(i, j) for i in range(mine) for j in range(i + 1, mine)] if first else []
    outer = [(i, mine + j) for i in range(mine) for j in range(others)]
    pairs = inner + outer
    shares = [1.0 / (count - 1)] * len(inner) + [0.5 / (count - 1)] * len(outer)
    live_count = counts_ref[region_ref[0]]

    def one_tile(at, total):
        start = pl.multiple_of(at * LANE, LANE)
        lanes = pl.ds(start, LANE)
        if first:
            turned = target_ref[lanes, :].astype(jnp.float32).T

        def rows_of(c):
            return [ref[c : c + 16, lanes].astype(jnp.float32) for ref in (*own_refs, *other_refs)]

        def fold(square):
            return square[:8] + square[8:]

        to_target = [jnp.zeros((8, LANE), jnp.float32)] * (mine if first else 0)
        apart = [jnp.zeros((8, LANE), jnp.float32)] * len(pairs)
        for c in range(0, channels, 16):
            values = rows_of(c)
            for i in range(len(to_target)):
                to_target[i] = to_target[i] + fold((values[i] - turned[c : c + 16]) ** 2)
            for p, (i, j) in enumerate(pairs):
                apart[p] = apart[p] + fold((values[i] - values[j]) ** 2)
        live = start + lax.broadcasted_iota(jnp.int32, (1, LANE), 1) < live_count
        score = jnp.zeros((1, LANE), jnp.float32)

        def inverse(square):
            squared = jnp.sum(square, axis=0, keepdims=True) + EPSILON
            inv = lax.rsqrt(squared)
            return squared * inv, inv

        inv_target, inv_pair = [], []
        for square in to_target:
            dist, inv = inverse(square)
            score = score + dist
            inv_target.append(jnp.broadcast_to(inv, (8, LANE)))
        for square, share in zip(apart, shares):
            dist, inv = inverse(square)
            score = score - dist * share
            inv_pair.append(jnp.broadcast_to(inv * (1.0 / (count - 1)), (8, LANE)))
        for c in range(0, channels, 16):
            values = rows_of(c)
            halves = []
            for h in (0, 8):
                near = [v[h : h + 8] for v in values]
                rows = slice(c + h, c + h + 8)
                if first:
                    grads = [(near[i] - turned[rows]) * inv_target[i] for i in range(mine)]
                else:
                    grads = [old_refs[i][rows, lanes] for i in range(mine)]
                for p, (i, j) in enumerate(pairs):
                    term = (near[i] - near[j]) * inv_pair[p]
                    grads[i] = grads[i] - term
                    if j < mine:
                        grads[j] = grads[j] + term
                halves.append(grads)
            for i in range(mine):
                grad = jnp.concatenate([halves[0][i], halves[1][i]], axis=0)
                if last:
                    grad = jnp.where(live, grad, 0.0)
                grad_refs[i][c : c + 16, lanes] = grad.astype(grad_refs[i].dtype)
        return total + jnp.where(live, score, 0.0)

    score_ref[...] = old_score + lax.fori_loop(0, slots // LANE, one_tile, jnp.zeros((1, LANE), jnp.float32))


def backward_kernel(members, ranks, region_ref, rank_ref, w_two_ref, w_three_ref, score_ref, *refs):
    saved = [refs[6 * m : 6 * (m + 1)] for m in range(members)]
    refs = refs[6 * members :]
    d_one_refs, piece_refs, (d_two_ref, stage_ref) = refs[:members], refs[members:-2], refs[-2:]
    w_two, w_three = w_two_ref[...] * 0.5, w_three_ref[...] * 0.5
    hidden, slots = saved[0][1].shape
    bias_one = jnp.zeros((hidden, LANE), jnp.float32)
    bias_two = jnp.zeros((hidden, LANE), jnp.float32)
    g_one, g_two, g_three = 0.0, 0.0, 0.0

    def lane_sum(values):
        return sum(values[:, lo : lo + LANE] for lo, _ in split(values.shape[1], LANE))

    for m in range(members):
        mixed_ref, act_one_ref, slope_one_ref, act_two_ref, slope_two_ref, d_dec_ref = saved[m]
        for lo, size in split(slots, CHUNK):
            lanes = slice(lo, lo + size)
            back = nn_dot(w_three, d_dec_ref[:, lanes]) * slope_two_ref[:, lanes].astype(jnp.float32)
            bias_two = bias_two + lane_sum(back)
            d_two = back.astype(jnp.bfloat16)
            d_two_ref[m, :, lanes] = d_two
            back = nn_dot(w_two, d_two) * slope_one_ref[:, lanes].astype(jnp.float32)
            bias_one = bias_one + lane_sum(back)
            d_one_refs[m][:, lanes] = back.astype(jnp.bfloat16)
        g_three = g_three + nt_dot(act_two_ref[...], d_dec_ref[...])
        g_two = g_two + nt_dot(act_one_ref[...], d_two_ref[m])
        g_one = g_one + nt_dot(mixed_ref[...], d_one_refs[m][...])
    half = hidden // 2
    region = lax.broadcasted_iota(jnp.int32, (1, hidden), 1) == region_ref[0]
    tally = jnp.where(region, jnp.sum(score_ref[...]), 0.0)
    high = tally.astype(jnp.bfloat16).astype(jnp.float32)
    parts = [
        g_one,
        g_two,
        jnp.concatenate([g_three[:half], g_three[half:]], axis=1),
        jnp.sum(bias_one.T, axis=0, keepdims=True),
        jnp.sum(bias_two.T, axis=0, keepdims=True),
        high,
        tally - high,
    ]
    used = sum(part.shape[0] for part in parts)
    parts.append(jnp.zeros((ranks * stage_ref.shape[1] - used, hidden), jnp.float32))
    stage_ref[...] = jnp.concatenate(parts, axis=0).astype(stage_ref.dtype).reshape(stage_ref.shape)
    for i in range(ranks):
        piece_refs[i][...] = stage_ref[rank_ref[0] ^ i]


def edges_kernel(members, region_ref, table_ref, w_one_ref, *refs):
    d_one_refs, d_mixed_refs, (one_ref, other_ref) = refs[:members], refs[members : 2 * members], refs[2 * members :]
    ext = table_ref.shape[0]
    rows = jnp.concatenate([table_ref[rows, :] for rows in rim_starts(region_ref, ext)], axis=0)
    for m in range(members):
        d_mixed = nn_dot(w_one_ref[...], d_one_refs[m][...]).astype(jnp.bfloat16)
        d_mixed_refs[m][...] = d_mixed
        grads = nt_dot(rows, d_mixed).astype(jnp.bfloat16)
        one_ref[m] = grads[:HALO]
        other_ref[m] = grads[HALO:]


def sum_kernel(count, *refs):
    for i in range(count):
        total = refs[i][...].astype(jnp.float32) + refs[count + i][...].astype(jnp.float32)
        refs[2 * count + i][...] = total.astype(refs[i].dtype)


def unpack_kernel(scale, rank_ref, *refs):
    *refs, stage_ref = refs
    ranks = stage_ref.shape[0]
    one_ref, b_one_ref, two_ref, b_two_ref, three_ref, tally_ref = refs[ranks:]
    for i in range(ranks):
        stage_ref[rank_ref[0] ^ i] = refs[i][...]
    width, hidden = one_ref.shape
    sums = stage_ref[...].reshape(-1, hidden).astype(jnp.float32)
    half, channels = hidden // 2, three_ref.shape[1]
    one_ref[...] = sums[:width]
    two_ref[...] = sums[width : width + hidden]
    base = width + hidden
    three_ref[:half] = sums[base : base + half, :channels]
    three_ref[half:] = sums[base : base + half, channels:]
    last = sums[base + half : base + half + 8]
    b_one_ref[...] = last[0:1]
    b_two_ref[...] = last[1:2]
    tally_ref[...] = (last[2:3] + last[3:4])[:, : tally_ref.shape[1]] * scale


def own_kernel(table_ref, *refs):
    *d_mixed_refs, own_ref = refs
    members, nodes, _ = own_ref.shape
    for m in range(members):
        own_ref[m] = nt_dot(table_ref[HALO : HALO + nodes, :], d_mixed_refs[m][...])


def finish_kernel(region_ref, own_ref, one_ref, other_ref, out_ref):
    nodes = own_ref.shape[1]
    out_ref[:, HALO : nodes - HALO] = own_ref[:, HALO : nodes - HALO].astype(jnp.bfloat16)
    for ref, rows in zip((one_ref, other_ref), rim_starts(region_ref, nodes)):
        out_ref[:, rows] = (own_ref[:, rows] + ref[...].astype(jnp.float32)).astype(jnp.bfloat16)


def exchanged(block, second):
    size = lax.axis_size("space")
    pairs = [(i, (i + 1) % size if i % 2 else (i - 1) % size) if second else (i, i ^ 1) for i in range(size)]
    return lax.ppermute(block, "space", pairs)


def swapped(block, axis, by):
    return lax.ppermute(block, axis, [(i, i ^ by) for i in range(lax.axis_size(axis))])


def per_device(latent, neighbours, weights, targets, counts, w_one, b_one, w_two, b_two, w_three):
    members, nodes, width = latent.shape
    slots, channels = targets.shape
    hidden = w_one.shape[1]
    ext = nodes + 2 * HALO
    region, regions = lax.axis_index("space"), lax.axis_size("space")
    rank, ranks = lax.axis_index("member"), lax.axis_size("member")
    share = slots // ranks
    bf16, f32 = jnp.bfloat16, jnp.float32
    shape = jax.ShapeDtypeStruct
    each = range(members)

    edge = shape((HALO, width), bf16)
    region_at = region[None].astype(jnp.int32)
    *rims, latent = kernel_call(
        rims_kernel, (edge, edge, shape(latent.shape, bf16)), flops=4 << 30, moved=3 * MIB, smem=1, operands=2
    )(region_at, latent)
    halo = [[exchanged(rims[0], False), exchanged(rims[1], True)]]
    rank_at = rank[None].astype(jnp.int32)

    table, part, *rims = kernel_call(
        table_kernel,
        (shape((ext, slots), bf16), shape((width, slots), f32)) + (edge,) * (2 * members - 2),
        flops=2 * width * nodes * slots,
        moved=12 * MIB,
        smem=3,
        operands=6,
    )(region_at, rank_at, counts, neighbours, weights, latent)
    halo += [[exchanged(rims[2 * m], False), exchanged(rims[2 * m + 1], True)] for m in range(members - 1)]

    saved_shape = shape((hidden, slots), bf16)
    mixed_shape = shape((width, slots), bf16)
    decoded_shape = shape((channels, slots), bf16)
    dense = width * hidden + hidden * hidden + hidden * channels
    saved, decoded, beside, across = [], [], [], []
    for m in each:
        *kept, block = kernel_call(
            lambda *refs: forward_kernel(m, *refs),
            (mixed_shape,) + (saved_shape,) * 4 + (decoded_shape,),
            flops=2 * slots * ((ext if m else 2 * HALO) * width + dense),
            moved=8 * MIB,
            smem=1,
            operands=10,
        )(region_at, latent if m else part, table, *halo[m], w_one, b_one[None], w_two, b_two[None], w_three)
        saved.append(kept)
        decoded.append(block)
        blocks, bit = {0: block}, 2
        while bit < ranks:
            blocks.update({i ^ bit: swapped(blocks[i], "member", bit) for i in sorted(blocks)})
            bit = 2 * bit
        across.append([blocks[i] for i in sorted(blocks) if i])
        beside.append(swapped(block, "member", 1))

    def scored(others, carried, first=False, last=False):
        operands = (region_at, counts, *decoded, *others, *carried)
        return kernel_call(
            lambda *refs: score_kernel(members, len(others), members * ranks, first, last, *refs),
            (shape((channels, slots), bf16 if last else f32),) * members + (shape((1, LANE), f32),),
            flops=4 * MIB,
            moved=2 * MIB,
            smem=2,
            operands=len(operands),
        )(*operands)

    carried = scored(beside + [block for blocks in across[:-1] for block in blocks], [targets], first=True)
    across[-1], carried = lax.optimization_barrier((across[-1], carried))
    others = [*across[-1]] + [swapped(block, "member", 1) for blocks in across for block in blocks]
    *grads, score = scored(others, carried, last=True)

    rows = -(-(width + hidden + hidden // 2 + 4) // (16 * ranks)) * 16
    piece = shape((rows, hidden), bf16)
    operands = [region_at, rank_at, w_two, w_three, score]
    for m in each:
        operands += [*saved[m], grads[m]]
    out = kernel_call(
        lambda *refs: backward_kernel(members, ranks, *refs),
        (saved_shape,) * members + (piece,) * ranks,
        flops=4 * members * slots * dense,
        moved=10 * MIB,
        scratch=(pltpu.VMEM((members, hidden, slots), bf16), pltpu.VMEM((ranks, rows, hidden), bf16)),
        smem=2,
        operands=len(operands),
    )(*operands)
    d_one, pieces = out[:members], out[members:]

    def summed(ones, others):
        return kernel_call(
            lambda *refs: sum_kernel(len(ones), *refs), (piece,) * len(ones), flops=MIB, moved=MIB, operands=2 * len(ones)
        )(*ones, *others)

    out = kernel_call(
        lambda *refs: edges_kernel(members, *refs),
        (mixed_shape,) * members + (shape((members, HALO, width), bf16),) * 2,
        flops=2 * members * slots * width * (hidden + 2 * HALO),
        moved=6 * MIB,
        smem=1,
        operands=3 + members,
    )(region_at, table, w_one, *d_one)
    d_mixed, rims = out[:members], out[members:]

    bit = 1
    while bit < ranks:
        received = [swapped(sent, "member", bit) for sent in pieces[1::2]]
        if bit == 1:
            received, rims = lax.optimization_barrier((received, rims))
        pieces = summed(pieces[::2], received)
        bit = 2 * bit
    own = kernel_call(
        own_kernel,
        shape((members, nodes, width), f32),
        flops=2 * members * nodes * width * slots,
        moved=6 * MIB,
        operands=1 + members,
    )(table, *d_mixed)
    other = exchanged(rims[1], True)
    (total,) = pieces
    step = 1
    while step < regions:
        received = swapped(total, "space", step)
        step = 2 * step
        if step == regions:
            received, other = lax.optimization_barrier((received, other))
        (total,) = summed([total], [received])
        if 2 * step == regions:
            total, own, rims = lax.optimization_barrier((total, own, rims))
            one = exchanged(rims[0], False)
    totals = {0: total}
    bit = 2
    while bit < ranks:
        totals.update({i ^ bit: swapped(totals[i], "member", bit) for i in sorted(totals)})
        bit = 2 * bit
    totals.update({i ^ 1: swapped(block, "member", 1) for i, block in totals.items()})
    latent_grad = kernel_call(
        finish_kernel,
        shape((members, nodes, width), bf16),
        flops=MIB,
        moved=3 * MIB,
        smem=1,
        operands=4,
    )(region_at, own, one, other)
    totals = [totals[i] for i in range(ranks)]
    totals, latent_grad = lax.optimization_barrier((totals, latent_grad))
    row = shape((1, hidden), f32)
    g_one, g_bone, g_two, g_btwo, g_three, tally = kernel_call(
        lambda *refs: unpack_kernel(1.0 / (OBS_MEAN * members * ranks), *refs),
        (shape((width, hidden), f32), row, shape((hidden, hidden), f32), row, shape((hidden, channels), f32),
         shape((1, regions), f32)),
        flops=MIB,
        moved=2 * MIB,
        scratch=(pltpu.VMEM((ranks, rows, hidden), bf16),),
        smem=1,
        operands=1 + ranks,
    )(rank_at, *totals)
    return (tally[0], latent_grad, g_one, g_bone[0], g_two, g_btwo[0], g_three)


def solution(mesh):
    in_specs = (
        P("member", ("groups", "space"), None),
        P(None, ("groups", "space")),
        P(None, ("groups", "space")),
        P(("groups", "space"), None),
        P("groups"),
        P(),
        P(),
        P(),
        P(),
        P(),
    )
    out_specs = (
        P("groups"),
        P("member", ("groups", "space"), None),
        P("groups", None),
        P("groups"),
        P("groups", None),
        P("groups"),
        P("groups", None),
    )
    return jax.shard_map(
        per_device, mesh=mesh, in_specs=in_specs, out_specs=out_specs, check_vma=False
    )
```

```python
import jax
import jax.numpy as jnp
from jax import lax
from jax.experimental import pallas as pl
from jax.experimental.pallas import tpu as pltpu
from jax.sharding import PartitionSpec as P

K = 4
OBS_MEAN = 512
HALO = 256
EPSILON = 1e-05
BLOCK = 256
LANE = 128
CHUNK = 768
MIB = 1 << 20


def split(total, step):
    return [(start, min(step, total - start)) for start in range(0, total, step)]


def nt_dot(left, right):
    return lax.dot_general(
        left, right, (((1,), (1,)), ((), ())), preferred_element_type=jnp.float32
    )


def nn_dot(left, right):
    return jnp.dot(left, right, preferred_element_type=jnp.float32)


def kernel_call(body, out_shape, flops, moved, scratch=(), smem=0, operands=0):
    vmem = pl.BlockSpec(memory_space=pltpu.VMEM)
    specs = [pl.BlockSpec(memory_space=pltpu.SMEM)] * smem
    return pl.pallas_call(
        body,
        out_shape=out_shape,
        in_specs=specs + [vmem] * (operands - len(specs)),
        out_specs=jax.tree.map(lambda _: vmem, out_shape),
        scratch_shapes=list(scratch),
        compiler_params=pltpu.CompilerParams(vmem_limit_bytes=24 * MIB),
        cost_estimate=pl.CostEstimate(flops=flops, bytes_accessed=moved, transcendentals=0),
    )


def rim_starts(region_ref, length):
    odd = lax.rem(region_ref[0], 2)
    far = length - HALO
    return [pl.ds(pl.multiple_of(start, HALO), HALO) for start in ((1 - odd) * far, odd * far)]


def cut_rims(region_ref, latent_ref, member, *rim_refs):
    for ref, rows in zip(rim_refs, rim_starts(region_ref, latent_ref.shape[1])):
        ref[...] = latent_ref[member, rows]


def rims_kernel(region_ref, latent_ref, one_ref, other_ref, copy_ref):
    cut_rims(region_ref, latent_ref, 0, one_ref, other_ref)
    copy_ref[...] = latent_ref[...]


def table_kernel(region_ref, rank_ref, counts_ref, nbr_ref, weight_ref, latent_ref, table_ref, part_ref, *rim_refs):
    members, nodes, _ = latent_ref.shape
    for m in range(1, members):
        cut_rims(region_ref, latent_ref, m, *rim_refs[2 * m - 2 : 2 * m])
    ext, slots = table_ref.shape
    live = lax.broadcasted_iota(jnp.int32, (1, slots), 1) < counts_ref[region_ref[0]]
    nbr = [nbr_ref[k : k + 1, :] for k in range(K)]
    own = [jnp.where(live, weight_ref[k : k + 1, :], 0.0) for k in range(K)]
    joint = []
    for k in range(K):
        total = own[k]
        for j in range(K):
            if j != k:
                total = total + jnp.where(nbr[j] == nbr[k], own[j], 0.0)
        joint.append(total)
    groups = BLOCK // 16
    rows = (
        lax.broadcasted_iota(jnp.int32, (groups, 16, LANE), 0) * 16
        + lax.broadcasted_iota(jnp.int32, (groups, 16, LANE), 1)
    ).astype(jnp.float32).astype(jnp.bfloat16)
    turned = latent_ref[0].T
    for start, length in split(slots, CHUNK):
        for lo, size in split(length, LANE):
            lanes = slice(start + lo, start + lo + size)
            wide = [jnp.broadcast_to(joint[k][:, lanes], (16, size)).astype(jnp.bfloat16) for k in range(K)]
            for b in range(ext // BLOCK):
                tile = jnp.zeros((groups, 16, size), jnp.bfloat16)
                for k in range(K):
                    near = (nbr[k][:, lanes] - b * BLOCK).astype(jnp.float32)
                    near = jnp.broadcast_to(near, (16, size)).astype(jnp.bfloat16)
                    tile = jnp.where(rows[:, :, :size] == near[None], wide[k][None], tile)
                table_ref[b * BLOCK : (b + 1) * BLOCK, lanes] = tile.reshape(BLOCK, size)
        lanes = slice(start, start + length)
        part_ref[:, lanes] = nn_dot(turned, table_ref[HALO : HALO + nodes, lanes])


def column(ref):
    height = ref.shape[1]
    return jnp.broadcast_to(ref[...], (LANE, height)).T


def forward_kernel(
    member, region_ref, own_ref, table_ref, one_ref, other_ref, w_one_ref, b_one_ref, w_two_ref, b_two_ref, w_three_ref,
    mixed_ref, act_one_ref, slope_one_ref, act_two_ref, slope_two_ref, decoded_ref,
):
    ext, slots = table_ref.shape
    w_one, w_two, w_three = w_one_ref[...].T * 0.5, w_two_ref[...].T * 0.5, w_three_ref[...].T
    b_one, b_two = column(b_one_ref) * 0.5, column(b_two_ref) * 0.5

    def layer(weight, bias, values, size):
        half = nn_dot(weight, values) + jnp.concatenate([bias] * (size // LANE), axis=1)
        gate = 1.0 + jnp.tanh(half)
        act = half * gate
        return act.astype(jnp.bfloat16), (gate + act * (2.0 - gate)).astype(jnp.bfloat16)

    edges = jnp.concatenate([one_ref[...].T, other_ref[...].T], axis=1)
    own = own_ref[member].T if member else None
    for lo, size in split(slots, CHUNK):
        lanes = slice(lo, lo + size)
        rims = jnp.concatenate([table_ref[rows, lanes] for rows in rim_starts(region_ref, ext)], axis=0)
        share = nn_dot(own, table_ref[HALO : ext - HALO, lanes]) if member else own_ref[:, lanes]
        mixed = share + nn_dot(edges, rims)
        mixed = mixed.astype(jnp.bfloat16)
        mixed_ref[:, lanes] = mixed
        act_one, slope_one_ref[:, lanes] = layer(w_one, b_one, mixed, size)
        act_one_ref[:, lanes] = act_one
        act_two, slope_two_ref[:, lanes] = layer(w_two, b_two, act_one, size)
        act_two_ref[:, lanes] = act_two
        decoded_ref[:, lanes] = nn_dot(w_three, act_two).astype(jnp.bfloat16)


def score_kernel(mine, others, count, first, last, region_ref, counts_ref, *refs):
    own_refs, refs = refs[:mine], refs[mine:]
    other_refs, refs = refs[:others], refs[others:]
    if first:
        target_ref, refs = refs[0], refs[1:]
        old_refs, old_score = None, 0.0
    else:
        old_refs, old_score, refs = refs[:mine], refs[mine][...], refs[mine + 1 :]
    grad_refs, score_ref = refs[:mine], refs[mine]
    channels, slots = own_refs[0].shape
    inner = [(i, j) for i in range(mine) for j in range(i + 1, mine)] if first else []
    outer = [(i, mine + j) for i in range(mine) for j in range(others)]
    pairs = inner + outer
    shares = [1.0 / (count - 1)] * len(inner) + [0.5 / (count - 1)] * len(outer)
    live_count = counts_ref[region_ref[0]]

    def one_tile(at, total):
        start = pl.multiple_of(at * LANE, LANE)
        lanes = pl.ds(start, LANE)
        if first:
            turned = target_ref[lanes, :].astype(jnp.float32).T

        def rows_of(c):
            return [ref[c : c + 16, lanes].astype(jnp.float32) for ref in (*own_refs, *other_refs)]

        def fold(square):
            return square[:8] + square[8:]

        to_target = [jnp.zeros((8, LANE), jnp.float32)] * (mine if first else 0)
        apart = [jnp.zeros((8, LANE), jnp.float32)] * len(pairs)
        for c in range(0, channels, 16):
            values = rows_of(c)
            for i in range(len(to_target)):
                to_target[i] = to_target[i] + fold((values[i] - turned[c : c + 16]) ** 2)
            for p, (i, j) in enumerate(pairs):
                apart[p] = apart[p] + fold((values[i] - values[j]) ** 2)
        live = start + lax.broadcasted_iota(jnp.int32, (1, LANE), 1) < live_count
        score = jnp.zeros((1, LANE), jnp.float32)

        def inverse(square):
            squared = jnp.sum(square, axis=0, keepdims=True) + EPSILON
            inv = lax.rsqrt(squared)
            return squared * inv, inv

        inv_target, inv_pair = [], []
        for square in to_target:
            dist, inv = inverse(square)
            score = score + dist
            inv_target.append(jnp.broadcast_to(inv, (8, LANE)))
        for square, share in zip(apart, shares):
            dist, inv = inverse(square)
            score = score - dist * share
            inv_pair.append(jnp.broadcast_to(inv * (1.0 / (count - 1)), (8, LANE)))
        for c in range(0, channels, 16):
            values = rows_of(c)
            halves = []
            for h in (0, 8):
                near = [v[h : h + 8] for v in values]
                rows = slice(c + h, c + h + 8)
                if first:
                    grads = [(near[i] - turned[rows]) * inv_target[i] for i in range(mine)]
                else:
                    grads = [old_refs[i][rows, lanes] for i in range(mine)]
                for p, (i, j) in enumerate(pairs):
                    term = (near[i] - near[j]) * inv_pair[p]
                    grads[i] = grads[i] - term
                    if j < mine:
                        grads[j] = grads[j] + term
                halves.append(grads)
            for i in range(mine):
                grad = jnp.concatenate([halves[0][i], halves[1][i]], axis=0)
                if last:
                    grad = jnp.where(live, grad, 0.0)
                grad_refs[i][c : c + 16, lanes] = grad.astype(grad_refs[i].dtype)
        return total + jnp.where(live, score, 0.0)

    score_ref[...] = old_score + lax.fori_loop(0, slots // LANE, one_tile, jnp.zeros((1, LANE), jnp.float32))


def backward_kernel(members, ranks, region_ref, rank_ref, w_two_ref, w_three_ref, score_ref, *refs):
    saved = [refs[6 * m : 6 * (m + 1)] for m in range(members)]
    refs = refs[6 * members :]
    d_one_refs, piece_refs, (d_two_ref, stage_ref) = refs[:members], refs[members:-2], refs[-2:]
    w_two, w_three = w_two_ref[...] * 0.5, w_three_ref[...] * 0.5
    hidden, slots = saved[0][1].shape
    bias_one = jnp.zeros((hidden, LANE), jnp.float32)
    bias_two = jnp.zeros((hidden, LANE), jnp.float32)
    g_one, g_two, g_three = 0.0, 0.0, 0.0

    def lane_sum(values):
        return sum(values[:, lo : lo + LANE] for lo, _ in split(values.shape[1], LANE))

    for m in range(members):
        mixed_ref, act_one_ref, slope_one_ref, act_two_ref, slope_two_ref, d_dec_ref = saved[m]
        for lo, size in split(slots, CHUNK):
            lanes = slice(lo, lo + size)
            back = nn_dot(w_three, d_dec_ref[:, lanes]) * slope_two_ref[:, lanes].astype(jnp.float32)
            bias_two = bias_two + lane_sum(back)
            d_two = back.astype(jnp.bfloat16)
            d_two_ref[m, :, lanes] = d_two
            back = nn_dot(w_two, d_two) * slope_one_ref[:, lanes].astype(jnp.float32)
            bias_one = bias_one + lane_sum(back)
            d_one_refs[m][:, lanes] = back.astype(jnp.bfloat16)
        g_three = g_three + nt_dot(act_two_ref[...], d_dec_ref[...])
        g_two = g_two + nt_dot(act_one_ref[...], d_two_ref[m])
        g_one = g_one + nt_dot(mixed_ref[...], d_one_refs[m][...])
    half = hidden // 2
    region = lax.broadcasted_iota(jnp.int32, (1, hidden), 1) == region_ref[0]
    tally = jnp.where(region, jnp.sum(score_ref[...]), 0.0)
    high = tally.astype(jnp.bfloat16).astype(jnp.float32)
    parts = [
        g_one,
        g_two,
        jnp.concatenate([g_three[:half], g_three[half:]], axis=1),
        jnp.sum(bias_one.T, axis=0, keepdims=True),
        jnp.sum(bias_two.T, axis=0, keepdims=True),
        high,
        tally - high,
    ]
    used = sum(part.shape[0] for part in parts)
    parts.append(jnp.zeros((ranks * stage_ref.shape[1] - used, hidden), jnp.float32))
    stage_ref[...] = jnp.concatenate(parts, axis=0).astype(stage_ref.dtype).reshape(stage_ref.shape)
    for i in range(ranks):
        piece_refs[i][...] = stage_ref[rank_ref[0] ^ i]


def edges_kernel(members, region_ref, table_ref, w_one_ref, *refs):
    d_one_refs, d_mixed_refs, (one_ref, *other_refs) = refs[:members], refs[members : 2 * members], refs[2 * members :]
    ext = table_ref.shape[0]
    rows = jnp.concatenate([table_ref[rows, :] for rows in rim_starts(region_ref, ext)], axis=0)
    for m in range(members):
        d_mixed = nn_dot(w_one_ref[...], d_one_refs[m][...]).astype(jnp.bfloat16)
        d_mixed_refs[m][...] = d_mixed
        grads = nt_dot(rows, d_mixed).astype(jnp.bfloat16)
        one_ref[m] = grads[:HALO]
        other_refs[m][...] = grads[HALO:]


def sum_kernel(count, *refs):
    for i in range(count):
        total = refs[i][...].astype(jnp.float32) + refs[count + i][...].astype(jnp.float32)
        refs[2 * count + i][...] = total.astype(refs[i].dtype)


def unpack_kernel(scale, rank_ref, *refs):
    *refs, stage_ref = refs
    ranks = stage_ref.shape[0]
    one_ref, b_one_ref, two_ref, b_two_ref, three_ref, tally_ref = refs[ranks:]
    for i in range(ranks):
        stage_ref[rank_ref[0] ^ i] = refs[i][...]
    width, hidden = one_ref.shape
    sums = stage_ref[...].reshape(-1, hidden).astype(jnp.float32)
    half, channels = hidden // 2, three_ref.shape[1]
    one_ref[...] = sums[:width]
    two_ref[...] = sums[width : width + hidden]
    base = width + hidden
    three_ref[:half] = sums[base : base + half, :channels]
    three_ref[half:] = sums[base : base + half, channels:]
    last = sums[base + half : base + half + 8]
    b_one_ref[...] = last[0:1]
    b_two_ref[...] = last[1:2]
    tally_ref[...] = (last[2:3] + last[3:4])[:, : tally_ref.shape[1]] * scale


def own_kernel(table_ref, *refs):
    *d_mixed_refs, own_ref = refs
    members, nodes, _ = own_ref.shape
    for m in range(members):
        own_ref[m] = nt_dot(table_ref[HALO : HALO + nodes, :], d_mixed_refs[m][...])


def finish_kernel(region_ref, own_ref, one_ref, *refs):
    *other_refs, out_ref = refs
    members, nodes, _ = own_ref.shape
    out_ref[:, HALO : nodes - HALO] = own_ref[:, HALO : nodes - HALO].astype(jnp.bfloat16)
    one_rows, other_rows = rim_starts(region_ref, nodes)
    out_ref[:, one_rows] = (own_ref[:, one_rows] + one_ref[...].astype(jnp.float32)).astype(jnp.bfloat16)
    for m in range(members):
        rows = own_ref[m, other_rows] + other_refs[m][...].astype(jnp.float32)
        out_ref[m, other_rows] = rows.astype(jnp.bfloat16)


def exchanged(block, second):
    size = lax.axis_size("space")
    pairs = [(i, (i + 1) % size if i % 2 else (i - 1) % size) if second else (i, i ^ 1) for i in range(size)]
    return lax.ppermute(block, "space", pairs)


def swapped(block, axis, by):
    return lax.ppermute(block, axis, [(i, i ^ by) for i in range(lax.axis_size(axis))])


def per_device(latent, neighbours, weights, targets, counts, w_one, b_one, w_two, b_two, w_three):
    members, nodes, width = latent.shape
    slots, channels = targets.shape
    hidden = w_one.shape[1]
    ext = nodes + 2 * HALO
    region, regions = lax.axis_index("space"), lax.axis_size("space")
    rank, ranks = lax.axis_index("member"), lax.axis_size("member")
    share = slots // ranks
    bf16, f32 = jnp.bfloat16, jnp.float32
    shape = jax.ShapeDtypeStruct
    each = range(members)

    edge = shape((HALO, width), bf16)
    region_at = region[None].astype(jnp.int32)
    *rims, latent = kernel_call(
        rims_kernel, (edge, edge, shape(latent.shape, bf16)), flops=4 << 30, moved=3 * MIB, smem=1, operands=2
    )(region_at, latent)
    halo = [[exchanged(rims[0], False), exchanged(rims[1], True)]]
    rank_at = rank[None].astype(jnp.int32)

    table, part, *rims = kernel_call(
        table_kernel,
        (shape((ext, slots), bf16), shape((width, slots), f32)) + (edge,) * (2 * members - 2),
        flops=2 * width * nodes * slots,
        moved=12 * MIB,
        smem=3,
        operands=6,
    )(region_at, rank_at, counts, neighbours, weights, latent)
    halo += [[exchanged(rims[2 * m], False), exchanged(rims[2 * m + 1], True)] for m in range(members - 1)]

    saved_shape = shape((hidden, slots), bf16)
    mixed_shape = shape((width, slots), bf16)
    decoded_shape = shape((channels, slots), bf16)
    dense = width * hidden + hidden * hidden + hidden * channels
    saved, decoded, beside, across = [], [], [], []
    for m in each:
        *kept, block = kernel_call(
            lambda *refs: forward_kernel(m, *refs),
            (mixed_shape,) + (saved_shape,) * 4 + (decoded_shape,),
            flops=2 * slots * ((ext if m else 2 * HALO) * width + dense),
            moved=8 * MIB,
            smem=1,
            operands=10,
        )(region_at, latent if m else part, table, *halo[m], w_one, b_one[None], w_two, b_two[None], w_three)
        saved.append(kept)
        decoded.append(block)
        blocks, bit = {0: block}, 2
        while bit < ranks:
            blocks.update({i ^ bit: swapped(blocks[i], "member", bit) for i in sorted(blocks)})
            bit = 2 * bit
        across.append([blocks[i] for i in sorted(blocks) if i])
        beside.append(swapped(block, "member", 1))

    def scored(others, carried, first=False, last=False):
        operands = (region_at, counts, *decoded, *others, *carried)
        return kernel_call(
            lambda *refs: score_kernel(members, len(others), members * ranks, first, last, *refs),
            (shape((channels, slots), bf16 if last else f32),) * members + (shape((1, LANE), f32),),
            flops=4 * MIB,
            moved=2 * MIB,
            smem=2,
            operands=len(operands),
        )(*operands)

    carried = scored(beside + [block for blocks in across[:-1] for block in blocks], [targets], first=True)
    across[-1], carried = lax.optimization_barrier((across[-1], carried))
    others = [*across[-1]] + [swapped(block, "member", 1) for blocks in across for block in blocks]
    *grads, score = scored(others, carried, last=True)

    rows = -(-(width + hidden + hidden // 2 + 4) // (16 * ranks)) * 16
    piece = shape((rows, hidden), bf16)
    operands = [region_at, rank_at, w_two, w_three, score]
    for m in each:
        operands += [*saved[m], grads[m]]
    out = kernel_call(
        lambda *refs: backward_kernel(members, ranks, *refs),
        (saved_shape,) * members + (piece,) * ranks,
        flops=4 * members * slots * dense,
        moved=10 * MIB,
        scratch=(pltpu.VMEM((members, hidden, slots), bf16), pltpu.VMEM((ranks, rows, hidden), bf16)),
        smem=2,
        operands=len(operands),
    )(*operands)
    d_one, pieces = out[:members], out[members:]

    def summed(ones, others):
        return kernel_call(
            lambda *refs: sum_kernel(len(ones), *refs), (piece,) * len(ones), flops=MIB, moved=MIB, operands=2 * len(ones)
        )(*ones, *others)

    out = kernel_call(
        lambda *refs: edges_kernel(members, *refs),
        (mixed_shape,) * members + (shape((members, HALO, width), bf16),) + (edge,) * members,
        flops=2 * members * slots * width * (hidden + 2 * HALO),
        moved=6 * MIB,
        smem=1,
        operands=3 + members,
    )(region_at, table, w_one, *d_one)
    d_mixed, rims = out[:members], out[members:]

    bit = 1
    while bit < ranks:
        received = [swapped(sent, "member", bit) for sent in pieces[1::2]]
        if bit == 1:
            received, rims = lax.optimization_barrier((received, rims))
        pieces = summed(pieces[::2], received)
        bit = 2 * bit
    own = kernel_call(
        own_kernel,
        shape((members, nodes, width), f32),
        flops=2 * members * nodes * width * slots,
        moved=6 * MIB,
        operands=1 + members,
    )(table, *d_mixed)
    other = [exchanged(block, True) for block in rims[1:]]
    (total,) = pieces
    step = 1
    while step < regions:
        received = swapped(total, "space", step)
        step = 2 * step
        if step == regions:
            received, other, own = lax.optimization_barrier((received, other, own))
        (total,) = summed([total], [received])
        if 2 * step == regions:
            total, rims = lax.optimization_barrier((total, rims))
            one = exchanged(rims[0], False)
    totals = {0: total}
    bit = 2
    while bit < ranks:
        totals.update({i ^ bit: swapped(totals[i], "member", bit) for i in sorted(totals)})
        bit = 2 * bit
    totals.update({i ^ 1: swapped(block, "member", 1) for i, block in totals.items()})
    latent_grad = kernel_call(
        finish_kernel,
        shape((members, nodes, width), bf16),
        flops=MIB,
        moved=3 * MIB,
        smem=1,
        operands=3 + members,
    )(region_at, own, one, *other)
    totals = [totals[i] for i in range(ranks)]
    totals, latent_grad = lax.optimization_barrier((totals, latent_grad))
    row = shape((1, hidden), f32)
    g_one, g_bone, g_two, g_btwo, g_three, tally = kernel_call(
        lambda *refs: unpack_kernel(1.0 / (OBS_MEAN * members * ranks), *refs),
        (shape((width, hidden), f32), row, shape((hidden, hidden), f32), row, shape((hidden, channels), f32),
         shape((1, regions), f32)),
        flops=MIB,
        moved=2 * MIB,
        scratch=(pltpu.VMEM((ranks, rows, hidden), bf16),),
        smem=1,
        operands=1 + ranks,
    )(rank_at, *totals)
    return (tally[0], latent_grad, g_one, g_bone[0], g_two, g_btwo[0], g_three)


def solution(mesh):
    in_specs = (
        P("member", ("groups", "space"), None),
        P(None, ("groups", "space")),
        P(None, ("groups", "space")),
        P(("groups", "space"), None),
        P("groups"),
        P(),
        P(),
        P(),
        P(),
        P(),
    )
    out_specs = (
        P("groups"),
        P("member", ("groups", "space"), None),
        P("groups", None),
        P("groups"),
        P("groups", None),
        P("groups"),
        P("groups", None),
    )
    return jax.shard_map(
        per_device, mesh=mesh, in_specs=in_specs, out_specs=out_specs, check_vma=False
    )
```

```python
import jax
import jax.numpy as jnp
from jax import lax
from jax.experimental import pallas as pl
from jax.experimental.pallas import tpu as pltpu
from jax.sharding import PartitionSpec as P

K = 4
OBS_MEAN = 512
HALO = 256
EPSILON = 1e-05
BLOCK = 256
LANE = 128
CHUNK = 768
BACK_CHUNK = 512
MIB = 1 << 20


def split(total, step):
    return [(start, min(step, total - start)) for start in range(0, total, step)]


def nt_dot(left, right):
    return lax.dot_general(
        left, right, (((1,), (1,)), ((), ())), preferred_element_type=jnp.float32
    )


def nn_dot(left, right):
    return jnp.dot(left, right, preferred_element_type=jnp.float32)


def kernel_call(body, out_shape, flops, moved, scratch=(), smem=0, operands=0):
    vmem = pl.BlockSpec(memory_space=pltpu.VMEM)
    specs = [pl.BlockSpec(memory_space=pltpu.SMEM)] * smem
    return pl.pallas_call(
        body,
        out_shape=out_shape,
        in_specs=specs + [vmem] * (operands - len(specs)),
        out_specs=jax.tree.map(lambda _: vmem, out_shape),
        scratch_shapes=list(scratch),
        compiler_params=pltpu.CompilerParams(vmem_limit_bytes=24 * MIB),
        cost_estimate=pl.CostEstimate(flops=flops, bytes_accessed=moved, transcendentals=0),
    )


def rim_starts(region_ref, length):
    odd = lax.rem(region_ref[0], 2)
    far = length - HALO
    return [pl.ds(pl.multiple_of(start, HALO), HALO) for start in ((1 - odd) * far, odd * far)]


def cut_rims(region_ref, latent_ref, member, *rim_refs):
    for ref, rows in zip(rim_refs, rim_starts(region_ref, latent_ref.shape[1])):
        ref[...] = latent_ref[member, rows]


def rims_kernel(region_ref, latent_ref, one_ref, other_ref, copy_ref):
    cut_rims(region_ref, latent_ref, 0, one_ref, other_ref)
    copy_ref[...] = latent_ref[...]


def table_kernel(region_ref, rank_ref, counts_ref, nbr_ref, weight_ref, latent_ref, table_ref, part_ref, *rim_refs):
    members, nodes, _ = latent_ref.shape
    for m in range(1, members):
        cut_rims(region_ref, latent_ref, m, *rim_refs[2 * m - 2 : 2 * m])
    ext, slots = table_ref.shape
    live = lax.broadcasted_iota(jnp.int32, (1, slots), 1) < counts_ref[region_ref[0]]
    nbr = [nbr_ref[k : k + 1, :] for k in range(K)]
    own = [jnp.where(live, weight_ref[k : k + 1, :], 0.0) for k in range(K)]
    joint = []
    for k in range(K):
        total = own[k]
        for j in range(K):
            if j != k:
                total = total + jnp.where(nbr[j] == nbr[k], own[j], 0.0)
        joint.append(total)
    groups = BLOCK // 16
    rows = (
        lax.broadcasted_iota(jnp.int32, (groups, 16, LANE), 0) * 16
        + lax.broadcasted_iota(jnp.int32, (groups, 16, LANE), 1)
    ).astype(jnp.float32).astype(jnp.bfloat16)
    turned = latent_ref[0].T
    for start, length in split(slots, CHUNK):
        for lo, size in split(length, LANE):
            lanes = slice(start + lo, start + lo + size)
            wide = [jnp.broadcast_to(joint[k][:, lanes], (16, size)).astype(jnp.bfloat16) for k in range(K)]
            for b in range(ext // BLOCK):
                tile = jnp.zeros((groups, 16, size), jnp.bfloat16)
                for k in range(K):
                    near = (nbr[k][:, lanes] - b * BLOCK).astype(jnp.float32)
                    near = jnp.broadcast_to(near, (16, size)).astype(jnp.bfloat16)
                    tile = jnp.where(rows[:, :, :size] == near[None], wide[k][None], tile)
                table_ref[b * BLOCK : (b + 1) * BLOCK, lanes] = tile.reshape(BLOCK, size)
        lanes = slice(start, start + length)
        part_ref[:, lanes] = nn_dot(turned, table_ref[HALO : HALO + nodes, lanes])


def column(ref):
    height = ref.shape[1]
    return jnp.broadcast_to(ref[...], (LANE, height)).T


def forward_kernel(
    member, region_ref, own_ref, table_ref, one_ref, other_ref, w_one_ref, b_one_ref, w_two_ref, b_two_ref, w_three_ref,
    mixed_ref, act_one_ref, slope_one_ref, act_two_ref, slope_two_ref, decoded_ref,
):
    ext, slots = table_ref.shape
    w_one, w_two, w_three = w_one_ref[...].T * 0.5, w_two_ref[...].T * 0.5, w_three_ref[...].T
    b_one, b_two = column(b_one_ref) * 0.5, column(b_two_ref) * 0.5

    def layer(weight, bias, values, size):
        half = nn_dot(weight, values) + jnp.concatenate([bias] * (size // LANE), axis=1)
        gate = 1.0 + jnp.tanh(half)
        act = half * gate
        return act.astype(jnp.bfloat16), (gate + act * (2.0 - gate)).astype(jnp.bfloat16)

    edges = jnp.concatenate([one_ref[...].T, other_ref[...].T], axis=1)
    own = own_ref[member].T if member else None
    for lo, size in split(slots, CHUNK):
        lanes = slice(lo, lo + size)
        rims = jnp.concatenate([table_ref[rows, lanes] for rows in rim_starts(region_ref, ext)], axis=0)
        share = nn_dot(own, table_ref[HALO : ext - HALO, lanes]) if member else own_ref[:, lanes]
        mixed = share + nn_dot(edges, rims)
        mixed = mixed.astype(jnp.bfloat16)
        mixed_ref[:, lanes] = mixed
        act_one, slope_one_ref[:, lanes] = layer(w_one, b_one, mixed, size)
        act_one_ref[:, lanes] = act_one
        act_two, slope_two_ref[:, lanes] = layer(w_two, b_two, act_one, size)
        act_two_ref[:, lanes] = act_two
        decoded_ref[:, lanes] = nn_dot(w_three, act_two).astype(jnp.bfloat16)


def score_kernel(mine, others, count, first, last, region_ref, counts_ref, *refs):
    own_refs, refs = refs[:mine], refs[mine:]
    other_refs, refs = refs[:others], refs[others:]
    if first:
        target_ref, refs = refs[0], refs[1:]
        old_refs, old_score = None, 0.0
    else:
        old_refs, old_score, refs = refs[:mine], refs[mine][...], refs[mine + 1 :]
    grad_refs, score_ref = refs[:mine], refs[mine]
    channels, slots = own_refs[0].shape
    inner = [(i, j) for i in range(mine) for j in range(i + 1, mine)] if first else []
    outer = [(i, mine + j) for i in range(mine) for j in range(others)]
    pairs = inner + outer
    shares = [1.0 / (count - 1)] * len(inner) + [0.5 / (count - 1)] * len(outer)
    live_count = counts_ref[region_ref[0]]

    def one_tile(at, total):
        start = pl.multiple_of(at * LANE, LANE)
        lanes = pl.ds(start, LANE)
        if first:
            turned = target_ref[lanes, :].astype(jnp.float32).T

        def rows_of(c):
            return [ref[c : c + 16, lanes].astype(jnp.float32) for ref in (*own_refs, *other_refs)]

        def fold(square):
            return square[:8] + square[8:]

        to_target = [jnp.zeros((8, LANE), jnp.float32)] * (mine if first else 0)
        apart = [jnp.zeros((8, LANE), jnp.float32)] * len(pairs)
        for c in range(0, channels, 16):
            values = rows_of(c)
            for i in range(len(to_target)):
                to_target[i] = to_target[i] + fold((values[i] - turned[c : c + 16]) ** 2)
            for p, (i, j) in enumerate(pairs):
                apart[p] = apart[p] + fold((values[i] - values[j]) ** 2)
        live = start + lax.broadcasted_iota(jnp.int32, (1, LANE), 1) < live_count
        score = jnp.zeros((1, LANE), jnp.float32)

        def inverse(square):
            squared = jnp.sum(square, axis=0, keepdims=True) + EPSILON
            inv = lax.rsqrt(squared)
            return squared * inv, inv

        inv_target, inv_pair = [], []
        for square in to_target:
            dist, inv = inverse(square)
            score = score + dist
            inv_target.append(jnp.broadcast_to(inv, (8, LANE)))
        for square, share in zip(apart, shares):
            dist, inv = inverse(square)
            score = score - dist * share
            inv_pair.append(jnp.broadcast_to(inv * (1.0 / (count - 1)), (8, LANE)))
        for c in range(0, channels, 16):
            values = rows_of(c)
            halves = []
            for h in (0, 8):
                near = [v[h : h + 8] for v in values]
                rows = slice(c + h, c + h + 8)
                if first:
                    grads = [(near[i] - turned[rows]) * inv_target[i] for i in range(mine)]
                else:
                    grads = [old_refs[i][rows, lanes] for i in range(mine)]
                for p, (i, j) in enumerate(pairs):
                    term = (near[i] - near[j]) * inv_pair[p]
                    grads[i] = grads[i] - term
                    if j < mine:
                        grads[j] = grads[j] + term
                halves.append(grads)
            for i in range(mine):
                grad = jnp.concatenate([halves[0][i], halves[1][i]], axis=0)
                if last:
                    grad = jnp.where(live, grad, 0.0)
                grad_refs[i][c : c + 16, lanes] = grad.astype(grad_refs[i].dtype)
        return total + jnp.where(live, score, 0.0)

    score_ref[...] = old_score + lax.fori_loop(0, slots // LANE, one_tile, jnp.zeros((1, LANE), jnp.float32))


def backward_kernel(members, ranks, region_ref, rank_ref, w_two_ref, w_three_ref, score_ref, *refs):
    saved = [refs[6 * m : 6 * (m + 1)] for m in range(members)]
    refs = refs[6 * members :]
    d_one_refs, piece_refs, (d_two_ref, stage_ref) = refs[:members], refs[members:-2], refs[-2:]
    w_two, w_three = w_two_ref[...] * 0.5, w_three_ref[...] * 0.5
    hidden, slots = saved[0][1].shape
    bias_one = jnp.zeros((hidden, LANE), jnp.float32)
    bias_two = jnp.zeros((hidden, LANE), jnp.float32)
    g_one, g_two, g_three = 0.0, 0.0, 0.0

    def lane_sum(values):
        return sum(values[:, lo : lo + LANE] for lo, _ in split(values.shape[1], LANE))

    for m in range(members):
        mixed_ref, act_one_ref, slope_one_ref, act_two_ref, slope_two_ref, d_dec_ref = saved[m]
        for lo, size in split(slots, BACK_CHUNK):
            lanes = slice(lo, lo + size)
            back = nn_dot(w_three, d_dec_ref[:, lanes]) * slope_two_ref[:, lanes].astype(jnp.float32)
            bias_two = bias_two + lane_sum(back)
            d_two = back.astype(jnp.bfloat16)
            d_two_ref[m, :, lanes] = d_two
            back = nn_dot(w_two, d_two) * slope_one_ref[:, lanes].astype(jnp.float32)
            bias_one = bias_one + lane_sum(back)
            d_one_refs[m][:, lanes] = back.astype(jnp.bfloat16)
        g_three = g_three + nt_dot(act_two_ref[...], d_dec_ref[...])
        g_two = g_two + nt_dot(act_one_ref[...], d_two_ref[m])
        g_one = g_one + nt_dot(mixed_ref[...], d_one_refs[m][...])
    half = hidden // 2
    region = lax.broadcasted_iota(jnp.int32, (1, hidden), 1) == region_ref[0]
    tally = jnp.where(region, jnp.sum(score_ref[...]), 0.0)
    high = tally.astype(jnp.bfloat16).astype(jnp.float32)
    parts = [
        g_one,
        g_two,
        jnp.concatenate([g_three[:half], g_three[half:]], axis=1),
        jnp.sum(bias_one.T, axis=0, keepdims=True),
        jnp.sum(bias_two.T, axis=0, keepdims=True),
        high,
        tally - high,
    ]
    used = sum(part.shape[0] for part in parts)
    parts.append(jnp.zeros((ranks * stage_ref.shape[1] - used, hidden), jnp.float32))
    stage_ref[...] = jnp.concatenate(parts, axis=0).astype(stage_ref.dtype).reshape(stage_ref.shape)
    for i in range(ranks):
        piece_refs[i][...] = stage_ref[rank_ref[0] ^ i]


def edges_kernel(members, region_ref, table_ref, w_one_ref, *refs):
    d_one_refs, d_mixed_refs, (one_ref, other_ref) = refs[:members], refs[members : 2 * members], refs[2 * members :]
    ext = table_ref.shape[0]
    rows = jnp.concatenate([table_ref[rows, :] for rows in rim_starts(region_ref, ext)], axis=0)
    for m in range(members):
        d_mixed = nn_dot(w_one_ref[...], d_one_refs[m][...]).astype(jnp.bfloat16)
        d_mixed_refs[m][...] = d_mixed
        grads = nt_dot(rows, d_mixed).astype(jnp.bfloat16)
        one_ref[m] = grads[:HALO]
        other_ref[m] = grads[HALO:]


def sum_kernel(count, *refs):
    for i in range(count):
        total = refs[i][...].astype(jnp.float32) + refs[count + i][...].astype(jnp.float32)
        refs[2 * count + i][...] = total.astype(refs[i].dtype)


def unpack_kernel(scale, rank_ref, *refs):
    *refs, stage_ref = refs
    ranks = stage_ref.shape[0]
    one_ref, b_one_ref, two_ref, b_two_ref, three_ref, tally_ref = refs[ranks:]
    for i in range(ranks):
        stage_ref[rank_ref[0] ^ i] = refs[i][...]
    width, hidden = one_ref.shape
    sums = stage_ref[...].reshape(-1, hidden).astype(jnp.float32)
    half, channels = hidden // 2, three_ref.shape[1]
    one_ref[...] = sums[:width]
    two_ref[...] = sums[width : width + hidden]
    base = width + hidden
    three_ref[:half] = sums[base : base + half, :channels]
    three_ref[half:] = sums[base : base + half, channels:]
    last = sums[base + half : base + half + 8]
    b_one_ref[...] = last[0:1]
    b_two_ref[...] = last[1:2]
    tally_ref[...] = (last[2:3] + last[3:4])[:, : tally_ref.shape[1]] * scale


def own_kernel(table_ref, *refs):
    *d_mixed_refs, own_ref = refs
    members, nodes, _ = own_ref.shape
    for m in range(members):
        own_ref[m] = nt_dot(table_ref[HALO : HALO + nodes, :], d_mixed_refs[m][...])


def finish_kernel(region_ref, own_ref, one_ref, other_ref, out_ref):
    nodes = own_ref.shape[1]
    out_ref[:, HALO : nodes - HALO] = own_ref[:, HALO : nodes - HALO].astype(jnp.bfloat16)
    for ref, rows in zip((one_ref, other_ref), rim_starts(region_ref, nodes)):
        out_ref[:, rows] = (own_ref[:, rows] + ref[...].astype(jnp.float32)).astype(jnp.bfloat16)


def exchanged(block, second):
    size = lax.axis_size("space")
    pairs = [(i, (i + 1) % size if i % 2 else (i - 1) % size) if second else (i, i ^ 1) for i in range(size)]
    return lax.ppermute(block, "space", pairs)


def swapped(block, axis, by):
    return lax.ppermute(block, axis, [(i, i ^ by) for i in range(lax.axis_size(axis))])


def per_device(latent, neighbours, weights, targets, counts, w_one, b_one, w_two, b_two, w_three):
    members, nodes, width = latent.shape
    slots, channels = targets.shape
    hidden = w_one.shape[1]
    ext = nodes + 2 * HALO
    region, regions = lax.axis_index("space"), lax.axis_size("space")
    rank, ranks = lax.axis_index("member"), lax.axis_size("member")
    share = slots // ranks
    bf16, f32 = jnp.bfloat16, jnp.float32
    shape = jax.ShapeDtypeStruct
    each = range(members)

    edge = shape((HALO, width), bf16)
    region_at = region[None].astype(jnp.int32)
    *rims, latent = kernel_call(
        rims_kernel, (edge, edge, shape(latent.shape, bf16)), flops=4 << 30, moved=3 * MIB, smem=1, operands=2
    )(region_at, latent)
    halo = [[exchanged(rims[0], False), exchanged(rims[1], True)]]
    rank_at = rank[None].astype(jnp.int32)

    table, part, *rims = kernel_call(
        table_kernel,
        (shape((ext, slots), bf16), shape((width, slots), f32)) + (edge,) * (2 * members - 2),
        flops=2 * width * nodes * slots,
        moved=12 * MIB,
        smem=3,
        operands=6,
    )(region_at, rank_at, counts, neighbours, weights, latent)
    halo += [[exchanged(rims[2 * m], False), exchanged(rims[2 * m + 1], True)] for m in range(members - 1)]

    saved_shape = shape((hidden, slots), bf16)
    mixed_shape = shape((width, slots), bf16)
    decoded_shape = shape((channels, slots), bf16)
    dense = width * hidden + hidden * hidden + hidden * channels
    saved, decoded, beside, across = [], [], [], []
    for m in each:
        *kept, block = kernel_call(
            lambda *refs: forward_kernel(m, *refs),
            (mixed_shape,) + (saved_shape,) * 4 + (decoded_shape,),
            flops=2 * slots * ((ext if m else 2 * HALO) * width + dense),
            moved=8 * MIB,
            smem=1,
            operands=10,
        )(region_at, latent if m else part, table, *halo[m], w_one, b_one[None], w_two, b_two[None], w_three)
        saved.append(kept)
        decoded.append(block)
        blocks, bit = {0: block}, 2
        while bit < ranks:
            blocks.update({i ^ bit: swapped(blocks[i], "member", bit) for i in sorted(blocks)})
            bit = 2 * bit
        across.append([blocks[i] for i in sorted(blocks) if i])
        beside.append(swapped(block, "member", 1))

    def scored(others, carried, first=False, last=False):
        operands = (region_at, counts, *decoded, *others, *carried)
        return kernel_call(
            lambda *refs: score_kernel(members, len(others), members * ranks, first, last, *refs),
            (shape((channels, slots), bf16 if last else f32),) * members + (shape((1, LANE), f32),),
            flops=4 * MIB,
            moved=2 * MIB,
            smem=2,
            operands=len(operands),
        )(*operands)

    carried = scored(beside + [block for blocks in across[:-1] for block in blocks], [targets], first=True)
    across[-1], carried = lax.optimization_barrier((across[-1], carried))
    others = [*across[-1]] + [swapped(block, "member", 1) for blocks in across for block in blocks]
    *grads, score = scored(others, carried, last=True)

    rows = -(-(width + hidden + hidden // 2 + 4) // (16 * ranks)) * 16
    piece = shape((rows, hidden), bf16)
    operands = [region_at, rank_at, w_two, w_three, score]
    for m in each:
        operands += [*saved[m], grads[m]]
    out = kernel_call(
        lambda *refs: backward_kernel(members, ranks, *refs),
        (saved_shape,) * members + (piece,) * ranks,
        flops=4 * members * slots * dense,
        moved=10 * MIB,
        scratch=(pltpu.VMEM((members, hidden, slots), bf16), pltpu.VMEM((ranks, rows, hidden), bf16)),
        smem=2,
        operands=len(operands),
    )(*operands)
    d_one, pieces = out[:members], out[members:]

    def summed(ones, others):
        return kernel_call(
            lambda *refs: sum_kernel(len(ones), *refs), (piece,) * len(ones), flops=MIB, moved=MIB, operands=2 * len(ones)
        )(*ones, *others)

    out = kernel_call(
        lambda *refs: edges_kernel(members, *refs),
        (mixed_shape,) * members + (shape((members, HALO, width), bf16),) * 2,
        flops=2 * members * slots * width * (hidden + 2 * HALO),
        moved=6 * MIB,
        smem=1,
        operands=3 + members,
    )(region_at, table, w_one, *d_one)
    d_mixed, rims = out[:members], out[members:]

    bit = 1
    while bit < ranks:
        received = [swapped(sent, "member", bit) for sent in pieces[1::2]]
        if bit == 1:
            received, rims = lax.optimization_barrier((received, rims))
        pieces = summed(pieces[::2], received)
        bit = 2 * bit
    own = kernel_call(
        own_kernel,
        shape((members, nodes, width), f32),
        flops=2 * members * nodes * width * slots,
        moved=6 * MIB,
        operands=1 + members,
    )(table, *d_mixed)
    other = exchanged(rims[1], True)
    (total,) = pieces
    step = 1
    while step < regions:
        received = swapped(total, "space", step)
        step = 2 * step
        if step == regions:
            received, other = lax.optimization_barrier((received, other))
        (total,) = summed([total], [received])
        if 2 * step == regions:
            total, own, rims = lax.optimization_barrier((total, own, rims))
            one = exchanged(rims[0], False)
    totals = {0: total}
    bit = 2
    while bit < ranks:
        totals.update({i ^ bit: swapped(totals[i], "member", bit) for i in sorted(totals)})
        bit = 2 * bit
    totals.update({i ^ 1: swapped(block, "member", 1) for i, block in totals.items()})
    latent_grad = kernel_call(
        finish_kernel,
        shape((members, nodes, width), bf16),
        flops=MIB,
        moved=3 * MIB,
        smem=1,
        operands=4,
    )(region_at, own, one, other)
    totals = [totals[i] for i in range(ranks)]
    totals, latent_grad = lax.optimization_barrier((totals, latent_grad))
    row = shape((1, hidden), f32)
    g_one, g_bone, g_two, g_btwo, g_three, tally = kernel_call(
        lambda *refs: unpack_kernel(1.0 / (OBS_MEAN * members * ranks), *refs),
        (shape((width, hidden), f32), row, shape((hidden, hidden), f32), row, shape((hidden, channels), f32),
         shape((1, regions), f32)),
        flops=MIB,
        moved=2 * MIB,
        scratch=(pltpu.VMEM((ranks, rows, hidden), bf16),),
        smem=1,
        operands=1 + ranks,
    )(rank_at, *totals)
    return (tally[0], latent_grad, g_one, g_bone[0], g_two, g_btwo[0], g_three)


def solution(mesh):
    in_specs = (
        P("member", ("groups", "space"), None),
        P(None, ("groups", "space")),
        P(None, ("groups", "space")),
        P(("groups", "space"), None),
        P("groups"),
        P(),
        P(),
        P(),
        P(),
        P(),
    )
    out_specs = (
        P("groups"),
        P("member", ("groups", "space"), None),
        P("groups", None),
        P("groups"),
        P("groups", None),
        P("groups"),
        P("groups", None),
    )
    return jax.shard_map(
        per_device, mesh=mesh, in_specs=in_specs, out_specs=out_specs, check_vma=False
    )
```

```python
import jax
import jax.numpy as jnp
from jax import lax
from jax.experimental import pallas as pl
from jax.experimental.pallas import tpu as pltpu
from jax.sharding import PartitionSpec as P

K = 4
OBS_MEAN = 512
HALO = 256
EPSILON = 1e-05
BLOCK = 256
LANE = 128
CHUNK = 768
BACK_CHUNK = 512
FORWARD_CHUNK = 1536
MIB = 1 << 20


def split(total, step):
    return [(start, min(step, total - start)) for start in range(0, total, step)]


def nt_dot(left, right):
    return lax.dot_general(
        left, right, (((1,), (1,)), ((), ())), preferred_element_type=jnp.float32
    )


def nn_dot(left, right):
    return jnp.dot(left, right, preferred_element_type=jnp.float32)


def kernel_call(body, out_shape, flops, moved, scratch=(), smem=0, operands=0):
    vmem = pl.BlockSpec(memory_space=pltpu.VMEM)
    specs = [pl.BlockSpec(memory_space=pltpu.SMEM)] * smem
    return pl.pallas_call(
        body,
        out_shape=out_shape,
        in_specs=specs + [vmem] * (operands - len(specs)),
        out_specs=jax.tree.map(lambda _: vmem, out_shape),
        scratch_shapes=list(scratch),
        compiler_params=pltpu.CompilerParams(vmem_limit_bytes=24 * MIB),
        cost_estimate=pl.CostEstimate(flops=flops, bytes_accessed=moved, transcendentals=0),
    )


def rim_starts(region_ref, length):
    odd = lax.rem(region_ref[0], 2)
    far = length - HALO
    return [pl.ds(pl.multiple_of(start, HALO), HALO) for start in ((1 - odd) * far, odd * far)]


def cut_rims(region_ref, latent_ref, member, *rim_refs):
    for ref, rows in zip(rim_refs, rim_starts(region_ref, latent_ref.shape[1])):
        ref[...] = latent_ref[member, rows]


def rims_kernel(region_ref, latent_ref, one_ref, other_ref, copy_ref):
    cut_rims(region_ref, latent_ref, 0, one_ref, other_ref)
    copy_ref[...] = latent_ref[...]


def table_kernel(region_ref, rank_ref, counts_ref, nbr_ref, weight_ref, latent_ref, table_ref, part_ref, *rim_refs):
    members, nodes, _ = latent_ref.shape
    for m in range(1, members):
        cut_rims(region_ref, latent_ref, m, *rim_refs[2 * m - 2 : 2 * m])
    ext, slots = table_ref.shape
    live = lax.broadcasted_iota(jnp.int32, (1, slots), 1) < counts_ref[region_ref[0]]
    nbr = [nbr_ref[k : k + 1, :] for k in range(K)]
    own = [jnp.where(live, weight_ref[k : k + 1, :], 0.0) for k in range(K)]
    joint = []
    for k in range(K):
        total = own[k]
        for j in range(K):
            if j != k:
                total = total + jnp.where(nbr[j] == nbr[k], own[j], 0.0)
        joint.append(total)
    groups = BLOCK // 16
    rows = (
        lax.broadcasted_iota(jnp.int32, (groups, 16, LANE), 0) * 16
        + lax.broadcasted_iota(jnp.int32, (groups, 16, LANE), 1)
    ).astype(jnp.float32).astype(jnp.bfloat16)
    turned = latent_ref[0].T
    for start, length in split(slots, CHUNK):
        for lo, size in split(length, LANE):
            lanes = slice(start + lo, start + lo + size)
            wide = [jnp.broadcast_to(joint[k][:, lanes], (16, size)).astype(jnp.bfloat16) for k in range(K)]
            for b in range(ext // BLOCK):
                tile = jnp.zeros((groups, 16, size), jnp.bfloat16)
                for k in range(K):
                    near = (nbr[k][:, lanes] - b * BLOCK).astype(jnp.float32)
                    near = jnp.broadcast_to(near, (16, size)).astype(jnp.bfloat16)
                    tile = jnp.where(rows[:, :, :size] == near[None], wide[k][None], tile)
                table_ref[b * BLOCK : (b + 1) * BLOCK, lanes] = tile.reshape(BLOCK, size)
        lanes = slice(start, start + length)
        part_ref[:, lanes] = nn_dot(turned, table_ref[HALO : HALO + nodes, lanes])


def column(ref):
    height = ref.shape[1]
    return jnp.broadcast_to(ref[...], (LANE, height)).T


def forward_kernel(
    member, region_ref, own_ref, table_ref, one_ref, other_ref, w_one_ref, b_one_ref, w_two_ref, b_two_ref, w_three_ref,
    mixed_ref, act_one_ref, slope_one_ref, act_two_ref, slope_two_ref, decoded_ref,
):
    ext, slots = table_ref.shape
    w_one, w_two, w_three = w_one_ref[...].T * 0.5, w_two_ref[...].T * 0.5, w_three_ref[...].T
    b_one, b_two = column(b_one_ref) * 0.5, column(b_two_ref) * 0.5

    def layer(weight, bias, values, size):
        half = nn_dot(weight, values) + jnp.concatenate([bias] * (size // LANE), axis=1)
        gate = 1.0 + jnp.tanh(half)
        act = half * gate
        return act.astype(jnp.bfloat16), (gate + act * (2.0 - gate)).astype(jnp.bfloat16)

    edges = jnp.concatenate([one_ref[...].T, other_ref[...].T], axis=1)
    own = own_ref[member].T if member else None
    for lo, size in split(slots, FORWARD_CHUNK):
        lanes = slice(lo, lo + size)
        rims = jnp.concatenate([table_ref[rows, lanes] for rows in rim_starts(region_ref, ext)], axis=0)
        share = nn_dot(own, table_ref[HALO : ext - HALO, lanes]) if member else own_ref[:, lanes]
        mixed = share + nn_dot(edges, rims)
        mixed = mixed.astype(jnp.bfloat16)
        mixed_ref[:, lanes] = mixed
        act_one, slope_one_ref[:, lanes] = layer(w_one, b_one, mixed, size)
        act_one_ref[:, lanes] = act_one
        act_two, slope_two_ref[:, lanes] = layer(w_two, b_two, act_one, size)
        act_two_ref[:, lanes] = act_two
        decoded_ref[:, lanes] = nn_dot(w_three, act_two).astype(jnp.bfloat16)


def score_kernel(mine, others, count, first, last, region_ref, counts_ref, *refs):
    own_refs, refs = refs[:mine], refs[mine:]
    other_refs, refs = refs[:others], refs[others:]
    if first:
        target_ref, refs = refs[0], refs[1:]
        old_refs, old_score = None, 0.0
    else:
        old_refs, old_score, refs = refs[:mine], refs[mine][...], refs[mine + 1 :]
    grad_refs, score_ref = refs[:mine], refs[mine]
    channels, slots = own_refs[0].shape
    inner = [(i, j) for i in range(mine) for j in range(i + 1, mine)] if first else []
    outer = [(i, mine + j) for i in range(mine) for j in range(others)]
    pairs = inner + outer
    shares = [1.0 / (count - 1)] * len(inner) + [0.5 / (count - 1)] * len(outer)
    live_count = counts_ref[region_ref[0]]

    def one_tile(at, total):
        start = pl.multiple_of(at * LANE, LANE)
        lanes = pl.ds(start, LANE)
        if first:
            turned = target_ref[lanes, :].astype(jnp.float32).T

        def rows_of(c):
            return [ref[c : c + 16, lanes].astype(jnp.float32) for ref in (*own_refs, *other_refs)]

        def fold(square):
            return square[:8] + square[8:]

        to_target = [jnp.zeros((8, LANE), jnp.float32)] * (mine if first else 0)
        apart = [jnp.zeros((8, LANE), jnp.float32)] * len(pairs)
        for c in range(0, channels, 16):
            values = rows_of(c)
            for i in range(len(to_target)):
                to_target[i] = to_target[i] + fold((values[i] - turned[c : c + 16]) ** 2)
            for p, (i, j) in enumerate(pairs):
                apart[p] = apart[p] + fold((values[i] - values[j]) ** 2)
        live = start + lax.broadcasted_iota(jnp.int32, (1, LANE), 1) < live_count
        score = jnp.zeros((1, LANE), jnp.float32)

        def inverse(square):
            squared = jnp.sum(square, axis=0, keepdims=True) + EPSILON
            inv = lax.rsqrt(squared)
            return squared * inv, inv

        inv_target, inv_pair = [], []
        for square in to_target:
            dist, inv = inverse(square)
            score = score + dist
            inv_target.append(jnp.broadcast_to(inv, (8, LANE)))
        for square, share in zip(apart, shares):
            dist, inv = inverse(square)
            score = score - dist * share
            inv_pair.append(jnp.broadcast_to(inv * (1.0 / (count - 1)), (8, LANE)))
        for c in range(0, channels, 16):
            values = rows_of(c)
            halves = []
            for h in (0, 8):
                near = [v[h : h + 8] for v in values]
                rows = slice(c + h, c + h + 8)
                if first:
                    grads = [(near[i] - turned[rows]) * inv_target[i] for i in range(mine)]
                else:
                    grads = [old_refs[i][rows, lanes] for i in range(mine)]
                for p, (i, j) in enumerate(pairs):
                    term = (near[i] - near[j]) * inv_pair[p]
                    grads[i] = grads[i] - term
                    if j < mine:
                        grads[j] = grads[j] + term
                halves.append(grads)
            for i in range(mine):
                grad = jnp.concatenate([halves[0][i], halves[1][i]], axis=0)
                if last:
                    grad = jnp.where(live, grad, 0.0)
                grad_refs[i][c : c + 16, lanes] = grad.astype(grad_refs[i].dtype)
        return total + jnp.where(live, score, 0.0)

    score_ref[...] = old_score + lax.fori_loop(0, slots // LANE, one_tile, jnp.zeros((1, LANE), jnp.float32))


def backward_kernel(members, ranks, region_ref, rank_ref, w_two_ref, w_three_ref, score_ref, *refs):
    saved = [refs[6 * m : 6 * (m + 1)] for m in range(members)]
    refs = refs[6 * members :]
    d_one_refs, piece_refs, (d_two_ref, stage_ref) = refs[:members], refs[members:-2], refs[-2:]
    w_two, w_three = w_two_ref[...] * 0.5, w_three_ref[...] * 0.5
    hidden, slots = saved[0][1].shape
    bias_one = jnp.zeros((hidden, LANE), jnp.float32)
    bias_two = jnp.zeros((hidden, LANE), jnp.float32)
    g_one, g_two, g_three = 0.0, 0.0, 0.0

    def lane_sum(values):
        return sum(values[:, lo : lo + LANE] for lo, _ in split(values.shape[1], LANE))

    for m in range(members):
        mixed_ref, act_one_ref, slope_one_ref, act_two_ref, slope_two_ref, d_dec_ref = saved[m]
        for lo, size in split(slots, BACK_CHUNK):
            lanes = slice(lo, lo + size)
            back = nn_dot(w_three, d_dec_ref[:, lanes]) * slope_two_ref[:, lanes].astype(jnp.float32)
            bias_two = bias_two + lane_sum(back)
            d_two = back.astype(jnp.bfloat16)
            d_two_ref[m, :, lanes] = d_two
            back = nn_dot(w_two, d_two) * slope_one_ref[:, lanes].astype(jnp.float32)
            bias_one = bias_one + lane_sum(back)
            d_one_refs[m][:, lanes] = back.astype(jnp.bfloat16)
        g_three = g_three + nt_dot(act_two_ref[...], d_dec_ref[...])
        g_two = g_two + nt_dot(act_one_ref[...], d_two_ref[m])
        g_one = g_one + nt_dot(mixed_ref[...], d_one_refs[m][...])
    half = hidden // 2
    region = lax.broadcasted_iota(jnp.int32, (1, hidden), 1) == region_ref[0]
    tally = jnp.where(region, jnp.sum(score_ref[...]), 0.0)
    high = tally.astype(jnp.bfloat16).astype(jnp.float32)
    parts = [
        g_one,
        g_two,
        jnp.concatenate([g_three[:half], g_three[half:]], axis=1),
        jnp.sum(bias_one.T, axis=0, keepdims=True),
        jnp.sum(bias_two.T, axis=0, keepdims=True),
        high,
        tally - high,
    ]
    used = sum(part.shape[0] for part in parts)
    parts.append(jnp.zeros((ranks * stage_ref.shape[1] - used, hidden), jnp.float32))
    stage_ref[...] = jnp.concatenate(parts, axis=0).astype(stage_ref.dtype).reshape(stage_ref.shape)
    for i in range(ranks):
        piece_refs[i][...] = stage_ref[rank_ref[0] ^ i]


def edges_kernel(members, region_ref, table_ref, w_one_ref, *refs):
    d_one_refs, d_mixed_refs, (one_ref, other_ref) = refs[:members], refs[members : 2 * members], refs[2 * members :]
    ext = table_ref.shape[0]
    rows = jnp.concatenate([table_ref[rows, :] for rows in rim_starts(region_ref, ext)], axis=0)
    for m in range(members):
        d_mixed = nn_dot(w_one_ref[...], d_one_refs[m][...]).astype(jnp.bfloat16)
        d_mixed_refs[m][...] = d_mixed
        grads = nt_dot(rows, d_mixed).astype(jnp.bfloat16)
        one_ref[m] = grads[:HALO]
        other_ref[m] = grads[HALO:]


def sum_kernel(count, *refs):
    for i in range(count):
        total = refs[i][...].astype(jnp.float32) + refs[count + i][...].astype(jnp.float32)
        refs[2 * count + i][...] = total.astype(refs[i].dtype)


def unpack_kernel(scale, rank_ref, *refs):
    *refs, stage_ref = refs
    ranks = stage_ref.shape[0]
    one_ref, b_one_ref, two_ref, b_two_ref, three_ref, tally_ref = refs[ranks:]
    for i in range(ranks):
        stage_ref[rank_ref[0] ^ i] = refs[i][...]
    width, hidden = one_ref.shape
    sums = stage_ref[...].reshape(-1, hidden).astype(jnp.float32)
    half, channels = hidden // 2, three_ref.shape[1]
    one_ref[...] = sums[:width]
    two_ref[...] = sums[width : width + hidden]
    base = width + hidden
    three_ref[:half] = sums[base : base + half, :channels]
    three_ref[half:] = sums[base : base + half, channels:]
    last = sums[base + half : base + half + 8]
    b_one_ref[...] = last[0:1]
    b_two_ref[...] = last[1:2]
    tally_ref[...] = (last[2:3] + last[3:4])[:, : tally_ref.shape[1]] * scale


def own_kernel(table_ref, *refs):
    *d_mixed_refs, own_ref = refs
    members, nodes, _ = own_ref.shape
    for m in range(members):
        own_ref[m] = nt_dot(table_ref[HALO : HALO + nodes, :], d_mixed_refs[m][...])


def finish_kernel(region_ref, own_ref, one_ref, other_ref, out_ref):
    nodes = own_ref.shape[1]
    out_ref[:, HALO : nodes - HALO] = own_ref[:, HALO : nodes - HALO].astype(jnp.bfloat16)
    for ref, rows in zip((one_ref, other_ref), rim_starts(region_ref, nodes)):
        out_ref[:, rows] = (own_ref[:, rows] + ref[...].astype(jnp.float32)).astype(jnp.bfloat16)


def exchanged(block, second):
    size = lax.axis_size("space")
    pairs = [(i, (i + 1) % size if i % 2 else (i - 1) % size) if second else (i, i ^ 1) for i in range(size)]
    return lax.ppermute(block, "space", pairs)


def swapped(block, axis, by):
    return lax.ppermute(block, axis, [(i, i ^ by) for i in range(lax.axis_size(axis))])


def per_device(latent, neighbours, weights, targets, counts, w_one, b_one, w_two, b_two, w_three):
    members, nodes, width = latent.shape
    slots, channels = targets.shape
    hidden = w_one.shape[1]
    ext = nodes + 2 * HALO
    region, regions = lax.axis_index("space"), lax.axis_size("space")
    rank, ranks = lax.axis_index("member"), lax.axis_size("member")
    share = slots // ranks
    bf16, f32 = jnp.bfloat16, jnp.float32
    shape = jax.ShapeDtypeStruct
    each = range(members)

    edge = shape((HALO, width), bf16)
    region_at = region[None].astype(jnp.int32)
    *rims, latent = kernel_call(
        rims_kernel, (edge, edge, shape(latent.shape, bf16)), flops=4 << 30, moved=3 * MIB, smem=1, operands=2
    )(region_at, latent)
    halo = [[exchanged(rims[0], False), exchanged(rims[1], True)]]
    rank_at = rank[None].astype(jnp.int32)

    table, part, *rims = kernel_call(
        table_kernel,
        (shape((ext, slots), bf16), shape((width, slots), f32)) + (edge,) * (2 * members - 2),
        flops=2 * width * nodes * slots,
        moved=12 * MIB,
        smem=3,
        operands=6,
    )(region_at, rank_at, counts, neighbours, weights, latent)
    halo += [[exchanged(rims[2 * m], False), exchanged(rims[2 * m + 1], True)] for m in range(members - 1)]

    saved_shape = shape((hidden, slots), bf16)
    mixed_shape = shape((width, slots), bf16)
    decoded_shape = shape((channels, slots), bf16)
    dense = width * hidden + hidden * hidden + hidden * channels
    saved, decoded, beside, across = [], [], [], []
    for m in each:
        *kept, block = kernel_call(
            lambda *refs: forward_kernel(m, *refs),
            (mixed_shape,) + (saved_shape,) * 4 + (decoded_shape,),
            flops=2 * slots * ((ext if m else 2 * HALO) * width + dense),
            moved=8 * MIB,
            smem=1,
            operands=10,
        )(region_at, latent if m else part, table, *halo[m], w_one, b_one[None], w_two, b_two[None], w_three)
        saved.append(kept)
        decoded.append(block)
        blocks, bit = {0: block}, 2
        while bit < ranks:
            blocks.update({i ^ bit: swapped(blocks[i], "member", bit) for i in sorted(blocks)})
            bit = 2 * bit
        across.append([blocks[i] for i in sorted(blocks) if i])
        beside.append(swapped(block, "member", 1))

    def scored(others, carried, first=False, last=False):
        operands = (region_at, counts, *decoded, *others, *carried)
        return kernel_call(
            lambda *refs: score_kernel(members, len(others), members * ranks, first, last, *refs),
            (shape((channels, slots), bf16 if last else f32),) * members + (shape((1, LANE), f32),),
            flops=4 * MIB,
            moved=2 * MIB,
            smem=2,
            operands=len(operands),
        )(*operands)

    carried = scored(beside + [block for blocks in across[:-1] for block in blocks], [targets], first=True)
    across[-1], carried = lax.optimization_barrier((across[-1], carried))
    others = [*across[-1]] + [swapped(block, "member", 1) for blocks in across for block in blocks]
    *grads, score = scored(others, carried, last=True)

    rows = -(-(width + hidden + hidden // 2 + 4) // (16 * ranks)) * 16
    piece = shape((rows, hidden), bf16)
    operands = [region_at, rank_at, w_two, w_three, score]
    for m in each:
        operands += [*saved[m], grads[m]]
    out = kernel_call(
        lambda *refs: backward_kernel(members, ranks, *refs),
        (saved_shape,) * members + (piece,) * ranks,
        flops=4 * members * slots * dense,
        moved=10 * MIB,
        scratch=(pltpu.VMEM((members, hidden, slots), bf16), pltpu.VMEM((ranks, rows, hidden), bf16)),
        smem=2,
        operands=len(operands),
    )(*operands)
    d_one, pieces = out[:members], out[members:]

    def summed(ones, others):
        return kernel_call(
            lambda *refs: sum_kernel(len(ones), *refs), (piece,) * len(ones), flops=MIB, moved=MIB, operands=2 * len(ones)
        )(*ones, *others)

    out = kernel_call(
        lambda *refs: edges_kernel(members, *refs),
        (mixed_shape,) * members + (shape((members, HALO, width), bf16),) * 2,
        flops=2 * members * slots * width * (hidden + 2 * HALO),
        moved=6 * MIB,
        smem=1,
        operands=3 + members,
    )(region_at, table, w_one, *d_one)
    d_mixed, rims = out[:members], out[members:]

    bit = 1
    while bit < ranks:
        received = [swapped(sent, "member", bit) for sent in pieces[1::2]]
        if bit == 1:
            received, rims = lax.optimization_barrier((received, rims))
        pieces = summed(pieces[::2], received)
        bit = 2 * bit
    own = kernel_call(
        own_kernel,
        shape((members, nodes, width), f32),
        flops=2 * members * nodes * width * slots,
        moved=6 * MIB,
        operands=1 + members,
    )(table, *d_mixed)
    other = exchanged(rims[1], True)
    (total,) = pieces
    step = 1
    while step < regions:
        received = swapped(total, "space", step)
        step = 2 * step
        if step == regions:
            received, other = lax.optimization_barrier((received, other))
        (total,) = summed([total], [received])
        if 2 * step == regions:
            total, own, rims = lax.optimization_barrier((total, own, rims))
            one = exchanged(rims[0], False)
    totals = {0: total}
    bit = 2
    while bit < ranks:
        totals.update({i ^ bit: swapped(totals[i], "member", bit) for i in sorted(totals)})
        bit = 2 * bit
    totals.update({i ^ 1: swapped(block, "member", 1) for i, block in totals.items()})
    latent_grad = kernel_call(
        finish_kernel,
        shape((members, nodes, width), bf16),
        flops=MIB,
        moved=3 * MIB,
        smem=1,
        operands=4,
    )(region_at, own, one, other)
    totals = [totals[i] for i in range(ranks)]
    totals, latent_grad = lax.optimization_barrier((totals, latent_grad))
    row = shape((1, hidden), f32)
    g_one, g_bone, g_two, g_btwo, g_three, tally = kernel_call(
        lambda *refs: unpack_kernel(1.0 / (OBS_MEAN * members * ranks), *refs),
        (shape((width, hidden), f32), row, shape((hidden, hidden), f32), row, shape((hidden, channels), f32),
         shape((1, regions), f32)),
        flops=MIB,
        moved=2 * MIB,
        scratch=(pltpu.VMEM((ranks, rows, hidden), bf16),),
        smem=1,
        operands=1 + ranks,
    )(rank_at, *totals)
    return (tally[0], latent_grad, g_one, g_bone[0], g_two, g_btwo[0], g_three)


def solution(mesh):
    in_specs = (
        P("member", ("groups", "space"), None),
        P(None, ("groups", "space")),
        P(None, ("groups", "space")),
        P(("groups", "space"), None),
        P("groups"),
        P(),
        P(),
        P(),
        P(),
        P(),
    )
    out_specs = (
        P("groups"),
        P("member", ("groups", "space"), None),
        P("groups", None),
        P("groups"),
        P("groups", None),
        P("groups"),
        P("groups", None),
    )
    return jax.shard_map(
        per_device, mesh=mesh, in_specs=in_specs, out_specs=out_specs, check_vma=False
    )
```

```python
import jax
import jax.numpy as jnp
from jax import lax
from jax.experimental import pallas as pl
from jax.experimental.pallas import tpu as pltpu
from jax.sharding import PartitionSpec as P

K = 4
OBS_MEAN = 512
HALO = 256
EPSILON = 1e-05
BLOCK = 256
LANE = 128
CHUNK = 768
BACK_CHUNK = 512
FORWARD_CHUNK = 1536
MIB = 1 << 20


def split(total, step):
    return [(start, min(step, total - start)) for start in range(0, total, step)]


def nt_dot(left, right):
    return lax.dot_general(
        left, right, (((1,), (1,)), ((), ())), preferred_element_type=jnp.float32
    )


def nn_dot(left, right):
    return jnp.dot(left, right, preferred_element_type=jnp.float32)


def kernel_call(body, out_shape, flops, moved, scratch=(), smem=0, operands=0):
    vmem = pl.BlockSpec(memory_space=pltpu.VMEM)
    specs = [pl.BlockSpec(memory_space=pltpu.SMEM)] * smem
    return pl.pallas_call(
        body,
        out_shape=out_shape,
        in_specs=specs + [vmem] * (operands - len(specs)),
        out_specs=jax.tree.map(lambda _: vmem, out_shape),
        scratch_shapes=list(scratch),
        compiler_params=pltpu.CompilerParams(vmem_limit_bytes=24 * MIB),
        cost_estimate=pl.CostEstimate(flops=flops, bytes_accessed=moved, transcendentals=0),
    )


def rim_starts(region_ref, length):
    odd = lax.rem(region_ref[0], 2)
    far = length - HALO
    return [pl.ds(pl.multiple_of(start, HALO), HALO) for start in ((1 - odd) * far, odd * far)]


def cut_rims(region_ref, latent_ref, member, *rim_refs):
    for ref, rows in zip(rim_refs, rim_starts(region_ref, latent_ref.shape[1])):
        ref[...] = latent_ref[member, rows]


def rims_kernel(region_ref, latent_ref, one_ref, other_ref, copy_ref):
    cut_rims(region_ref, latent_ref, 0, one_ref, other_ref)
    copy_ref[...] = latent_ref[...]


def table_kernel(region_ref, rank_ref, counts_ref, nbr_ref, weight_ref, latent_ref, table_ref, part_ref, *rim_refs):
    members, nodes, _ = latent_ref.shape
    for m in range(1, members):
        cut_rims(region_ref, latent_ref, m, *rim_refs[2 * m - 2 : 2 * m])
    ext, slots = table_ref.shape
    live = lax.broadcasted_iota(jnp.int32, (1, slots), 1) < counts_ref[region_ref[0]]
    nbr = [nbr_ref[k : k + 1, :] for k in range(K)]
    own = [jnp.where(live, weight_ref[k : k + 1, :], 0.0) for k in range(K)]
    joint = []
    for k in range(K):
        total = own[k]
        for j in range(K):
            if j != k:
                total = total + jnp.where(nbr[j] == nbr[k], own[j], 0.0)
        joint.append(total)
    groups = BLOCK // 16
    rows = (
        lax.broadcasted_iota(jnp.int32, (groups, 16, LANE), 0) * 16
        + lax.broadcasted_iota(jnp.int32, (groups, 16, LANE), 1)
    ).astype(jnp.float32).astype(jnp.bfloat16)
    turned = latent_ref[0].T
    for start, length in split(slots, CHUNK):
        for lo, size in split(length, LANE):
            lanes = slice(start + lo, start + lo + size)
            wide = [jnp.broadcast_to(joint[k][:, lanes], (16, size)).astype(jnp.bfloat16) for k in range(K)]
            for b in range(ext // BLOCK):
                tile = jnp.zeros((groups, 16, size), jnp.bfloat16)
                for k in range(K):
                    near = (nbr[k][:, lanes] - b * BLOCK).astype(jnp.float32)
                    near = jnp.broadcast_to(near, (16, size)).astype(jnp.bfloat16)
                    tile = jnp.where(rows[:, :, :size] == near[None], wide[k][None], tile)
                table_ref[b * BLOCK : (b + 1) * BLOCK, lanes] = tile.reshape(BLOCK, size)
        lanes = slice(start, start + length)
        part_ref[:, lanes] = nn_dot(turned, table_ref[HALO : HALO + nodes, lanes])


def column(ref):
    height = ref.shape[1]
    return jnp.broadcast_to(ref[...], (LANE, height)).T


def forward_kernel(
    member, region_ref, own_ref, table_ref, one_ref, other_ref, w_one_ref, b_one_ref, w_two_ref, b_two_ref, w_three_ref,
    mixed_ref, act_one_ref, slope_one_ref, act_two_ref, slope_two_ref, decoded_ref,
):
    ext, slots = table_ref.shape
    w_one, w_two, w_three = w_one_ref[...].T * 0.5, w_two_ref[...].T * 0.5, w_three_ref[...].T
    b_one, b_two = column(b_one_ref) * 0.5, column(b_two_ref) * 0.5

    def layer(weight, bias, values, size):
        half = nn_dot(weight, values) + jnp.concatenate([bias] * (size // LANE), axis=1)
        gate = 1.0 + jnp.tanh(half)
        act = half * gate
        return act.astype(jnp.bfloat16), (gate + act * (2.0 - gate)).astype(jnp.bfloat16)

    edges = jnp.concatenate([one_ref[...].T, other_ref[...].T], axis=1)
    own = own_ref[member].T if member else None
    for lo, size in split(slots, FORWARD_CHUNK):
        lanes = slice(lo, lo + size)
        rims = jnp.concatenate([table_ref[rows, lanes] for rows in rim_starts(region_ref, ext)], axis=0)
        share = nn_dot(own, table_ref[HALO : ext - HALO, lanes]) if member else own_ref[:, lanes]
        mixed = share + nn_dot(edges, rims)
        mixed = mixed.astype(jnp.bfloat16)
        mixed_ref[:, lanes] = mixed
        act_one, slope_one_ref[:, lanes] = layer(w_one, b_one, mixed, size)
        act_one_ref[:, lanes] = act_one
        act_two, slope_two_ref[:, lanes] = layer(w_two, b_two, act_one, size)
        act_two_ref[:, lanes] = act_two
        decoded_ref[:, lanes] = nn_dot(w_three, act_two).astype(jnp.bfloat16)


def score_kernel(mine, others, count, first, last, region_ref, counts_ref, *refs):
    own_refs, refs = refs[:mine], refs[mine:]
    other_refs, refs = refs[:others], refs[others:]
    if first:
        target_ref, refs = refs[0], refs[1:]
        old_refs, old_score = None, 0.0
    else:
        old_refs, old_score, refs = refs[:mine], refs[mine][...], refs[mine + 1 :]
    grad_refs, score_ref = refs[:mine], refs[mine]
    channels, slots = own_refs[0].shape
    inner = [(i, j) for i in range(mine) for j in range(i + 1, mine)] if first else []
    outer = [(i, mine + j) for i in range(mine) for j in range(others)]
    pairs = inner + outer
    shares = [1.0 / (count - 1)] * len(inner) + [0.5 / (count - 1)] * len(outer)
    live_count = counts_ref[region_ref[0]]

    def one_tile(at, total):
        start = pl.multiple_of(at * LANE, LANE)
        lanes = pl.ds(start, LANE)
        if first:
            turned = target_ref[lanes, :].astype(jnp.float32).T

        def rows_of(c):
            return [ref[c : c + 16, lanes].astype(jnp.float32) for ref in (*own_refs, *other_refs)]

        def fold(square):
            return square[:8] + square[8:]

        to_target = [jnp.zeros((8, LANE), jnp.float32)] * (mine if first else 0)
        apart = [jnp.zeros((8, LANE), jnp.float32)] * len(pairs)
        for c in range(0, channels, 16):
            values = rows_of(c)
            for i in range(len(to_target)):
                to_target[i] = to_target[i] + fold((values[i] - turned[c : c + 16]) ** 2)
            for p, (i, j) in enumerate(pairs):
                apart[p] = apart[p] + fold((values[i] - values[j]) ** 2)
        live = start + lax.broadcasted_iota(jnp.int32, (1, LANE), 1) < live_count
        score = jnp.zeros((1, LANE), jnp.float32)

        def inverse(square):
            squared = jnp.sum(square, axis=0, keepdims=True) + EPSILON
            inv = lax.rsqrt(squared)
            return squared * inv, inv

        inv_target, inv_pair = [], []
        for square in to_target:
            dist, inv = inverse(square)
            score = score + dist
            inv_target.append(jnp.broadcast_to(inv, (8, LANE)))
        for square, share in zip(apart, shares):
            dist, inv = inverse(square)
            score = score - dist * share
            inv_pair.append(jnp.broadcast_to(inv * (1.0 / (count - 1)), (8, LANE)))
        for c in range(0, channels, 16):
            values = rows_of(c)
            halves = []
            for h in (0, 8):
                near = [v[h : h + 8] for v in values]
                rows = slice(c + h, c + h + 8)
                if first:
                    grads = [(near[i] - turned[rows]) * inv_target[i] for i in range(mine)]
                else:
                    grads = [old_refs[i][rows, lanes] for i in range(mine)]
                for p, (i, j) in enumerate(pairs):
                    term = (near[i] - near[j]) * inv_pair[p]
                    grads[i] = grads[i] - term
                    if j < mine:
                        grads[j] = grads[j] + term
                halves.append(grads)
            for i in range(mine):
                grad = jnp.concatenate([halves[0][i], halves[1][i]], axis=0)
                if last:
                    grad = jnp.where(live, grad, 0.0)
                grad_refs[i][c : c + 16, lanes] = grad.astype(grad_refs[i].dtype)
        return total + jnp.where(live, score, 0.0)

    score_ref[...] = old_score + lax.fori_loop(0, slots // LANE, one_tile, jnp.zeros((1, LANE), jnp.float32))


def backward_kernel(members, ranks, region_ref, rank_ref, w_two_ref, w_three_ref, score_ref, *refs):
    saved = [refs[6 * m : 6 * (m + 1)] for m in range(members)]
    refs = refs[6 * members :]
    d_one_refs, piece_refs, (d_two_ref, stage_ref) = refs[:members], refs[members:-2], refs[-2:]
    w_two, w_three = w_two_ref[...] * 0.5, w_three_ref[...] * 0.5
    hidden, slots = saved[0][1].shape
    bias_one = jnp.zeros((hidden, LANE), jnp.float32)
    bias_two = jnp.zeros((hidden, LANE), jnp.float32)
    g_one, g_two, g_three = 0.0, 0.0, 0.0

    def lane_sum(values):
        return sum(values[:, lo : lo + LANE] for lo, _ in split(values.shape[1], LANE))

    for m in range(members):
        mixed_ref, act_one_ref, slope_one_ref, act_two_ref, slope_two_ref, d_dec_ref = saved[m]
        for lo, size in split(slots, BACK_CHUNK):
            lanes = slice(lo, lo + size)
            back = nn_dot(w_three, d_dec_ref[:, lanes]) * slope_two_ref[:, lanes].astype(jnp.float32)
            bias_two = bias_two + lane_sum(back)
            d_two = back.astype(jnp.bfloat16)
            d_two_ref[m, :, lanes] = d_two
            back = nn_dot(w_two, d_two) * slope_one_ref[:, lanes].astype(jnp.float32)
            bias_one = bias_one + lane_sum(back)
            d_one_refs[m][:, lanes] = back.astype(jnp.bfloat16)
        g_three = g_three + nt_dot(act_two_ref[...], d_dec_ref[...])
        g_two = g_two + nt_dot(act_one_ref[...], d_two_ref[m])
        g_one = g_one + nt_dot(mixed_ref[...], d_one_refs[m][...])
    half = hidden // 2
    region = lax.broadcasted_iota(jnp.int32, (1, hidden), 1) == region_ref[0]
    tally = jnp.where(region, jnp.sum(score_ref[...]), 0.0)
    high = tally.astype(jnp.bfloat16).astype(jnp.float32)
    parts = [
        g_one,
        g_two,
        jnp.concatenate([g_three[:half], g_three[half:]], axis=1),
        jnp.sum(bias_one.T, axis=0, keepdims=True),
        jnp.sum(bias_two.T, axis=0, keepdims=True),
        high,
        tally - high,
    ]
    used = sum(part.shape[0] for part in parts)
    parts.append(jnp.zeros((ranks * stage_ref.shape[1] - used, hidden), jnp.float32))
    stage_ref[...] = jnp.concatenate(parts, axis=0).astype(stage_ref.dtype).reshape(stage_ref.shape)
    for i in range(ranks):
        piece_refs[i][...] = stage_ref[rank_ref[0] ^ i]


def edges_kernel(members, region_ref, table_ref, w_one_ref, *refs):
    d_one_refs, d_mixed_refs, (one_ref, other_ref) = refs[:members], refs[members : 2 * members], refs[2 * members :]
    ext = table_ref.shape[0]
    rows = jnp.concatenate([table_ref[rows, :] for rows in rim_starts(region_ref, ext)], axis=0)
    for m in range(members):
        d_mixed_refs[m][...] = nn_dot(w_one_ref[...], d_one_refs[m][...]).astype(jnp.bfloat16)
    width = one_ref.shape[2]
    grads = nt_dot(rows, jnp.concatenate([ref[...] for ref in d_mixed_refs], axis=0)).astype(jnp.bfloat16)
    for m in range(members):
        one_ref[m] = grads[:HALO, m * width : (m + 1) * width]
        other_ref[m] = grads[HALO:, m * width : (m + 1) * width]


def sum_kernel(count, *refs):
    for i in range(count):
        total = refs[i][...].astype(jnp.float32) + refs[count + i][...].astype(jnp.float32)
        refs[2 * count + i][...] = total.astype(refs[i].dtype)


def unpack_kernel(scale, rank_ref, *refs):
    *refs, stage_ref = refs
    ranks = stage_ref.shape[0]
    one_ref, b_one_ref, two_ref, b_two_ref, three_ref, tally_ref = refs[ranks:]
    for i in range(ranks):
        stage_ref[rank_ref[0] ^ i] = refs[i][...]
    width, hidden = one_ref.shape
    sums = stage_ref[...].reshape(-1, hidden).astype(jnp.float32)
    half, channels = hidden // 2, three_ref.shape[1]
    one_ref[...] = sums[:width]
    two_ref[...] = sums[width : width + hidden]
    base = width + hidden
    three_ref[:half] = sums[base : base + half, :channels]
    three_ref[half:] = sums[base : base + half, channels:]
    last = sums[base + half : base + half + 8]
    b_one_ref[...] = last[0:1]
    b_two_ref[...] = last[1:2]
    tally_ref[...] = (last[2:3] + last[3:4])[:, : tally_ref.shape[1]] * scale


def own_kernel(table_ref, *refs):
    *d_mixed_refs, own_ref = refs
    members, nodes, _ = own_ref.shape
    for m in range(members):
        own_ref[m] = nt_dot(table_ref[HALO : HALO + nodes, :], d_mixed_refs[m][...])


def finish_kernel(region_ref, own_ref, one_ref, other_ref, out_ref):
    nodes = own_ref.shape[1]
    out_ref[:, HALO : nodes - HALO] = own_ref[:, HALO : nodes - HALO].astype(jnp.bfloat16)
    for ref, rows in zip((one_ref, other_ref), rim_starts(region_ref, nodes)):
        out_ref[:, rows] = (own_ref[:, rows] + ref[...].astype(jnp.float32)).astype(jnp.bfloat16)


def exchanged(block, second):
    size = lax.axis_size("space")
    pairs = [(i, (i + 1) % size if i % 2 else (i - 1) % size) if second else (i, i ^ 1) for i in range(size)]
    return lax.ppermute(block, "space", pairs)


def swapped(block, axis, by):
    return lax.ppermute(block, axis, [(i, i ^ by) for i in range(lax.axis_size(axis))])


def per_device(latent, neighbours, weights, targets, counts, w_one, b_one, w_two, b_two, w_three):
    members, nodes, width = latent.shape
    slots, channels = targets.shape
    hidden = w_one.shape[1]
    ext = nodes + 2 * HALO
    region, regions = lax.axis_index("space"), lax.axis_size("space")
    rank, ranks = lax.axis_index("member"), lax.axis_size("member")
    share = slots // ranks
    bf16, f32 = jnp.bfloat16, jnp.float32
    shape = jax.ShapeDtypeStruct
    each = range(members)

    edge = shape((HALO, width), bf16)
    region_at = region[None].astype(jnp.int32)
    *rims, latent = kernel_call(
        rims_kernel, (edge, edge, shape(latent.shape, bf16)), flops=4 << 30, moved=3 * MIB, smem=1, operands=2
    )(region_at, latent)
    halo = [[exchanged(rims[0], False), exchanged(rims[1], True)]]
    rank_at = rank[None].astype(jnp.int32)

    table, part, *rims = kernel_call(
        table_kernel,
        (shape((ext, slots), bf16), shape((width, slots), f32)) + (edge,) * (2 * members - 2),
        flops=2 * width * nodes * slots,
        moved=12 * MIB,
        smem=3,
        operands=6,
    )(region_at, rank_at, counts, neighbours, weights, latent)
    halo += [[exchanged(rims[2 * m], False), exchanged(rims[2 * m + 1], True)] for m in range(members - 1)]

    saved_shape = shape((hidden, slots), bf16)
    mixed_shape = shape((width, slots), bf16)
    decoded_shape = shape((channels, slots), bf16)
    dense = width * hidden + hidden * hidden + hidden * channels
    saved, decoded, beside, across = [], [], [], []
    for m in each:
        *kept, block = kernel_call(
            lambda *refs: forward_kernel(m, *refs),
            (mixed_shape,) + (saved_shape,) * 4 + (decoded_shape,),
            flops=2 * slots * ((ext if m else 2 * HALO) * width + dense),
            moved=8 * MIB,
            smem=1,
            operands=10,
        )(region_at, latent if m else part, table, *halo[m], w_one, b_one[None], w_two, b_two[None], w_three)
        saved.append(kept)
        decoded.append(block)
        blocks, bit = {0: block}, 2
        while bit < ranks:
            blocks.update({i ^ bit: swapped(blocks[i], "member", bit) for i in sorted(blocks)})
            bit = 2 * bit
        across.append([blocks[i] for i in sorted(blocks) if i])
        beside.append(swapped(block, "member", 1))

    def scored(others, carried, first=False, last=False):
        operands = (region_at, counts, *decoded, *others, *carried)
        return kernel_call(
            lambda *refs: score_kernel(members, len(others), members * ranks, first, last, *refs),
            (shape((channels, slots), bf16 if last else f32),) * members + (shape((1, LANE), f32),),
            flops=4 * MIB,
            moved=2 * MIB,
            smem=2,
            operands=len(operands),
        )(*operands)

    carried = scored(beside + [block for blocks in across[:-1] for block in blocks], [targets], first=True)
    across[-1], carried = lax.optimization_barrier((across[-1], carried))
    others = [*across[-1]] + [swapped(block, "member", 1) for blocks in across for block in blocks]
    *grads, score = scored(others, carried, last=True)

    rows = -(-(width + hidden + hidden // 2 + 4) // (16 * ranks)) * 16
    piece = shape((rows, hidden), bf16)
    operands = [region_at, rank_at, w_two, w_three, score]
    for m in each:
        operands += [*saved[m], grads[m]]
    out = kernel_call(
        lambda *refs: backward_kernel(members, ranks, *refs),
        (saved_shape,) * members + (piece,) * ranks,
        flops=4 * members * slots * dense,
        moved=10 * MIB,
        scratch=(pltpu.VMEM((members, hidden, slots), bf16), pltpu.VMEM((ranks, rows, hidden), bf16)),
        smem=2,
        operands=len(operands),
    )(*operands)
    d_one, pieces = out[:members], out[members:]

    def summed(ones, others):
        return kernel_call(
            lambda *refs: sum_kernel(len(ones), *refs), (piece,) * len(ones), flops=MIB, moved=MIB, operands=2 * len(ones)
        )(*ones, *others)

    out = kernel_call(
        lambda *refs: edges_kernel(members, *refs),
        (mixed_shape,) * members + (shape((members, HALO, width), bf16),) * 2,
        flops=2 * members * slots * width * (hidden + 2 * HALO),
        moved=6 * MIB,
        smem=1,
        operands=3 + members,
    )(region_at, table, w_one, *d_one)
    d_mixed, rims = out[:members], out[members:]

    bit = 1
    while bit < ranks:
        received = [swapped(sent, "member", bit) for sent in pieces[1::2]]
        if bit == 1:
            received, rims = lax.optimization_barrier((received, rims))
        pieces = summed(pieces[::2], received)
        bit = 2 * bit
    own = kernel_call(
        own_kernel,
        shape((members, nodes, width), f32),
        flops=2 * members * nodes * width * slots,
        moved=6 * MIB,
        operands=1 + members,
    )(table, *d_mixed)
    other = exchanged(rims[1], True)
    (total,) = pieces
    step = 1
    while step < regions:
        received = swapped(total, "space", step)
        step = 2 * step
        if step == regions:
            received, other = lax.optimization_barrier((received, other))
        (total,) = summed([total], [received])
        if 2 * step == regions:
            total, own, rims = lax.optimization_barrier((total, own, rims))
            one = exchanged(rims[0], False)
    totals = {0: total}
    bit = 2
    while bit < ranks:
        totals.update({i ^ bit: swapped(totals[i], "member", bit) for i in sorted(totals)})
        bit = 2 * bit
    totals.update({i ^ 1: swapped(block, "member", 1) for i, block in totals.items()})
    latent_grad = kernel_call(
        finish_kernel,
        shape((members, nodes, width), bf16),
        flops=MIB,
        moved=3 * MIB,
        smem=1,
        operands=4,
    )(region_at, own, one, other)
    totals = [totals[i] for i in range(ranks)]
    totals, latent_grad = lax.optimization_barrier((totals, latent_grad))
    row = shape((1, hidden), f32)
    g_one, g_bone, g_two, g_btwo, g_three, tally = kernel_call(
        lambda *refs: unpack_kernel(1.0 / (OBS_MEAN * members * ranks), *refs),
        (shape((width, hidden), f32), row, shape((hidden, hidden), f32), row, shape((hidden, channels), f32),
         shape((1, regions), f32)),
        flops=MIB,
        moved=2 * MIB,
        scratch=(pltpu.VMEM((ranks, rows, hidden), bf16),),
        smem=1,
        operands=1 + ranks,
    )(rank_at, *totals)
    return (tally[0], latent_grad, g_one, g_bone[0], g_two, g_btwo[0], g_three)


def solution(mesh):
    in_specs = (
        P("member", ("groups", "space"), None),
        P(None, ("groups", "space")),
        P(None, ("groups", "space")),
        P(("groups", "space"), None),
        P("groups"),
        P(),
        P(),
        P(),
        P(),
        P(),
    )
    out_specs = (
        P("groups"),
        P("member", ("groups", "space"), None),
        P("groups", None),
        P("groups"),
        P("groups", None),
        P("groups"),
        P("groups", None),
    )
    return jax.shard_map(
        per_device, mesh=mesh, in_specs=in_specs, out_specs=out_specs, check_vma=False
    )
```
